32 devices in a mesh: dp: 4 (over x, core), blk: 8 (over z, y).
Axes of the slice: x: 2, y: 2, z: 4, core: 2. Of those that a mesh axis runs over, the one named last changes fastest.
Arguments:
- queries: bfloat16 [4, 1536, 512], P('dp', 'blk'), may hold values from -6 to 6, as said below
- key_in: bfloat16 [4, 1536, 512], P('dp', 'blk'), may hold values from -6 to 6, as said below
- value_in: bfloat16 [4, 1536, 512], P('dp', 'blk'), may hold values from -6 to 6
- out_weight: bfloat16 [512, 1024], replicated, may hold values from -2 to 2
- conv_kernel: float32 [31, 1024], replicated, may hold values from -1 to 1
- cotangent: bfloat16 [4, 1536, 1024], P('dp', 'blk'), may hold values from -6 to 6
Outputs:
- out_frames: bfloat16 [4, 1536, 1024], P('dp', 'blk')
- query_grad: bfloat16 [4, 1536, 512], P('dp', 'blk')
- key_grad: bfloat16 [4, 1536, 512], P('dp', 'blk')
- value_grad: bfloat16 [4, 1536, 512], P('dp', 'blk')
- weight_grad: float32 [512, 1024], replicated
- kernel_grad: float32 [31, 1024], replicated
The draws below stay inside these ranges and needn't reach their ends.
Inputs may be any that keep to these rules, and one draw needn't show every extreme that they name: `queries`: independent entries. `key_in`: independent entries.
All inputs are finite; a program needn't handle non-finite values.
Results may differ from the reference program's by a relative error of at most 0.024.
Values may be sent and summed in bfloat16 or wider, within the bound.
No kernel may reach another device: no remote copies, remote signals or barrier semaphores. Data moves between devices by JAX's collectives and lax.ppermute only.
A program may use at most 64 MiB of HBM per device.

```python
import math
import jax
import jax.numpy as jnp
from jax import lax

D = 1024
ATT_HEADS = 8
HEAD_DIM = 64
KW = 31
BLOCK = 96
CTX = 2
ATT = 512
SEQS = 4
FRAMES = 1536


def drawn_rows(key):
    base = jax.random.normal(key, (SEQS, FRAMES, ATT), jnp.float32)
    return jnp.clip(base, -6.0, 6.0)


def draw_queries(key, part):
    base = drawn_rows(jax.random.fold_in(key, 1))
    return base.astype(jnp.bfloat16)


def draw_key_in(key, part):
    base = drawn_rows(jax.random.fold_in(key, 2))
    return base.astype(jnp.bfloat16)


def levels(stream_key, dims, split, smallest, top_value):
    gain = 1.0
    for axis_at, parts in split:
        heights = jax.random.uniform(jax.random.fold_in(jax.random.fold_in(stream_key, 6), axis_at), (parts,), jnp.float32, smallest / len(split), top_value / len(split))
        gain = gain * jnp.repeat(jnp.exp(heights), dims[axis_at] // parts).reshape((-1,) + (1,) * (len(dims) - 1 - axis_at))
    return gain


def bell_draw(key, shape, width, reach, split=(), kind=jnp.bfloat16):
    drawn = width * jax.random.normal(key, shape, jnp.float32)
    if split:
        drawn = drawn * levels(key, shape, split, -0.22, 0.18)
    return jnp.clip(drawn, -reach, reach).astype(kind)


def setup_inputs(seed: int = 0) -> dict:
    seeds = jax.random.split(jax.random.key(seed), 7)
    queries = draw_queries(jax.random.fold_in(seeds[6], 71), 0)
    key_in = draw_key_in(jax.random.fold_in(seeds[6], 71), 0)
    value_in = bell_draw(seeds[2], (SEQS, FRAMES, ATT), 1.0, 6.0, ((0, 4), (1, 8)))
    out_weight = bell_draw(seeds[3], (ATT, D), (HEAD_DIM // 8) ** -0.5, 2.0)
    conv_kernel = bell_draw(seeds[4], (KW, D), KW ** -0.5, 1.0, (), jnp.float32)
    cotangent = bell_draw(seeds[5], (SEQS, FRAMES, D), 1.0, 6.0, ((0, 4), (1, 8)))
    return {"queries": queries, "key_in": key_in, "value_in": value_in, "out_weight": out_weight, "conv_kernel": conv_kernel, "cotangent": cotangent}


NEGATIVE = -1e+30

def rounded(field):
    return lax.optimization_barrier(field.astype(jnp.bfloat16)).astype(jnp.float32)

def window_scores(query_block, key_block, start, left_span, score_scale):
    pair_len = query_block.shape[0]
    query_pos = start + jnp.arange(pair_len, dtype=jnp.int32)
    key_pos = start - left_span + jnp.arange(left_span + pair_len, dtype=jnp.int32)
    distance = query_pos[:, None] - key_pos[None, :]
    visible = (distance >= 0) & (distance < left_span) & (key_pos[None, :] >= 0)
    scores = jnp.einsum('qhd,khd->hqk', query_block.astype(jnp.float32), key_block.astype(jnp.float32)) * score_scale
    return (jnp.where(visible[None], scores, NEGATIVE), visible[None])

def attend(queries, keys_seq, values_seq, left_span, score_scale):
    pair_len = 2 * BLOCK
    key_pad = jnp.pad(keys_seq, ((left_span, 0), (0, 0), (0, 0)))
    value_pad = jnp.pad(values_seq, ((left_span, 0), (0, 0), (0, 0)))

    def one_block(block_id):
        start = block_id * pair_len
        query_block = lax.dynamic_slice_in_dim(queries, start, pair_len, 0)
        key_block = lax.dynamic_slice_in_dim(key_pad, start, left_span + pair_len, 0)
        value_block = lax.dynamic_slice_in_dim(value_pad, start, left_span + pair_len, 0)
        scores, visible = window_scores(query_block, key_block, start, left_span, score_scale)
        row_max = lax.optimization_barrier(jnp.max(scores, axis=-1, keepdims=True))
        weights = jnp.where(visible, jnp.exp(scores - row_max), 0.0)
        row_sum = lax.optimization_barrier(jnp.sum(weights, axis=-1, keepdims=True))
        mixed = jnp.einsum('hqk,khd->hqd', rounded(weights), value_block.astype(jnp.float32)) / row_sum
        return (jnp.transpose(mixed, (1, 0, 2)).astype(jnp.bfloat16), (row_max + jnp.log(row_sum))[..., 0])
    attended, log_sums = lax.map(one_block, jnp.arange(FRAMES // pair_len, dtype=jnp.int32))
    return (attended.reshape(FRAMES, ATT_HEADS, HEAD_DIM), log_sums)

def attend_back(queries, keys_seq, values_seq, dattended, log_sums, deltas, left_span, score_scale):
    pair_len = 2 * BLOCK
    span_len = left_span + pair_len
    key_pad = jnp.pad(keys_seq, ((left_span, 0), (0, 0), (0, 0)))
    value_pad = jnp.pad(values_seq, ((left_span, 0), (0, 0), (0, 0)))
    zero_pad = jnp.zeros((FRAMES + left_span, ATT_HEADS, HEAD_DIM), jnp.float32)

    def one_block(carry, block_id):
        dkey_pad, dvalue_pad = carry
        start = block_id * pair_len
        query_block = lax.dynamic_slice_in_dim(queries, start, pair_len, 0).astype(jnp.float32)
        dout_block = lax.dynamic_slice_in_dim(dattended, start, pair_len, 0).astype(jnp.float32)
        key_block = lax.dynamic_slice_in_dim(key_pad, start, span_len, 0)
        value_block = lax.dynamic_slice_in_dim(value_pad, start, span_len, 0).astype(jnp.float32)
        scores, visible = window_scores(query_block, key_block, start, left_span, score_scale)
        probs = jnp.where(visible, jnp.exp(scores - log_sums[block_id][..., None]), 0.0)
        dvalue_block = jnp.einsum('hqk,qhd->khd', rounded(probs), dout_block)
        dprobs = jnp.einsum('qhd,khd->hqk', dout_block, value_block)
        dscores = rounded(probs * (dprobs - deltas[block_id][..., None]))
        dquery_block = jnp.einsum('hqk,khd->qhd', dscores, key_block.astype(jnp.float32)) * score_scale
        dkey_block = jnp.einsum('hqk,qhd->khd', dscores, query_block) * score_scale
        dkey_pad = lax.dynamic_update_slice_in_dim(dkey_pad, lax.dynamic_slice_in_dim(dkey_pad, start, span_len, 0) + dkey_block, start, 0)
        dvalue_pad = lax.dynamic_update_slice_in_dim(dvalue_pad, lax.dynamic_slice_in_dim(dvalue_pad, start, span_len, 0) + dvalue_block, start, 0)
        return ((dkey_pad, dvalue_pad), dquery_block.astype(jnp.bfloat16))
    (dkey_pad, dvalue_pad), dquery = lax.scan(one_block, (zero_pad, zero_pad), jnp.arange(FRAMES // pair_len, dtype=jnp.int32))
    return (dquery.reshape(FRAMES, ATT), dkey_pad[left_span:].astype(jnp.bfloat16).reshape(FRAMES, ATT), dvalue_pad[left_span:].astype(jnp.bfloat16).reshape(FRAMES, ATT))

def conv_forward(hidden, conv_kernel):
    hidden_pad = jnp.pad(hidden, ((KW - 1, 0), (0, 0)))

    def add_tap(tap_index, running):
        return running + conv_kernel[tap_index] * lax.dynamic_slice_in_dim(hidden_pad, KW - 1 - tap_index, FRAMES, 0)
    return (lax.fori_loop(0, KW, add_tap, jnp.zeros_like(hidden)), hidden_pad)

def conv_back(dmixed, hidden_pad, conv_kernel):
    dmixed_pad = jnp.pad(dmixed, ((0, KW - 1), (0, 0)))

    def add_tap(tap_index, running):
        return running + conv_kernel[tap_index] * lax.dynamic_slice_in_dim(dmixed_pad, tap_index, FRAMES, 0)
    dhidden = lax.fori_loop(0, KW, add_tap, jnp.zeros_like(dmixed))

    def kernel_tap(tap_index):
        return lax.optimization_barrier(jnp.sum(dmixed * lax.dynamic_slice_in_dim(hidden_pad, KW - 1 - tap_index, FRAMES, 0), axis=0))
    return (dhidden, lax.map(kernel_tap, jnp.arange(KW, dtype=jnp.int32)))

def reference(queries, key_in, value_in, out_weight, conv_kernel, cotangent):
    score_scale = 1.0 / math.sqrt(HEAD_DIM)
    left_span = CTX * 2 * BLOCK

    def one_sequence(items):
        query_seq, key_seq, value_seq, grad_seq = items
        query_nat = query_seq.reshape(FRAMES, ATT_HEADS, HEAD_DIM)
        key_nat = key_seq.reshape(FRAMES, ATT_HEADS, HEAD_DIM)
        value_nat = value_seq.reshape(FRAMES, ATT_HEADS, HEAD_DIM)
        attended, log_sums = attend(query_nat, key_nat, value_nat, left_span, score_scale)
        flat = attended.reshape(FRAMES, ATT)
        hidden = jnp.dot(flat, out_weight, preferred_element_type=jnp.float32).astype(jnp.bfloat16)
        mixed, hidden_pad = conv_forward(hidden.astype(jnp.float32), conv_kernel)
        sigma = jax.nn.sigmoid(mixed)
        out_nat = (mixed * sigma).astype(jnp.bfloat16)
        grad_nat = grad_seq.astype(jnp.float32)
        dmixed = grad_nat * sigma * (1.0 + mixed * (1.0 - sigma))
        dhidden, kernel_term = conv_back(dmixed, hidden_pad, conv_kernel)
        dhidden = dhidden.astype(jnp.bfloat16)
        dattended = jnp.dot(dhidden, out_weight.T, preferred_element_type=jnp.float32).astype(jnp.bfloat16)
        weight_term = jnp.dot(flat.T, dhidden, preferred_element_type=jnp.float32)
        dattended = dattended.reshape(FRAMES, ATT_HEADS, HEAD_DIM)
        delta_flat = jnp.einsum('qhd,qhd->hq', dattended.astype(jnp.float32), attended.astype(jnp.float32))
        deltas = jnp.transpose(delta_flat.reshape(ATT_HEADS, FRAMES // (2 * BLOCK), 2 * BLOCK), (1, 0, 2))
        dquery, dkey, dvalue = attend_back(query_nat, key_nat, value_nat, dattended, log_sums, deltas, left_span, score_scale)
        return (out_nat, dquery, dkey, dvalue, weight_term, kernel_term)
    results = lax.map(one_sequence, (queries, key_in, value_in, cotangent))
    return (results[0], results[1], results[2], results[3], lax.optimization_barrier(jnp.sum(results[4], axis=0)), lax.optimization_barrier(jnp.sum(results[5], axis=0)))
```

```python
import functools
import math

import jax
import jax.numpy as jnp
from jax import lax
from jax.experimental import pallas as pl
from jax.experimental.pallas import tpu as pltpu
from jax.sharding import PartitionSpec as P

HEAD_DIM = 64
CTX_MAX = 3
LANES = 128
NEGATIVE = -1e30
VMEM_LIMIT = 40 * 1024 * 1024

NN = (((1,), (0,)), ((), ()))
NT = (((1,), (1,)), ((), ()))
TN = (((0,), (0,)), ((), ()))


def dot(a, b, dims, precision=None):
    return lax.dot_general(a, b, dims, precision=precision, preferred_element_type=jnp.float32)


def shifted(x, by):
    devices = range(lax.axis_size("blk"))
    return lax.ppermute(x, "blk", [(i, i + by) for i in devices if i + by in devices])


def head_masks():
    lane = lax.broadcasted_iota(jnp.int32, (1, LANES), 1)
    first = jnp.where(lane < HEAD_DIM, 1.0, 0.0)
    return first.astype(jnp.bfloat16), (1.0 - first).astype(jnp.bfloat16)


def stack_heads(pair):
    first, second = head_masks()
    return jnp.concatenate([pair * first, pair * second], axis=0)


def merge_heads(stacked):
    rows = stacked.shape[0] // 2
    lane = lax.broadcasted_iota(jnp.int32, (rows, LANES), 1)
    return jnp.where(lane < HEAD_DIM, stacked[:rows], stacked[rows:])


def forward_kernel(context, rows, edge, taps, *refs):
    tiles = context + 1
    device_ref, q_ref, q_tail_ref = refs[:3]
    k_refs = refs[3 : 3 + tiles]
    v_refs = refs[3 + tiles : 3 + 2 * tiles]
    far_ref, near_ref, w_ref, conv_ref, cot_ref = refs[3 + 2 * tiles : 8 + 2 * tiles]
    out_ref, att_ref, lse_ref, dhid_ref, wpart_ref, kpart_ref = refs[8 + 2 * tiles : 14 + 2 * tiles]
    qx, kx, vx, ax, lx, hid, cotx, dm, bias = refs[14 + 2 * tiles :]

    att = q_ref.shape[1]
    width = w_ref.shape[1]
    span = context * rows
    query_rows = rows + 2 * edge
    block = LANES
    keys = span + block
    scale = 1.0 / math.sqrt(HEAD_DIM)
    start = device_ref[0] * rows

    qx[:edge] = q_tail_ref[...] * scale
    qx[edge : edge + rows] = q_ref[...] * scale
    qx[edge + rows :] = near_ref[2 * edge : 3 * edge] * scale
    for ext, own, far_at, near_at in ((kx, k_refs, 0, 0), (vx, v_refs, edge, edge)):
        ext[:edge] = far_ref[far_at : far_at + edge]
        for offset in range(tiles):
            first = edge + (context - offset) * rows
            ext[first : first + rows] = own[offset][...]
        ext[edge + span + rows :] = near_ref[near_at : near_at + edge]
    for chunk in range(width // LANES):
        columns = slice(chunk * LANES, (chunk + 1) * LANES)
        cotx[chunk, :rows] = cot_ref[:, columns].astype(jnp.float32)
        part, lane = divmod(chunk * LANES, att)
        cotx[chunk, rows:] = near_ref[
            (3 + part) * edge : (4 + part) * edge, lane : lane + LANES
        ].astype(jnp.float32)

    lane_id = lax.broadcasted_iota(jnp.int32, (block, LANES), 1)
    for b in range(query_rows // block):
        row_id = lax.broadcasted_iota(jnp.int32, (block, keys), 0)
        key_id = lax.broadcasted_iota(jnp.int32, (block, keys), 1)
        distance = row_id - key_id + span
        key_time = key_id + (start - edge - span + b * block)
        visible = (distance >= 0) & (distance < span) & (key_time >= 0)
        bias[...] = jnp.where(visible, 0.0, NEGATIVE)
        log_sums = jnp.zeros((block, LANES), jnp.float32)
        for pair in range(att // LANES):
            columns = slice(pair * LANES, (pair + 1) * LANES)
            qs = stack_heads(qx[b * block : (b + 1) * block, columns])
            kp = kx[b * block : b * block + keys, columns]
            vp = vx[b * block : b * block + keys, columns]
            scores = dot(qs, kp, NT)
            hidden_pairs = bias[...]
            scores = scores + jnp.concatenate([hidden_pairs, hidden_pairs], axis=0)
            row_max = jnp.max(scores, axis=1, keepdims=True)
            weights = jnp.exp(scores - row_max)
            row_sum = jnp.sum(weights, axis=1, keepdims=True)
            mixed = dot(weights.astype(jnp.bfloat16), vp, NN) / row_sum
            ax[b * block : (b + 1) * block, columns] = merge_heads(mixed).astype(jnp.bfloat16)
            log_sum = row_max + jnp.log(row_sum)
            log_sums = jnp.where(lane_id == 2 * pair, log_sum[:block], log_sums)
            log_sums = jnp.where(lane_id == 2 * pair + 1, log_sum[block:], log_sums)
        lx[b * block : (b + 1) * block] = log_sums
    att_ref[...] = ax[edge : edge + rows]
    lse_ref[...] = jnp.transpose(lx[...])[: lse_ref.shape[0], edge : edge + rows]

    step = 2 * LANES
    for part in range(width // step):
        product = dot(ax[...], w_ref[:, part * step : (part + 1) * step], NN)
        product = product.astype(jnp.bfloat16).astype(jnp.float32)
        time = lax.broadcasted_iota(jnp.int32, product.shape, 0) + (start - edge)
        product = jnp.where(time >= 0, product, 0.0)
        hid[2 * part] = product[:, :LANES]
        hid[2 * part + 1] = product[:, LANES:]

    def convolve(chunk, carry):
        columns = pl.ds(pl.multiple_of(chunk * LANES, LANES), LANES)
        mixed = jnp.zeros((rows + edge, LANES), jnp.float32)
        for tap in range(taps):
            mixed += conv_ref[tap : tap + 1, columns] * hid[chunk, edge - tap : 2 * edge + rows - tap]
        sigma = jax.nn.sigmoid(mixed)
        out_ref[:, columns] = (mixed * sigma)[:rows].astype(jnp.bfloat16)
        dm[...] = cotx[chunk] * sigma * (1.0 + mixed * (1.0 - sigma))
        dhidden = jnp.zeros((rows, LANES), jnp.float32)
        for tap in range(taps):
            dhidden += conv_ref[tap : tap + 1, columns] * dm[tap : tap + rows]
        dhid_ref[:, columns] = dhidden.astype(jnp.bfloat16)
        own = dm[:rows]
        for tap in range(taps):
            product = own * hid[chunk, edge - tap : edge + rows - tap]
            kpart_ref[tap : tap + 1, columns] = jnp.sum(product, axis=0, keepdims=True)
        return carry

    lax.fori_loop(0, width // LANES, convolve, 0)
    own = ax[edge : edge + rows]
    for part in range(width // step):
        columns = slice(part * step, (part + 1) * step)
        wpart_ref[:, columns] = dot(own, dhid_ref[:, columns], TN).astype(wpart_ref.dtype)


def backward_kernel(context, rows, *refs):
    tiles = context + 1
    device_ref, q_ref = refs[:2]
    k_refs = refs[2 : 2 + tiles]
    v_refs = refs[2 + tiles : 2 + 2 * tiles]
    att_ref, lse_ref, dhid_ref, w_ref = refs[2 + 2 * tiles : 6 + 2 * tiles]
    dq_ref, dk_ref, dv_ref = refs[6 + 2 * tiles : 9 + 2 * tiles]
    message_refs = refs[9 + 2 * tiles : 9 + 2 * tiles + context]
    datt, bias = refs[9 + 2 * tiles + context :]

    att = q_ref.shape[1]
    heads = att // HEAD_DIM
    span = context * rows
    scale = 1.0 / math.sqrt(HEAD_DIM)
    start = device_ref[0] * rows

    dattended = dot(dhid_ref[...], w_ref[...], NT).astype(jnp.bfloat16)
    datt[...] = dattended
    product = dattended.astype(jnp.float32) * att_ref[...].astype(jnp.float32)
    head_id = lax.broadcasted_iota(jnp.int32, (heads, att), 0)
    feature_id = lax.broadcasted_iota(jnp.int32, (heads, att), 1)
    ours = (feature_id >= head_id * HEAD_DIM) & (feature_id < (head_id + 1) * HEAD_DIM)
    deltas = dot(jnp.where(ours, 1.0, 0.0), product, NT, lax.Precision.HIGHEST)

    for offset in range(tiles):
        key_id = lax.broadcasted_iota(jnp.int32, (rows, rows), 0)
        row_id = lax.broadcasted_iota(jnp.int32, (rows, rows), 1)
        distance = row_id - key_id + offset * rows
        key_time = key_id + (start - offset * rows)
        visible = (distance >= 0) & (distance < span) & (key_time >= 0)
        bias[offset] = jnp.where(visible, 0.0, NEGATIVE)

    for pair in range(att // LANES):
        columns = slice(pair * LANES, (pair + 1) * LANES)
        qs = stack_heads(q_ref[:, columns] * scale)
        ds = stack_heads(datt[:, columns])
        log_sum = [lse_ref[2 * pair + i : 2 * pair + i + 1] for i in (0, 1)]
        delta = [deltas[2 * pair + i : 2 * pair + i + 1] for i in (0, 1)]
        log_sum = jnp.concatenate(log_sum, axis=1)
        delta = jnp.concatenate(delta, axis=1)
        dquery = jnp.zeros((2 * rows, LANES), jnp.float32)
        for offset in range(tiles):
            kp = k_refs[offset][:, columns]
            vp = v_refs[offset][:, columns]
            hidden_pairs = jnp.concatenate([bias[offset], bias[offset]], axis=1)
            probs = jnp.exp(dot(kp, qs, NT) + hidden_pairs - log_sum)
            dprobs = dot(vp, ds, NT)
            dscores = (probs * (dprobs - delta)).astype(jnp.bfloat16)
            dvalue = dot(probs.astype(jnp.bfloat16), ds, NN)
            dkey = dot(dscores, qs, NN)
            dquery += dot(dscores, kp, TN)
            if offset == 0:
                dk_ref[:, columns] = dkey
                dv_ref[:, columns] = dvalue
            else:
                message_refs[offset - 1][:rows, columns] = dkey.astype(jnp.bfloat16)
                message_refs[offset - 1][rows:, columns] = dvalue.astype(jnp.bfloat16)
        dq_ref[:, columns] = (merge_heads(dquery) * scale).astype(jnp.bfloat16)


def sum_weights(weight_part, kernel_part):
    weight = lax.psum(weight_part, ("dp", "blk"))
    kernel = lax.psum(kernel_part, ("dp", "blk"))
    return weight.astype(jnp.float32), kernel


def per_device(queries, key_in, value_in, out_weight, conv_kernel, cotangent):
    bf16, f32 = jnp.bfloat16, jnp.float32
    query, key, value, cot = queries[0], key_in[0], value_in[0], cotangent[0]
    runs = lax.axis_size("blk")
    device = lax.axis_index("blk").astype(jnp.int32)[None]
    rows, att = query.shape
    width = out_weight.shape[1]
    heads = att // HEAD_DIM
    taps = conv_kernel.shape[0]
    edge = -(-(taps - 1) // 16) * 16
    context = min(CTX_MAX, runs // 4)

    keys = [key] + [shifted(key, o) for o in range(1, context + 1)]
    values = [value] + [shifted(value, o) for o in range(1, context + 1)]
    query_tail = shifted(query[-edge:], 1)
    far = shifted(jnp.concatenate([key[-edge:], value[-edge:]]), context + 1)
    pieces = [key, value, query] + [cot[:, i : i + att] for i in range(0, width, att)]
    near = shifted(jnp.concatenate([piece[:edge] for piece in pieces]), -1)

    query_rows = rows + 2 * edge
    key_rows = query_rows + context * rows
    vmem = pl.BlockSpec(memory_space=pltpu.VMEM)
    smem = pl.BlockSpec(memory_space=pltpu.SMEM)
    params = pltpu.CompilerParams(vmem_limit_bytes=VMEM_LIMIT)
    out_frames, attended, log_sums, dhidden, weight_part, kernel_part = pl.pallas_call(
        functools.partial(forward_kernel, context, rows, edge, taps),
        out_shape=(
            jax.ShapeDtypeStruct((rows, width), bf16),
            jax.ShapeDtypeStruct((rows, att), bf16),
            jax.ShapeDtypeStruct((heads, rows), f32),
            jax.ShapeDtypeStruct((rows, width), bf16),
            jax.ShapeDtypeStruct((att, width), bf16),
            jax.ShapeDtypeStruct((taps, width), f32),
        ),
        in_specs=[smem] + [vmem] * (7 + 2 * (context + 1)),
        out_specs=(vmem,) * 6,
        scratch_shapes=[
            pltpu.VMEM((query_rows, att), bf16),
            pltpu.VMEM((key_rows, att), bf16),
            pltpu.VMEM((key_rows, att), bf16),
            pltpu.VMEM((query_rows, att), bf16),
            pltpu.VMEM((query_rows, LANES), f32),
            pltpu.VMEM((width // LANES, query_rows, LANES), f32),
            pltpu.VMEM((width // LANES, rows + edge, LANES), f32),
            pltpu.VMEM((rows + edge, LANES), f32),
            pltpu.VMEM((LANES, context * rows + LANES), f32),
        ],
        compiler_params=params,
        name="forward",
    )(device, query, query_tail, *keys, *values, far, near, out_weight, conv_kernel, cot)

    weight_total, kernel_total = sum_weights(weight_part, kernel_part)

    outs = pl.pallas_call(
        functools.partial(backward_kernel, context, rows),
        out_shape=(
            jax.ShapeDtypeStruct((rows, att), bf16),
            jax.ShapeDtypeStruct((rows, att), f32),
            jax.ShapeDtypeStruct((rows, att), f32),
        )
        + (jax.ShapeDtypeStruct((2 * rows, att), bf16),) * context,
        in_specs=[smem] + [vmem] * (5 + 2 * (context + 1)),
        out_specs=(vmem,) * (3 + context),
        scratch_shapes=[
            pltpu.VMEM((rows, att), bf16),
            pltpu.VMEM((context + 1, rows, rows), f32),
        ],
        compiler_params=params,
        name="backward",
    )(device, query, *keys, *values, attended, log_sums, dhidden, out_weight)
    query_grad, dkey, dvalue = outs[:3]
    for offset, message in enumerate(outs[3:], 1):
        arrived = shifted(message, -offset).astype(f32)
        dkey = dkey + arrived[:rows]
        dvalue = dvalue + arrived[rows:]
    key_grad = dkey.astype(bf16)
    value_grad = dvalue.astype(bf16)
    return (
        out_frames[None],
        query_grad[None],
        key_grad[None],
        value_grad[None],
        weight_total,
        kernel_total,
    )


def solution(mesh):
    frames = P("dp", "blk", None)
    return jax.shard_map(
        per_device,
        mesh=mesh,
        in_specs=(frames, frames, frames, P(), P(), frames),
        out_specs=(frames, frames, frames, frames, P(), P()),
        check_vma=False,
    )
```

```python
import functools
import math

import jax
import jax.numpy as jnp
from jax import lax
from jax.experimental import pallas as pl
from jax.experimental.pallas import tpu as pltpu
from jax.sharding import PartitionSpec as P

HEAD_DIM = 64
CTX_MAX = 3
LANES = 128
NEGATIVE = -1e30
VMEM_LIMIT = 40 * 1024 * 1024

NN = (((1,), (0,)), ((), ()))
NT = (((1,), (1,)), ((), ()))
TN = (((0,), (0,)), ((), ()))


def dot(a, b, dims, precision=None):
    return lax.dot_general(a, b, dims, precision=precision, preferred_element_type=jnp.float32)


def shifted(x, by):
    devices = range(lax.axis_size("blk"))
    return lax.ppermute(x, "blk", [(i, i + by) for i in devices if i + by in devices])


def head_masks():
    lane = lax.broadcasted_iota(jnp.int32, (1, LANES), 1)
    first = jnp.where(lane < HEAD_DIM, 1.0, 0.0)
    return first.astype(jnp.bfloat16), (1.0 - first).astype(jnp.bfloat16)


def stack_heads(pair):
    first, second = head_masks()
    return jnp.concatenate([pair * first, pair * second], axis=0)


def merge_heads(stacked):
    rows = stacked.shape[0] // 2
    lane = lax.broadcasted_iota(jnp.int32, (rows, LANES), 1)
    return jnp.where(lane < HEAD_DIM, stacked[:rows], stacked[rows:])


def pack_kernel(edge, k_ref, v_ref, q_ref, cot_ref, own_ref, far_ref, near_ref, sems):
    rows, att = k_ref.shape
    width = cot_ref.shape[1]
    head, tail = pl.ds(0, edge), pl.ds(rows - edge, edge)
    moves = [
        (k_ref, own_ref.at[pl.ds(0, rows)]),
        (v_ref, own_ref.at[pl.ds(rows, rows)]),
        (q_ref.at[tail], own_ref.at[pl.ds(2 * rows, edge)]),
        (k_ref.at[tail], far_ref.at[pl.ds(0, edge)]),
        (v_ref.at[tail], far_ref.at[pl.ds(edge, edge)]),
        (k_ref.at[head], near_ref.at[pl.ds(0, edge)]),
        (v_ref.at[head], near_ref.at[pl.ds(edge, edge)]),
        (q_ref.at[head], near_ref.at[pl.ds(2 * edge, edge)]),
    ]
    for part in range(width // att):
        piece = cot_ref.at[head, pl.ds(part * att, att)]
        moves.append((piece, near_ref.at[pl.ds((3 + part) * edge, edge)]))
    copies = [pltpu.make_async_copy(a, b, sems.at[i]) for i, (a, b) in enumerate(moves)]
    for copy in copies:
        copy.start()
    for copy in copies:
        copy.wait()


def forward_kernel(context, rows, edge, taps, *refs):
    tiles = context + 1
    device_ref, q_hbm = refs[:2]
    own_refs = refs[2 : 2 + tiles]
    far_ref, near_ref, w_hbm, conv_hbm, cot_hbm = refs[2 + tiles : 7 + tiles]
    out_ref, att_ref, lse_ref, dhid_ref, part_ref = refs[7 + tiles : 12 + tiles]
    qx, kx, vx, ax, lx, hid, cotx, dm, bias, kp = refs[12 + tiles : 22 + tiles]
    q_ref, w_ref, conv_ref, cot_ref, sems = refs[22 + tiles :]

    att = q_ref.shape[1]
    width = w_ref.shape[1]
    span = context * rows
    query_rows = rows + 2 * edge
    block = LANES
    keys = span + block
    scale = 1.0 / math.sqrt(HEAD_DIM)
    start = device_ref[0] * rows

    fetches = [
        pltpu.make_async_copy(source, target, sems.at[i])
        for i, (source, target) in enumerate(
            ((q_hbm, q_ref), (w_hbm, w_ref), (cot_hbm, cot_ref), (conv_hbm, conv_ref))
        )
    ]
    for fetch in fetches:
        fetch.start()

    for ext, own_at, far_at in ((kx, 0, 0), (vx, rows, edge)):
        ext[:edge] = far_ref[far_at : far_at + edge]
        for offset in range(tiles):
            first = edge + (context - offset) * rows
            ext[first : first + rows] = own_refs[offset][own_at : own_at + rows]
        ext[edge + span + rows :] = near_ref[far_at : far_at + edge]
    qx[:edge] = own_refs[1][2 * rows : 2 * rows + edge] * scale
    qx[edge + rows :] = near_ref[2 * edge : 3 * edge] * scale
    fetches[0].wait()
    qx[edge : edge + rows] = q_ref[...] * scale

    lane_id = lax.broadcasted_iota(jnp.int32, (block, LANES), 1)
    for b in range(query_rows // block):
        row_id = lax.broadcasted_iota(jnp.int32, (block, keys), 0)
        key_id = lax.broadcasted_iota(jnp.int32, (block, keys), 1)
        distance = row_id - key_id + span
        key_time = key_id + (start - edge - span + b * block)
        visible = (distance >= 0) & (distance < span) & (key_time >= 0)
        bias[...] = jnp.where(visible, 0.0, NEGATIVE)
        log_sums = jnp.zeros((block, LANES), jnp.float32)
        for pair in range(att // LANES):
            columns = slice(pair * LANES, (pair + 1) * LANES)
            qs = stack_heads(qx[b * block : (b + 1) * block, columns])
            kp_tile = kx[b * block : b * block + keys, columns]
            vp_tile = vx[b * block : b * block + keys, columns]
            scores = dot(qs, kp_tile, NT)
            hidden_pairs = bias[...]
            scores = scores + jnp.concatenate([hidden_pairs, hidden_pairs], axis=0)
            row_max = jnp.max(scores, axis=1, keepdims=True)
            weights = jnp.exp(scores - row_max)
            row_sum = jnp.sum(weights, axis=1, keepdims=True)
            mixed = dot(weights.astype(jnp.bfloat16), vp_tile, NN) / row_sum
            ax[b * block : (b + 1) * block, columns] = merge_heads(mixed).astype(jnp.bfloat16)
            log_sum = row_max + jnp.log(row_sum)
            log_sums = jnp.where(lane_id == 2 * pair, log_sum[:block], log_sums)
            log_sums = jnp.where(lane_id == 2 * pair + 1, log_sum[block:], log_sums)
        lx[b * block : (b + 1) * block] = log_sums
    att_ref[...] = ax[edge : edge + rows]
    lse_ref[...] = jnp.transpose(lx[...])[: lse_ref.shape[0], edge : edge + rows]

    fetches[1].wait()
    step = 2 * LANES
    for part in range(width // step):
        product = dot(ax[...], w_ref[:, part * step : (part + 1) * step], NN)
        product = product.astype(jnp.bfloat16).astype(jnp.float32)
        time = lax.broadcasted_iota(jnp.int32, product.shape, 0) + (start - edge)
        product = jnp.where(time >= 0, product, 0.0)
        hid[2 * part] = product[:, :LANES]
        hid[2 * part + 1] = product[:, LANES:]

    fetches[2].wait()
    fetches[3].wait()
    for chunk in range(width // LANES):
        columns = slice(chunk * LANES, (chunk + 1) * LANES)
        cotx[chunk, :rows] = cot_ref[:, columns].astype(jnp.float32)
        part, lane = divmod(chunk * LANES, att)
        cotx[chunk, rows:] = near_ref[
            (3 + part) * edge : (4 + part) * edge, lane : lane + LANES
        ].astype(jnp.float32)
    kp[...] = jnp.zeros_like(kp)

    def convolve(chunk, carry):
        columns = pl.ds(pl.multiple_of(chunk * LANES, LANES), LANES)
        mixed = jnp.zeros((rows + edge, LANES), jnp.float32)
        for tap in range(taps):
            mixed += conv_ref[tap : tap + 1, columns] * hid[chunk, edge - tap : 2 * edge + rows - tap]
        sigma = jax.nn.sigmoid(mixed)
        out_ref[:, columns] = (mixed * sigma)[:rows].astype(jnp.bfloat16)
        dm[...] = cotx[chunk] * sigma * (1.0 + mixed * (1.0 - sigma))
        dhidden = jnp.zeros((rows, LANES), jnp.float32)
        for tap in range(taps):
            dhidden += conv_ref[tap : tap + 1, columns] * dm[tap : tap + rows]
        dhid_ref[:, columns] = dhidden.astype(jnp.bfloat16)
        own = dm[:rows]
        for tap in range(taps):
            product = own * hid[chunk, edge - tap : edge + rows - tap]
            kp[chunk, tap : tap + 1] = jnp.sum(product, axis=0, keepdims=True)
        return carry

    lax.fori_loop(0, width // LANES, convolve, 0)

    pieces, piece_rows, _ = part_ref.shape
    chunks = width // LANES
    group = att // pieces
    own = ax[edge : edge + rows]
    for part in range(width // step):
        product = dot(own, dhid_ref[:, part * step : (part + 1) * step], TN).astype(jnp.bfloat16)
        for half in range(2):
            chunk = 2 * part + half
            tile = product[:, half * LANES : (half + 1) * LANES]
            for piece in range(pieces):
                part_ref[piece, chunk * group : (chunk + 1) * group] = tile[
                    piece * group : (piece + 1) * group
                ]
    rest = jnp.zeros((piece_rows - chunks * (group + 1), LANES), jnp.float32)
    for piece in range(pieces):
        row = [kp[chunk, piece : piece + 1] for chunk in range(chunks)]
        part_ref[piece, chunks * group :] = jnp.concatenate(row + [rest], axis=0).astype(
            jnp.bfloat16
        )


def unpack_kernel(total_ref, weight_ref, kernel_ref):
    pieces, piece_rows, _ = total_ref.shape
    att, width = weight_ref.shape
    taps = kernel_ref.shape[0]
    chunks = width // LANES
    group = att // pieces
    for piece in range(pieces):
        for chunk in range(chunks):
            weight_ref[
                piece * group : (piece + 1) * group, chunk * LANES : (chunk + 1) * LANES
            ] = total_ref[piece, chunk * group : (chunk + 1) * group].astype(jnp.float32)
        if piece < taps:
            rows = total_ref[piece, chunks * group :].astype(jnp.float32)
            for chunk in range(chunks):
                kernel_ref[piece : piece + 1, chunk * LANES : (chunk + 1) * LANES] = rows[
                    chunk : chunk + 1
                ]


def backward_kernel(context, rows, *refs):
    tiles = context + 1
    device_ref, q_ref = refs[:2]
    own_refs = refs[2 : 2 + tiles]
    att_ref, lse_ref, dhid_ref, w_ref = refs[2 + tiles : 6 + tiles]
    dq_ref, dk_ref, dv_ref = refs[6 + tiles : 9 + tiles]
    message_refs = refs[9 + tiles : 9 + tiles + context]
    datt, bias = refs[9 + tiles + context :]

    att = q_ref.shape[1]
    heads = att // HEAD_DIM
    span = context * rows
    scale = 1.0 / math.sqrt(HEAD_DIM)
    start = device_ref[0] * rows

    dattended = dot(dhid_ref[...], w_ref[...], NT).astype(jnp.bfloat16)
    datt[...] = dattended
    product = dattended.astype(jnp.float32) * att_ref[...].astype(jnp.float32)
    head_id = lax.broadcasted_iota(jnp.int32, (heads, att), 0)
    feature_id = lax.broadcasted_iota(jnp.int32, (heads, att), 1)
    ours = (feature_id >= head_id * HEAD_DIM) & (feature_id < (head_id + 1) * HEAD_DIM)
    deltas = dot(jnp.where(ours, 1.0, 0.0), product, NT, lax.Precision.HIGHEST)

    for offset in range(tiles):
        key_id = lax.broadcasted_iota(jnp.int32, (rows, rows), 0)
        row_id = lax.broadcasted_iota(jnp.int32, (rows, rows), 1)
        distance = row_id - key_id + offset * rows
        key_time = key_id + (start - offset * rows)
        visible = (distance >= 0) & (distance < span) & (key_time >= 0)
        bias[offset] = jnp.where(visible, 0.0, NEGATIVE)

    for pair in range(att // LANES):
        columns = slice(pair * LANES, (pair + 1) * LANES)
        qs = stack_heads(q_ref[:, columns] * scale)
        ds = stack_heads(datt[:, columns])
        log_sum = [lse_ref[2 * pair + i : 2 * pair + i + 1] for i in (0, 1)]
        delta = [deltas[2 * pair + i : 2 * pair + i + 1] for i in (0, 1)]
        log_sum = jnp.concatenate(log_sum, axis=1)
        delta = jnp.concatenate(delta, axis=1)
        dquery = jnp.zeros((2 * rows, LANES), jnp.float32)
        for offset in range(tiles):
            kp = own_refs[offset][:rows, columns]
            vp = own_refs[offset][rows : 2 * rows, columns]
            hidden_pairs = jnp.concatenate([bias[offset], bias[offset]], axis=1)
            probs = jnp.exp(dot(kp, qs, NT) + hidden_pairs - log_sum)
            dprobs = dot(vp, ds, NT)
            dscores = (probs * (dprobs - delta)).astype(jnp.bfloat16)
            dvalue = dot(probs.astype(jnp.bfloat16), ds, NN)
            dkey = dot(dscores, qs, NN)
            dquery += dot(dscores, kp, TN)
            if offset == 0:
                dk_ref[:, columns] = dkey
                dv_ref[:, columns] = dvalue
            else:
                message_refs[offset - 1][:rows, columns] = dkey.astype(jnp.bfloat16)
                message_refs[offset - 1][rows:, columns] = dvalue.astype(jnp.bfloat16)
        dq_ref[:, columns] = (merge_heads(dquery) * scale).astype(jnp.bfloat16)


def exchange(x, axis):
    return lax.all_to_all(x, axis, 0, 0, tiled=True)


def summed(x):
    return jnp.sum(x.astype(jnp.float32), axis=0).astype(x.dtype)


def sum_parts(parts):
    pieces, rows, lanes = parts.shape
    outer, inner = lax.axis_size("dp"), lax.axis_size("blk")
    if pieces != outer * inner:
        return lax.psum(parts, ("dp", "blk"))
    mine = summed(exchange(parts.reshape(outer, inner * rows, lanes), "dp"))
    mine = summed(exchange(mine.reshape(inner, rows, lanes), "blk"))
    mine = exchange(jnp.broadcast_to(mine, (inner, rows, lanes)), "blk")
    mine = mine.reshape(inner * rows, lanes)
    mine = exchange(jnp.broadcast_to(mine, (outer, inner * rows, lanes)), "dp")
    return mine.reshape(pieces, rows, lanes)


def per_device(queries, key_in, value_in, out_weight, conv_kernel, cotangent):
    bf16, f32 = jnp.bfloat16, jnp.float32
    query, key, value, cot = queries[0], key_in[0], value_in[0], cotangent[0]
    runs = lax.axis_size("blk")
    device = lax.axis_index("blk").astype(jnp.int32)[None]
    rows, att = query.shape
    width = out_weight.shape[1]
    heads = att // HEAD_DIM
    taps = conv_kernel.shape[0]
    edge = -(-(taps - 1) // 16) * 16
    context = min(CTX_MAX, runs // 4)

    query_rows = rows + 2 * edge
    key_rows = query_rows + context * rows
    chunks = width // LANES
    vmem = pl.BlockSpec(memory_space=pltpu.VMEM)
    smem = pl.BlockSpec(memory_space=pltpu.SMEM)
    hbm = pl.BlockSpec(memory_space=pltpu.HBM)
    params = pltpu.CompilerParams(vmem_limit_bytes=VMEM_LIMIT)

    own, far, near = pl.pallas_call(
        functools.partial(pack_kernel, edge),
        out_shape=(
            jax.ShapeDtypeStruct((2 * rows + edge, att), bf16),
            jax.ShapeDtypeStruct((2 * edge, att), bf16),
            jax.ShapeDtypeStruct(((3 + width // att) * edge, att), bf16),
        ),
        in_specs=[hbm] * 4,
        out_specs=(vmem,) * 3,
        scratch_shapes=[pltpu.SemaphoreType.DMA((8 + width // att,))],
        compiler_params=params,
        name="pack",
    )(key, value, query, cot)
    tiles = [own] + [shifted(own, o) for o in range(1, context + 1)]
    far = shifted(far, context + 1)
    near = shifted(near, -1)

    pieces = att // 16
    piece_rows = -(-(chunks * 16 + chunks) // 16) * 16
    out_frames, attended, log_sums, dhidden, parts = pl.pallas_call(
        functools.partial(forward_kernel, context, rows, edge, taps),
        out_shape=(
            jax.ShapeDtypeStruct((rows, width), bf16),
            jax.ShapeDtypeStruct((rows, att), bf16),
            jax.ShapeDtypeStruct((heads, rows), f32),
            jax.ShapeDtypeStruct((rows, width), bf16),
            jax.ShapeDtypeStruct((pieces, piece_rows, LANES), bf16),
        ),
        in_specs=[smem, hbm] + [vmem] * (3 + context) + [hbm] * 3,
        out_specs=(vmem,) * 5,
        scratch_shapes=[
            pltpu.VMEM((query_rows, att), bf16),
            pltpu.VMEM((key_rows, att), bf16),
            pltpu.VMEM((key_rows, att), bf16),
            pltpu.VMEM((query_rows, att), bf16),
            pltpu.VMEM((query_rows, LANES), f32),
            pltpu.VMEM((chunks, query_rows, LANES), f32),
            pltpu.VMEM((chunks, rows + edge, LANES), f32),
            pltpu.VMEM((rows + edge, LANES), f32),
            pltpu.VMEM((LANES, context * rows + LANES), f32),
            pltpu.VMEM((chunks, pieces, LANES), f32),
            pltpu.VMEM((rows, att), bf16),
            pltpu.VMEM((att, width), bf16),
            pltpu.VMEM((taps, width), f32),
            pltpu.VMEM((rows, width), bf16),
            pltpu.SemaphoreType.DMA((4,)),
        ],
        compiler_params=params,
        name="forward",
    )(device, query, *tiles, far, near, out_weight, conv_kernel, cot)

    weight_total, kernel_total = pl.pallas_call(
        unpack_kernel,
        out_shape=(
            jax.ShapeDtypeStruct((att, width), f32),
            jax.ShapeDtypeStruct((taps, width), f32),
        ),
        in_specs=[vmem],
        out_specs=(vmem, vmem),
        compiler_params=params,
        name="unpack",
    )(sum_parts(parts))

    outs = pl.pallas_call(
        functools.partial(backward_kernel, context, rows),
        out_shape=(
            jax.ShapeDtypeStruct((rows, att), bf16),
            jax.ShapeDtypeStruct((rows, att), f32),
            jax.ShapeDtypeStruct((rows, att), f32),
        )
        + (jax.ShapeDtypeStruct((2 * rows, att), bf16),) * context,
        in_specs=[smem] + [vmem] * (6 + context),
        out_specs=(vmem,) * (3 + context),
        scratch_shapes=[
            pltpu.VMEM((rows, att), bf16),
            pltpu.VMEM((context + 1, rows, rows), f32),
        ],
        compiler_params=params,
        name="backward",
    )(device, query, *tiles, attended, log_sums, dhidden, out_weight)
    query_grad, dkey, dvalue = outs[:3]
    for offset, message in enumerate(outs[3:], 1):
        arrived = shifted(message, -offset).astype(f32)
        dkey = dkey + arrived[:rows]
        dvalue = dvalue + arrived[rows:]
    key_grad = dkey.astype(bf16)
    value_grad = dvalue.astype(bf16)
    return (
        out_frames[None],
        query_grad[None],
        key_grad[None],
        value_grad[None],
        weight_total,
        kernel_total,
    )


def solution(mesh):
    frames = P("dp", "blk", None)
    return jax.shard_map(
        per_device,
        mesh=mesh,
        in_specs=(frames, frames, frames, P(), P(), frames),
        out_specs=(frames, frames, frames, frames, P(), P()),
        check_vma=False,
    )
```

```python
import functools
import math

import jax
import jax.numpy as jnp
from jax import lax
from jax.experimental import pallas as pl
from jax.experimental.pallas import tpu as pltpu
from jax.sharding import Mesh
from jax.sharding import PartitionSpec as P

HEAD_DIM = 64
CTX_MAX = 3
LANES = 128
NEGATIVE = -1e30
RUN_AXES = ("z", "y")
CHIP_AXES = ("x", "z", "y")
VMEM_LIMIT = 40 * 1024 * 1024

NN = (((1,), (0,)), ((), ()))
NT = (((1,), (1,)), ((), ()))
TN = (((0,), (0,)), ((), ()))


def dot(a, b, dims, precision=None):
    return lax.dot_general(a, b, dims, precision=precision, preferred_element_type=jnp.float32)


def shifted(x, by):
    devices = range(lax.axis_size(RUN_AXES))
    return lax.ppermute(x, RUN_AXES, [(i, i + by) for i in devices if i + by in devices])


def in_hbm(x):
    return pltpu.with_memory_space_constraint(x, pltpu.HBM)


def cost(flops, data):
    return pl.CostEstimate(flops=flops, bytes_accessed=data, transcendentals=0)


def head_masks():
    lane = lax.broadcasted_iota(jnp.int32, (1, LANES), 1)
    first = jnp.where(lane < HEAD_DIM, 1.0, 0.0)
    return first.astype(jnp.bfloat16), (1.0 - first).astype(jnp.bfloat16)


def stack_heads(pair):
    first, second = head_masks()
    return jnp.concatenate([pair * first, pair * second], axis=0)


def merge_heads(stacked):
    rows = stacked.shape[0] // 2
    lane = lax.broadcasted_iota(jnp.int32, (rows, LANES), 1)
    return jnp.where(lane < HEAD_DIM, stacked[:rows], stacked[rows:])


def pack_kernel(edge, k_ref, v_ref, q_ref, cot_ref, own_ref, far_ref, near_ref, sems):
    rows, att = k_ref.shape
    width = cot_ref.shape[1]
    head, tail = pl.ds(0, edge), pl.ds(rows - edge, edge)
    moves = [
        (k_ref, own_ref.at[pl.ds(0, rows)]),
        (v_ref, own_ref.at[pl.ds(rows, rows)]),
        (q_ref.at[tail], own_ref.at[pl.ds(2 * rows, edge)]),
        (k_ref.at[tail], far_ref.at[pl.ds(0, edge)]),
        (v_ref.at[tail], far_ref.at[pl.ds(edge, edge)]),
        (k_ref.at[head], near_ref.at[pl.ds(0, edge)]),
        (v_ref.at[head], near_ref.at[pl.ds(edge, edge)]),
        (q_ref.at[head], near_ref.at[pl.ds(2 * edge, edge)]),
    ]
    for part in range(width // att):
        piece = cot_ref.at[head, pl.ds(part * att, att)]
        moves.append((piece, near_ref.at[pl.ds((3 + part) * edge, edge)]))
    copies = [pltpu.make_async_copy(a, b, sems.at[i]) for i, (a, b) in enumerate(moves)]
    for copy in copies:
        copy.start()
    for copy in copies:
        copy.wait()


def forward_kernel(context, rows, edge, taps, *refs):
    tiles = context + 1
    device_ref, q_hbm = refs[:2]
    own_refs = refs[2 : 2 + tiles]
    far_ref, near_ref, w_hbm, conv_hbm, cot_hbm = refs[2 + tiles : 7 + tiles]
    out_ref, att_ref, lse_ref, dhid_ref, keep_ref, give_ref = refs[7 + tiles : 13 + tiles]
    qx, kx, vx, ax, lx, hid, cotx, dm, bias, kp, parts = refs[13 + tiles : 24 + tiles]
    q_ref, w_ref, conv_ref, cot_ref, sems = refs[24 + tiles :]

    att = q_ref.shape[1]
    width = w_ref.shape[1]
    span = context * rows
    query_rows = rows + 2 * edge
    block = LANES
    keys = span + block
    scale = 1.0 / math.sqrt(HEAD_DIM)
    start = device_ref[0] * rows

    fetches = [
        pltpu.make_async_copy(source, target, sems.at[i])
        for i, (source, target) in enumerate(
            ((q_hbm, q_ref), (w_hbm, w_ref), (cot_hbm, cot_ref), (conv_hbm, conv_ref))
        )
    ]
    for fetch in fetches:
        fetch.start()

    for ext, own_at, far_at in ((kx, 0, 0), (vx, rows, edge)):
        ext[:edge] = far_ref[far_at : far_at + edge]
        for offset in range(tiles):
            first = edge + (context - offset) * rows
            ext[first : first + rows] = own_refs[offset][own_at : own_at + rows]
        ext[edge + span + rows :] = near_ref[far_at : far_at + edge]
    qx[:edge] = own_refs[1][2 * rows : 2 * rows + edge] * scale
    qx[edge + rows :] = near_ref[2 * edge : 3 * edge] * scale
    fetches[0].wait()
    qx[edge : edge + rows] = q_ref[...] * scale

    lane_id = lax.broadcasted_iota(jnp.int32, (block, LANES), 1)
    for b in range(query_rows // block):
        row_id = lax.broadcasted_iota(jnp.int32, (block, keys), 0)
        key_id = lax.broadcasted_iota(jnp.int32, (block, keys), 1)
        distance = row_id - key_id + span
        key_time = key_id + (start - edge - span + b * block)
        visible = (distance >= 0) & (distance < span) & (key_time >= 0)
        bias[...] = jnp.where(visible, 0.0, NEGATIVE)
        log_sums = jnp.zeros((block, LANES), jnp.float32)
        for pair in range(att // LANES):
            columns = slice(pair * LANES, (pair + 1) * LANES)
            qs = stack_heads(qx[b * block : (b + 1) * block, columns])
            kp_tile = kx[b * block : b * block + keys, columns]
            vp_tile = vx[b * block : b * block + keys, columns]
            scores = dot(qs, kp_tile, NT)
            hidden_pairs = bias[...]
            scores = scores + jnp.concatenate([hidden_pairs, hidden_pairs], axis=0)
            row_max = jnp.max(scores, axis=1, keepdims=True)
            weights = jnp.exp(scores - row_max)
            row_sum = jnp.sum(weights, axis=1, keepdims=True)
            mixed = dot(weights.astype(jnp.bfloat16), vp_tile, NN) / row_sum
            ax[b * block : (b + 1) * block, columns] = merge_heads(mixed).astype(jnp.bfloat16)
            log_sum = row_max + jnp.log(row_sum)
            log_sums = jnp.where(lane_id == 2 * pair, log_sum[:block], log_sums)
            log_sums = jnp.where(lane_id == 2 * pair + 1, log_sum[block:], log_sums)
        lx[b * block : (b + 1) * block] = log_sums
    att_ref[...] = ax[edge : edge + rows]
    lse_ref[...] = jnp.transpose(lx[...])[: lse_ref.shape[0], edge : edge + rows]

    fetches[1].wait()
    step = 2 * LANES
    for part in range(width // step):
        product = dot(ax[...], w_ref[:, part * step : (part + 1) * step], NN)
        product = product.astype(jnp.bfloat16).astype(jnp.float32)
        time = lax.broadcasted_iota(jnp.int32, product.shape, 0) + (start - edge)
        product = jnp.where(time >= 0, product, 0.0)
        hid[2 * part] = product[:, :LANES]
        hid[2 * part + 1] = product[:, LANES:]

    fetches[2].wait()
    fetches[3].wait()
    for chunk in range(width // LANES):
        columns = slice(chunk * LANES, (chunk + 1) * LANES)
        cotx[chunk, :rows] = cot_ref[:, columns].astype(jnp.float32)
        part, lane = divmod(chunk * LANES, att)
        cotx[chunk, rows:] = near_ref[
            (3 + part) * edge : (4 + part) * edge, lane : lane + LANES
        ].astype(jnp.float32)
    kp[...] = jnp.zeros_like(kp)

    def convolve(chunk, carry):
        columns = pl.ds(pl.multiple_of(chunk * LANES, LANES), LANES)
        mixed = jnp.zeros((rows + edge, LANES), jnp.float32)
        for tap in range(taps):
            mixed += conv_ref[tap : tap + 1, columns] * hid[chunk, edge - tap : 2 * edge + rows - tap]
        sigma = jax.nn.sigmoid(mixed)
        out_ref[:, columns] = (mixed * sigma)[:rows].astype(jnp.bfloat16)
        dm[...] = cotx[chunk] * sigma * (1.0 + mixed * (1.0 - sigma))
        dhidden = jnp.zeros((rows, LANES), jnp.float32)
        for tap in range(taps):
            dhidden += conv_ref[tap : tap + 1, columns] * dm[tap : tap + rows]
        dhid_ref[:, columns] = dhidden.astype(jnp.bfloat16)
        own = dm[:rows]
        for tap in range(taps):
            product = own * hid[chunk, edge - tap : edge + rows - tap]
            kp[chunk, tap : tap + 1] = jnp.sum(product, axis=0, keepdims=True)
        return carry

    lax.fori_loop(0, width // LANES, convolve, 0)

    _, pieces, piece_rows, _ = parts.shape
    chunks = width // LANES
    group = att // (2 * pieces)
    core = device_ref[1]
    own = ax[edge : edge + rows]
    for part in range(width // step):
        product = dot(own, dhid_ref[:, part * step : (part + 1) * step], TN).astype(jnp.bfloat16)
        for chunk in (2 * part, 2 * part + 1):
            tile = product[:, (chunk - 2 * part) * LANES : (chunk - 2 * part + 1) * LANES]
            for half in range(2):
                for piece in range(pieces):
                    first = (half * pieces + piece) * group
                    parts[half, piece, chunk * group : (chunk + 1) * group] = tile[
                        first : first + group
                    ]
    rest = jnp.zeros((piece_rows - chunks * (group + 1), LANES), jnp.float32)
    for half in range(2):
        for piece in range(pieces):
            tap = half * pieces + piece
            row = [kp[chunk, tap : tap + 1] for chunk in range(chunks)]
            row = jnp.concatenate(row + [rest], axis=0).astype(jnp.bfloat16)
            parts[half, piece, chunks * group :] = row
    keep_ref[...] = parts[core]
    give_ref[...] = parts[1 - core]


def unpack_kernel(device_ref, near_ref, far_ref, weight_ref, kernel_ref):
    pieces, piece_rows, _ = near_ref.shape
    att, width = weight_ref.shape
    taps = kernel_ref.shape[0]
    chunks = width // LANES
    group = att // (2 * pieces)
    core = device_ref[1]

    def write(refs):
        for half, ref in enumerate(refs):
            for piece in range(pieces):
                tap = half * pieces + piece
                for chunk in range(chunks):
                    columns = slice(chunk * LANES, (chunk + 1) * LANES)
                    tile = ref[piece, chunk * group : (chunk + 1) * group].astype(jnp.float32)
                    weight_ref[tap * group : (tap + 1) * group, columns] = tile
                if tap < taps:
                    row = ref[piece, chunks * group :].astype(jnp.float32)
                    for chunk in range(chunks):
                        columns = slice(chunk * LANES, (chunk + 1) * LANES)
                        kernel_ref[tap : tap + 1, columns] = row[chunk : chunk + 1]

    pl.when(core == 0)(lambda: write((near_ref, far_ref)))
    pl.when(core != 0)(lambda: write((far_ref, near_ref)))


def backward_kernel(context, rows, *refs):
    tiles = context + 1
    device_ref, q_ref = refs[:2]
    own_refs = refs[2 : 2 + tiles]
    att_ref, lse_ref, dhid_ref, w_ref = refs[2 + tiles : 6 + tiles]
    dq_ref, dk_ref, dv_ref = refs[6 + tiles : 9 + tiles]
    message_refs = refs[9 + tiles : 9 + tiles + context]
    datt, bias = refs[9 + tiles + context :]

    att = q_ref.shape[1]
    heads = att // HEAD_DIM
    span = context * rows
    scale = 1.0 / math.sqrt(HEAD_DIM)
    start = device_ref[0] * rows

    dattended = dot(dhid_ref[...], w_ref[...], NT).astype(jnp.bfloat16)
    datt[...] = dattended
    product = dattended.astype(jnp.float32) * att_ref[...].astype(jnp.float32)
    head_id = lax.broadcasted_iota(jnp.int32, (heads, att), 0)
    feature_id = lax.broadcasted_iota(jnp.int32, (heads, att), 1)
    ours = (feature_id >= head_id * HEAD_DIM) & (feature_id < (head_id + 1) * HEAD_DIM)
    deltas = dot(jnp.where(ours, 1.0, 0.0), product, NT, lax.Precision.HIGHEST)

    for offset in range(tiles):
        key_id = lax.broadcasted_iota(jnp.int32, (rows, rows), 0)
        row_id = lax.broadcasted_iota(jnp.int32, (rows, rows), 1)
        distance = row_id - key_id + offset * rows
        key_time = key_id + (start - offset * rows)
        visible = (distance >= 0) & (distance < span) & (key_time >= 0)
        bias[offset] = jnp.where(visible, 0.0, NEGATIVE)

    for pair in range(att // LANES):
        columns = slice(pair * LANES, (pair + 1) * LANES)
        qs = stack_heads(q_ref[:, columns] * scale)
        ds = stack_heads(datt[:, columns])
        log_sum = [lse_ref[2 * pair + i : 2 * pair + i + 1] for i in (0, 1)]
        delta = [deltas[2 * pair + i : 2 * pair + i + 1] for i in (0, 1)]
        log_sum = jnp.concatenate(log_sum, axis=1)
        delta = jnp.concatenate(delta, axis=1)
        dquery = jnp.zeros((2 * rows, LANES), jnp.float32)
        for offset in range(tiles):
            kp = own_refs[offset][:rows, columns]
            vp = own_refs[offset][rows : 2 * rows, columns]
            hidden_pairs = jnp.concatenate([bias[offset], bias[offset]], axis=1)
            probs = jnp.exp(dot(kp, qs, NT) + hidden_pairs - log_sum)
            dprobs = dot(vp, ds, NT)
            dscores = (probs * (dprobs - delta)).astype(jnp.bfloat16)
            dvalue = dot(probs.astype(jnp.bfloat16), ds, NN)
            dkey = dot(dscores, qs, NN)
            dquery += dot(dscores, kp, TN)
            if offset == 0:
                dk_ref[:, columns] = dkey
                dv_ref[:, columns] = dvalue
            else:
                message_refs[offset - 1][:rows, columns] = dkey.astype(jnp.bfloat16)
                message_refs[offset - 1][rows:, columns] = dvalue.astype(jnp.bfloat16)
        dq_ref[:, columns] = (merge_heads(dquery) * scale).astype(jnp.bfloat16)


def exchange(x):
    return lax.all_to_all(x, CHIP_AXES, 0, 0, tiled=True)


def other_core(x):
    return lax.ppermute(x, "core", [(0, 1), (1, 0)])


def per_device(queries, key_in, value_in, out_weight, conv_kernel, cotangent):
    bf16, f32 = jnp.bfloat16, jnp.float32
    query, key, value, cot = queries[0], key_in[0], value_in[0], cotangent[0]
    runs = lax.axis_size(RUN_AXES)
    device = lax.axis_index(RUN_AXES).astype(jnp.int32)
    rows, att = query.shape
    width = out_weight.shape[1]
    heads = att // HEAD_DIM
    taps = conv_kernel.shape[0]
    edge = -(-(taps - 1) // 16) * 16
    context = min(CTX_MAX, runs // 4)

    query_rows = rows + 2 * edge
    key_rows = query_rows + context * rows
    chunks = width // LANES
    vmem = pl.BlockSpec(memory_space=pltpu.VMEM)
    smem = pl.BlockSpec(memory_space=pltpu.SMEM)
    hbm = pl.BlockSpec(memory_space=pltpu.HBM)
    params = pltpu.CompilerParams(vmem_limit_bytes=VMEM_LIMIT)

    own, far, near = pl.pallas_call(
        functools.partial(pack_kernel, edge),
        out_shape=(
            jax.ShapeDtypeStruct((2 * rows + edge, att), bf16),
            jax.ShapeDtypeStruct((2 * edge, att), bf16),
            jax.ShapeDtypeStruct(((3 + width // att) * edge, att), bf16),
        ),
        in_specs=[hbm] * 4,
        out_specs=(vmem,) * 3,
        scratch_shapes=[pltpu.SemaphoreType.DMA((8 + width // att,))],
        compiler_params=params,
        name="pack",
    )(in_hbm(key), in_hbm(value), in_hbm(query), in_hbm(cot))
    tiles = [own] + [shifted(own, o) for o in range(1, context + 1)]
    far = shifted(far, context + 1)
    near = shifted(near, -1)

    pieces = att // 32
    split = pieces == lax.axis_size(CHIP_AXES)
    core = lax.axis_index("core").astype(jnp.int32) if split else jnp.int32(0)
    place = jnp.stack([device, core])
    piece_rows = -(-(chunks * 16 + chunks) // 16) * 16
    out_frames, attended, log_sums, dhidden, keep, give = pl.pallas_call(
        functools.partial(forward_kernel, context, rows, edge, taps),
        out_shape=(
            jax.ShapeDtypeStruct((rows, width), bf16),
            jax.ShapeDtypeStruct((rows, att), bf16),
            jax.ShapeDtypeStruct((heads, rows), f32),
            jax.ShapeDtypeStruct((rows, width), bf16),
        )
        + (jax.ShapeDtypeStruct((pieces, piece_rows, LANES), bf16),) * 2,
        in_specs=[smem, hbm] + [vmem] * (3 + context) + [hbm] * 3,
        out_specs=(vmem,) * 6,
        scratch_shapes=[
            pltpu.VMEM((query_rows, att), bf16),
            pltpu.VMEM((key_rows, att), bf16),
            pltpu.VMEM((key_rows, att), bf16),
            pltpu.VMEM((query_rows, att), bf16),
            pltpu.VMEM((query_rows, LANES), f32),
            pltpu.VMEM((chunks, query_rows, LANES), f32),
            pltpu.VMEM((chunks, rows + edge, LANES), f32),
            pltpu.VMEM((rows + edge, LANES), f32),
            pltpu.VMEM((LANES, context * rows + LANES), f32),
            pltpu.VMEM((chunks, 2 * pieces, LANES), f32),
            pltpu.VMEM((2, pieces, piece_rows, LANES), bf16),
            pltpu.VMEM((rows, att), bf16),
            pltpu.VMEM((att, width), bf16),
            pltpu.VMEM((taps, width), f32),
            pltpu.VMEM((rows, width), bf16),
            pltpu.SemaphoreType.DMA((4,)),
        ],
        compiler_params=params,
        cost_estimate=cost(8 * 10**9, 10**7),
        name="forward",
    )(place, in_hbm(query), *tiles, far, near, in_hbm(out_weight), in_hbm(conv_kernel), in_hbm(cot))

    outs = pl.pallas_call(
        functools.partial(backward_kernel, context, rows),
        out_shape=(
            jax.ShapeDtypeStruct((rows, att), bf16),
            jax.ShapeDtypeStruct((rows, att), f32),
            jax.ShapeDtypeStruct((rows, att), f32),
        )
        + (jax.ShapeDtypeStruct((2 * rows, att), bf16),) * context,
        in_specs=[smem] + [vmem] * (6 + context),
        out_specs=(vmem,) * (3 + context),
        scratch_shapes=[
            pltpu.VMEM((rows, att), bf16),
            pltpu.VMEM((context + 1, rows, rows), f32),
        ],
        compiler_params=params,
        cost_estimate=cost(5 * 10**9, 10**7),
        name="backward",
    )(place, query, *tiles, attended, log_sums, dhidden, out_weight)
    query_grad, dkey, dvalue = outs[:3]
    messages = outs[3:]
    if split:
        mine = (keep.astype(f32) + other_core(give).astype(f32)).astype(bf16)
        mine, *messages = lax.optimization_barrier((mine, *messages))
        mine = jnp.sum(exchange(mine).astype(f32), axis=0).astype(bf16)
        mine = exchange(jnp.broadcast_to(mine, keep.shape))
        halves = (mine, other_core(mine))
    else:
        halves = lax.psum((keep, give), ("x", "core", "z", "y"))
    for offset, message in enumerate(messages, 1):
        arrived = shifted(message, -offset).astype(f32)
        dkey = dkey + arrived[:rows]
        dvalue = dvalue + arrived[rows:]
    weight_total, kernel_total = pl.pallas_call(
        unpack_kernel,
        out_shape=(
            jax.ShapeDtypeStruct((att, width), f32),
            jax.ShapeDtypeStruct((taps, width), f32),
        ),
        in_specs=[smem, vmem, vmem],
        out_specs=(vmem, vmem),
        compiler_params=params,
        name="unpack",
    )(place, *halves)
    key_grad = dkey.astype(bf16)
    value_grad = dvalue.astype(bf16)
    return (
        out_frames[None],
        query_grad[None],
        key_grad[None],
        value_grad[None],
        weight_total,
        kernel_total,
    )


def solution(mesh):
    sizes = (mesh.shape["dp"] // 2, 2, mesh.shape["blk"] // 2, 2)
    fine = Mesh(mesh.devices.reshape(sizes), ("x", "core", "z", "y"))
    frames = P(("x", "core"), RUN_AXES, None)
    return jax.shard_map(
        per_device,
        mesh=fine,
        in_specs=(frames, frames, frames, P(), P(), frames),
        out_specs=(frames, frames, frames, frames, P(), P()),
        check_vma=False,
    )
```

```python
import functools
import math

import jax
import jax.numpy as jnp
from jax import lax
from jax.experimental import pallas as pl
from jax.experimental.pallas import tpu as pltpu
from jax.sharding import Mesh
from jax.sharding import PartitionSpec as P

HEAD_DIM = 64
CTX_MAX = 3
LANES = 128
NEGATIVE = -1e30
RUN_AXES = ("z", "y")
PLANE_AXES = ("x", "y")
CHIP_AXES = ("x", "y", "z")
VMEM_LIMIT = 40 * 1024 * 1024

NN = (((1,), (0,)), ((), ()))
NT = (((1,), (1,)), ((), ()))
TN = (((0,), (0,)), ((), ()))


def dot(a, b, dims, precision=None):
    return lax.dot_general(a, b, dims, precision=precision, preferred_element_type=jnp.float32)


def shifted(x, by):
    devices = range(lax.axis_size(RUN_AXES))
    return lax.ppermute(x, RUN_AXES, [(i, i + by) for i in devices if i + by in devices])


def in_hbm(x):
    return pltpu.with_memory_space_constraint(x, pltpu.HBM)


def cost(flops, data):
    return pl.CostEstimate(flops=flops, bytes_accessed=data, transcendentals=0)


def head_masks():
    lane = lax.broadcasted_iota(jnp.int32, (1, LANES), 1)
    first = jnp.where(lane < HEAD_DIM, 1.0, 0.0)
    return first.astype(jnp.bfloat16), (1.0 - first).astype(jnp.bfloat16)


def stack_heads(pair):
    first, second = head_masks()
    return jnp.concatenate([pair * first, pair * second], axis=0)


def merge_heads(stacked):
    rows = stacked.shape[0] // 2
    lane = lax.broadcasted_iota(jnp.int32, (rows, LANES), 1)
    return jnp.where(lane < HEAD_DIM, stacked[:rows], stacked[rows:])


def pack_kernel(edge, k_ref, v_ref, q_ref, cot_ref, own_ref, far_ref, near_ref, sems):
    rows, att = k_ref.shape
    width = cot_ref.shape[1]
    head, tail = pl.ds(0, edge), pl.ds(rows - edge, edge)
    moves = [
        (k_ref, own_ref.at[pl.ds(0, rows)]),
        (v_ref, own_ref.at[pl.ds(rows, rows)]),
        (q_ref.at[tail], own_ref.at[pl.ds(2 * rows, edge)]),
        (k_ref.at[tail], far_ref.at[pl.ds(0, edge)]),
        (v_ref.at[tail], far_ref.at[pl.ds(edge, edge)]),
        (k_ref.at[head], near_ref.at[pl.ds(0, edge)]),
        (v_ref.at[head], near_ref.at[pl.ds(edge, edge)]),
        (q_ref.at[head], near_ref.at[pl.ds(2 * edge, edge)]),
    ]
    for part in range(width // att):
        piece = cot_ref.at[head, pl.ds(part * att, att)]
        moves.append((piece, near_ref.at[pl.ds((3 + part) * edge, edge)]))
    copies = [pltpu.make_async_copy(a, b, sems.at[i]) for i, (a, b) in enumerate(moves)]
    for copy in copies:
        copy.start()
    for copy in copies:
        copy.wait()


def forward_kernel(context, rows, edge, taps, *refs):
    tiles = context + 1
    device_ref, q_hbm = refs[:2]
    own_refs = refs[2 : 2 + tiles]
    far_ref, near_ref, w_hbm, conv_hbm, cot_hbm = refs[2 + tiles : 7 + tiles]
    out_ref, att_ref, lse_ref, dhid_ref, keep_ref, give_ref = refs[7 + tiles : 13 + tiles]
    qx, kx, vx, ax, lx, hid, cotx, dm, bias, kp, parts = refs[13 + tiles : 24 + tiles]
    q_ref, w_ref, conv_ref, cot_ref, sems = refs[24 + tiles :]

    att = q_ref.shape[1]
    width = w_ref.shape[1]
    span = context * rows
    query_rows = rows + 2 * edge
    block = LANES
    keys = span + block
    scale = 1.0 / math.sqrt(HEAD_DIM)
    start = device_ref[0] * rows

    fetches = [
        pltpu.make_async_copy(source, target, sems.at[i])
        for i, (source, target) in enumerate(
            ((q_hbm, q_ref), (w_hbm, w_ref), (cot_hbm, cot_ref), (conv_hbm, conv_ref))
        )
    ]
    for fetch in fetches:
        fetch.start()

    for ext, own_at, far_at in ((kx, 0, 0), (vx, rows, edge)):
        ext[:edge] = far_ref[far_at : far_at + edge]
        for offset in range(tiles):
            first = edge + (context - offset) * rows
            ext[first : first + rows] = own_refs[offset][own_at : own_at + rows]
        ext[edge + span + rows :] = near_ref[far_at : far_at + edge]
    qx[:edge] = own_refs[1][2 * rows : 2 * rows + edge] * scale
    qx[edge + rows :] = near_ref[2 * edge : 3 * edge] * scale
    fetches[0].wait()
    qx[edge : edge + rows] = q_ref[...] * scale

    lane_id = lax.broadcasted_iota(jnp.int32, (block, LANES), 1)
    for b in range(query_rows // block):
        row_id = lax.broadcasted_iota(jnp.int32, (block, keys), 0)
        key_id = lax.broadcasted_iota(jnp.int32, (block, keys), 1)
        distance = row_id - key_id + span
        key_time = key_id + (start - edge - span + b * block)
        visible = (distance >= 0) & (distance < span) & (key_time >= 0)
        bias[...] = jnp.where(visible, 0.0, NEGATIVE)
        log_sums = jnp.zeros((block, LANES), jnp.float32)
        for pair in range(att // LANES):
            columns = slice(pair * LANES, (pair + 1) * LANES)
            qs = stack_heads(qx[b * block : (b + 1) * block, columns])
            kp_tile = kx[b * block : b * block + keys, columns]
            vp_tile = vx[b * block : b * block + keys, columns]
            scores = dot(qs, kp_tile, NT)
            hidden_pairs = bias[...]
            scores = scores + jnp.concatenate([hidden_pairs, hidden_pairs], axis=0)
            row_max = jnp.max(scores, axis=1, keepdims=True)
            weights = jnp.exp(scores - row_max)
            row_sum = jnp.sum(weights, axis=1, keepdims=True)
            mixed = dot(weights.astype(jnp.bfloat16), vp_tile, NN) / row_sum
            ax[b * block : (b + 1) * block, columns] = merge_heads(mixed).astype(jnp.bfloat16)
            log_sum = row_max + jnp.log(row_sum)
            log_sums = jnp.where(lane_id == 2 * pair, log_sum[:block], log_sums)
            log_sums = jnp.where(lane_id == 2 * pair + 1, log_sum[block:], log_sums)
        lx[b * block : (b + 1) * block] = log_sums
    att_ref[...] = ax[edge : edge + rows]
    lse_ref[...] = jnp.transpose(lx[...])[: lse_ref.shape[0], edge : edge + rows]

    fetches[1].wait()
    step = 2 * LANES
    for part in range(width // step):
        product = dot(ax[...], w_ref[:, part * step : (part + 1) * step], NN)
        product = product.astype(jnp.bfloat16).astype(jnp.float32)
        time = lax.broadcasted_iota(jnp.int32, product.shape, 0) + (start - edge)
        product = jnp.where(time >= 0, product, 0.0)
        hid[2 * part] = product[:, :LANES]
        hid[2 * part + 1] = product[:, LANES:]

    fetches[2].wait()
    fetches[3].wait()
    for chunk in range(width // LANES):
        columns = slice(chunk * LANES, (chunk + 1) * LANES)
        cotx[chunk, :rows] = cot_ref[:, columns].astype(jnp.float32)
        part, lane = divmod(chunk * LANES, att)
        cotx[chunk, rows:] = near_ref[
            (3 + part) * edge : (4 + part) * edge, lane : lane + LANES
        ].astype(jnp.float32)
    kp[...] = jnp.zeros_like(kp)

    def convolve(chunk, carry):
        columns = pl.ds(pl.multiple_of(chunk * LANES, LANES), LANES)
        mixed = jnp.zeros((rows + edge, LANES), jnp.float32)
        for tap in range(taps):
            mixed += conv_ref[tap : tap + 1, columns] * hid[chunk, edge - tap : 2 * edge + rows - tap]
        sigma = jax.nn.sigmoid(mixed)
        out_ref[:, columns] = (mixed * sigma)[:rows].astype(jnp.bfloat16)
        dm[...] = cotx[chunk] * sigma * (1.0 + mixed * (1.0 - sigma))
        dhidden = jnp.zeros((rows, LANES), jnp.float32)
        for tap in range(taps):
            dhidden += conv_ref[tap : tap + 1, columns] * dm[tap : tap + rows]
        dhid_ref[:, columns] = dhidden.astype(jnp.bfloat16)
        own = dm[:rows]
        for tap in range(taps):
            product = own * hid[chunk, edge - tap : edge + rows - tap]
            kp[chunk, tap : tap + 1] = jnp.sum(product, axis=0, keepdims=True)
        return carry

    lax.fori_loop(0, width // LANES, convolve, 0)

    _, pieces, piece_rows, _ = parts.shape
    chunks = width // LANES
    group = att // (2 * pieces)
    core = device_ref[1]
    own = ax[edge : edge + rows]
    for part in range(width // step):
        product = dot(own, dhid_ref[:, part * step : (part + 1) * step], TN).astype(jnp.bfloat16)
        for chunk in (2 * part, 2 * part + 1):
            tile = product[:, (chunk - 2 * part) * LANES : (chunk - 2 * part + 1) * LANES]
            for half in range(2):
                for piece in range(pieces):
                    first = (half * pieces + piece) * group
                    parts[half, piece, chunk * group : (chunk + 1) * group] = tile[
                        first : first + group
                    ]
    rest = jnp.zeros((piece_rows - chunks * (group + 1), LANES), jnp.float32)
    for half in range(2):
        for piece in range(pieces):
            tap = half * pieces + piece
            row = [kp[chunk, tap : tap + 1] for chunk in range(chunks)]
            row = jnp.concatenate(row + [rest], axis=0).astype(jnp.bfloat16)
            parts[half, piece, chunks * group :] = row
    keep_ref[...] = parts[core]
    give_ref[...] = parts[1 - core]


def unpack_kernel(device_ref, near_ref, far_ref, weight_ref, kernel_ref):
    pieces, piece_rows, _ = near_ref.shape
    att, width = weight_ref.shape
    taps = kernel_ref.shape[0]
    chunks = width // LANES
    group = att // (2 * pieces)
    core = device_ref[1]

    def write(refs):
        for half, ref in enumerate(refs):
            for piece in range(pieces):
                tap = half * pieces + piece
                for chunk in range(chunks):
                    columns = slice(chunk * LANES, (chunk + 1) * LANES)
                    tile = ref[piece, chunk * group : (chunk + 1) * group].astype(jnp.float32)
                    weight_ref[tap * group : (tap + 1) * group, columns] = tile
                if tap < taps:
                    row = ref[piece, chunks * group :].astype(jnp.float32)
                    for chunk in range(chunks):
                        columns = slice(chunk * LANES, (chunk + 1) * LANES)
                        kernel_ref[tap : tap + 1, columns] = row[chunk : chunk + 1]

    pl.when(core == 0)(lambda: write((near_ref, far_ref)))
    pl.when(core != 0)(lambda: write((far_ref, near_ref)))


def backward_kernel(context, rows, *refs):
    tiles = context + 1
    device_ref, q_ref = refs[:2]
    own_refs = refs[2 : 2 + tiles]
    att_ref, lse_ref, dhid_ref, w_ref = refs[2 + tiles : 6 + tiles]
    dq_ref, own_ref = refs[6 + tiles : 8 + tiles]
    message_refs = refs[8 + tiles : 8 + tiles + context]
    datt, bias = refs[8 + tiles + context :]

    att = q_ref.shape[1]
    heads = att // HEAD_DIM
    span = context * rows
    scale = 1.0 / math.sqrt(HEAD_DIM)
    start = device_ref[0] * rows

    dattended = dot(dhid_ref[...], w_ref[...], NT).astype(jnp.bfloat16)
    datt[...] = dattended
    product = dattended.astype(jnp.float32) * att_ref[...].astype(jnp.float32)
    head_id = lax.broadcasted_iota(jnp.int32, (heads, att), 0)
    feature_id = lax.broadcasted_iota(jnp.int32, (heads, att), 1)
    ours = (feature_id >= head_id * HEAD_DIM) & (feature_id < (head_id + 1) * HEAD_DIM)
    deltas = dot(jnp.where(ours, 1.0, 0.0), product, NT, lax.Precision.HIGHEST)

    for offset in range(tiles):
        key_id = lax.broadcasted_iota(jnp.int32, (rows, rows), 0)
        row_id = lax.broadcasted_iota(jnp.int32, (rows, rows), 1)
        distance = row_id - key_id + offset * rows
        key_time = key_id + (start - offset * rows)
        visible = (distance >= 0) & (distance < span) & (key_time >= 0)
        bias[offset] = jnp.where(visible, 0.0, NEGATIVE)

    for pair in range(att // LANES):
        columns = slice(pair * LANES, (pair + 1) * LANES)
        qs = stack_heads(q_ref[:, columns] * scale)
        ds = stack_heads(datt[:, columns])
        log_sum = [lse_ref[2 * pair + i : 2 * pair + i + 1] for i in (0, 1)]
        delta = [deltas[2 * pair + i : 2 * pair + i + 1] for i in (0, 1)]
        log_sum = jnp.concatenate(log_sum, axis=1)
        delta = jnp.concatenate(delta, axis=1)
        dquery = jnp.zeros((2 * rows, LANES), jnp.float32)
        for offset in range(tiles):
            kp = own_refs[offset][:rows, columns]
            vp = own_refs[offset][rows : 2 * rows, columns]
            hidden_pairs = jnp.concatenate([bias[offset], bias[offset]], axis=1)
            probs = jnp.exp(dot(kp, qs, NT) + hidden_pairs - log_sum)
            dprobs = dot(vp, ds, NT)
            dscores = (probs * (dprobs - delta)).astype(jnp.bfloat16)
            dvalue = dot(probs.astype(jnp.bfloat16), ds, NN)
            dkey = dot(dscores, qs, NN)
            dquery += dot(dscores, kp, TN)
            target = message_refs[offset - 1] if offset else own_ref
            target[:rows, columns] = dkey.astype(target.dtype)
            target[rows:, columns] = dvalue.astype(target.dtype)
        dq_ref[:, columns] = (merge_heads(dquery) * scale).astype(jnp.bfloat16)


def merge_kernel(*refs):
    own_ref, *message_refs, dk_ref, dv_ref = refs
    rows = dk_ref.shape[0]
    total = own_ref[...]
    for message_ref in message_refs:
        total += message_ref[...].astype(jnp.float32)
    total = total.astype(jnp.bfloat16)
    dk_ref[...] = total[:rows]
    dv_ref[...] = total[rows:]


def exchange(x, axes):
    return lax.all_to_all(x, axes, 0, 0, tiled=True)


def collected(x, axes):
    parts = lax.axis_size(axes)
    x = exchange(x.reshape(parts, -1, LANES), axes)
    return jnp.sum(x.astype(jnp.float32), axis=0).astype(x.dtype)


def other_core(x):
    return lax.ppermute(x, "core", [(0, 1), (1, 0)])


def per_device(queries, key_in, value_in, out_weight, conv_kernel, cotangent):
    bf16, f32 = jnp.bfloat16, jnp.float32
    query, key, value, cot = queries[0], key_in[0], value_in[0], cotangent[0]
    runs = lax.axis_size(RUN_AXES)
    device = lax.axis_index(RUN_AXES).astype(jnp.int32)
    rows, att = query.shape
    width = out_weight.shape[1]
    heads = att // HEAD_DIM
    taps = conv_kernel.shape[0]
    edge = -(-(taps - 1) // 16) * 16
    context = min(CTX_MAX, runs // 4)

    query_rows = rows + 2 * edge
    key_rows = query_rows + context * rows
    chunks = width // LANES
    vmem = pl.BlockSpec(memory_space=pltpu.VMEM)
    smem = pl.BlockSpec(memory_space=pltpu.SMEM)
    hbm = pl.BlockSpec(memory_space=pltpu.HBM)
    params = pltpu.CompilerParams(vmem_limit_bytes=VMEM_LIMIT)

    own, far, near = pl.pallas_call(
        functools.partial(pack_kernel, edge),
        out_shape=(
            jax.ShapeDtypeStruct((2 * rows + edge, att), bf16),
            jax.ShapeDtypeStruct((2 * edge, att), bf16),
            jax.ShapeDtypeStruct(((3 + width // att) * edge, att), bf16),
        ),
        in_specs=[hbm] * 4,
        out_specs=(vmem,) * 3,
        scratch_shapes=[pltpu.SemaphoreType.DMA((8 + width // att,))],
        compiler_params=params,
        name="pack",
    )(in_hbm(key), in_hbm(value), in_hbm(query), in_hbm(cot))
    tiles = [own] + [shifted(own, o) for o in range(1, context + 1)]
    far = shifted(far, context + 1)
    near = shifted(near, -1)

    pieces = att // 32
    split = pieces == lax.axis_size(CHIP_AXES)
    core = lax.axis_index("core").astype(jnp.int32) if split else jnp.int32(0)
    place = jnp.stack([device, core])
    piece_rows = -(-(chunks * 16 + chunks) // 16) * 16
    out_frames, attended, log_sums, dhidden, keep, give = pl.pallas_call(
        functools.partial(forward_kernel, context, rows, edge, taps),
        out_shape=(
            jax.ShapeDtypeStruct((rows, width), bf16),
            jax.ShapeDtypeStruct((rows, att), bf16),
            jax.ShapeDtypeStruct((heads, rows), f32),
            jax.ShapeDtypeStruct((rows, width), bf16),
        )
        + (jax.ShapeDtypeStruct((pieces, piece_rows, LANES), bf16),) * 2,
        in_specs=[smem, hbm] + [vmem] * (3 + context) + [hbm] * 3,
        out_specs=(vmem,) * 6,
        scratch_shapes=[
            pltpu.VMEM((query_rows, att), bf16),
            pltpu.VMEM((key_rows, att), bf16),
            pltpu.VMEM((key_rows, att), bf16),
            pltpu.VMEM((query_rows, att), bf16),
            pltpu.VMEM((query_rows, LANES), f32),
            pltpu.VMEM((chunks, query_rows, LANES), f32),
            pltpu.VMEM((chunks, rows + edge, LANES), f32),
            pltpu.VMEM((rows + edge, LANES), f32),
            pltpu.VMEM((LANES, context * rows + LANES), f32),
            pltpu.VMEM((chunks, 2 * pieces, LANES), f32),
            pltpu.VMEM((2, pieces, piece_rows, LANES), bf16),
            pltpu.VMEM((rows, att), bf16),
            pltpu.VMEM((att, width), bf16),
            pltpu.VMEM((taps, width), f32),
            pltpu.VMEM((rows, width), bf16),
            pltpu.SemaphoreType.DMA((4,)),
        ],
        compiler_params=params,
        cost_estimate=cost(8 * 10**9, 10**7),
        name="forward",
    )(place, in_hbm(query), *tiles, far, near, in_hbm(out_weight), in_hbm(conv_kernel), in_hbm(cot))

    if split:
        mine = (keep.astype(f32) + other_core(give).astype(f32)).astype(bf16)
        mine, dhidden = lax.optimization_barrier((mine, dhidden))
    query_grad, own_grads, *messages = pl.pallas_call(
        functools.partial(backward_kernel, context, rows),
        out_shape=(
            jax.ShapeDtypeStruct((rows, att), bf16),
            jax.ShapeDtypeStruct((2 * rows, att), f32),
        )
        + (jax.ShapeDtypeStruct((2 * rows, att), bf16),) * context,
        in_specs=[smem] + [vmem] * (6 + context),
        out_specs=(vmem,) * (2 + context),
        scratch_shapes=[
            pltpu.VMEM((rows, att), bf16),
            pltpu.VMEM((context + 1, rows, rows), f32),
        ],
        compiler_params=params,
        cost_estimate=cost(6 * 10**9, 10**7),
        name="backward",
    )(place, query, *tiles, attended, log_sums, dhidden, out_weight)
    messages = [shifted(message, -offset) for offset, message in enumerate(messages, 1)]
    if split:
        mine = collected(collected(mine, PLANE_AXES), "z")
        mine, *messages = lax.optimization_barrier((mine, *messages))
        mine = exchange(jnp.broadcast_to(mine, keep.shape), CHIP_AXES)
        halves = (mine, other_core(mine))
    else:
        halves = lax.psum((keep, give), ("x", "core", "z", "y"))
    key_grad, value_grad = pl.pallas_call(
        merge_kernel,
        out_shape=(jax.ShapeDtypeStruct((rows, att), bf16),) * 2,
        in_specs=[vmem] * (1 + context),
        out_specs=(vmem,) * 2,
        compiler_params=params,
        name="merge",
    )(own_grads, *messages)
    weight_total, kernel_total = pl.pallas_call(
        unpack_kernel,
        out_shape=(
            jax.ShapeDtypeStruct((att, width), f32),
            jax.ShapeDtypeStruct((taps, width), f32),
        ),
        in_specs=[smem, vmem, vmem],
        out_specs=(vmem, vmem),
        compiler_params=params,
        name="unpack",
    )(place, *halves)
    return (
        out_frames[None],
        query_grad[None],
        key_grad[None],
        value_grad[None],
        weight_total,
        kernel_total,
    )


def solution(mesh):
    sizes = (mesh.shape["dp"] // 2, 2, mesh.shape["blk"] // 2, 2)
    fine = Mesh(mesh.devices.reshape(sizes), ("x", "core", "z", "y"))
    frames = P(("x", "core"), RUN_AXES, None)
    return jax.shard_map(
        per_device,
        mesh=fine,
        in_specs=(frames, frames, frames, P(), P(), frames),
        out_specs=(frames, frames, frames, frames, P(), P()),
        check_vma=False,
    )
```

```python
import functools
import math

import jax
import jax.numpy as jnp
from jax import lax
from jax.experimental import pallas as pl
from jax.experimental.pallas import tpu as pltpu
from jax.sharding import Mesh
from jax.sharding import PartitionSpec as P

HEAD_DIM = 64
CTX_MAX = 3
LANES = 128
SUBLANES = 8
NEGATIVE = -1e30
RUN_AXES = ("z", "y")
PLANE_AXES = ("x", "y")
VMEM_LIMIT = 40 * 1024 * 1024

NN = (((1,), (0,)), ((), ()))
NT = (((1,), (1,)), ((), ()))
TN = (((0,), (0,)), ((), ()))


def dot(a, b, dims, precision=None):
    return lax.dot_general(a, b, dims, precision=precision, preferred_element_type=jnp.float32)


def shifted(x, by):
    devices = range(lax.axis_size(RUN_AXES))
    return lax.ppermute(x, RUN_AXES, [(i, i + by) for i in devices if i + by in devices])


def in_hbm(x):
    return pltpu.with_memory_space_constraint(x, pltpu.HBM)


def cost(flops, data):
    return pl.CostEstimate(flops=flops, bytes_accessed=data, transcendentals=0)


def head_masks():
    lane = lax.broadcasted_iota(jnp.int32, (1, LANES), 1)
    first = jnp.where(lane < HEAD_DIM, 1.0, 0.0)
    return first.astype(jnp.bfloat16), (1.0 - first).astype(jnp.bfloat16)


def stack_heads(pair):
    first, second = head_masks()
    return jnp.concatenate([pair * first, pair * second], axis=0)


def merge_heads(stacked):
    rows = stacked.shape[0] // 2
    lane = lax.broadcasted_iota(jnp.int32, (rows, LANES), 1)
    return jnp.where(lane < HEAD_DIM, stacked[:rows], stacked[rows:])


def pack_kernel(edge, k_ref, v_ref, q_ref, cot_ref, own_ref, far_ref, near_ref, sems):
    rows, att = k_ref.shape
    width = cot_ref.shape[1]
    head, tail = pl.ds(0, edge), pl.ds(rows - edge, edge)
    moves = [
        (k_ref, own_ref.at[pl.ds(0, rows)]),
        (v_ref, own_ref.at[pl.ds(rows, rows)]),
        (q_ref.at[tail], own_ref.at[pl.ds(2 * rows, edge)]),
        (k_ref.at[tail], far_ref.at[pl.ds(0, edge)]),
        (v_ref.at[tail], far_ref.at[pl.ds(edge, edge)]),
        (k_ref.at[head], near_ref.at[pl.ds(0, edge)]),
        (v_ref.at[head], near_ref.at[pl.ds(edge, edge)]),
        (q_ref.at[head], near_ref.at[pl.ds(2 * edge, edge)]),
    ]
    for part in range(width // att):
        piece = cot_ref.at[head, pl.ds(part * att, att)]
        moves.append((piece, near_ref.at[pl.ds((3 + part) * edge, edge)]))
    copies = [pltpu.make_async_copy(a, b, sems.at[i]) for i, (a, b) in enumerate(moves)]
    for copy in copies:
        copy.start()
    for copy in copies:
        copy.wait()


def forward_kernel(context, rows, edge, taps, *refs):
    tiles = context + 1
    device_ref, q_hbm = refs[:2]
    own_refs = refs[2 : 2 + tiles]
    far_ref, near_ref, w_hbm, conv_hbm, cot_hbm = refs[2 + tiles : 7 + tiles]
    out_ref, att_ref, lse_ref, dhid_ref, keep_ref, give_ref = refs[7 + tiles : 13 + tiles]
    q_ref, w_ref = refs[13 + tiles : 15 + tiles]
    qx, kx, vx, ax, lx, hid, cotx, dm, bias, kp, ks, parts = refs[15 + tiles : 27 + tiles]
    conv_ref, cot_ref, sems = refs[27 + tiles :]

    att = q_ref.shape[1]
    width = w_ref.shape[1]
    span = context * rows
    query_rows = rows + 2 * edge
    block = LANES
    keys = span + block
    scale = 1.0 / math.sqrt(HEAD_DIM)
    start = device_ref[0] * rows

    fetches = [
        pltpu.make_async_copy(source, target, sems.at[i])
        for i, (source, target) in enumerate(
            ((q_hbm, q_ref), (w_hbm, w_ref), (cot_hbm, cot_ref), (conv_hbm, conv_ref))
        )
    ]
    for fetch in fetches:
        fetch.start()

    for ext, own_at, far_at in ((kx, 0, 0), (vx, rows, edge)):
        ext[:edge] = far_ref[far_at : far_at + edge]
        for offset in range(tiles):
            first = edge + (context - offset) * rows
            ext[first : first + rows] = own_refs[offset][own_at : own_at + rows]
        ext[edge + span + rows :] = near_ref[far_at : far_at + edge]
    qx[:edge] = own_refs[1][2 * rows : 2 * rows + edge] * scale
    qx[edge + rows :] = near_ref[2 * edge : 3 * edge] * scale
    fetches[0].wait()
    qx[edge : edge + rows] = q_ref[...] * scale

    lane_id = lax.broadcasted_iota(jnp.int32, (block, LANES), 1)
    for b in range(query_rows // block):
        row_id = lax.broadcasted_iota(jnp.int32, (block, keys), 0)
        key_id = lax.broadcasted_iota(jnp.int32, (block, keys), 1)
        distance = row_id - key_id + span
        key_time = key_id + (start - edge - span + b * block)
        visible = (distance >= 0) & (distance < span) & (key_time >= 0)
        bias[...] = jnp.where(visible, 0.0, NEGATIVE)
        log_sums = jnp.zeros((block, LANES), jnp.float32)
        for pair in range(att // LANES):
            columns = slice(pair * LANES, (pair + 1) * LANES)
            qs = stack_heads(qx[b * block : (b + 1) * block, columns])
            kp_tile = kx[b * block : b * block + keys, columns]
            vp_tile = vx[b * block : b * block + keys, columns]
            scores = dot(qs, kp_tile, NT)
            hidden_pairs = bias[...]
            scores = scores + jnp.concatenate([hidden_pairs, hidden_pairs], axis=0)
            row_max = jnp.max(scores, axis=1, keepdims=True)
            weights = jnp.exp(scores - row_max)
            row_sum = jnp.sum(weights, axis=1, keepdims=True)
            mixed = dot(weights.astype(jnp.bfloat16), vp_tile, NN) / row_sum
            ax[b * block : (b + 1) * block, columns] = merge_heads(mixed).astype(jnp.bfloat16)
            log_sum = row_max + jnp.log(row_sum)
            log_sums = jnp.where(lane_id == 2 * pair, log_sum[:block], log_sums)
            log_sums = jnp.where(lane_id == 2 * pair + 1, log_sum[block:], log_sums)
        lx[b * block : (b + 1) * block] = log_sums
    att_ref[...] = ax[edge : edge + rows]
    lse_ref[...] = jnp.transpose(lx[...])[: lse_ref.shape[0], edge : edge + rows]

    fetches[1].wait()
    step = 2 * LANES
    for part in range(width // step):
        product = dot(ax[...], w_ref[:, part * step : (part + 1) * step], NN)
        product = product.astype(jnp.bfloat16).astype(jnp.float32)
        time = lax.broadcasted_iota(jnp.int32, product.shape, 0) + (start - edge)
        product = jnp.where(time >= 0, product, 0.0)
        hid[2 * part] = product[:, :LANES]
        hid[2 * part + 1] = product[:, LANES:]

    fetches[2].wait()
    fetches[3].wait()
    for chunk in range(width // LANES):
        columns = slice(chunk * LANES, (chunk + 1) * LANES)
        cotx[chunk, :rows] = cot_ref[:, columns].astype(jnp.float32)
        part, lane = divmod(chunk * LANES, att)
        cotx[chunk, rows:] = near_ref[
            (3 + part) * edge : (4 + part) * edge, lane : lane + LANES
        ].astype(jnp.float32)
    kp[...] = jnp.zeros_like(kp)
    dm[rows + edge :] = jnp.zeros_like(dm[rows + edge :])

    apart = -(-taps // SUBLANES)
    reach = (apart - 1) * SUBLANES
    part_rows = (rows + edge) // 2

    def convolve(chunk, carry):
        columns = pl.ds(pl.multiple_of(chunk * LANES, LANES), LANES)
        for first in range(0, rows + edge, part_rows):
            mixed = jnp.zeros((part_rows, LANES), jnp.float32)
            for shift in range(SUBLANES):
                low = edge + first - shift - reach
                window = hid[chunk, low : low + part_rows + reach]
                for tap in range(shift, taps, SUBLANES):
                    at = reach - (tap - shift)
                    mixed += conv_ref[tap : tap + 1, columns] * window[at : at + part_rows]
            sigma = jax.nn.sigmoid(mixed)
            kept = min(part_rows, rows - first)
            out_ref[first : first + kept, columns] = (mixed * sigma)[:kept].astype(jnp.bfloat16)
            dm[first : first + part_rows] = (
                cotx[chunk, first : first + part_rows] * sigma * (1.0 + mixed * (1.0 - sigma))
            )
        part = rows // 2
        for first in range(0, rows, part):
            dhidden = jnp.zeros((part, LANES), jnp.float32)
            for shift in range(SUBLANES):
                low = first + shift
                window = dm[low : low + part + reach]
                for tap in range(shift, taps, SUBLANES):
                    at = tap - shift
                    dhidden += conv_ref[tap : tap + 1, columns] * window[at : at + part]
            dhid_ref[first : first + part, columns] = dhidden.astype(jnp.bfloat16)
        for shift in range(SUBLANES):
            sums = [jnp.zeros((SUBLANES, LANES), jnp.float32)] * apart
            for first in range(0, rows, part):
                low = edge + first - shift - reach
                window = hid[chunk, low : low + part + reach]
                own = dm[first : first + part]
                for tap in range(shift, taps, SUBLANES):
                    at = reach - (tap - shift)
                    product = (own * window[at : at + part]).reshape(-1, SUBLANES, LANES)
                    sums[tap // SUBLANES] += jnp.sum(product, axis=0)
            for tap in range(shift, taps, SUBLANES):
                ks[tap * SUBLANES : (tap + 1) * SUBLANES] = sums[tap // SUBLANES]
        total = ks[pl.ds(0, taps, SUBLANES)]
        for row in range(1, SUBLANES):
            total += ks[pl.ds(row, taps, SUBLANES)]
        kp[chunk, :taps] = total
        return carry

    lax.fori_loop(0, width // LANES, convolve, 0)

    _, pieces, piece_rows, _ = parts.shape
    chunks = width // LANES
    group = att // (2 * pieces)
    core = device_ref[1]
    own = ax[edge : edge + rows]
    for part in range(width // step):
        product = dot(own, dhid_ref[:, part * step : (part + 1) * step], TN).astype(jnp.bfloat16)
        for chunk in (2 * part, 2 * part + 1):
            tile = product[:, (chunk - 2 * part) * LANES : (chunk - 2 * part + 1) * LANES]
            for half in range(2):
                for piece in range(pieces):
                    first = (half * pieces + piece) * group
                    parts[half, piece, chunk * group : (chunk + 1) * group] = tile[
                        first : first + group
                    ]
    rest = jnp.zeros((piece_rows - chunks * (group + 1), LANES), jnp.float32)
    for half in range(2):
        for piece in range(pieces):
            tap = half * pieces + piece
            row = [kp[chunk, tap : tap + 1] for chunk in range(chunks)]
            row = jnp.concatenate(row + [rest], axis=0).astype(jnp.bfloat16)
            parts[half, piece, chunks * group :] = row
    keep_ref[...] = parts[core]
    give_ref[...] = parts[1 - core]


def unpack_kernel(device_ref, near_ref, far_ref, weight_ref, kernel_ref):
    pieces, piece_rows, _ = near_ref.shape
    att, width = weight_ref.shape
    taps = kernel_ref.shape[0]
    chunks = width // LANES
    group = att // (2 * pieces)
    core = device_ref[1]

    def write(refs):
        for half, ref in enumerate(refs):
            for piece in range(pieces):
                tap = half * pieces + piece
                for chunk in range(chunks):
                    columns = slice(chunk * LANES, (chunk + 1) * LANES)
                    tile = ref[piece, chunk * group : (chunk + 1) * group].astype(jnp.float32)
                    weight_ref[tap * group : (tap + 1) * group, columns] = tile
                if tap < taps:
                    row = ref[piece, chunks * group :].astype(jnp.float32)
                    for chunk in range(chunks):
                        columns = slice(chunk * LANES, (chunk + 1) * LANES)
                        kernel_ref[tap : tap + 1, columns] = row[chunk : chunk + 1]

    pl.when(core == 0)(lambda: write((near_ref, far_ref)))
    pl.when(core != 0)(lambda: write((far_ref, near_ref)))


def backward_kernel(context, rows, *refs):
    tiles = context + 1
    device_ref, q_ref = refs[:2]
    own_refs = refs[2 : 2 + tiles]
    att_ref, lse_ref, dhid_ref, w_ref = refs[2 + tiles : 6 + tiles]
    dq_ref, own_ref = refs[6 + tiles : 8 + tiles]
    message_refs = refs[8 + tiles : 8 + tiles + context]
    datt, bias = refs[8 + tiles + context :]

    att = q_ref.shape[1]
    heads = att // HEAD_DIM
    span = context * rows
    scale = 1.0 / math.sqrt(HEAD_DIM)
    start = device_ref[0] * rows

    dattended = dot(dhid_ref[...], w_ref[...], NT).astype(jnp.bfloat16)
    datt[...] = dattended
    product = dattended.astype(jnp.float32) * att_ref[...].astype(jnp.float32)
    head_id = lax.broadcasted_iota(jnp.int32, (heads, att), 0)
    feature_id = lax.broadcasted_iota(jnp.int32, (heads, att), 1)
    ours = (feature_id >= head_id * HEAD_DIM) & (feature_id < (head_id + 1) * HEAD_DIM)
    deltas = dot(jnp.where(ours, 1.0, 0.0), product, NT, lax.Precision.HIGHEST)

    for offset in range(tiles):
        key_id = lax.broadcasted_iota(jnp.int32, (rows, rows), 0)
        row_id = lax.broadcasted_iota(jnp.int32, (rows, rows), 1)
        distance = row_id - key_id + offset * rows
        key_time = key_id + (start - offset * rows)
        visible = (distance >= 0) & (distance < span) & (key_time >= 0)
        bias[offset] = jnp.where(visible, 0.0, NEGATIVE)

    for pair in range(att // LANES):
        columns = slice(pair * LANES, (pair + 1) * LANES)
        qs = stack_heads(q_ref[:, columns] * scale)
        ds = stack_heads(datt[:, columns])
        log_sum = [lse_ref[2 * pair + i : 2 * pair + i + 1] for i in (0, 1)]
        delta = [deltas[2 * pair + i : 2 * pair + i + 1] for i in (0, 1)]
        log_sum = jnp.concatenate(log_sum, axis=1)
        delta = jnp.concatenate(delta, axis=1)
        dquery = jnp.zeros((2 * rows, LANES), jnp.float32)
        for offset in range(tiles):
            kp = own_refs[offset][:rows, columns]
            vp = own_refs[offset][rows : 2 * rows, columns]
            hidden_pairs = jnp.concatenate([bias[offset], bias[offset]], axis=1)
            probs = jnp.exp(dot(kp, qs, NT) + hidden_pairs - log_sum)
            dprobs = dot(vp, ds, NT)
            dscores = (probs * (dprobs - delta)).astype(jnp.bfloat16)
            dvalue = dot(probs.astype(jnp.bfloat16), ds, NN)
            dkey = dot(dscores, qs, NN)
            dquery += dot(dscores, kp, TN)
            target = message_refs[offset - 1] if offset else own_ref
            target[:rows, columns] = dkey.astype(target.dtype)
            target[rows:, columns] = dvalue.astype(target.dtype)
        dq_ref[:, columns] = (merge_heads(dquery) * scale).astype(jnp.bfloat16)


def merge_kernel(*refs):
    own_ref, *message_refs, dk_ref, dv_ref = refs
    rows = dk_ref.shape[0]
    total = own_ref[...]
    for message_ref in message_refs:
        total += message_ref[...].astype(jnp.float32)
    total = total.astype(jnp.bfloat16)
    dk_ref[...] = total[:rows]
    dv_ref[...] = total[rows:]


def exchange(x):
    return lax.all_to_all(x, PLANE_AXES, 0, 0, tiled=True)


def collected(x):
    x = exchange(x.reshape(lax.axis_size(PLANE_AXES), -1, LANES))
    return jnp.sum(x.astype(jnp.float32), axis=0).astype(x.dtype)


def summed_along(x, axis):
    size, step = lax.axis_size(axis), 1
    while step < size:
        other = lax.ppermute(x, axis, [(i, i ^ step) for i in range(size)])
        x = (x.astype(jnp.float32) + other.astype(jnp.float32)).astype(x.dtype)
        step *= 2
    return x


def other_core(x):
    return lax.ppermute(x, "core", [(0, 1), (1, 0)])


def per_device(queries, key_in, value_in, out_weight, conv_kernel, cotangent):
    bf16, f32 = jnp.bfloat16, jnp.float32
    query, key, value, cot = queries[0], key_in[0], value_in[0], cotangent[0]
    runs = lax.axis_size(RUN_AXES)
    device = lax.axis_index(RUN_AXES).astype(jnp.int32)
    rows, att = query.shape
    width = out_weight.shape[1]
    heads = att // HEAD_DIM
    taps = conv_kernel.shape[0]
    edge = -(-(taps - 1) // 16) * 16
    context = min(CTX_MAX, runs // 4)

    query_rows = rows + 2 * edge
    key_rows = query_rows + context * rows
    chunks = width // LANES
    vmem = pl.BlockSpec(memory_space=pltpu.VMEM)
    smem = pl.BlockSpec(memory_space=pltpu.SMEM)
    hbm = pl.BlockSpec(memory_space=pltpu.HBM)
    params = pltpu.CompilerParams(vmem_limit_bytes=VMEM_LIMIT)

    own, far, near = pl.pallas_call(
        functools.partial(pack_kernel, edge),
        out_shape=(
            jax.ShapeDtypeStruct((2 * rows + edge, att), bf16),
            jax.ShapeDtypeStruct((2 * edge, att), bf16),
            jax.ShapeDtypeStruct(((3 + width // att) * edge, att), bf16),
        ),
        in_specs=[hbm] * 4,
        out_specs=(vmem,) * 3,
        scratch_shapes=[pltpu.SemaphoreType.DMA((8 + width // att,))],
        compiler_params=params,
        name="pack",
    )(in_hbm(key), in_hbm(value), in_hbm(query), in_hbm(cot))
    tiles = [own] + [shifted(own, o) for o in range(1, context + 1)]
    far = shifted(far, context + 1)
    near = shifted(near, -1)

    pieces = att // 32
    layers = lax.axis_size("z")
    split = pieces == layers * lax.axis_size(PLANE_AXES) and layers & (layers - 1) == 0
    core = lax.axis_index("core").astype(jnp.int32) if split else jnp.int32(0)
    place = jnp.stack([device, core])
    piece_rows = -(-(chunks * 16 + chunks) // 16) * 16
    out_frames, attended, log_sums, dhidden, keep, give, query, out_weight = pl.pallas_call(
        functools.partial(forward_kernel, context, rows, edge, taps),
        out_shape=(
            jax.ShapeDtypeStruct((rows, width), bf16),
            jax.ShapeDtypeStruct((rows, att), bf16),
            jax.ShapeDtypeStruct((heads, rows), f32),
            jax.ShapeDtypeStruct((rows, width), bf16),
        )
        + (jax.ShapeDtypeStruct((pieces, piece_rows, LANES), bf16),) * 2
        + (
            jax.ShapeDtypeStruct((rows, att), bf16),
            jax.ShapeDtypeStruct((att, width), bf16),
        ),
        in_specs=[smem, hbm] + [vmem] * (3 + context) + [hbm] * 3,
        out_specs=(vmem,) * 8,
        scratch_shapes=[
            pltpu.VMEM((query_rows, att), bf16),
            pltpu.VMEM((key_rows, att), bf16),
            pltpu.VMEM((key_rows, att), bf16),
            pltpu.VMEM((query_rows, att), bf16),
            pltpu.VMEM((query_rows, LANES), f32),
            pltpu.VMEM((chunks, query_rows, LANES), f32),
            pltpu.VMEM((chunks, rows + edge, LANES), f32),
            pltpu.VMEM((rows + edge + 8, LANES), f32),
            pltpu.VMEM((LANES, context * rows + LANES), f32),
            pltpu.VMEM((chunks, 2 * pieces, LANES), f32),
            pltpu.VMEM((taps * SUBLANES, LANES), f32),
            pltpu.VMEM((2, pieces, piece_rows, LANES), bf16),
            pltpu.VMEM((taps, width), f32),
            pltpu.VMEM((rows, width), bf16),
            pltpu.SemaphoreType.DMA((4,)),
        ],
        compiler_params=params,
        cost_estimate=cost(8 * 10**9, 10**7),
        name="forward",
    )(place, in_hbm(query), *tiles, far, near, in_hbm(out_weight), in_hbm(conv_kernel), in_hbm(cot))

    if split:
        mine = (keep.astype(f32) + other_core(give).astype(f32)).astype(bf16)
        mine, dhidden = lax.optimization_barrier((mine, dhidden))
    query_grad, own_grads, *messages = pl.pallas_call(
        functools.partial(backward_kernel, context, rows),
        out_shape=(
            jax.ShapeDtypeStruct((rows, att), bf16),
            jax.ShapeDtypeStruct((2 * rows, att), f32),
        )
        + (jax.ShapeDtypeStruct((2 * rows, att), bf16),) * context,
        in_specs=[smem] + [vmem] * (6 + context),
        out_specs=(vmem,) * (2 + context),
        scratch_shapes=[
            pltpu.VMEM((rows, att), bf16),
            pltpu.VMEM((context + 1, rows, rows), f32),
        ],
        compiler_params=params,
        cost_estimate=cost(6 * 10**9, 10**7),
        name="backward",
    )(place, query, *tiles, attended, log_sums, dhidden, out_weight)
    if split:
        mine = summed_along(collected(mine), "z")
        mine, *messages = lax.optimization_barrier((mine, *messages))
        mine = exchange(jnp.broadcast_to(mine, (lax.axis_size(PLANE_AXES), *mine.shape)))
        mine = mine.reshape(keep.shape)
    messages = [shifted(message, -offset) for offset, message in enumerate(messages, 1)]
    if split:
        mine, *messages = lax.optimization_barrier((mine, *messages))
        halves = (mine, other_core(mine))
    else:
        halves = lax.psum((keep, give), ("x", "core", "z", "y"))
    key_grad, value_grad = pl.pallas_call(
        merge_kernel,
        out_shape=(jax.ShapeDtypeStruct((rows, att), bf16),) * 2,
        in_specs=[vmem] * (1 + context),
        out_specs=(vmem,) * 2,
        compiler_params=params,
        name="merge",
    )(own_grads, *messages)
    weight_total, kernel_total = pl.pallas_call(
        unpack_kernel,
        out_shape=(
            jax.ShapeDtypeStruct((att, width), f32),
            jax.ShapeDtypeStruct((taps, width), f32),
        ),
        in_specs=[smem, vmem, vmem],
        out_specs=(vmem, vmem),
        compiler_params=params,
        name="unpack",
    )(place, *halves)
    return (
        out_frames[None],
        query_grad[None],
        key_grad[None],
        value_grad[None],
        weight_total,
        kernel_total,
    )


def solution(mesh):
    sizes = (mesh.shape["dp"] // 2, 2, mesh.shape["blk"] // 2, 2)
    fine = Mesh(mesh.devices.reshape(sizes), ("x", "core", "z", "y"))
    frames = P(("x", "core"), RUN_AXES, None)
    return jax.shard_map(
        per_device,
        mesh=fine,
        in_specs=(frames, frames, frames, P(), P(), frames),
        out_specs=(frames, frames, frames, frames, P(), P()),
        check_vma=False,
    )
```

```python
import functools
import math

import jax
import jax.numpy as jnp
from jax import lax
from jax.experimental import pallas as pl
from jax.experimental.pallas import tpu as pltpu
from jax.sharding import Mesh
from jax.sharding import PartitionSpec as P

HEAD_DIM = 64
CTX_MAX = 3
LANES = 128
SUBLANES = 8
NEGATIVE = -1e30
RUN_AXES = ("z", "y")
PLANE_AXES = ("x", "y")
VMEM_LIMIT = 40 * 1024 * 1024

NN = (((1,), (0,)), ((), ()))
NT = (((1,), (1,)), ((), ()))
TN = (((0,), (0,)), ((), ()))


def dot(a, b, dims, precision=None):
    return lax.dot_general(a, b, dims, precision=precision, preferred_element_type=jnp.float32)


def shifted(x, by):
    devices = range(lax.axis_size(RUN_AXES))
    return lax.ppermute(x, RUN_AXES, [(i, i + by) for i in devices if i + by in devices])


def in_hbm(x):
    return pltpu.with_memory_space_constraint(x, pltpu.HBM)


def cost(flops, data):
    return pl.CostEstimate(flops=flops, bytes_accessed=data, transcendentals=0)


def head_masks():
    lane = lax.broadcasted_iota(jnp.int32, (1, LANES), 1)
    first = jnp.where(lane < HEAD_DIM, 1.0, 0.0)
    return first.astype(jnp.bfloat16), (1.0 - first).astype(jnp.bfloat16)


def stack_heads(pair):
    first, second = head_masks()
    return jnp.concatenate([pair * first, pair * second], axis=0)


def merge_heads(stacked):
    rows = stacked.shape[0] // 2
    lane = lax.broadcasted_iota(jnp.int32, (rows, LANES), 1)
    return jnp.where(lane < HEAD_DIM, stacked[:rows], stacked[rows:])


def pack_kernel(edge, k_ref, v_ref, q_ref, cot_ref, own_ref, far_ref, near_ref, sems):
    rows, att = k_ref.shape
    width = cot_ref.shape[1]
    head, tail = pl.ds(0, edge), pl.ds(rows - edge, edge)
    moves = [
        (k_ref, own_ref.at[pl.ds(0, rows)]),
        (v_ref, own_ref.at[pl.ds(rows, rows)]),
        (q_ref.at[tail], own_ref.at[pl.ds(2 * rows, edge)]),
        (k_ref.at[tail], far_ref.at[pl.ds(0, edge)]),
        (v_ref.at[tail], far_ref.at[pl.ds(edge, edge)]),
        (k_ref.at[head], near_ref.at[pl.ds(0, edge)]),
        (v_ref.at[head], near_ref.at[pl.ds(edge, edge)]),
        (q_ref.at[head], near_ref.at[pl.ds(2 * edge, edge)]),
    ]
    for part in range(width // att):
        piece = cot_ref.at[head, pl.ds(part * att, att)]
        moves.append((piece, near_ref.at[pl.ds((3 + part) * edge, edge)]))
    copies = [pltpu.make_async_copy(a, b, sems.at[i]) for i, (a, b) in enumerate(moves)]
    for copy in copies:
        copy.start()
    for copy in copies:
        copy.wait()


def forward_kernel(context, rows, edge, taps, *refs):
    tiles = context + 1
    device_ref, q_hbm = refs[:2]
    own_refs = refs[2 : 2 + tiles]
    far_ref, near_ref, w_hbm, conv_hbm, cot_hbm = refs[2 + tiles : 7 + tiles]
    out_ref, att_ref, lse_ref, dhid_ref, keep_ref, give_ref = refs[7 + tiles : 13 + tiles]
    qx, kx, vx, ax, lx, hid, cotx, dm, bias, kp, ks, parts = refs[13 + tiles : 25 + tiles]
    q_ref, w_ref, conv_ref, cot_ref, sems = refs[25 + tiles :]

    att = q_ref.shape[1]
    width = w_ref.shape[1]
    span = context * rows
    query_rows = rows + 2 * edge
    block = LANES
    keys = span + block
    scale = 1.0 / math.sqrt(HEAD_DIM)
    start = device_ref[0] * rows

    fetches = [
        pltpu.make_async_copy(source, target, sems.at[i])
        for i, (source, target) in enumerate(
            ((q_hbm, q_ref), (w_hbm, w_ref), (cot_hbm, cot_ref), (conv_hbm, conv_ref))
        )
    ]
    for fetch in fetches:
        fetch.start()

    for ext, own_at, far_at in ((kx, 0, 0), (vx, rows, edge)):
        ext[:edge] = far_ref[far_at : far_at + edge]
        for offset in range(tiles):
            first = edge + (context - offset) * rows
            ext[first : first + rows] = own_refs[offset][own_at : own_at + rows]
        ext[edge + span + rows :] = near_ref[far_at : far_at + edge]
    qx[:edge] = own_refs[1][2 * rows : 2 * rows + edge] * scale
    qx[edge + rows :] = near_ref[2 * edge : 3 * edge] * scale
    fetches[0].wait()
    qx[edge : edge + rows] = q_ref[...] * scale

    lane_id = lax.broadcasted_iota(jnp.int32, (block, LANES), 1)
    for b in range(query_rows // block):
        row_id = lax.broadcasted_iota(jnp.int32, (block, keys), 0)
        key_id = lax.broadcasted_iota(jnp.int32, (block, keys), 1)
        distance = row_id - key_id + span
        key_time = key_id + (start - edge - span + b * block)
        visible = (distance >= 0) & (distance < span) & (key_time >= 0)
        bias[...] = jnp.where(visible, 0.0, NEGATIVE)
        log_sums = jnp.zeros((block, LANES), jnp.float32)
        for pair in range(att // LANES):
            columns = slice(pair * LANES, (pair + 1) * LANES)
            qs = stack_heads(qx[b * block : (b + 1) * block, columns])
            kp_tile = kx[b * block : b * block + keys, columns]
            vp_tile = vx[b * block : b * block + keys, columns]
            scores = dot(qs, kp_tile, NT)
            hidden_pairs = bias[...]
            scores = scores + jnp.concatenate([hidden_pairs, hidden_pairs], axis=0)
            row_max = jnp.max(scores, axis=1, keepdims=True)
            weights = jnp.exp(scores - row_max)
            row_sum = jnp.sum(weights, axis=1, keepdims=True)
            mixed = dot(weights.astype(jnp.bfloat16), vp_tile, NN) / row_sum
            ax[b * block : (b + 1) * block, columns] = merge_heads(mixed).astype(jnp.bfloat16)
            log_sum = row_max + jnp.log(row_sum)
            log_sums = jnp.where(lane_id == 2 * pair, log_sum[:block], log_sums)
            log_sums = jnp.where(lane_id == 2 * pair + 1, log_sum[block:], log_sums)
        lx[b * block : (b + 1) * block] = log_sums
    att_ref[...] = ax[edge : edge + rows]
    lse_ref[...] = jnp.transpose(lx[...])[: lse_ref.shape[0], edge : edge + rows]

    fetches[1].wait()
    step = 2 * LANES
    for part in range(width // step):
        product = dot(ax[...], w_ref[:, part * step : (part + 1) * step], NN)
        product = product.astype(jnp.bfloat16).astype(jnp.float32)
        time = lax.broadcasted_iota(jnp.int32, product.shape, 0) + (start - edge)
        product = jnp.where(time >= 0, product, 0.0)
        hid[2 * part] = product[:, :LANES]
        hid[2 * part + 1] = product[:, LANES:]

    fetches[2].wait()
    fetches[3].wait()
    for chunk in range(width // LANES):
        columns = slice(chunk * LANES, (chunk + 1) * LANES)
        cotx[chunk, :rows] = cot_ref[:, columns].astype(jnp.float32)
        part, lane = divmod(chunk * LANES, att)
        cotx[chunk, rows:] = near_ref[
            (3 + part) * edge : (4 + part) * edge, lane : lane + LANES
        ].astype(jnp.float32)
    kp[...] = jnp.zeros_like(kp)
    dm[rows + edge :] = jnp.zeros_like(dm[rows + edge :])

    apart = -(-taps // SUBLANES)
    reach = (apart - 1) * SUBLANES
    part_rows = (rows + edge) // 2

    def convolve(chunk, carry):
        columns = pl.ds(pl.multiple_of(chunk * LANES, LANES), LANES)
        for first in range(0, rows + edge, part_rows):
            mixed = jnp.zeros((part_rows, LANES), jnp.float32)
            for shift in range(SUBLANES):
                low = edge + first - shift - reach
                window = hid[chunk, low : low + part_rows + reach]
                for tap in range(shift, taps, SUBLANES):
                    at = reach - (tap - shift)
                    mixed += conv_ref[tap : tap + 1, columns] * window[at : at + part_rows]
            sigma = jax.nn.sigmoid(mixed)
            kept = min(part_rows, rows - first)
            out_ref[first : first + kept, columns] = (mixed * sigma)[:kept].astype(jnp.bfloat16)
            dm[first : first + part_rows] = (
                cotx[chunk, first : first + part_rows] * sigma * (1.0 + mixed * (1.0 - sigma))
            )
        part = rows // 2
        for first in range(0, rows, part):
            dhidden = jnp.zeros((part, LANES), jnp.float32)
            for shift in range(SUBLANES):
                low = first + shift
                window = dm[low : low + part + reach]
                for tap in range(shift, taps, SUBLANES):
                    at = tap - shift
                    dhidden += conv_ref[tap : tap + 1, columns] * window[at : at + part]
            dhid_ref[first : first + part, columns] = dhidden.astype(jnp.bfloat16)
        for shift in range(SUBLANES):
            sums = [jnp.zeros((SUBLANES, LANES), jnp.float32)] * apart
            for first in range(0, rows, part):
                low = edge + first - shift - reach
                window = hid[chunk, low : low + part + reach]
                own = dm[first : first + part]
                for tap in range(shift, taps, SUBLANES):
                    at = reach - (tap - shift)
                    product = (own * window[at : at + part]).reshape(-1, SUBLANES, LANES)
                    sums[tap // SUBLANES] += jnp.sum(product, axis=0)
            for tap in range(shift, taps, SUBLANES):
                ks[tap * SUBLANES : (tap + 1) * SUBLANES] = sums[tap // SUBLANES]
        total = ks[pl.ds(0, taps, SUBLANES)]
        for row in range(1, SUBLANES):
            total += ks[pl.ds(row, taps, SUBLANES)]
        kp[chunk, :taps] = total
        return carry

    lax.fori_loop(0, width // LANES, convolve, 0)

    _, pieces, piece_rows, _ = parts.shape
    chunks = width // LANES
    group = att // (2 * pieces)
    core = device_ref[1]
    own = ax[edge : edge + rows]
    for part in range(width // step):
        product = dot(own, dhid_ref[:, part * step : (part + 1) * step], TN).astype(jnp.bfloat16)
        for chunk in (2 * part, 2 * part + 1):
            tile = product[:, (chunk - 2 * part) * LANES : (chunk - 2 * part + 1) * LANES]
            for half in range(2):
                for piece in range(pieces):
                    first = (half * pieces + piece) * group
                    parts[half, piece, chunk * group : (chunk + 1) * group] = tile[
                        first : first + group
                    ]
    rest = jnp.zeros((piece_rows - chunks * (group + 1), LANES), jnp.float32)
    for half in range(2):
        for piece in range(pieces):
            tap = half * pieces + piece
            row = [kp[chunk, tap : tap + 1] for chunk in range(chunks)]
            row = jnp.concatenate(row + [rest], axis=0).astype(jnp.bfloat16)
            parts[half, piece, chunks * group :] = row
    keep_ref[...] = parts[core]
    give_ref[...] = parts[1 - core]


def unpack_kernel(device_ref, near_ref, far_ref, weight_ref, kernel_ref):
    pieces, piece_rows, _ = near_ref.shape
    att, width = weight_ref.shape
    taps = kernel_ref.shape[0]
    chunks = width // LANES
    group = att // (2 * pieces)
    core = device_ref[1]

    def write(refs):
        for half, ref in enumerate(refs):
            for piece in range(pieces):
                tap = half * pieces + piece
                for chunk in range(chunks):
                    columns = slice(chunk * LANES, (chunk + 1) * LANES)
                    tile = ref[piece, chunk * group : (chunk + 1) * group].astype(jnp.float32)
                    weight_ref[tap * group : (tap + 1) * group, columns] = tile
                if tap < taps:
                    row = ref[piece, chunks * group :].astype(jnp.float32)
                    for chunk in range(chunks):
                        columns = slice(chunk * LANES, (chunk + 1) * LANES)
                        kernel_ref[tap : tap + 1, columns] = row[chunk : chunk + 1]

    pl.when(core == 0)(lambda: write((near_ref, far_ref)))
    pl.when(core != 0)(lambda: write((far_ref, near_ref)))


def backward_kernel(context, rows, *refs):
    tiles = context + 1
    device_ref, q_hbm = refs[:2]
    own_refs = refs[2 : 2 + tiles]
    att_ref, lse_ref, dhid_hbm, w_hbm = refs[2 + tiles : 6 + tiles]
    dq_ref, own_ref = refs[6 + tiles : 8 + tiles]
    message_refs = refs[8 + tiles : 8 + tiles + context]
    q_ref, dhid_ref, w_ref, datt, bias, sems = refs[8 + tiles + context :]

    att = q_ref.shape[1]
    heads = att // HEAD_DIM
    span = context * rows
    scale = 1.0 / math.sqrt(HEAD_DIM)
    start = device_ref[0] * rows

    fetches = [
        pltpu.make_async_copy(source, target, sems.at[i])
        for i, (source, target) in enumerate(
            ((q_hbm, q_ref), (dhid_hbm, dhid_ref), (w_hbm, w_ref))
        )
    ]
    for fetch in fetches:
        fetch.start()
    for offset in range(tiles):
        key_id = lax.broadcasted_iota(jnp.int32, (rows, rows), 0)
        row_id = lax.broadcasted_iota(jnp.int32, (rows, rows), 1)
        distance = row_id - key_id + offset * rows
        key_time = key_id + (start - offset * rows)
        visible = (distance >= 0) & (distance < span) & (key_time >= 0)
        bias[offset] = jnp.where(visible, 0.0, NEGATIVE)

    for fetch in fetches:
        fetch.wait()
    dattended = dot(dhid_ref[...], w_ref[...], NT).astype(jnp.bfloat16)
    datt[...] = dattended
    product = dattended.astype(jnp.float32) * att_ref[...].astype(jnp.float32)
    head_id = lax.broadcasted_iota(jnp.int32, (heads, att), 0)
    feature_id = lax.broadcasted_iota(jnp.int32, (heads, att), 1)
    ours = (feature_id >= head_id * HEAD_DIM) & (feature_id < (head_id + 1) * HEAD_DIM)
    deltas = dot(jnp.where(ours, 1.0, 0.0), product, NT, lax.Precision.HIGHEST)

    for pair in range(att // LANES):
        columns = slice(pair * LANES, (pair + 1) * LANES)
        qs = stack_heads(q_ref[:, columns] * scale)
        ds = stack_heads(datt[:, columns])
        log_sum = [lse_ref[2 * pair + i : 2 * pair + i + 1] for i in (0, 1)]
        delta = [deltas[2 * pair + i : 2 * pair + i + 1] for i in (0, 1)]
        log_sum = jnp.concatenate(log_sum, axis=1)
        delta = jnp.concatenate(delta, axis=1)
        dquery = jnp.zeros((2 * rows, LANES), jnp.float32)
        for offset in range(tiles):
            kp = own_refs[offset][:rows, columns]
            vp = own_refs[offset][rows : 2 * rows, columns]
            hidden_pairs = jnp.concatenate([bias[offset], bias[offset]], axis=1)
            probs = jnp.exp(dot(kp, qs, NT) + hidden_pairs - log_sum)
            dprobs = dot(vp, ds, NT)
            dscores = (probs * (dprobs - delta)).astype(jnp.bfloat16)
            dvalue = dot(probs.astype(jnp.bfloat16), ds, NN)
            dkey = dot(dscores, qs, NN)
            dquery += dot(dscores, kp, TN)
            target = message_refs[offset - 1] if offset else own_ref
            target[:rows, columns] = dkey.astype(target.dtype)
            target[rows:, columns] = dvalue.astype(target.dtype)
        dq_ref[:, columns] = (merge_heads(dquery) * scale).astype(jnp.bfloat16)


def relay_kernel(device_ref, own_ref, swapped_ref, message_ref, own_out, message_out):
    odd = lax.rem(device_ref[0], 2).astype(jnp.float32)
    swapped = swapped_ref[...].astype(jnp.float32)
    own_out[...] = own_ref[...] + swapped * (1.0 - odd)
    message_out[...] = (message_ref[...].astype(jnp.float32) + swapped * odd).astype(jnp.bfloat16)


def merge_kernel(*refs):
    own_ref, *message_refs, dk_ref, dv_ref = refs
    rows = dk_ref.shape[0]
    total = own_ref[...]
    for message_ref in message_refs:
        total += message_ref[...].astype(jnp.float32)
    total = total.astype(jnp.bfloat16)
    dk_ref[...] = total[:rows]
    dv_ref[...] = total[rows:]


def exchange(x):
    return lax.all_to_all(x, PLANE_AXES, 0, 0, tiled=True)


def collected(x):
    x = exchange(x.reshape(lax.axis_size(PLANE_AXES), -1, LANES))
    return jnp.sum(x.astype(jnp.float32), axis=0).astype(x.dtype)


def summed_along(x, axis):
    size, step = lax.axis_size(axis), 1
    while step < size:
        other = lax.ppermute(x, axis, [(i, i ^ step) for i in range(size)])
        x = (x.astype(jnp.float32) + other.astype(jnp.float32)).astype(x.dtype)
        step *= 2
    return x


def other_core(x):
    return lax.ppermute(x, "core", [(0, 1), (1, 0)])


def per_device(queries, key_in, value_in, out_weight, conv_kernel, cotangent):
    bf16, f32 = jnp.bfloat16, jnp.float32
    query, key, value, cot = queries[0], key_in[0], value_in[0], cotangent[0]
    runs = lax.axis_size(RUN_AXES)
    device = lax.axis_index(RUN_AXES).astype(jnp.int32)
    rows, att = query.shape
    width = out_weight.shape[1]
    heads = att // HEAD_DIM
    taps = conv_kernel.shape[0]
    edge = -(-(taps - 1) // 16) * 16
    context = min(CTX_MAX, runs // 4)

    query_rows = rows + 2 * edge
    key_rows = query_rows + context * rows
    chunks = width // LANES
    vmem = pl.BlockSpec(memory_space=pltpu.VMEM)
    smem = pl.BlockSpec(memory_space=pltpu.SMEM)
    hbm = pl.BlockSpec(memory_space=pltpu.HBM)
    params = pltpu.CompilerParams(vmem_limit_bytes=VMEM_LIMIT)

    own, far, near = pl.pallas_call(
        functools.partial(pack_kernel, edge),
        out_shape=(
            jax.ShapeDtypeStruct((2 * rows + edge, att), bf16),
            jax.ShapeDtypeStruct((2 * edge, att), bf16),
            jax.ShapeDtypeStruct(((3 + width // att) * edge, att), bf16),
        ),
        in_specs=[hbm] * 4,
        out_specs=(vmem,) * 3,
        scratch_shapes=[pltpu.SemaphoreType.DMA((8 + width // att,))],
        compiler_params=params,
        name="pack",
    )(in_hbm(key), in_hbm(value), in_hbm(query), in_hbm(cot))
    tiles = [own] + [shifted(own, o) for o in range(1, context + 1)]
    far = shifted(far, context + 1)
    near = shifted(near, -1)

    pieces = att // 32
    layers = lax.axis_size("z")
    split = pieces == layers * lax.axis_size(PLANE_AXES) and layers & (layers - 1) == 0
    core = lax.axis_index("core").astype(jnp.int32) if split else jnp.int32(0)
    place = jnp.stack([device, core])
    piece_rows = -(-(chunks * 16 + chunks) // 16) * 16
    out_frames, attended, log_sums, dhidden, keep, give = pl.pallas_call(
        functools.partial(forward_kernel, context, rows, edge, taps),
        out_shape=(
            jax.ShapeDtypeStruct((rows, width), bf16),
            jax.ShapeDtypeStruct((rows, att), bf16),
            jax.ShapeDtypeStruct((heads, rows), f32),
            jax.ShapeDtypeStruct((rows, width), bf16),
        )
        + (jax.ShapeDtypeStruct((pieces, piece_rows, LANES), bf16),) * 2,
        in_specs=[smem, hbm] + [vmem] * (3 + context) + [hbm] * 3,
        out_specs=(vmem,) * 6,
        scratch_shapes=[
            pltpu.VMEM((query_rows, att), bf16),
            pltpu.VMEM((key_rows, att), bf16),
            pltpu.VMEM((key_rows, att), bf16),
            pltpu.VMEM((query_rows, att), bf16),
            pltpu.VMEM((query_rows, LANES), f32),
            pltpu.VMEM((chunks, query_rows, LANES), f32),
            pltpu.VMEM((chunks, rows + edge, LANES), f32),
            pltpu.VMEM((rows + edge + 8, LANES), f32),
            pltpu.VMEM((LANES, context * rows + LANES), f32),
            pltpu.VMEM((chunks, 2 * pieces, LANES), f32),
            pltpu.VMEM((taps * SUBLANES, LANES), f32),
            pltpu.VMEM((2, pieces, piece_rows, LANES), bf16),
            pltpu.VMEM((rows, att), bf16),
            pltpu.VMEM((att, width), bf16),
            pltpu.VMEM((taps, width), f32),
            pltpu.VMEM((rows, width), bf16),
            pltpu.SemaphoreType.DMA((4,)),
        ],
        compiler_params=params,
        cost_estimate=cost(8 * 10**9, 10**7),
        name="forward",
    )(place, in_hbm(query), *tiles, far, near, in_hbm(out_weight), in_hbm(conv_kernel), in_hbm(cot))

    if split:
        mine = (keep.astype(f32) + other_core(give).astype(f32)).astype(bf16)
        mine, dhidden = lax.optimization_barrier((mine, dhidden))
    query_grad, own_grads, *messages = pl.pallas_call(
        functools.partial(backward_kernel, context, rows),
        out_shape=(
            jax.ShapeDtypeStruct((rows, att), bf16),
            jax.ShapeDtypeStruct((2 * rows, att), f32),
        )
        + (jax.ShapeDtypeStruct((2 * rows, att), bf16),) * context,
        in_specs=[smem, hbm] + [vmem] * (3 + context) + [hbm] * 2,
        out_specs=(vmem,) * (2 + context),
        scratch_shapes=[
            pltpu.VMEM((rows, att), bf16),
            pltpu.VMEM((rows, width), bf16),
            pltpu.VMEM((att, width), bf16),
            pltpu.VMEM((rows, att), bf16),
            pltpu.VMEM((context + 1, rows, rows), f32),
            pltpu.SemaphoreType.DMA((3,)),
        ],
        compiler_params=params,
        cost_estimate=cost(6 * 10**9, 10**7),
        name="backward",
    )(place, in_hbm(query), *tiles, attended, log_sums, in_hbm(dhidden), in_hbm(out_weight))
    if split:
        mine, own_grads, *messages = lax.optimization_barrier(
            (collected(mine), own_grads, *messages)
        )
    messages = dict(enumerate(messages, 1))
    if context > 1:
        swapped = lax.ppermute(messages.pop(1), "y", [(0, 1), (1, 0)])
        own_grads, messages[2] = pl.pallas_call(
            relay_kernel,
            out_shape=(
                jax.ShapeDtypeStruct((2 * rows, att), f32),
                jax.ShapeDtypeStruct((2 * rows, att), bf16),
            ),
            in_specs=[smem] + [vmem] * 3,
            out_specs=(vmem,) * 2,
            compiler_params=params,
            cost_estimate=cost(10**9, 3 * 10**6),
            name="relay",
        )(place, own_grads, swapped, messages[2])
    if split:
        mine = summed_along(mine, "z")
        mine, messages = lax.optimization_barrier((mine, messages))
        mine = exchange(jnp.broadcast_to(mine, (lax.axis_size(PLANE_AXES), *mine.shape)))
        mine = mine.reshape(keep.shape)
    messages = [shifted(message, -offset) for offset, message in messages.items()]
    if split:
        mine, *messages = lax.optimization_barrier((mine, *messages))
        halves = (mine, other_core(mine))
    else:
        halves = lax.psum((keep, give), ("x", "core", "z", "y"))
    key_grad, value_grad = pl.pallas_call(
        merge_kernel,
        out_shape=(jax.ShapeDtypeStruct((rows, att), bf16),) * 2,
        in_specs=[vmem] * (1 + len(messages)),
        out_specs=(vmem,) * 2,
        compiler_params=params,
        name="merge",
    )(own_grads, *messages)
    weight_total, kernel_total = pl.pallas_call(
        unpack_kernel,
        out_shape=(
            jax.ShapeDtypeStruct((att, width), f32),
            jax.ShapeDtypeStruct((taps, width), f32),
        ),
        in_specs=[smem, vmem, vmem],
        out_specs=(vmem, vmem),
        compiler_params=params,
        name="unpack",
    )(place, *halves)
    return (
        out_frames[None],
        query_grad[None],
        key_grad[None],
        value_grad[None],
        weight_total,
        kernel_total,
    )


def solution(mesh):
    sizes = (mesh.shape["dp"] // 2, 2, mesh.shape["blk"] // 2, 2)
    fine = Mesh(mesh.devices.reshape(sizes), ("x", "core", "z", "y"))
    frames = P(("x", "core"), RUN_AXES, None)
    return jax.shard_map(
        per_device,
        mesh=fine,
        in_specs=(frames, frames, frames, P(), P(), frames),
        out_specs=(frames, frames, frames, frames, P(), P()),
        check_vma=False,
    )
```

```python
import functools
import math

import jax
import jax.numpy as jnp
from jax import lax
from jax.experimental import pallas as pl
from jax.experimental.pallas import tpu as pltpu
from jax.sharding import Mesh
from jax.sharding import PartitionSpec as P

HEAD_DIM = 64
CTX_MAX = 3
LANES = 128
SUBLANES = 8
NEGATIVE = -1e30
RUN_AXES = ("z", "y")
PLANE_AXES = ("x", "y")
VMEM_LIMIT = 28 * 1024 * 1024

NN = (((1,), (0,)), ((), ()))
NT = (((1,), (1,)), ((), ()))
TN = (((0,), (0,)), ((), ()))


def dot(a, b, dims, precision=None):
    return lax.dot_general(a, b, dims, precision=precision, preferred_element_type=jnp.float32)


def shifted(x, by):
    devices = range(lax.axis_size(RUN_AXES))
    return lax.ppermute(x, RUN_AXES, [(i, i + by) for i in devices if i + by in devices])


def in_hbm(x):
    return pltpu.with_memory_space_constraint(x, pltpu.HBM)


def cost(flops, data):
    return pl.CostEstimate(flops=flops, bytes_accessed=data, transcendentals=0)


def head_masks():
    lane = lax.broadcasted_iota(jnp.int32, (1, LANES), 1)
    first = jnp.where(lane < HEAD_DIM, 1.0, 0.0)
    return first.astype(jnp.bfloat16), (1.0 - first).astype(jnp.bfloat16)


def stack_heads(pair):
    first, second = head_masks()
    return jnp.concatenate([pair * first, pair * second], axis=0)


def merge_heads(stacked):
    rows = stacked.shape[0] // 2
    lane = lax.broadcasted_iota(jnp.int32, (rows, LANES), 1)
    return jnp.where(lane < HEAD_DIM, stacked[:rows], stacked[rows:])


def pack_kernel(
    edge, k_ref, v_ref, q_ref, cot_ref, own_ref, keys_ref, values_ref, far_ref, near_ref, sems
):
    rows, att = k_ref.shape
    width = cot_ref.shape[1]
    head, tail = pl.ds(0, edge), pl.ds(rows - edge, edge)
    moves = [
        (k_ref, own_ref.at[pl.ds(0, rows)]),
        (v_ref, own_ref.at[pl.ds(rows, rows)]),
        (k_ref, keys_ref.at[pl.ds(0, rows)]),
        (q_ref.at[tail], keys_ref.at[pl.ds(rows, edge)]),
        (v_ref, values_ref),
        (k_ref.at[tail], far_ref.at[pl.ds(0, edge)]),
        (v_ref.at[tail], far_ref.at[pl.ds(edge, edge)]),
        (k_ref.at[head], near_ref.at[pl.ds(0, edge)]),
        (v_ref.at[head], near_ref.at[pl.ds(edge, edge)]),
        (q_ref.at[head], near_ref.at[pl.ds(2 * edge, edge)]),
    ]
    for part in range(width // att):
        piece = cot_ref.at[head, pl.ds(part * att, att)]
        moves.append((piece, near_ref.at[pl.ds((3 + part) * edge, edge)]))
    copies = [pltpu.make_async_copy(a, b, sems.at[i]) for i, (a, b) in enumerate(moves)]
    for copy in copies:
        copy.start()
    for copy in copies:
        copy.wait()


def choose_kernel(device_ref, even_ref, odd_ref, out_ref):
    odd = lax.rem(device_ref[0], 2)
    rows = out_ref.shape[0]

    @pl.when(odd == 0)
    def _():
        out_ref[...] = even_ref[...]

    @pl.when(odd != 0)
    def _():
        out_ref[...] = odd_ref[odd_ref.shape[0] - rows :]


def tile_places(rows, own_ref, keys_ref, values_ref, *further_refs):
    places = [(own_ref, 0, own_ref, rows), (keys_ref, 0, values_ref, 0)]
    return places + [(ref, 0, ref, rows) for ref in further_refs]


def forward_kernel(context, rows, edge, taps, *refs):
    tiles = context + 2
    device_ref, q_hbm = refs[:2]
    places = tile_places(rows, *refs[2 : 2 + tiles])
    keys_ref = refs[3]
    far_ref, near_ref, w_hbm, conv_hbm, cot_hbm = refs[2 + tiles : 7 + tiles]
    out_ref, att_ref, lse_ref, dhid_ref, keep_ref, give_ref = refs[7 + tiles : 13 + tiles]
    qx, kx, vx, ax, lx, hid, cotx, dm, bias, kp, ks, parts = refs[13 + tiles : 25 + tiles]
    q_ref, w_ref, conv_ref, cot_ref, sems = refs[25 + tiles :]

    att = q_ref.shape[1]
    width = w_ref.shape[1]
    span = context * rows
    query_rows = rows + 2 * edge
    block = LANES
    keys = span + block
    scale = 1.0 / math.sqrt(HEAD_DIM)
    start = device_ref[0] * rows

    fetches = [
        pltpu.make_async_copy(source, target, sems.at[i])
        for i, (source, target) in enumerate(
            ((q_hbm, q_ref), (w_hbm, w_ref), (cot_hbm, cot_ref), (conv_hbm, conv_ref))
        )
    ]
    for fetch in fetches:
        fetch.start()

    for offset, (k_ref, k_at, v_ref, v_at) in enumerate(places):
        first = edge + (context - offset) * rows
        kx[first : first + rows] = k_ref[k_at : k_at + rows]
        vx[first : first + rows] = v_ref[v_at : v_at + rows]
    for ext, at in ((kx, 0), (vx, edge)):
        ext[:edge] = far_ref[at : at + edge]
        ext[edge + span + rows :] = near_ref[at : at + edge]
    qx[:edge] = keys_ref[rows : rows + edge] * scale
    qx[edge + rows :] = near_ref[2 * edge : 3 * edge] * scale
    fetches[0].wait()
    qx[edge : edge + rows] = q_ref[...] * scale

    lane_id = lax.broadcasted_iota(jnp.int32, (block, LANES), 1)
    for b in range(query_rows // block):
        row_id = lax.broadcasted_iota(jnp.int32, (block, keys), 0)
        key_id = lax.broadcasted_iota(jnp.int32, (block, keys), 1)
        distance = row_id - key_id + span
        key_time = key_id + (start - edge - span + b * block)
        visible = (distance >= 0) & (distance < span) & (key_time >= 0)
        bias[...] = jnp.where(visible, 0.0, NEGATIVE)
        log_sums = jnp.zeros((block, LANES), jnp.float32)
        for pair in range(att // LANES):
            columns = slice(pair * LANES, (pair + 1) * LANES)
            qs = stack_heads(qx[b * block : (b + 1) * block, columns])
            kp_tile = kx[b * block : b * block + keys, columns]
            vp_tile = vx[b * block : b * block + keys, columns]
            scores = dot(qs, kp_tile, NT)
            hidden_pairs = bias[...]
            scores = scores + jnp.concatenate([hidden_pairs, hidden_pairs], axis=0)
            row_max = jnp.max(scores, axis=1, keepdims=True)
            weights = jnp.exp(scores - row_max)
            row_sum = jnp.sum(weights, axis=1, keepdims=True)
            mixed = dot(weights.astype(jnp.bfloat16), vp_tile, NN) / row_sum
            ax[b * block : (b + 1) * block, columns] = merge_heads(mixed).astype(jnp.bfloat16)
            log_sum = row_max + jnp.log(row_sum)
            log_sums = jnp.where(lane_id == 2 * pair, log_sum[:block], log_sums)
            log_sums = jnp.where(lane_id == 2 * pair + 1, log_sum[block:], log_sums)
        lx[b * block : (b + 1) * block] = log_sums
    att_ref[...] = ax[edge : edge + rows]
    lse_ref[...] = jnp.transpose(lx[...])[: lse_ref.shape[0], edge : edge + rows]

    fetches[1].wait()
    step = 2 * LANES
    for part in range(width // step):
        product = dot(ax[...], w_ref[:, part * step : (part + 1) * step], NN)
        product = product.astype(jnp.bfloat16).astype(jnp.float32)
        time = lax.broadcasted_iota(jnp.int32, product.shape, 0) + (start - edge)
        product = jnp.where(time >= 0, product, 0.0)
        hid[2 * part] = product[:, :LANES]
        hid[2 * part + 1] = product[:, LANES:]

    fetches[2].wait()
    fetches[3].wait()
    for chunk in range(width // LANES):
        columns = slice(chunk * LANES, (chunk + 1) * LANES)
        cotx[chunk, :rows] = cot_ref[:, columns].astype(jnp.float32)
        part, lane = divmod(chunk * LANES, att)
        cotx[chunk, rows:] = near_ref[
            (3 + part) * edge : (4 + part) * edge, lane : lane + LANES
        ].astype(jnp.float32)
    kp[...] = jnp.zeros_like(kp)
    dm[rows + edge :] = jnp.zeros_like(dm[rows + edge :])

    apart = -(-taps // SUBLANES)
    reach = (apart - 1) * SUBLANES
    part_rows = (rows + edge) // 2

    def convolve(chunk, carry):
        columns = pl.ds(pl.multiple_of(chunk * LANES, LANES), LANES)
        for first in range(0, rows + edge, part_rows):
            mixed = jnp.zeros((part_rows, LANES), jnp.float32)
            for shift in range(SUBLANES):
                low = edge + first - shift - reach
                window = hid[chunk, low : low + part_rows + reach]
                for tap in range(shift, taps, SUBLANES):
                    at = reach - (tap - shift)
                    mixed += conv_ref[tap : tap + 1, columns] * window[at : at + part_rows]
            sigma = jax.nn.sigmoid(mixed)
            kept = min(part_rows, rows - first)
            out_ref[first : first + kept, columns] = (mixed * sigma)[:kept].astype(jnp.bfloat16)
            dm[first : first + part_rows] = (
                cotx[chunk, first : first + part_rows] * sigma * (1.0 + mixed * (1.0 - sigma))
            )
        part = rows // 2
        for first in range(0, rows, part):
            dhidden = jnp.zeros((part, LANES), jnp.float32)
            for shift in range(SUBLANES):
                low = first + shift
                window = dm[low : low + part + reach]
                for tap in range(shift, taps, SUBLANES):
                    at = tap - shift
                    dhidden += conv_ref[tap : tap + 1, columns] * window[at : at + part]
            dhid_ref[first : first + part, columns] = dhidden.astype(jnp.bfloat16)
        for shift in range(SUBLANES):
            sums = [jnp.zeros((SUBLANES, LANES), jnp.float32)] * apart
            for first in range(0, rows, part):
                low = edge + first - shift - reach
                window = hid[chunk, low : low + part + reach]
                own = dm[first : first + part]
                for tap in range(shift, taps, SUBLANES):
                    at = reach - (tap - shift)
                    product = (own * window[at : at + part]).reshape(-1, SUBLANES, LANES)
                    sums[tap // SUBLANES] += jnp.sum(product, axis=0)
            for tap in range(shift, taps, SUBLANES):
                ks[tap * SUBLANES : (tap + 1) * SUBLANES] = sums[tap // SUBLANES]
        total = ks[pl.ds(0, taps, SUBLANES)]
        for row in range(1, SUBLANES):
            total += ks[pl.ds(row, taps, SUBLANES)]
        kp[chunk, :taps] = total
        return carry

    lax.fori_loop(0, width // LANES, convolve, 0)

    _, pieces, piece_rows, _ = parts.shape
    chunks = width // LANES
    group = att // (2 * pieces)
    core = device_ref[1]
    own = ax[edge : edge + rows]
    for part in range(width // step):
        product = dot(own, dhid_ref[:, part * step : (part + 1) * step], TN).astype(jnp.bfloat16)
        for chunk in (2 * part, 2 * part + 1):
            tile = product[:, (chunk - 2 * part) * LANES : (chunk - 2 * part + 1) * LANES]
            for half in range(2):
                for piece in range(pieces):
                    first = (half * pieces + piece) * group
                    parts[half, piece, chunk * group : (chunk + 1) * group] = tile[
                        first : first + group
                    ]
    rest = jnp.zeros((piece_rows - chunks * (group + 1), LANES), jnp.float32)
    for half in range(2):
        for piece in range(pieces):
            tap = half * pieces + piece
            row = [kp[chunk, tap : tap + 1] for chunk in range(chunks)]
            row = jnp.concatenate(row + [rest], axis=0).astype(jnp.bfloat16)
            parts[half, piece, chunks * group :] = row
    keep_ref[...] = parts[core]
    give_ref[...] = parts[1 - core]


def unpack_kernel(device_ref, near_ref, far_ref, weight_ref, kernel_ref):
    pieces, piece_rows, _ = near_ref.shape
    att, width = weight_ref.shape
    taps = kernel_ref.shape[0]
    chunks = width // LANES
    group = att // (2 * pieces)
    core = device_ref[1]

    def write(refs):
        for half, ref in enumerate(refs):
            for piece in range(pieces):
                tap = half * pieces + piece
                for chunk in range(chunks):
                    columns = slice(chunk * LANES, (chunk + 1) * LANES)
                    tile = ref[piece, chunk * group : (chunk + 1) * group].astype(jnp.float32)
                    weight_ref[tap * group : (tap + 1) * group, columns] = tile
                if tap < taps:
                    row = ref[piece, chunks * group :].astype(jnp.float32)
                    for chunk in range(chunks):
                        columns = slice(chunk * LANES, (chunk + 1) * LANES)
                        kernel_ref[tap : tap + 1, columns] = row[chunk : chunk + 1]

    pl.when(core == 0)(lambda: write((near_ref, far_ref)))
    pl.when(core != 0)(lambda: write((far_ref, near_ref)))


def backward_kernel(context, rows, *refs):
    tiles = context + 2
    device_ref, q_hbm = refs[:2]
    places = tile_places(rows, *refs[2 : 2 + tiles])
    att_ref, lse_ref, dhid_hbm, w_hbm = refs[2 + tiles : 6 + tiles]
    dq_ref, own_ref = refs[6 + tiles : 8 + tiles]
    message_refs = refs[8 + tiles : 8 + tiles + context]
    q_ref, dhid_ref, w_ref, datt, bias, sems = refs[8 + tiles + context :]

    att = q_ref.shape[1]
    heads = att // HEAD_DIM
    span = context * rows
    scale = 1.0 / math.sqrt(HEAD_DIM)
    start = device_ref[0] * rows

    fetches = [
        pltpu.make_async_copy(source, target, sems.at[i])
        for i, (source, target) in enumerate(
            ((q_hbm, q_ref), (dhid_hbm, dhid_ref), (w_hbm, w_ref))
        )
    ]
    for fetch in fetches:
        fetch.start()
    for offset in range(context + 1):
        key_id = lax.broadcasted_iota(jnp.int32, (rows, rows), 0)
        row_id = lax.broadcasted_iota(jnp.int32, (rows, rows), 1)
        distance = row_id - key_id + offset * rows
        key_time = key_id + (start - offset * rows)
        visible = (distance >= 0) & (distance < span) & (key_time >= 0)
        bias[offset] = jnp.where(visible, 0.0, NEGATIVE)

    for fetch in fetches:
        fetch.wait()
    dattended = dot(dhid_ref[...], w_ref[...], NT).astype(jnp.bfloat16)
    datt[...] = dattended
    product = dattended.astype(jnp.float32) * att_ref[...].astype(jnp.float32)
    head_id = lax.broadcasted_iota(jnp.int32, (heads, att), 0)
    feature_id = lax.broadcasted_iota(jnp.int32, (heads, att), 1)
    ours = (feature_id >= head_id * HEAD_DIM) & (feature_id < (head_id + 1) * HEAD_DIM)
    deltas = dot(jnp.where(ours, 1.0, 0.0), product, NT, lax.Precision.HIGHEST)

    for pair in range(att // LANES):
        columns = slice(pair * LANES, (pair + 1) * LANES)
        qs = stack_heads(q_ref[:, columns] * scale)
        ds = stack_heads(datt[:, columns])
        log_sum = [lse_ref[2 * pair + i : 2 * pair + i + 1] for i in (0, 1)]
        delta = [deltas[2 * pair + i : 2 * pair + i + 1] for i in (0, 1)]
        log_sum = jnp.concatenate(log_sum, axis=1)
        delta = jnp.concatenate(delta, axis=1)
        dquery = jnp.zeros((2 * rows, LANES), jnp.float32)
        for offset, (k_ref, k_at, v_ref, v_at) in enumerate(places):
            kp = k_ref[k_at : k_at + rows, columns]
            vp = v_ref[v_at : v_at + rows, columns]
            hidden_pairs = jnp.concatenate([bias[offset], bias[offset]], axis=1)
            probs = jnp.exp(dot(kp, qs, NT) + hidden_pairs - log_sum)
            dprobs = dot(vp, ds, NT)
            dscores = (probs * (dprobs - delta)).astype(jnp.bfloat16)
            dvalue = dot(probs.astype(jnp.bfloat16), ds, NN)
            dkey = dot(dscores, qs, NN)
            dquery += dot(dscores, kp, TN)
            target = message_refs[offset - 1] if offset else own_ref
            target[:rows, columns] = dkey.astype(target.dtype)
            target[rows:, columns] = dvalue.astype(target.dtype)
        dq_ref[:, columns] = (merge_heads(dquery) * scale).astype(jnp.bfloat16)


def relay_kernel(device_ref, own_ref, swapped_ref, message_ref, own_out, message_out):
    odd = lax.rem(device_ref[0], 2).astype(jnp.float32)
    swapped = swapped_ref[...].astype(jnp.float32)
    own_out[...] = own_ref[...] + swapped * (1.0 - odd)
    message_out[...] = (message_ref[...].astype(jnp.float32) + swapped * odd).astype(jnp.bfloat16)


def merge_kernel(*refs):
    own_ref, *message_refs, dk_ref, dv_ref = refs
    rows = dk_ref.shape[0]
    total = own_ref[...]
    for message_ref in message_refs:
        total += message_ref[...].astype(jnp.float32)
    total = total.astype(jnp.bfloat16)
    dk_ref[...] = total[:rows]
    dv_ref[...] = total[rows:]


def exchange(x):
    return lax.all_to_all(x, PLANE_AXES, 0, 0, tiled=True)


def collected(x):
    x = exchange(x.reshape(lax.axis_size(PLANE_AXES), -1, LANES))
    return jnp.sum(x.astype(jnp.float32), axis=0).astype(x.dtype)


def summed_along(x, axis):
    size, step = lax.axis_size(axis), 1
    while step < size:
        other = lax.ppermute(x, axis, [(i, i ^ step) for i in range(size)])
        x = (x.astype(jnp.float32) + other.astype(jnp.float32)).astype(x.dtype)
        step *= 2
    return x


def other_core(x):
    return lax.ppermute(x, "core", [(0, 1), (1, 0)])


def per_device(queries, key_in, value_in, out_weight, conv_kernel, cotangent):
    bf16, f32 = jnp.bfloat16, jnp.float32
    query, key, value, cot = queries[0], key_in[0], value_in[0], cotangent[0]
    runs = lax.axis_size(RUN_AXES)
    device = lax.axis_index(RUN_AXES).astype(jnp.int32)
    rows, att = query.shape
    width = out_weight.shape[1]
    heads = att // HEAD_DIM
    taps = conv_kernel.shape[0]
    edge = -(-(taps - 1) // 16) * 16
    context = min(CTX_MAX, runs // 4)

    query_rows = rows + 2 * edge
    key_rows = query_rows + context * rows
    chunks = width // LANES
    vmem = pl.BlockSpec(memory_space=pltpu.VMEM)
    smem = pl.BlockSpec(memory_space=pltpu.SMEM)
    hbm = pl.BlockSpec(memory_space=pltpu.HBM)
    params = pltpu.CompilerParams(vmem_limit_bytes=VMEM_LIMIT)

    own, keys, values, far, near = pl.pallas_call(
        functools.partial(pack_kernel, edge),
        out_shape=(
            jax.ShapeDtypeStruct((2 * rows, att), bf16),
            jax.ShapeDtypeStruct((rows + edge, att), bf16),
            jax.ShapeDtypeStruct((rows, att), bf16),
            jax.ShapeDtypeStruct((2 * edge, att), bf16),
            jax.ShapeDtypeStruct(((3 + width // att) * edge, att), bf16),
        ),
        in_specs=[hbm] * 4,
        out_specs=(vmem,) * 5,
        scratch_shapes=[pltpu.SemaphoreType.DMA((10 + width // att,))],
        compiler_params=params,
        name="pack",
    )(in_hbm(key), in_hbm(value), in_hbm(query), in_hbm(cot))
    further = [shifted(own, offset) for offset in range(2, context + 1)]
    keys = shifted(keys, 1)
    near = shifted(near, -1)
    if further:
        near, values = lax.optimization_barrier((near, values))
        values = pl.pallas_call(
            choose_kernel,
            out_shape=jax.ShapeDtypeStruct((rows, att), bf16),
            in_specs=[smem, vmem, vmem],
            out_specs=vmem,
            compiler_params=params,
            name="choose",
        )(device[None], values, further[0])
        values = lax.ppermute(values, "y", [(0, 1), (1, 0)])
    else:
        values = shifted(values, 1)
    tiles = [own, keys, values, *further]
    far = shifted(far, context + 1)

    pieces = att // 32
    layers = lax.axis_size("z")
    split = pieces == layers * lax.axis_size(PLANE_AXES) and layers & (layers - 1) == 0
    core = lax.axis_index("core").astype(jnp.int32) if split else jnp.int32(0)
    place = jnp.stack([device, core])
    piece_rows = -(-(chunks * 16 + chunks) // 16) * 16
    out_frames, attended, log_sums, dhidden, keep, give = pl.pallas_call(
        functools.partial(forward_kernel, context, rows, edge, taps),
        out_shape=(
            jax.ShapeDtypeStruct((rows, width), bf16),
            jax.ShapeDtypeStruct((rows, att), bf16),
            jax.ShapeDtypeStruct((heads, rows), f32),
            jax.ShapeDtypeStruct((rows, width), bf16),
        )
        + (jax.ShapeDtypeStruct((pieces, piece_rows, LANES), bf16),) * 2,
        in_specs=[smem, hbm] + [vmem] * (4 + context) + [hbm] * 3,
        out_specs=(vmem,) * 6,
        scratch_shapes=[
            pltpu.VMEM((query_rows, att), bf16),
            pltpu.VMEM((key_rows, att), bf16),
            pltpu.VMEM((key_rows, att), bf16),
            pltpu.VMEM((query_rows, att), bf16),
            pltpu.VMEM((query_rows, LANES), f32),
            pltpu.VMEM((chunks, query_rows, LANES), f32),
            pltpu.VMEM((chunks, rows + edge, LANES), f32),
            pltpu.VMEM((rows + edge + 8, LANES), f32),
            pltpu.VMEM((LANES, context * rows + LANES), f32),
            pltpu.VMEM((chunks, 2 * pieces, LANES), f32),
            pltpu.VMEM((taps * SUBLANES, LANES), f32),
            pltpu.VMEM((2, pieces, piece_rows, LANES), bf16),
            pltpu.VMEM((rows, att), bf16),
            pltpu.VMEM((att, width), bf16),
            pltpu.VMEM((taps, width), f32),
            pltpu.VMEM((rows, width), bf16),
            pltpu.SemaphoreType.DMA((4,)),
        ],
        compiler_params=params,
        cost_estimate=cost(8 * 10**9, 10**7),
        name="forward",
    )(place, in_hbm(query), *tiles, far, near, in_hbm(out_weight), in_hbm(conv_kernel), in_hbm(cot))

    if split:
        mine = (keep.astype(f32) + other_core(give).astype(f32)).astype(bf16)
        mine, dhidden = lax.optimization_barrier((mine, dhidden))
    query_grad, own_grads, *messages = pl.pallas_call(
        functools.partial(backward_kernel, context, rows),
        out_shape=(
            jax.ShapeDtypeStruct((rows, att), bf16),
            jax.ShapeDtypeStruct((2 * rows, att), f32),
        )
        + (jax.ShapeDtypeStruct((2 * rows, att), bf16),) * context,
        in_specs=[smem, hbm] + [vmem] * (4 + context) + [hbm] * 2,
        out_specs=(vmem,) * (2 + context),
        scratch_shapes=[
            pltpu.VMEM((rows, att), bf16),
            pltpu.VMEM((rows, width), bf16),
            pltpu.VMEM((att, width), bf16),
            pltpu.VMEM((rows, att), bf16),
            pltpu.VMEM((context + 1, rows, rows), f32),
            pltpu.SemaphoreType.DMA((3,)),
        ],
        compiler_params=params,
        cost_estimate=cost(6 * 10**9, 10**7),
        name="backward",
    )(place, in_hbm(query), *tiles, attended, log_sums, in_hbm(dhidden), in_hbm(out_weight))
    if split:
        mine, own_grads, *messages = lax.optimization_barrier(
            (collected(mine), own_grads, *messages)
        )
    messages = dict(enumerate(messages, 1))
    if context > 1:
        swapped = lax.ppermute(messages.pop(1), "y", [(0, 1), (1, 0)])
        own_grads, messages[2] = pl.pallas_call(
            relay_kernel,
            out_shape=(
                jax.ShapeDtypeStruct((2 * rows, att), f32),
                jax.ShapeDtypeStruct((2 * rows, att), bf16),
            ),
            in_specs=[smem] + [vmem] * 3,
            out_specs=(vmem,) * 2,
            compiler_params=params,
            cost_estimate=cost(10**9, 3 * 10**6),
            name="relay",
        )(place, own_grads, swapped, messages[2])
    if split:
        mine = summed_along(mine, "z")
        mine, messages = lax.optimization_barrier((mine, messages))
        mine = exchange(jnp.broadcast_to(mine, (lax.axis_size(PLANE_AXES), *mine.shape)))
        mine = mine.reshape(keep.shape)
    messages = [shifted(message, -offset) for offset, message in messages.items()]
    if split:
        mine, *messages = lax.optimization_barrier((mine, *messages))
        halves = (mine, other_core(mine))
    else:
        halves = lax.psum((keep, give), ("x", "core", "z", "y"))
    key_grad, value_grad = pl.pallas_call(
        merge_kernel,
        out_shape=(jax.ShapeDtypeStruct((rows, att), bf16),) * 2,
        in_specs=[vmem] * (1 + len(messages)),
        out_specs=(vmem,) * 2,
        compiler_params=params,
        name="merge",
    )(own_grads, *messages)
    weight_total, kernel_total = pl.pallas_call(
        unpack_kernel,
        out_shape=(
            jax.ShapeDtypeStruct((att, width), f32),
            jax.ShapeDtypeStruct((taps, width), f32),
        ),
        in_specs=[smem, vmem, vmem],
        out_specs=(vmem, vmem),
        compiler_params=params,
        name="unpack",
    )(place, *halves)
    return (
        out_frames[None],
        query_grad[None],
        key_grad[None],
        value_grad[None],
        weight_total,
        kernel_total,
    )


def solution(mesh):
    sizes = (mesh.shape["dp"] // 2, 2, mesh.shape["blk"] // 2, 2)
    fine = Mesh(mesh.devices.reshape(sizes), ("x", "core", "z", "y"))
    frames = P(("x", "core"), RUN_AXES, None)
    return jax.shard_map(
        per_device,
        mesh=fine,
        in_specs=(frames, frames, frames, P(), P(), frames),
        out_specs=(frames, frames, frames, frames, P(), P()),
        check_vma=False,
    )
```

```python
import functools
import math

import jax
import jax.numpy as jnp
from jax import lax
from jax.experimental import pallas as pl
from jax.experimental.pallas import tpu as pltpu
from jax.sharding import Mesh
from jax.sharding import PartitionSpec as P

HEAD_DIM = 64
CTX_MAX = 3
LANES = 128
SUBLANES = 8
NEGATIVE = -1e30
RUN_AXES = ("z", "y")
PLANE_AXES = ("x", "y")
VMEM_LIMIT = 28 * 1024 * 1024

NN = (((1,), (0,)), ((), ()))
NT = (((1,), (1,)), ((), ()))
TN = (((0,), (0,)), ((), ()))


def dot(a, b, dims, precision=None):
    return lax.dot_general(a, b, dims, precision=precision, preferred_element_type=jnp.float32)


def shifted(x, by):
    devices = range(lax.axis_size(RUN_AXES))
    return lax.ppermute(x, RUN_AXES, [(i, i + by) for i in devices if i + by in devices])


def in_hbm(x):
    return pltpu.with_memory_space_constraint(x, pltpu.HBM)


def cost(flops, data):
    return pl.CostEstimate(flops=flops, bytes_accessed=data, transcendentals=0)


def head_masks():
    lane = lax.broadcasted_iota(jnp.int32, (1, LANES), 1)
    first = jnp.where(lane < HEAD_DIM, 1.0, 0.0)
    return first.astype(jnp.bfloat16), (1.0 - first).astype(jnp.bfloat16)


def stack_heads(pair):
    first, second = head_masks()
    return jnp.concatenate([pair * first, pair * second], axis=0)


def merge_heads(stacked):
    rows = stacked.shape[0] // 2
    lane = lax.broadcasted_iota(jnp.int32, (rows, LANES), 1)
    return jnp.where(lane < HEAD_DIM, stacked[:rows], stacked[rows:])


def pack_kernel(
    edge, k_ref, v_ref, q_ref, cot_ref, own_ref, keys_ref, values_ref, far_ref, near_ref, sems
):
    rows, att = k_ref.shape
    width = cot_ref.shape[1]
    head, tail = pl.ds(0, edge), pl.ds(rows - edge, edge)
    moves = [
        (k_ref, own_ref.at[pl.ds(0, rows)]),
        (v_ref, own_ref.at[pl.ds(rows, rows)]),
        (k_ref, keys_ref.at[pl.ds(0, rows)]),
        (q_ref.at[tail], keys_ref.at[pl.ds(rows, edge)]),
        (v_ref, values_ref),
        (k_ref.at[tail], far_ref.at[pl.ds(0, edge)]),
        (v_ref.at[tail], far_ref.at[pl.ds(edge, edge)]),
        (k_ref.at[head], near_ref.at[pl.ds(0, edge)]),
        (v_ref.at[head], near_ref.at[pl.ds(edge, edge)]),
        (q_ref.at[head], near_ref.at[pl.ds(2 * edge, edge)]),
    ]
    for part in range(width // att):
        piece = cot_ref.at[head, pl.ds(part * att, att)]
        moves.append((piece, near_ref.at[pl.ds((3 + part) * edge, edge)]))
    copies = [pltpu.make_async_copy(a, b, sems.at[i]) for i, (a, b) in enumerate(moves)]
    for copy in copies:
        copy.start()
    for copy in copies:
        copy.wait()


def choose_kernel(device_ref, even_ref, odd_ref, out_ref):
    odd = lax.rem(device_ref[0], 2)
    rows = out_ref.shape[0]

    @pl.when(odd == 0)
    def _():
        out_ref[...] = even_ref[...]

    @pl.when(odd != 0)
    def _():
        out_ref[...] = odd_ref[odd_ref.shape[0] - rows :]


def tile_places(rows, own_ref, keys_ref, values_ref, *further_refs):
    places = [(own_ref, 0, own_ref, rows), (keys_ref, 0, values_ref, 0)]
    return places + [(ref, 0, ref, rows) for ref in further_refs]


def scores_kernel(context, rows, edge, *refs):
    device_ref, q_hbm, own_ref, keys_ref = refs[:4]
    further_refs = refs[4 : 3 + context]
    far_ref, near_ref, weights_ref, lse_ref, qx, kx, lx, q_ref, bias, sem = refs[3 + context :]
    att = q_ref.shape[1]
    pairs = att // LANES
    span = context * rows
    block = LANES
    keys = span + block
    scale = 1.0 / math.sqrt(HEAD_DIM)
    start = device_ref[0] * rows

    fetch = pltpu.make_async_copy(q_hbm, q_ref, sem)
    fetch.start()
    kx[:edge] = far_ref[:edge]
    for offset, ref in enumerate((own_ref, keys_ref, *further_refs)):
        first = edge + (context - offset) * rows
        kx[first : first + rows] = ref[:rows]
    kx[edge + span + rows :] = near_ref[:edge]
    qx[:edge] = keys_ref[rows : rows + edge] * scale
    qx[edge + rows :] = near_ref[2 * edge : 3 * edge] * scale
    fetch.wait()
    qx[edge : edge + rows] = q_ref[...] * scale

    lane_id = lax.broadcasted_iota(jnp.int32, (block, LANES), 1)
    for b in range(qx.shape[0] // block):
        row_id = lax.broadcasted_iota(jnp.int32, (block, keys), 0)
        key_id = lax.broadcasted_iota(jnp.int32, (block, keys), 1)
        distance = row_id - key_id + span
        key_time = key_id + (start - edge - span + b * block)
        visible = (distance >= 0) & (distance < span) & (key_time >= 0)
        bias[...] = jnp.where(visible, 0.0, NEGATIVE)
        log_sums = jnp.zeros((block, LANES), jnp.float32)
        for pair in range(pairs):
            columns = slice(pair * LANES, (pair + 1) * LANES)
            qs = stack_heads(qx[b * block : (b + 1) * block, columns])
            scores = dot(qs, kx[b * block : b * block + keys, columns], NT)
            hidden_pairs = bias[...]
            scores = scores + jnp.concatenate([hidden_pairs, hidden_pairs], axis=0)
            row_max = jnp.max(scores, axis=1, keepdims=True)
            weights = jnp.exp(scores - row_max)
            row_sum = jnp.sum(weights, axis=1, keepdims=True)
            weights_ref[b * pairs + pair] = (weights * (1.0 / row_sum)).astype(jnp.bfloat16)
            log_sum = row_max + jnp.log(row_sum)
            log_sums = jnp.where(lane_id == 2 * pair, log_sum[:block], log_sums)
            log_sums = jnp.where(lane_id == 2 * pair + 1, log_sum[block:], log_sums)
        lx[b * block : (b + 1) * block] = log_sums
    lse_ref[...] = jnp.transpose(lx[...])[: lse_ref.shape[0], edge : edge + rows]


def forward_kernel(context, rows, edge, taps, *refs):
    tiles = context + 2
    device_ref, weights_ref = refs[:2]
    places = tile_places(rows, *refs[2 : 2 + tiles])
    far_ref, near_ref, w_hbm, conv_hbm, cot_hbm = refs[2 + tiles : 7 + tiles]
    out_ref, att_ref, dhid_ref, keep_ref, give_ref = refs[7 + tiles : 12 + tiles]
    vx, ax, hid, cotx, dm, kp, ks, parts = refs[12 + tiles : 20 + tiles]
    w_ref, conv_ref, cot_ref, sems = refs[20 + tiles :]

    att = ax.shape[1]
    width = w_ref.shape[1]
    span = context * rows
    query_rows = rows + 2 * edge
    block = LANES
    keys = span + block
    start = device_ref[0] * rows

    fetches = [
        pltpu.make_async_copy(source, target, sems.at[i])
        for i, (source, target) in enumerate(
            ((w_hbm, w_ref), (cot_hbm, cot_ref), (conv_hbm, conv_ref))
        )
    ]
    for fetch in fetches:
        fetch.start()

    vx[:edge] = far_ref[edge:]
    for offset, (_, _, ref, at) in enumerate(places):
        first = edge + (context - offset) * rows
        vx[first : first + rows] = ref[at : at + rows]
    vx[edge + span + rows :] = near_ref[edge : 2 * edge]

    pairs = att // LANES
    for b in range(query_rows // block):
        for pair in range(pairs):
            columns = slice(pair * LANES, (pair + 1) * LANES)
            values = vx[b * block : b * block + keys, columns]
            mixed = dot(weights_ref[b * pairs + pair], values, NN)
            ax[b * block : (b + 1) * block, columns] = merge_heads(mixed).astype(jnp.bfloat16)
    att_ref[...] = ax[edge : edge + rows]

    fetches[0].wait()
    step = 2 * LANES
    for part in range(width // step):
        product = dot(ax[...], w_ref[:, part * step : (part + 1) * step], NN)
        product = product.astype(jnp.bfloat16).astype(jnp.float32)
        time = lax.broadcasted_iota(jnp.int32, product.shape, 0) + (start - edge)
        product = jnp.where(time >= 0, product, 0.0)
        hid[2 * part] = product[:, :LANES]
        hid[2 * part + 1] = product[:, LANES:]

    fetches[1].wait()
    fetches[2].wait()
    for chunk in range(width // LANES):
        columns = slice(chunk * LANES, (chunk + 1) * LANES)
        cotx[chunk, :rows] = cot_ref[:, columns].astype(jnp.float32)
        part, lane = divmod(chunk * LANES, att)
        cotx[chunk, rows:] = near_ref[
            (3 + part) * edge : (4 + part) * edge, lane : lane + LANES
        ].astype(jnp.float32)
    kp[...] = jnp.zeros_like(kp)
    dm[rows + edge :] = jnp.zeros_like(dm[rows + edge :])

    apart = -(-taps // SUBLANES)
    reach = (apart - 1) * SUBLANES
    part_rows = (rows + edge) // 2

    def convolve(chunk, carry):
        columns = pl.ds(pl.multiple_of(chunk * LANES, LANES), LANES)
        for first in range(0, rows + edge, part_rows):
            mixed = jnp.zeros((part_rows, LANES), jnp.float32)
            for shift in range(SUBLANES):
                low = edge + first - shift - reach
                window = hid[chunk, low : low + part_rows + reach]
                for tap in range(shift, taps, SUBLANES):
                    at = reach - (tap - shift)
                    mixed += conv_ref[tap : tap + 1, columns] * window[at : at + part_rows]
            sigma = jax.nn.sigmoid(mixed)
            kept = min(part_rows, rows - first)
            out_ref[first : first + kept, columns] = (mixed * sigma)[:kept].astype(jnp.bfloat16)
            dm[first : first + part_rows] = (
                cotx[chunk, first : first + part_rows] * sigma * (1.0 + mixed * (1.0 - sigma))
            )
        part = rows // 2
        for first in range(0, rows, part):
            dhidden = jnp.zeros((part, LANES), jnp.float32)
            for shift in range(SUBLANES):
                low = first + shift
                window = dm[low : low + part + reach]
                for tap in range(shift, taps, SUBLANES):
                    at = tap - shift
                    dhidden += conv_ref[tap : tap + 1, columns] * window[at : at + part]
            dhid_ref[first : first + part, columns] = dhidden.astype(jnp.bfloat16)
        for shift in range(SUBLANES):
            sums = [jnp.zeros((SUBLANES, LANES), jnp.float32)] * apart
            for first in range(0, rows, part):
                low = edge + first - shift - reach
                window = hid[chunk, low : low + part + reach]
                own = dm[first : first + part]
                for tap in range(shift, taps, SUBLANES):
                    at = reach - (tap - shift)
                    product = (own * window[at : at + part]).reshape(-1, SUBLANES, LANES)
                    sums[tap // SUBLANES] += jnp.sum(product, axis=0)
            for tap in range(shift, taps, SUBLANES):
                ks[tap * SUBLANES : (tap + 1) * SUBLANES] = sums[tap // SUBLANES]
        total = ks[pl.ds(0, taps, SUBLANES)]
        for row in range(1, SUBLANES):
            total += ks[pl.ds(row, taps, SUBLANES)]
        kp[chunk, :taps] = total
        return carry

    lax.fori_loop(0, width // LANES, convolve, 0)

    _, pieces, piece_rows, _ = parts.shape
    chunks = width // LANES
    group = att // (2 * pieces)
    core = device_ref[1]
    own = ax[edge : edge + rows]
    for part in range(width // step):
        product = dot(own, dhid_ref[:, part * step : (part + 1) * step], TN).astype(jnp.bfloat16)
        for chunk in (2 * part, 2 * part + 1):
            tile = product[:, (chunk - 2 * part) * LANES : (chunk - 2 * part + 1) * LANES]
            for half in range(2):
                for piece in range(pieces):
                    first = (half * pieces + piece) * group
                    parts[half, piece, chunk * group : (chunk + 1) * group] = tile[
                        first : first + group
                    ]
    rest = jnp.zeros((piece_rows - chunks * (group + 1), LANES), jnp.float32)
    for half in range(2):
        for piece in range(pieces):
            tap = half * pieces + piece
            row = [kp[chunk, tap : tap + 1] for chunk in range(chunks)]
            row = jnp.concatenate(row + [rest], axis=0).astype(jnp.bfloat16)
            parts[half, piece, chunks * group :] = row
    keep_ref[...] = parts[core]
    give_ref[...] = parts[1 - core]


def unpack_kernel(device_ref, near_ref, far_ref, weight_ref, kernel_ref):
    pieces, piece_rows, _ = near_ref.shape
    att, width = weight_ref.shape
    taps = kernel_ref.shape[0]
    chunks = width // LANES
    group = att // (2 * pieces)
    core = device_ref[1]

    def write(refs):
        for half, ref in enumerate(refs):
            for piece in range(pieces):
                tap = half * pieces + piece
                for chunk in range(chunks):
                    columns = slice(chunk * LANES, (chunk + 1) * LANES)
                    tile = ref[piece, chunk * group : (chunk + 1) * group].astype(jnp.float32)
                    weight_ref[tap * group : (tap + 1) * group, columns] = tile
                if tap < taps:
                    row = ref[piece, chunks * group :].astype(jnp.float32)
                    for chunk in range(chunks):
                        columns = slice(chunk * LANES, (chunk + 1) * LANES)
                        kernel_ref[tap : tap + 1, columns] = row[chunk : chunk + 1]

    pl.when(core == 0)(lambda: write((near_ref, far_ref)))
    pl.when(core != 0)(lambda: write((far_ref, near_ref)))


def backward_kernel(context, rows, *refs):
    tiles = context + 2
    device_ref, q_hbm = refs[:2]
    places = tile_places(rows, *refs[2 : 2 + tiles])
    att_hbm, lse_ref, dhid_hbm, w_hbm = refs[2 + tiles : 6 + tiles]
    dq_ref, own_ref = refs[6 + tiles : 8 + tiles]
    message_refs = refs[8 + tiles : 8 + tiles + context]
    q_ref, dhid_ref, w_ref, att_ref, datt, bias, sems = refs[8 + tiles + context :]

    att = q_ref.shape[1]
    heads = att // HEAD_DIM
    span = context * rows
    scale = 1.0 / math.sqrt(HEAD_DIM)
    start = device_ref[0] * rows

    fetches = [
        pltpu.make_async_copy(source, target, sems.at[i])
        for i, (source, target) in enumerate(
            ((w_hbm, w_ref), (dhid_hbm, dhid_ref), (q_hbm, q_ref), (att_hbm, att_ref))
        )
    ]
    for fetch in fetches:
        fetch.start()
    for offset in range(context + 1):
        key_id = lax.broadcasted_iota(jnp.int32, (rows, rows), 0)
        row_id = lax.broadcasted_iota(jnp.int32, (rows, rows), 1)
        distance = row_id - key_id + offset * rows
        key_time = key_id + (start - offset * rows)
        visible = (distance >= 0) & (distance < span) & (key_time >= 0)
        bias[offset] = jnp.where(visible, 0.0, NEGATIVE)

    for fetch in fetches:
        fetch.wait()
    dattended = dot(dhid_ref[...], w_ref[...], NT).astype(jnp.bfloat16)
    datt[...] = dattended
    product = dattended.astype(jnp.float32) * att_ref[...].astype(jnp.float32)
    head_id = lax.broadcasted_iota(jnp.int32, (heads, att), 0)
    feature_id = lax.broadcasted_iota(jnp.int32, (heads, att), 1)
    ours = (feature_id >= head_id * HEAD_DIM) & (feature_id < (head_id + 1) * HEAD_DIM)
    deltas = dot(jnp.where(ours, 1.0, 0.0), product, NT, lax.Precision.HIGHEST)

    for pair in range(att // LANES):
        columns = slice(pair * LANES, (pair + 1) * LANES)
        qs = stack_heads(q_ref[:, columns] * scale)
        ds = stack_heads(datt[:, columns])
        log_sum = [lse_ref[2 * pair + i : 2 * pair + i + 1] for i in (0, 1)]
        delta = [deltas[2 * pair + i : 2 * pair + i + 1] for i in (0, 1)]
        log_sum = jnp.concatenate(log_sum, axis=1)
        delta = jnp.concatenate(delta, axis=1)
        dquery = jnp.zeros((2 * rows, LANES), jnp.float32)
        for offset, (k_ref, k_at, v_ref, v_at) in enumerate(places):
            kp = k_ref[k_at : k_at + rows, columns]
            vp = v_ref[v_at : v_at + rows, columns]
            hidden_pairs = jnp.concatenate([bias[offset], bias[offset]], axis=1)
            probs = jnp.exp(dot(kp, qs, NT) + hidden_pairs - log_sum)
            dprobs = dot(vp, ds, NT)
            dscores = (probs * (dprobs - delta)).astype(jnp.bfloat16)
            dvalue = dot(probs.astype(jnp.bfloat16), ds, NN)
            dkey = dot(dscores, qs, NN)
            dquery += dot(dscores, kp, TN)
            target = message_refs[offset - 1] if offset else own_ref
            target[:rows, columns] = dkey.astype(target.dtype)
            target[rows:, columns] = dvalue.astype(target.dtype)
        dq_ref[:, columns] = (merge_heads(dquery) * scale).astype(jnp.bfloat16)


def relay_kernel(device_ref, own_ref, swapped_ref, message_ref, own_out, message_out):
    odd = lax.rem(device_ref[0], 2).astype(jnp.float32)
    swapped = swapped_ref[...].astype(jnp.float32)
    own_out[...] = own_ref[...] + swapped * (1.0 - odd)
    message_out[...] = (message_ref[...].astype(jnp.float32) + swapped * odd).astype(jnp.bfloat16)


def merge_kernel(*refs):
    own_ref, *message_refs, dk_ref, dv_ref = refs
    rows = dk_ref.shape[0]
    total = own_ref[...]
    for message_ref in message_refs:
        total += message_ref[...].astype(jnp.float32)
    total = total.astype(jnp.bfloat16)
    dk_ref[...] = total[:rows]
    dv_ref[...] = total[rows:]


def exchange(x):
    return lax.all_to_all(x, PLANE_AXES, 0, 0, tiled=True)


def collected(x):
    x = exchange(x.reshape(lax.axis_size(PLANE_AXES), -1, LANES))
    return jnp.sum(x.astype(jnp.float32), axis=0).astype(x.dtype)


def summed_along(x, axis):
    size, step = lax.axis_size(axis), 1
    while step < size:
        other = lax.ppermute(x, axis, [(i, i ^ step) for i in range(size)])
        x = (x.astype(jnp.float32) + other.astype(jnp.float32)).astype(x.dtype)
        step *= 2
    return x


def other_core(x):
    return lax.ppermute(x, "core", [(0, 1), (1, 0)])


def per_device(queries, key_in, value_in, out_weight, conv_kernel, cotangent):
    bf16, f32 = jnp.bfloat16, jnp.float32
    query, key, value, cot = queries[0], key_in[0], value_in[0], cotangent[0]
    runs = lax.axis_size(RUN_AXES)
    device = lax.axis_index(RUN_AXES).astype(jnp.int32)
    rows, att = query.shape
    width = out_weight.shape[1]
    heads = att // HEAD_DIM
    taps = conv_kernel.shape[0]
    edge = -(-(taps - 1) // 16) * 16
    context = min(CTX_MAX, runs // 4)

    query_rows = rows + 2 * edge
    key_rows = query_rows + context * rows
    chunks = width // LANES
    vmem = pl.BlockSpec(memory_space=pltpu.VMEM)
    smem = pl.BlockSpec(memory_space=pltpu.SMEM)
    hbm = pl.BlockSpec(memory_space=pltpu.HBM)
    params = pltpu.CompilerParams(vmem_limit_bytes=VMEM_LIMIT)

    own, keys, values, far, near = pl.pallas_call(
        functools.partial(pack_kernel, edge),
        out_shape=(
            jax.ShapeDtypeStruct((2 * rows, att), bf16),
            jax.ShapeDtypeStruct((rows + edge, att), bf16),
            jax.ShapeDtypeStruct((rows, att), bf16),
            jax.ShapeDtypeStruct((2 * edge, att), bf16),
            jax.ShapeDtypeStruct(((3 + width // att) * edge, att), bf16),
        ),
        in_specs=[hbm] * 4,
        out_specs=(vmem,) * 5,
        scratch_shapes=[pltpu.SemaphoreType.DMA((10 + width // att,))],
        compiler_params=params,
        name="pack",
    )(in_hbm(key), in_hbm(value), in_hbm(query), in_hbm(cot))
    further = [shifted(own, offset) for offset in range(2, context + 1)]
    keys = shifted(keys, 1)
    near = shifted(near, -1)
    if further:
        near, values = lax.optimization_barrier((near, values))
        values = pl.pallas_call(
            choose_kernel,
            out_shape=jax.ShapeDtypeStruct((rows, att), bf16),
            in_specs=[smem, vmem, vmem],
            out_specs=vmem,
            compiler_params=params,
            name="choose",
        )(device[None], values, further[0])
        values = lax.ppermute(values, "y", [(0, 1), (1, 0)])
    else:
        values = shifted(values, 1)
    tiles = [own, keys, values, *further]
    far = shifted(far, context + 1)

    pieces = att // 32
    layers = lax.axis_size("z")
    split = pieces == layers * lax.axis_size(PLANE_AXES) and layers & (layers - 1) == 0
    core = lax.axis_index("core").astype(jnp.int32) if split else jnp.int32(0)
    place = jnp.stack([device, core])
    piece_rows = -(-(chunks * 16 + chunks) // 16) * 16
    blocks = query_rows // LANES * (att // LANES)
    key_span = context * rows + LANES
    weights, log_sums = pl.pallas_call(
        functools.partial(scores_kernel, context, rows, edge),
        out_shape=(
            jax.ShapeDtypeStruct((blocks, 2 * LANES, key_span), bf16),
            jax.ShapeDtypeStruct((heads, rows), f32),
        ),
        in_specs=[smem, hbm] + [vmem] * (3 + context),
        out_specs=(vmem,) * 2,
        scratch_shapes=[
            pltpu.VMEM((query_rows, att), bf16),
            pltpu.VMEM((key_rows, att), bf16),
            pltpu.VMEM((query_rows, LANES), f32),
            pltpu.VMEM((rows, att), bf16),
            pltpu.VMEM((LANES, key_span), f32),
            pltpu.SemaphoreType.DMA,
        ],
        compiler_params=params,
        cost_estimate=cost(8 * 10**9, 10**7),
        name="scores",
    )(place, in_hbm(query), own, keys, *further, far, near)
    out_frames, attended, dhidden, keep, give = pl.pallas_call(
        functools.partial(forward_kernel, context, rows, edge, taps),
        out_shape=(
            jax.ShapeDtypeStruct((rows, width), bf16),
            jax.ShapeDtypeStruct((rows, att), bf16),
            jax.ShapeDtypeStruct((rows, width), bf16),
        )
        + (jax.ShapeDtypeStruct((pieces, piece_rows, LANES), bf16),) * 2,
        in_specs=[smem] + [vmem] * (5 + context) + [hbm] * 3,
        out_specs=(vmem,) * 5,
        scratch_shapes=[
            pltpu.VMEM((key_rows, att), bf16),
            pltpu.VMEM((query_rows, att), bf16),
            pltpu.VMEM((chunks, query_rows, LANES), f32),
            pltpu.VMEM((chunks, rows + edge, LANES), f32),
            pltpu.VMEM((rows + edge + 8, LANES), f32),
            pltpu.VMEM((chunks, 2 * pieces, LANES), f32),
            pltpu.VMEM((taps * SUBLANES, LANES), f32),
            pltpu.VMEM((2, pieces, piece_rows, LANES), bf16),
            pltpu.VMEM((att, width), bf16),
            pltpu.VMEM((taps, width), f32),
            pltpu.VMEM((rows, width), bf16),
            pltpu.SemaphoreType.DMA((3,)),
        ],
        compiler_params=params,
        cost_estimate=cost(8 * 10**9, 10**7),
        name="forward",
    )(place, weights, *tiles, far, near, in_hbm(out_weight), in_hbm(conv_kernel), in_hbm(cot))

    if split:
        mine = (keep.astype(f32) + other_core(give).astype(f32)).astype(bf16)
        mine, dhidden = lax.optimization_barrier((mine, dhidden))
    query_grad, own_grads, *messages = pl.pallas_call(
        functools.partial(backward_kernel, context, rows),
        out_shape=(
            jax.ShapeDtypeStruct((rows, att), bf16),
            jax.ShapeDtypeStruct((2 * rows, att), f32),
        )
        + (jax.ShapeDtypeStruct((2 * rows, att), bf16),) * context,
        in_specs=[smem, hbm] + [vmem] * (2 + context) + [hbm, vmem, hbm, hbm],
        out_specs=(vmem,) * (2 + context),
        scratch_shapes=[
            pltpu.VMEM((rows, att), bf16),
            pltpu.VMEM((rows, width), bf16),
            pltpu.VMEM((att, width), bf16),
            pltpu.VMEM((rows, att), bf16),
            pltpu.VMEM((rows, att), bf16),
            pltpu.VMEM((context + 1, rows, rows), f32),
            pltpu.SemaphoreType.DMA((4,)),
        ],
        compiler_params=params,
        cost_estimate=cost(6 * 10**9, 10**7),
        name="backward",
    )(place, in_hbm(query), *tiles, in_hbm(attended), log_sums, in_hbm(dhidden), in_hbm(out_weight))
    if split:
        mine, own_grads, *messages = lax.optimization_barrier(
            (collected(mine), own_grads, *messages)
        )
    messages = dict(enumerate(messages, 1))
    if context > 1:
        swapped = lax.ppermute(messages.pop(1), "y", [(0, 1), (1, 0)])
        own_grads, messages[2] = pl.pallas_call(
            relay_kernel,
            out_shape=(
                jax.ShapeDtypeStruct((2 * rows, att), f32),
                jax.ShapeDtypeStruct((2 * rows, att), bf16),
            ),
            in_specs=[smem] + [vmem] * 3,
            out_specs=(vmem,) * 2,
            compiler_params=params,
            cost_estimate=cost(5 * 10**9, 10**7),
            name="relay",
        )(place, own_grads, swapped, messages[2])
    if split:
        mine = summed_along(mine, "z")
        mine, messages = lax.optimization_barrier((mine, messages))
        mine = exchange(jnp.broadcast_to(mine, (lax.axis_size(PLANE_AXES), *mine.shape)))
        mine = mine.reshape(keep.shape)
    messages = [shifted(message, -offset) for offset, message in messages.items()]
    key_grad, value_grad = pl.pallas_call(
        merge_kernel,
        out_shape=(jax.ShapeDtypeStruct((rows, att), bf16),) * 2,
        in_specs=[vmem] * (1 + len(messages)),
        out_specs=(vmem,) * 2,
        compiler_params=params,
        cost_estimate=cost(8 * 10**9, 10**7),
        name="merge",
    )(own_grads, *messages)
    if split:
        mine, key_grad, value_grad = lax.optimization_barrier((mine, key_grad, value_grad))
        halves = (mine, other_core(mine))
    else:
        halves = lax.psum((keep, give), ("x", "core", "z", "y"))
    weight_total, kernel_total = pl.pallas_call(
        unpack_kernel,
        out_shape=(
            jax.ShapeDtypeStruct((att, width), f32),
            jax.ShapeDtypeStruct((taps, width), f32),
        ),
        in_specs=[smem, vmem, vmem],
        out_specs=(vmem, vmem),
        compiler_params=params,
        name="unpack",
    )(place, *halves)
    return (
        out_frames[None],
        query_grad[None],
        key_grad[None],
        value_grad[None],
        weight_total,
        kernel_total,
    )


def solution(mesh):
    sizes = (mesh.shape["dp"] // 2, 2, mesh.shape["blk"] // 2, 2)
    fine = Mesh(mesh.devices.reshape(sizes), ("x", "core", "z", "y"))
    frames = P(("x", "core"), RUN_AXES, None)
    return jax.shard_map(
        per_device,
        mesh=fine,
        in_specs=(frames, frames, frames, P(), P(), frames),
        out_specs=(frames, frames, frames, frames, P(), P()),
        check_vma=False,
    )
```

```python
import functools
import math

import jax
import jax.numpy as jnp
from jax import lax
from jax.experimental import pallas as pl
from jax.experimental.pallas import tpu as pltpu
from jax.sharding import Mesh
from jax.sharding import PartitionSpec as P

HEAD_DIM = 64
CTX_MAX = 3
LANES = 128
SUBLANES = 8
NEGATIVE = -1e30
RUN_AXES = ("z", "y")
PLANE_AXES = ("x", "y")
VMEM_LIMIT = 28 * 1024 * 1024

NN = (((1,), (0,)), ((), ()))
NT = (((1,), (1,)), ((), ()))
TN = (((0,), (0,)), ((), ()))


def dot(a, b, dims, precision=None):
    return lax.dot_general(a, b, dims, precision=precision, preferred_element_type=jnp.float32)


def shifted(x, by):
    devices = range(lax.axis_size(RUN_AXES))
    return lax.ppermute(x, RUN_AXES, [(i, i + by) for i in devices if i + by in devices])


def in_hbm(x):
    return pltpu.with_memory_space_constraint(x, pltpu.HBM)


def cost(flops, data):
    return pl.CostEstimate(flops=flops, bytes_accessed=data, transcendentals=0)


def head_masks():
    lane = lax.broadcasted_iota(jnp.int32, (1, LANES), 1)
    first = jnp.where(lane < HEAD_DIM, 1.0, 0.0)
    return first.astype(jnp.bfloat16), (1.0 - first).astype(jnp.bfloat16)


def stack_heads(pair):
    first, second = head_masks()
    return jnp.concatenate([pair * first, pair * second], axis=0)


def merge_heads(stacked):
    rows = stacked.shape[0] // 2
    lane = lax.broadcasted_iota(jnp.int32, (rows, LANES), 1)
    return jnp.where(lane < HEAD_DIM, stacked[:rows], stacked[rows:])


def pack_kernel(
    edge, k_ref, v_ref, q_ref, cot_ref, own_ref, keys_ref, values_ref, far_ref, near_ref, sems
):
    rows, att = k_ref.shape
    width = cot_ref.shape[1]
    head, tail = pl.ds(0, edge), pl.ds(rows - edge, edge)
    moves = [
        (k_ref, own_ref.at[pl.ds(0, rows)]),
        (v_ref, own_ref.at[pl.ds(rows, rows)]),
        (k_ref, keys_ref.at[pl.ds(0, rows)]),
        (q_ref.at[tail], keys_ref.at[pl.ds(rows, edge)]),
        (v_ref, values_ref),
        (k_ref.at[tail], far_ref.at[pl.ds(0, edge)]),
        (v_ref.at[tail], far_ref.at[pl.ds(edge, edge)]),
        (k_ref.at[head], near_ref.at[pl.ds(0, edge)]),
        (v_ref.at[head], near_ref.at[pl.ds(edge, edge)]),
        (q_ref.at[head], near_ref.at[pl.ds(2 * edge, edge)]),
    ]
    for part in range(width // att):
        piece = cot_ref.at[head, pl.ds(part * att, att)]
        moves.append((piece, near_ref.at[pl.ds((3 + part) * edge, edge)]))
    copies = [pltpu.make_async_copy(a, b, sems.at[i]) for i, (a, b) in enumerate(moves)]
    for copy in copies:
        copy.start()
    for copy in copies:
        copy.wait()


def choose_kernel(device_ref, even_ref, odd_ref, out_ref):
    odd = lax.rem(device_ref[0], 2)
    rows = out_ref.shape[0]

    @pl.when(odd == 0)
    def _():
        out_ref[...] = even_ref[...]

    @pl.when(odd != 0)
    def _():
        out_ref[...] = odd_ref[odd_ref.shape[0] - rows :]


def tile_places(rows, own_ref, keys_ref, values_ref, *further_refs):
    places = [(own_ref, 0, own_ref, rows), (keys_ref, 0, values_ref, 0)]
    return places + [(ref, 0, ref, rows) for ref in further_refs]


def scores_kernel(context, rows, edge, blocks, *refs):
    device_ref, q_hbm, own_ref, keys_ref = refs[:4]
    further_refs = refs[4 : 3 + context]
    edge_ref, weights_ref, lse_ref, qx, kx, lx, q_ref, bias, sem = refs[3 + context :]
    att = q_ref.shape[1]
    pairs = att // LANES
    span = context * rows
    block = LANES
    keys = span + block
    scale = 1.0 / math.sqrt(HEAD_DIM)
    start = device_ref[0] * rows

    fetch = pltpu.make_async_copy(q_hbm, q_ref, sem)
    fetch.start()
    for offset, ref in enumerate((own_ref, keys_ref, *further_refs)):
        first = edge + (context - offset) * rows
        kx[first : first + rows] = ref[:rows]
    if blocks[0] == 0:
        kx[:edge] = edge_ref[:edge]
        qx[:edge] = keys_ref[rows : rows + edge] * scale
    else:
        kx[edge + span + rows :] = edge_ref[:edge]
        qx[edge + rows :] = edge_ref[2 * edge : 3 * edge] * scale
    fetch.wait()
    qx[edge : edge + rows] = q_ref[...] * scale

    lane_id = lax.broadcasted_iota(jnp.int32, (block, LANES), 1)
    for place, b in enumerate(blocks):
        row_id = lax.broadcasted_iota(jnp.int32, (block, keys), 0)
        key_id = lax.broadcasted_iota(jnp.int32, (block, keys), 1)
        distance = row_id - key_id + span
        key_time = key_id + (start - edge - span + b * block)
        visible = (distance >= 0) & (distance < span) & (key_time >= 0)
        bias[...] = jnp.where(visible, 0.0, NEGATIVE)
        log_sums = jnp.zeros((block, LANES), jnp.float32)
        for pair in range(pairs):
            columns = slice(pair * LANES, (pair + 1) * LANES)
            qs = stack_heads(qx[b * block : (b + 1) * block, columns])
            scores = dot(qs, kx[b * block : b * block + keys, columns], NT)
            hidden_pairs = bias[...]
            scores = scores + jnp.concatenate([hidden_pairs, hidden_pairs], axis=0)
            row_max = jnp.max(scores, axis=1, keepdims=True)
            weights = jnp.exp(scores - row_max)
            row_sum = jnp.sum(weights, axis=1, keepdims=True)
            weights_ref[place * pairs + pair] = (weights * (1.0 / row_sum)).astype(jnp.bfloat16)
            log_sum = row_max + jnp.log(row_sum)
            log_sums = jnp.where(lane_id == 2 * pair, log_sum[:block], log_sums)
            log_sums = jnp.where(lane_id == 2 * pair + 1, log_sum[block:], log_sums)
        lx[place * block : (place + 1) * block] = log_sums
    lse_ref[...] = jnp.transpose(lx[...])[: lse_ref.shape[0]]


def forward_kernel(context, rows, edge, taps, *refs):
    tiles = context + 2
    device_ref, late_ref, early_ref = refs[:3]
    places = tile_places(rows, *refs[3 : 3 + tiles])
    far_ref, near_ref, w_hbm, conv_hbm, cot_hbm = refs[3 + tiles : 8 + tiles]
    out_hbm, att_hbm, dhid_hbm, keep_ref, give_ref, hid, dm = refs[8 + tiles : 15 + tiles]
    vx, ax, cotx, parts, w_ref, conv_ref, cot_ref, out_ref, dhid_ref, sems = refs[15 + tiles :]

    att = ax.shape[1]
    width = w_ref.shape[1]
    span = context * rows
    query_rows = rows + 2 * edge
    block = LANES
    keys = span + block
    start = device_ref[0] * rows

    fetches = [
        pltpu.make_async_copy(source, target, sems.at[i])
        for i, (source, target) in enumerate(
            ((w_hbm, w_ref), (cot_hbm, cot_ref), (conv_hbm, conv_ref))
        )
    ]
    for fetch in fetches:
        fetch.start()

    vx[:edge] = far_ref[edge:]
    for offset, (_, _, ref, at) in enumerate(places):
        first = edge + (context - offset) * rows
        vx[first : first + rows] = ref[at : at + rows]
    vx[edge + span + rows :] = near_ref[edge : 2 * edge]

    pairs = att // LANES
    for b in range(query_rows // block):
        for pair in range(pairs):
            columns = slice(pair * LANES, (pair + 1) * LANES)
            values = vx[b * block : b * block + keys, columns]
            weights = early_ref[(b - 1) * pairs + pair] if b else late_ref[pair]
            mixed = dot(weights, values, NN)
            ax[b * block : (b + 1) * block, columns] = merge_heads(mixed).astype(jnp.bfloat16)
    stores = [pltpu.make_async_copy(ax.at[pl.ds(edge, rows)], att_hbm, sems.at[3])]
    stores[0].start()

    fetches[0].wait()
    step = 2 * LANES
    for part in range(width // step):
        product = dot(ax[...], w_ref[:, part * step : (part + 1) * step], NN)
        product = product.astype(jnp.bfloat16).astype(jnp.float32)
        time = lax.broadcasted_iota(jnp.int32, product.shape, 0) + (start - edge)
        product = jnp.where(time >= 0, product, 0.0)
        hid[2 * part] = product[:, :LANES]
        hid[2 * part + 1] = product[:, LANES:]

    fetches[1].wait()
    fetches[2].wait()
    for chunk in range(width // LANES):
        columns = slice(chunk * LANES, (chunk + 1) * LANES)
        cotx[chunk, :rows] = cot_ref[:, columns].astype(jnp.float32)
        part, lane = divmod(chunk * LANES, att)
        cotx[chunk, rows:] = near_ref[
            (3 + part) * edge : (4 + part) * edge, lane : lane + LANES
        ].astype(jnp.float32)
    dm[:, rows + edge :] = jnp.zeros_like(dm[:, rows + edge :])

    apart = -(-taps // SUBLANES)
    reach = (apart - 1) * SUBLANES
    part_rows = (rows + edge) // 2

    def convolve(chunk, carry):
        columns = pl.ds(pl.multiple_of(chunk * LANES, LANES), LANES)
        for first in range(0, rows + edge, part_rows):
            mixed = jnp.zeros((part_rows, LANES), jnp.float32)
            for shift in range(SUBLANES):
                low = edge + first - shift - reach
                window = hid[chunk, low : low + part_rows + reach]
                for tap in range(shift, taps, SUBLANES):
                    at = reach - (tap - shift)
                    mixed += conv_ref[tap : tap + 1, columns] * window[at : at + part_rows]
            sigma = jax.nn.sigmoid(mixed)
            kept = min(part_rows, rows - first)
            out_ref[first : first + kept, columns] = (mixed * sigma)[:kept].astype(jnp.bfloat16)
            dm[chunk, first : first + part_rows] = (
                cotx[chunk, first : first + part_rows] * sigma * (1.0 + mixed * (1.0 - sigma))
            )
        part = rows // 2
        for first in range(0, rows, part):
            dhidden = jnp.zeros((part, LANES), jnp.float32)
            for shift in range(SUBLANES):
                low = first + shift
                window = dm[chunk, low : low + part + reach]
                for tap in range(shift, taps, SUBLANES):
                    at = tap - shift
                    dhidden += conv_ref[tap : tap + 1, columns] * window[at : at + part]
            dhid_ref[first : first + part, columns] = dhidden.astype(jnp.bfloat16)
        return carry

    lax.fori_loop(0, width // LANES, convolve, 0)
    stores.append(pltpu.make_async_copy(out_ref, out_hbm, sems.at[4]))
    stores.append(pltpu.make_async_copy(dhid_ref, dhid_hbm, sems.at[5]))
    for store in stores[1:]:
        store.start()

    _, pieces, _, _ = parts.shape
    group = att // (2 * pieces)
    core = device_ref[1]
    own = ax[edge : edge + rows]
    for part in range(width // step):
        product = dot(own, dhid_ref[:, part * step : (part + 1) * step], TN).astype(jnp.bfloat16)
        for chunk in (2 * part, 2 * part + 1):
            tile = product[:, (chunk - 2 * part) * LANES : (chunk - 2 * part + 1) * LANES]
            for half in range(2):
                for piece in range(pieces):
                    first = (half * pieces + piece) * group
                    parts[half, piece, chunk * group : (chunk + 1) * group] = tile[
                        first : first + group
                    ]
    keep_ref[...] = parts[core]
    give_ref[...] = parts[1 - core]
    for store in stores:
        store.wait()


def kernel_grad_kernel(rows, edge, taps, hid, dm, rows_ref, ks, kp):
    chunks = hid.shape[0]
    pieces = rows_ref.shape[0]
    apart = -(-taps // SUBLANES)
    reach = (apart - 1) * SUBLANES
    part = rows // 2
    kp[...] = jnp.zeros_like(kp)

    def correlate(chunk, carry):
        for shift in range(SUBLANES):
            sums = [jnp.zeros((SUBLANES, LANES), jnp.float32)] * apart
            for first in range(0, rows, part):
                low = edge + first - shift - reach
                window = hid[chunk, low : low + part + reach]
                own = dm[chunk, first : first + part]
                for tap in range(shift, taps, SUBLANES):
                    at = reach - (tap - shift)
                    product = (own * window[at : at + part]).reshape(-1, SUBLANES, LANES)
                    sums[tap // SUBLANES] += jnp.sum(product, axis=0)
            for tap in range(shift, taps, SUBLANES):
                ks[tap * SUBLANES : (tap + 1) * SUBLANES] = sums[tap // SUBLANES]
        total = ks[pl.ds(0, taps, SUBLANES)]
        for row in range(1, SUBLANES):
            total += ks[pl.ds(row, taps, SUBLANES)]
        kp[chunk, :taps] = total
        return carry

    lax.fori_loop(0, chunks, correlate, 0)
    for piece in range(pieces):
        block = [kp[chunk, tap : tap + 1] for tap in (piece, pieces + piece) for chunk in range(chunks)]
        rows_ref[piece] = jnp.concatenate(block, axis=0).astype(jnp.bfloat16)


def join_kernel(keep_ref, given_ref, rows_ref, mine_ref):
    split = keep_ref.shape[1]
    total = keep_ref[...].astype(jnp.float32) + given_ref[...].astype(jnp.float32)
    mine_ref[:, :split] = total.astype(jnp.bfloat16)
    mine_ref[:, split:] = rows_ref[...]


def write_half(ref, half, scratch, weight_hbm, sem):
    pieces = ref.shape[0]
    half_rows, width = scratch.shape
    group = half_rows // pieces
    for piece in range(pieces):
        for chunk in range(width // LANES):
            tile = ref[piece, chunk * group : (chunk + 1) * group].astype(jnp.float32)
            scratch[
                piece * group : (piece + 1) * group, chunk * LANES : (chunk + 1) * LANES
            ] = tile
    first = pl.multiple_of(half * half_rows, half_rows)
    copy = pltpu.make_async_copy(scratch, weight_hbm.at[pl.ds(first, half_rows)], sem)
    copy.start()
    return copy


def unpack_near_kernel(device_ref, near_ref, weight_hbm, scratch, sem):
    write_half(near_ref, device_ref[1], scratch, weight_hbm, sem).wait()


def unpack_far_kernel(
    device_ref, near_ref, far_ref, partial_hbm, weight_hbm, kernel_ref, scratch, sem
):
    copy = write_half(far_ref, 1 - device_ref[1], scratch, weight_hbm, sem)
    pieces, piece_rows, _ = near_ref.shape
    taps, width = kernel_ref.shape
    chunks = width // LANES
    for piece in range(pieces):
        total = near_ref[piece, piece_rows - 2 * chunks :].astype(jnp.float32)
        total += far_ref[piece, piece_rows - 2 * chunks :].astype(jnp.float32)
        for half in range(2):
            tap = half * pieces + piece
            if tap < taps:
                for chunk in range(chunks):
                    at = half * chunks + chunk
                    columns = slice(chunk * LANES, (chunk + 1) * LANES)
                    kernel_ref[tap : tap + 1, columns] = total[at : at + 1]
    copy.wait()


def backward_kernel(context, rows, *refs):
    tiles = context + 2
    device_ref, q_hbm = refs[:2]
    places = tile_places(rows, *refs[2 : 2 + tiles])
    att_hbm, late_ref, early_ref, dhid_hbm, w_hbm = refs[2 + tiles : 7 + tiles]
    dq_ref, own_ref = refs[7 + tiles : 9 + tiles]
    message_refs = refs[9 + tiles : 9 + tiles + context]
    q_ref, dhid_ref, w_ref, att_ref, datt, bias, lse_ref, sems = refs[9 + tiles + context :]

    att = q_ref.shape[1]
    heads = att // HEAD_DIM
    span = context * rows
    scale = 1.0 / math.sqrt(HEAD_DIM)
    start = device_ref[0] * rows

    fetches = [
        pltpu.make_async_copy(source, target, sems.at[i])
        for i, (source, target) in enumerate(
            ((w_hbm, w_ref), (dhid_hbm, dhid_ref), (q_hbm, q_ref), (att_hbm, att_ref))
        )
    ]
    for fetch in fetches:
        fetch.start()
    edge = (late_ref.shape[1] + early_ref.shape[1] - rows) // 2
    log_sums = jnp.concatenate([late_ref[...], early_ref[...]], axis=1)
    lse_ref[...] = log_sums[:, edge : edge + rows]
    for offset in range(context + 1):
        key_id = lax.broadcasted_iota(jnp.int32, (rows, rows), 0)
        row_id = lax.broadcasted_iota(jnp.int32, (rows, rows), 1)
        distance = row_id - key_id + offset * rows
        key_time = key_id + (start - offset * rows)
        visible = (distance >= 0) & (distance < span) & (key_time >= 0)
        bias[offset] = jnp.where(visible, 0.0, NEGATIVE)

    for fetch in fetches:
        fetch.wait()
    dattended = dot(dhid_ref[...], w_ref[...], NT).astype(jnp.bfloat16)
    datt[...] = dattended
    product = dattended.astype(jnp.float32) * att_ref[...].astype(jnp.float32)
    head_id = lax.broadcasted_iota(jnp.int32, (heads, att), 0)
    feature_id = lax.broadcasted_iota(jnp.int32, (heads, att), 1)
    ours = (feature_id >= head_id * HEAD_DIM) & (feature_id < (head_id + 1) * HEAD_DIM)
    deltas = dot(jnp.where(ours, 1.0, 0.0), product, NT, lax.Precision.HIGHEST)

    for pair in range(att // LANES):
        columns = slice(pair * LANES, (pair + 1) * LANES)
        qs = stack_heads(q_ref[:, columns] * scale)
        ds = stack_heads(datt[:, columns])
        log_sum = [lse_ref[2 * pair + i : 2 * pair + i + 1] for i in (0, 1)]
        delta = [deltas[2 * pair + i : 2 * pair + i + 1] for i in (0, 1)]
        log_sum = jnp.concatenate(log_sum, axis=1)
        delta = jnp.concatenate(delta, axis=1)
        dquery = jnp.zeros((2 * rows, LANES), jnp.float32)
        for offset, (k_ref, k_at, v_ref, v_at) in enumerate(places):
            kp = k_ref[k_at : k_at + rows, columns]
            vp = v_ref[v_at : v_at + rows, columns]
            hidden_pairs = jnp.concatenate([bias[offset], bias[offset]], axis=1)
            probs = jnp.exp(dot(kp, qs, NT) + hidden_pairs - log_sum)
            dprobs = dot(vp, ds, NT)
            dscores = (probs * (dprobs - delta)).astype(jnp.bfloat16)
            dvalue = dot(probs.astype(jnp.bfloat16), ds, NN)
            dkey = dot(dscores, qs, NN)
            dquery += dot(dscores, kp, TN)
            target = message_refs[offset - 1] if offset else own_ref
            target[:rows, columns] = dkey.astype(target.dtype)
            target[rows:, columns] = dvalue.astype(target.dtype)
        dq_ref[:, columns] = (merge_heads(dquery) * scale).astype(jnp.bfloat16)


def relay_kernel(device_ref, own_ref, swapped_ref, message_ref, own_out, message_out):
    odd = lax.rem(device_ref[0], 2).astype(jnp.float32)
    swapped = swapped_ref[...].astype(jnp.float32)
    own_out[...] = own_ref[...] + swapped * (1.0 - odd)
    message_out[...] = (message_ref[...].astype(jnp.float32) + swapped * odd).astype(jnp.bfloat16)


def merge_kernel(*refs):
    own_ref, *message_refs, dk_ref, dv_ref = refs
    rows = dk_ref.shape[0]
    total = own_ref[...]
    for message_ref in message_refs:
        total += message_ref[...].astype(jnp.float32)
    total = total.astype(jnp.bfloat16)
    dk_ref[...] = total[:rows]
    dv_ref[...] = total[rows:]


def exchange(x):
    return lax.all_to_all(x, PLANE_AXES, 0, 0, tiled=True)


def collected(x):
    x = exchange(x.reshape(lax.axis_size(PLANE_AXES), -1, LANES))
    return jnp.sum(x.astype(jnp.float32), axis=0).astype(x.dtype)


def summed_along(x, axis):
    size, step = lax.axis_size(axis), 1
    while step < size:
        other = lax.ppermute(x, axis, [(i, i ^ step) for i in range(size)])
        x = (x.astype(jnp.float32) + other.astype(jnp.float32)).astype(x.dtype)
        step *= 2
    return x


def other_core(x):
    return lax.ppermute(x, "core", [(0, 1), (1, 0)])


def per_device(queries, key_in, value_in, out_weight, conv_kernel, cotangent):
    bf16, f32 = jnp.bfloat16, jnp.float32
    query, key, value, cot = queries[0], key_in[0], value_in[0], cotangent[0]
    runs = lax.axis_size(RUN_AXES)
    device = lax.axis_index(RUN_AXES).astype(jnp.int32)
    rows, att = query.shape
    width = out_weight.shape[1]
    heads = att // HEAD_DIM
    taps = conv_kernel.shape[0]
    edge = -(-(taps - 1) // 16) * 16
    context = min(CTX_MAX, runs // 4)

    query_rows = rows + 2 * edge
    key_rows = query_rows + context * rows
    chunks = width // LANES
    vmem = pl.BlockSpec(memory_space=pltpu.VMEM)
    smem = pl.BlockSpec(memory_space=pltpu.SMEM)
    hbm = pl.BlockSpec(memory_space=pltpu.HBM)
    params = pltpu.CompilerParams(vmem_limit_bytes=VMEM_LIMIT)

    own, keys, values, far, near = pl.pallas_call(
        functools.partial(pack_kernel, edge),
        out_shape=(
            jax.ShapeDtypeStruct((2 * rows, att), bf16),
            jax.ShapeDtypeStruct((rows + edge, att), bf16),
            jax.ShapeDtypeStruct((rows, att), bf16),
            jax.ShapeDtypeStruct((2 * edge, att), bf16),
            jax.ShapeDtypeStruct(((3 + width // att) * edge, att), bf16),
        ),
        in_specs=[hbm] * 4,
        out_specs=(vmem,) * 5,
        scratch_shapes=[pltpu.SemaphoreType.DMA((10 + width // att,))],
        compiler_params=params,
        name="pack",
    )(in_hbm(key), in_hbm(value), in_hbm(query), in_hbm(cot))
    further = [shifted(own, offset) for offset in range(2, context + 1)]
    keys = shifted(keys, 1)
    near = shifted(near, -1)
    if further:
        near, values = lax.optimization_barrier((near, values))
        values = pl.pallas_call(
            choose_kernel,
            out_shape=jax.ShapeDtypeStruct((rows, att), bf16),
            in_specs=[smem, vmem, vmem],
            out_specs=vmem,
            compiler_params=params,
            name="choose",
        )(device[None], values, further[0])
        values = lax.ppermute(values, "y", [(0, 1), (1, 0)])
    else:
        values = shifted(values, 1)
    tiles = [own, keys, values, *further]
    far = shifted(far, context + 1)

    pieces = att // 32
    layers = lax.axis_size("z")
    split = pieces == layers * lax.axis_size(PLANE_AXES) and layers & (layers - 1) == 0
    core = lax.axis_index("core").astype(jnp.int32) if split else jnp.int32(0)
    place = jnp.stack([device, core])
    blocks = query_rows // LANES
    key_span = context * rows + LANES

    def score(blocks, edge_rows):
        return pl.pallas_call(
            functools.partial(scores_kernel, context, rows, edge, blocks),
            out_shape=(
                jax.ShapeDtypeStruct((len(blocks) * (att // LANES), 2 * LANES, key_span), bf16),
                jax.ShapeDtypeStruct((heads, len(blocks) * LANES), f32),
            ),
            in_specs=[smem, hbm] + [vmem] * (2 + context),
            out_specs=(vmem,) * 2,
            scratch_shapes=[
                pltpu.VMEM((query_rows, att), bf16),
                pltpu.VMEM((key_rows, att), bf16),
                pltpu.VMEM((len(blocks) * LANES, LANES), f32),
                pltpu.VMEM((rows, att), bf16),
                pltpu.VMEM((LANES, key_span), f32),
                pltpu.SemaphoreType.DMA,
            ],
            compiler_params=params,
            cost_estimate=cost(5 * 10**9, 10**7),
            name="scores",
        )(place, in_hbm(query), own, keys, *further, edge_rows)

    early, early_sums = score(list(range(1, blocks)), near)
    late, late_sums = score([0], far)
    log_sums = (late_sums, early_sums)
    out_frames, attended, dhidden, keep, give, hidden, dmixed = pl.pallas_call(
        functools.partial(forward_kernel, context, rows, edge, taps),
        out_shape=(
            jax.ShapeDtypeStruct((rows, width), bf16),
            jax.ShapeDtypeStruct((rows, att), bf16),
            jax.ShapeDtypeStruct((rows, width), bf16),
        )
        + (jax.ShapeDtypeStruct((pieces, chunks * 16, LANES), bf16),) * 2
        + (
            jax.ShapeDtypeStruct((chunks, query_rows, LANES), f32),
            jax.ShapeDtypeStruct((chunks, rows + edge + 8, LANES), f32),
        ),
        in_specs=[smem] + [vmem] * (6 + context) + [hbm] * 3,
        out_specs=(hbm,) * 3 + (vmem,) * 4,
        scratch_shapes=[
            pltpu.VMEM((key_rows, att), bf16),
            pltpu.VMEM((query_rows, att), bf16),
            pltpu.VMEM((chunks, rows + edge, LANES), f32),
            pltpu.VMEM((2, pieces, chunks * 16, LANES), bf16),
            pltpu.VMEM((att, width), bf16),
            pltpu.VMEM((taps, width), f32),
            pltpu.VMEM((rows, width), bf16),
            pltpu.VMEM((rows, width), bf16),
            pltpu.VMEM((rows, width), bf16),
            pltpu.SemaphoreType.DMA((6,)),
        ],
        compiler_params=params,
        cost_estimate=cost(8 * 10**9, 10**7),
        name="forward",
    )(
        place,
        late,
        early,
        *tiles,
        far,
        near,
        in_hbm(out_weight),
        in_hbm(conv_kernel),
        in_hbm(cot),
    )
    kernel_rows = pl.pallas_call(
        functools.partial(kernel_grad_kernel, rows, edge, taps),
        out_shape=jax.ShapeDtypeStruct((pieces, 2 * chunks, LANES), bf16),
        in_specs=[vmem, vmem],
        out_specs=vmem,
        scratch_shapes=[
            pltpu.VMEM((taps * SUBLANES, LANES), f32),
            pltpu.VMEM((chunks, 2 * pieces, LANES), f32),
        ],
        compiler_params=params,
        cost_estimate=cost(2 * 10**9, 3 * 10**6),
        name="kernel_grad",
    )(hidden, dmixed)

    if split:
        mine = pl.pallas_call(
            join_kernel,
            out_shape=jax.ShapeDtypeStruct((pieces, 18 * chunks, LANES), bf16),
            in_specs=[vmem] * 3,
            out_specs=vmem,
            compiler_params=params,
            name="join",
        )(keep, other_core(give), kernel_rows)
        mine, dhidden = lax.optimization_barrier((mine, dhidden))
    query_grad, own_grads, *messages = pl.pallas_call(
        functools.partial(backward_kernel, context, rows),
        out_shape=(
            jax.ShapeDtypeStruct((rows, att), bf16),
            jax.ShapeDtypeStruct((2 * rows, att), f32),
        )
        + (jax.ShapeDtypeStruct((2 * rows, att), bf16),) * context,
        in_specs=[smem, hbm] + [vmem] * (2 + context) + [hbm, vmem, vmem, hbm, hbm],
        out_specs=(vmem,) * (2 + context),
        scratch_shapes=[
            pltpu.VMEM((rows, att), bf16),
            pltpu.VMEM((rows, width), bf16),
            pltpu.VMEM((att, width), bf16),
            pltpu.VMEM((rows, att), bf16),
            pltpu.VMEM((rows, att), bf16),
            pltpu.VMEM((context + 1, rows, rows), f32),
            pltpu.VMEM((heads, rows), f32),
            pltpu.SemaphoreType.DMA((4,)),
        ],
        compiler_params=params,
        cost_estimate=cost(6 * 10**9, 10**7),
        name="backward",
    )(place, in_hbm(query), *tiles, in_hbm(attended), *log_sums, in_hbm(dhidden), in_hbm(out_weight))
    if split:
        mine, own_grads, *messages = lax.optimization_barrier(
            (collected(mine), own_grads, *messages)
        )
    messages = dict(enumerate(messages, 1))
    if context > 1:
        swapped = lax.ppermute(messages.pop(1), "y", [(0, 1), (1, 0)])
        own_grads, messages[2] = pl.pallas_call(
            relay_kernel,
            out_shape=(
                jax.ShapeDtypeStruct((2 * rows, att), f32),
                jax.ShapeDtypeStruct((2 * rows, att), bf16),
            ),
            in_specs=[smem] + [vmem] * 3,
            out_specs=(vmem,) * 2,
            compiler_params=params,
            cost_estimate=cost(5 * 10**9, 10**7),
            name="relay",
        )(place, own_grads, swapped, messages[2])
    if split:
        mine = summed_along(mine, "z")
        mine, messages = lax.optimization_barrier((mine, messages))
        mine = exchange(jnp.broadcast_to(mine, (lax.axis_size(PLANE_AXES), *mine.shape)))
        mine = mine.reshape(pieces, -1, LANES)
    messages = [shifted(message, -offset) for offset, message in messages.items()]
    key_grad, value_grad = pl.pallas_call(
        merge_kernel,
        out_shape=(jax.ShapeDtypeStruct((rows, att), bf16),) * 2,
        in_specs=[vmem] * (1 + len(messages)),
        out_specs=(vmem,) * 2,
        compiler_params=params,
        cost_estimate=cost(8 * 10**9, 10**7),
        name="merge",
    )(own_grads, *messages)
    if split:
        mine, key_grad, value_grad = lax.optimization_barrier((mine, key_grad, value_grad))
        halves = (mine, other_core(mine))
    else:
        totals = lax.psum((keep, give, kernel_rows), ("x", "core", "z", "y"))
        halves = [
            jnp.concatenate([totals[0], totals[2]], axis=1),
            jnp.concatenate([totals[1], jnp.zeros_like(totals[2])], axis=1),
        ]
    scratch = [pltpu.VMEM((att // 2, width), f32), pltpu.SemaphoreType.DMA]
    weight_total = pl.pallas_call(
        unpack_near_kernel,
        out_shape=jax.ShapeDtypeStruct((att, width), f32),
        in_specs=[smem, vmem],
        out_specs=hbm,
        scratch_shapes=scratch,
        compiler_params=params,
        name="unpack_near",
    )(place, halves[0])
    weight_total, kernel_total = pl.pallas_call(
        unpack_far_kernel,
        out_shape=(
            jax.ShapeDtypeStruct((att, width), f32),
            jax.ShapeDtypeStruct((taps, width), f32),
        ),
        in_specs=[smem, vmem, vmem, hbm],
        out_specs=(hbm, vmem),
        scratch_shapes=scratch,
        input_output_aliases={3: 0},
        compiler_params=params,
        name="unpack_far",
    )(place, *halves, weight_total)
    return (
        out_frames[None],
        query_grad[None],
        key_grad[None],
        value_grad[None],
        weight_total,
        kernel_total,
    )


def solution(mesh):
    sizes = (mesh.shape["dp"] // 2, 2, mesh.shape["blk"] // 2, 2)
    fine = Mesh(mesh.devices.reshape(sizes), ("x", "core", "z", "y"))
    frames = P(("x", "core"), RUN_AXES, None)
    return jax.shard_map(
        per_device,
        mesh=fine,
        in_specs=(frames, frames, frames, P(), P(), frames),
        out_specs=(frames, frames, frames, frames, P(), P()),
        check_vma=False,
    )
```

```python
import functools
import math

import jax
import jax.numpy as jnp
from jax import lax
from jax.experimental import pallas as pl
from jax.experimental.pallas import tpu as pltpu
from jax.sharding import Mesh
from jax.sharding import PartitionSpec as P

HEAD_DIM = 64
CTX_MAX = 3
LANES = 128
SUBLANES = 8
NEGATIVE = -1e30
RUN_AXES = ("z", "y")
PLANE_AXES = ("x", "y")
VMEM_LIMIT = 28 * 1024 * 1024

NN = (((1,), (0,)), ((), ()))
NT = (((1,), (1,)), ((), ()))
TN = (((0,), (0,)), ((), ()))


def dot(a, b, dims, precision=None):
    return lax.dot_general(a, b, dims, precision=precision, preferred_element_type=jnp.float32)


def shifted(x, by):
    devices = range(lax.axis_size(RUN_AXES))
    return lax.ppermute(x, RUN_AXES, [(i, i + by) for i in devices if i + by in devices])


def in_hbm(x):
    return pltpu.with_memory_space_constraint(x, pltpu.HBM)


def cost(flops, data):
    return pl.CostEstimate(flops=flops, bytes_accessed=data, transcendentals=0)


def head_masks():
    lane = lax.broadcasted_iota(jnp.int32, (1, LANES), 1)
    first = jnp.where(lane < HEAD_DIM, 1.0, 0.0)
    return first.astype(jnp.bfloat16), (1.0 - first).astype(jnp.bfloat16)


def stack_heads(pair):
    first, second = head_masks()
    return jnp.concatenate([pair * first, pair * second], axis=0)


def merge_heads(stacked):
    rows = stacked.shape[0] // 2
    lane = lax.broadcasted_iota(jnp.int32, (rows, LANES), 1)
    return jnp.where(lane < HEAD_DIM, stacked[:rows], stacked[rows:])


def pack_kernel(
    edge,
    k_ref,
    v_ref,
    q_ref,
    cot_ref,
    own_ref,
    keys_ref,
    values_ref,
    queries_ref,
    far_ref,
    near_ref,
    sems,
):
    rows, att = k_ref.shape
    width = cot_ref.shape[1]
    head, tail = pl.ds(0, edge), pl.ds(rows - edge, edge)
    moves = [
        (k_ref, own_ref.at[pl.ds(0, rows)]),
        (v_ref, own_ref.at[pl.ds(rows, rows)]),
        (k_ref, keys_ref.at[pl.ds(0, rows)]),
        (q_ref.at[tail], keys_ref.at[pl.ds(rows, edge)]),
        (v_ref, values_ref),
        (q_ref, queries_ref),
        (k_ref.at[tail], far_ref.at[pl.ds(0, edge)]),
        (v_ref.at[tail], far_ref.at[pl.ds(edge, edge)]),
        (k_ref.at[head], near_ref.at[pl.ds(0, edge)]),
        (v_ref.at[head], near_ref.at[pl.ds(edge, edge)]),
        (q_ref.at[head], near_ref.at[pl.ds(2 * edge, edge)]),
    ]
    for part in range(width // att):
        piece = cot_ref.at[head, pl.ds(part * att, att)]
        moves.append((piece, near_ref.at[pl.ds((3 + part) * edge, edge)]))
    copies = [pltpu.make_async_copy(a, b, sems.at[i]) for i, (a, b) in enumerate(moves)]
    for copy in copies:
        copy.start()
    for copy in copies:
        copy.wait()


def choose_kernel(device_ref, even_ref, odd_ref, out_ref):
    odd = lax.rem(device_ref[0], 2)
    rows = out_ref.shape[0]

    @pl.when(odd == 0)
    def _():
        out_ref[...] = even_ref[...]

    @pl.when(odd != 0)
    def _():
        out_ref[...] = odd_ref[odd_ref.shape[0] - rows :]


def tile_places(rows, own_ref, keys_ref, values_ref, *further_refs):
    places = [(own_ref, 0, own_ref, rows), (keys_ref, 0, values_ref, 0)]
    return places + [(ref, 0, ref, rows) for ref in further_refs]


def score_block(b, place, start, span, qx, kx, bias, weights_ref):
    pairs = qx.shape[1] // LANES
    block = LANES
    keys = span + block
    row_id = lax.broadcasted_iota(jnp.int32, (block, keys), 0)
    key_id = lax.broadcasted_iota(jnp.int32, (block, keys), 1)
    distance = row_id - key_id + span
    key_time = key_id + (start - span + b * block)
    visible = (distance >= 0) & (distance < span) & (key_time >= 0)
    bias[...] = jnp.where(visible, 0.0, NEGATIVE)
    lane_id = lax.broadcasted_iota(jnp.int32, (block, LANES), 1)
    log_sums = jnp.zeros((block, LANES), jnp.float32)
    for pair in range(pairs):
        columns = slice(pair * LANES, (pair + 1) * LANES)
        qs = stack_heads(qx[b * block : (b + 1) * block, columns])
        scores = dot(qs, kx[b * block : b * block + keys, columns], NT)
        hidden_pairs = bias[...]
        scores = scores + jnp.concatenate([hidden_pairs, hidden_pairs], axis=0)
        row_max = jnp.max(scores, axis=1, keepdims=True)
        weights = jnp.exp(scores - row_max)
        row_sum = jnp.sum(weights, axis=1, keepdims=True)
        weights_ref[place * pairs + pair] = (weights * (1.0 / row_sum)).astype(jnp.bfloat16)
        log_sum = row_max + jnp.log(row_sum)
        log_sums = jnp.where(lane_id == 2 * pair, log_sum[:block], log_sums)
        log_sums = jnp.where(lane_id == 2 * pair + 1, log_sum[block:], log_sums)
    return log_sums


def scores_kernel(context, rows, edge, device_ref, q_ref, *refs):
    own_refs = refs[: 1 + context]
    near_ref, weights_ref, lse_ref, qx, kx, lx, bias = refs[1 + context :]
    span = context * rows
    scale = 1.0 / math.sqrt(HEAD_DIM)
    start = device_ref[0] * rows - edge
    for offset, ref in enumerate(own_refs):
        first = edge + (context - offset) * rows
        kx[first : first + rows] = ref[:rows]
    kx[edge + span + rows :] = near_ref[:edge]
    qx[edge : edge + rows] = q_ref[...] * scale
    qx[edge + rows :] = near_ref[2 * edge : 3 * edge] * scale
    for place in range(qx.shape[0] // LANES - 1):
        lx[place * LANES : (place + 1) * LANES] = score_block(
            place + 1, place, start, span, qx, kx, bias, weights_ref
        )
    lse_ref[...] = jnp.transpose(lx[...])[: lse_ref.shape[0]]


def forward_kernel(context, rows, edge, taps, *refs):
    tiles = context + 2
    device_ref, q_ref, early_ref = refs[:3]
    keys_ref = refs[4]
    places = tile_places(rows, *refs[3 : 3 + tiles])
    far_ref, near_ref, w_hbm, conv_hbm, cot_hbm = refs[3 + tiles : 8 + tiles]
    out_hbm, att_hbm, lse_ref, dhid_hbm, keep_ref, give_ref, hid, dm = refs[8 + tiles : 16 + tiles]
    qx, kx, vx, ax, late, bias, cotx, parts = refs[16 + tiles : 24 + tiles]
    w_ref, conv_ref, cot_ref, out_ref, dhid_ref, sems = refs[24 + tiles :]

    att = ax.shape[1]
    width = w_ref.shape[1]
    span = context * rows
    query_rows = rows + 2 * edge
    block = LANES
    keys = span + block
    start = device_ref[0] * rows

    fetches = [
        pltpu.make_async_copy(source, target, sems.at[i])
        for i, (source, target) in enumerate(
            ((w_hbm, w_ref), (cot_hbm, cot_ref), (conv_hbm, conv_ref))
        )
    ]
    for fetch in fetches:
        fetch.start()

    scale = 1.0 / math.sqrt(HEAD_DIM)
    qx[:edge] = keys_ref[rows : rows + edge] * scale
    qx[edge:] = q_ref[: block - edge] * scale
    kx[:edge] = far_ref[:edge]
    vx[:edge] = far_ref[edge:]
    for offset, (k_ref, k_at, v_ref, v_at) in enumerate(places):
        first = edge + (context - offset) * rows
        count = min(rows, keys - first)
        kx[first : first + count] = k_ref[k_at : k_at + count]
        vx[first : first + rows] = v_ref[v_at : v_at + rows]
    vx[edge + span + rows :] = near_ref[edge : 2 * edge]
    log_sums = score_block(0, 0, start - edge, span, qx, kx, bias, late)
    lse_ref[...] = jnp.transpose(log_sums)[: lse_ref.shape[0]]

    pairs = att // LANES
    for b in range(query_rows // block):
        for pair in range(pairs):
            columns = slice(pair * LANES, (pair + 1) * LANES)
            values = vx[b * block : b * block + keys, columns]
            weights = early_ref[(b - 1) * pairs + pair] if b else late[pair]
            mixed = dot(weights, values, NN)
            ax[b * block : (b + 1) * block, columns] = merge_heads(mixed).astype(jnp.bfloat16)
    stores = [pltpu.make_async_copy(ax.at[pl.ds(edge, rows)], att_hbm, sems.at[3])]
    stores[0].start()

    fetches[0].wait()
    step = 2 * LANES
    for part in range(width // step):
        product = dot(ax[...], w_ref[:, part * step : (part + 1) * step], NN)
        product = product.astype(jnp.bfloat16).astype(jnp.float32)
        time = lax.broadcasted_iota(jnp.int32, product.shape, 0) + (start - edge)
        product = jnp.where(time >= 0, product, 0.0)
        hid[2 * part] = product[:, :LANES]
        hid[2 * part + 1] = product[:, LANES:]

    fetches[1].wait()
    fetches[2].wait()
    for chunk in range(width // LANES):
        columns = slice(chunk * LANES, (chunk + 1) * LANES)
        cotx[chunk, :rows] = cot_ref[:, columns].astype(jnp.float32)
        part, lane = divmod(chunk * LANES, att)
        cotx[chunk, rows:] = near_ref[
            (3 + part) * edge : (4 + part) * edge, lane : lane + LANES
        ].astype(jnp.float32)
    dm[:, rows + edge :] = jnp.zeros_like(dm[:, rows + edge :])

    apart = -(-taps // SUBLANES)
    reach = (apart - 1) * SUBLANES
    part_rows = (rows + edge) // 2

    def convolve(chunk, carry):
        columns = pl.ds(pl.multiple_of(chunk * LANES, LANES), LANES)
        for first in range(0, rows + edge, part_rows):
            mixed = jnp.zeros((part_rows, LANES), jnp.float32)
            for shift in range(SUBLANES):
                low = edge + first - shift - reach
                window = hid[chunk, low : low + part_rows + reach]
                for tap in range(shift, taps, SUBLANES):
                    at = reach - (tap - shift)
                    mixed += conv_ref[tap : tap + 1, columns] * window[at : at + part_rows]
            sigma = jax.nn.sigmoid(mixed)
            kept = min(part_rows, rows - first)
            out_ref[first : first + kept, columns] = (mixed * sigma)[:kept].astype(jnp.bfloat16)
            dm[chunk, first : first + part_rows] = (
                cotx[chunk, first : first + part_rows] * sigma * (1.0 + mixed * (1.0 - sigma))
            )
        part = rows // 2
        for first in range(0, rows, part):
            dhidden = jnp.zeros((part, LANES), jnp.float32)
            for shift in range(SUBLANES):
                low = first + shift
                window = dm[chunk, low : low + part + reach]
                for tap in range(shift, taps, SUBLANES):
                    at = tap - shift
                    dhidden += conv_ref[tap : tap + 1, columns] * window[at : at + part]
            dhid_ref[first : first + part, columns] = dhidden.astype(jnp.bfloat16)
        return carry

    lax.fori_loop(0, width // LANES, convolve, 0)
    stores.append(pltpu.make_async_copy(out_ref, out_hbm, sems.at[4]))
    stores.append(pltpu.make_async_copy(dhid_ref, dhid_hbm, sems.at[5]))
    for store in stores[1:]:
        store.start()

    _, pieces, _, _ = parts.shape
    group = att // (2 * pieces)
    core = device_ref[1]
    own = ax[edge : edge + rows]
    for part in range(width // step):
        product = dot(own, dhid_ref[:, part * step : (part + 1) * step], TN).astype(jnp.bfloat16)
        for chunk in (2 * part, 2 * part + 1):
            tile = product[:, (chunk - 2 * part) * LANES : (chunk - 2 * part + 1) * LANES]
            for half in range(2):
                for piece in range(pieces):
                    first = (half * pieces + piece) * group
                    parts[half, piece, chunk * group : (chunk + 1) * group] = tile[
                        first : first + group
                    ]
    keep_ref[...] = parts[core]
    give_ref[...] = parts[1 - core]
    for store in stores:
        store.wait()


def kernel_grad_kernel(rows, edge, taps, hid, dm, rows_ref, ks, kp):
    chunks = hid.shape[0]
    pieces = rows_ref.shape[0]
    apart = -(-taps // SUBLANES)
    reach = (apart - 1) * SUBLANES
    part = rows // 2
    kp[...] = jnp.zeros_like(kp)

    def correlate(chunk, carry):
        for shift in range(SUBLANES):
            sums = [jnp.zeros((SUBLANES, LANES), jnp.float32)] * apart
            for first in range(0, rows, part):
                low = edge + first - shift - reach
                window = hid[chunk, low : low + part + reach]
                own = dm[chunk, first : first + part]
                for tap in range(shift, taps, SUBLANES):
                    at = reach - (tap - shift)
                    product = (own * window[at : at + part]).reshape(-1, SUBLANES, LANES)
                    sums[tap // SUBLANES] += jnp.sum(product, axis=0)
            for tap in range(shift, taps, SUBLANES):
                ks[tap * SUBLANES : (tap + 1) * SUBLANES] = sums[tap // SUBLANES]
        total = ks[pl.ds(0, taps, SUBLANES)]
        for row in range(1, SUBLANES):
            total += ks[pl.ds(row, taps, SUBLANES)]
        kp[chunk, :taps] = total
        return carry

    lax.fori_loop(0, chunks, correlate, 0)
    for piece in range(pieces):
        block = [kp[chunk, tap : tap + 1] for tap in (piece, pieces + piece) for chunk in range(chunks)]
        rows_ref[piece] = jnp.concatenate(block, axis=0).astype(jnp.bfloat16)


def join_kernel(keep_ref, given_ref, rows_ref, mine_ref):
    split = keep_ref.shape[1]
    total = keep_ref[...].astype(jnp.float32) + given_ref[...].astype(jnp.float32)
    mine_ref[:, :split] = total.astype(jnp.bfloat16)
    mine_ref[:, split:] = rows_ref[...]


def write_half(ref, half, scratch, weight_hbm, sem):
    pieces = ref.shape[0]
    half_rows, width = scratch.shape
    group = half_rows // pieces
    for piece in range(pieces):
        for chunk in range(width // LANES):
            tile = ref[piece, chunk * group : (chunk + 1) * group].astype(jnp.float32)
            scratch[
                piece * group : (piece + 1) * group, chunk * LANES : (chunk + 1) * LANES
            ] = tile
    first = pl.multiple_of(half * half_rows, half_rows)
    copy = pltpu.make_async_copy(scratch, weight_hbm.at[pl.ds(first, half_rows)], sem)
    copy.start()
    return copy


def unpack_near_kernel(device_ref, near_ref, weight_hbm, scratch, sem):
    write_half(near_ref, device_ref[1], scratch, weight_hbm, sem).wait()


def unpack_far_kernel(
    device_ref,
    near_ref,
    far_ref,
    partial_hbm,
    weight_hbm,
    kernel_hbm,
    scratch,
    blocks,
    kernel_ref,
    sem,
    kernel_sem,
):
    copy = write_half(far_ref, 1 - device_ref[1], scratch, weight_hbm, sem)
    pieces, piece_rows, _ = near_ref.shape
    taps, width = kernel_ref.shape
    chunks = width // LANES
    size = 2 * chunks
    for piece in range(pieces):
        total = near_ref[piece, piece_rows - size :].astype(jnp.float32)
        total += far_ref[piece, piece_rows - size :].astype(jnp.float32)
        blocks[piece * size : (piece + 1) * size] = total
    for half in range(2):
        first = half * pieces
        count = min(pieces, taps - first)
        for chunk in range(chunks):
            columns = slice(chunk * LANES, (chunk + 1) * LANES)
            tap_rows = blocks[pl.ds(half * chunks + chunk, count, size)]
            kernel_ref[first : first + count, columns] = tap_rows
    kernel_copy = pltpu.make_async_copy(kernel_ref, kernel_hbm, kernel_sem)
    kernel_copy.start()
    copy.wait()
    kernel_copy.wait()


def backward_kernel(context, rows, *refs):
    tiles = context + 2
    device_ref, q_hbm = refs[:2]
    places = tile_places(rows, *refs[2 : 2 + tiles])
    att_hbm, late_ref, early_ref, dhid_hbm, w_hbm = refs[2 + tiles : 7 + tiles]
    dq_ref, own_ref = refs[7 + tiles : 9 + tiles]
    message_refs = refs[9 + tiles : 9 + tiles + context]
    q_ref, dhid_ref, w_ref, att_ref, datt, bias, lse_ref, sems = refs[9 + tiles + context :]

    att = q_ref.shape[1]
    heads = att // HEAD_DIM
    span = context * rows
    scale = 1.0 / math.sqrt(HEAD_DIM)
    start = device_ref[0] * rows

    fetches = [
        pltpu.make_async_copy(source, target, sems.at[i])
        for i, (source, target) in enumerate(
            ((w_hbm, w_ref), (dhid_hbm, dhid_ref), (q_hbm, q_ref), (att_hbm, att_ref))
        )
    ]
    for fetch in fetches:
        fetch.start()
    edge = (late_ref.shape[1] + early_ref.shape[1] - rows) // 2
    log_sums = jnp.concatenate([late_ref[...], early_ref[...]], axis=1)
    lse_ref[...] = log_sums[:, edge : edge + rows]
    for offset in range(context + 1):
        key_id = lax.broadcasted_iota(jnp.int32, (rows, rows), 0)
        row_id = lax.broadcasted_iota(jnp.int32, (rows, rows), 1)
        distance = row_id - key_id + offset * rows
        key_time = key_id + (start - offset * rows)
        visible = (distance >= 0) & (distance < span) & (key_time >= 0)
        bias[offset] = jnp.where(visible, 0.0, NEGATIVE)

    for fetch in fetches:
        fetch.wait()
    dattended = dot(dhid_ref[...], w_ref[...], NT).astype(jnp.bfloat16)
    datt[...] = dattended
    product = dattended.astype(jnp.float32) * att_ref[...].astype(jnp.float32)
    head_id = lax.broadcasted_iota(jnp.int32, (heads, att), 0)
    feature_id = lax.broadcasted_iota(jnp.int32, (heads, att), 1)
    ours = (feature_id >= head_id * HEAD_DIM) & (feature_id < (head_id + 1) * HEAD_DIM)
    deltas = dot(jnp.where(ours, 1.0, 0.0), product, NT, lax.Precision.HIGHEST)

    for pair in range(att // LANES):
        columns = slice(pair * LANES, (pair + 1) * LANES)
        qs = stack_heads(q_ref[:, columns] * scale)
        ds = stack_heads(datt[:, columns])
        log_sum = [lse_ref[2 * pair + i : 2 * pair + i + 1] for i in (0, 1)]
        delta = [deltas[2 * pair + i : 2 * pair + i + 1] for i in (0, 1)]
        log_sum = jnp.concatenate(log_sum, axis=1)
        delta = jnp.concatenate(delta, axis=1)
        dquery = jnp.zeros((2 * rows, LANES), jnp.float32)
        for offset, (k_ref, k_at, v_ref, v_at) in enumerate(places):
            kp = k_ref[k_at : k_at + rows, columns]
            vp = v_ref[v_at : v_at + rows, columns]
            hidden_pairs = jnp.concatenate([bias[offset], bias[offset]], axis=1)
            probs = jnp.exp(dot(kp, qs, NT) + hidden_pairs - log_sum)
            dprobs = dot(vp, ds, NT)
            dscores = (probs * (dprobs - delta)).astype(jnp.bfloat16)
            dvalue = dot(probs.astype(jnp.bfloat16), ds, NN)
            dkey = dot(dscores, qs, NN)
            dquery += dot(dscores, kp, TN)
            target = message_refs[offset - 1] if offset else own_ref
            target[:rows, columns] = dkey.astype(target.dtype)
            target[rows:, columns] = dvalue.astype(target.dtype)
        dq_ref[:, columns] = (merge_heads(dquery) * scale).astype(jnp.bfloat16)


def relay_kernel(device_ref, swapped_ref, message_ref, out_ref):
    odd = lax.rem(device_ref[0], 2).astype(jnp.float32)
    swapped = swapped_ref[...].astype(jnp.float32) * odd
    out_ref[...] = (message_ref[...].astype(jnp.float32) + swapped).astype(jnp.bfloat16)


def merge_kernel(device_ref, *refs):
    *message_refs, swapped_ref, own_ref, dk_ref, dv_ref = refs
    rows = dk_ref.shape[0]
    even = 1.0 - lax.rem(device_ref[0], 2).astype(jnp.float32)
    total = swapped_ref[...].astype(jnp.float32) * even
    for message_ref in message_refs:
        total += message_ref[...].astype(jnp.float32)
    total = (total + own_ref[...]).astype(jnp.bfloat16)
    dk_ref[...] = total[:rows]
    dv_ref[...] = total[rows:]


def exchange(x):
    return lax.all_to_all(x, PLANE_AXES, 0, 0, tiled=True)


def collected(x):
    x = exchange(x.reshape(lax.axis_size(PLANE_AXES), -1, LANES))
    return jnp.sum(x.astype(jnp.float32), axis=0).astype(x.dtype)


def summed_along(x, axis):
    size, step = lax.axis_size(axis), 1
    while step < size:
        other = lax.ppermute(x, axis, [(i, i ^ step) for i in range(size)])
        x = (x.astype(jnp.float32) + other.astype(jnp.float32)).astype(x.dtype)
        step *= 2
    return x


def other_core(x):
    return lax.ppermute(x, "core", [(0, 1), (1, 0)])


def per_device(queries, key_in, value_in, out_weight, conv_kernel, cotangent):
    bf16, f32 = jnp.bfloat16, jnp.float32
    query, key, value, cot = queries[0], key_in[0], value_in[0], cotangent[0]
    runs = lax.axis_size(RUN_AXES)
    device = lax.axis_index(RUN_AXES).astype(jnp.int32)
    rows, att = query.shape
    width = out_weight.shape[1]
    heads = att // HEAD_DIM
    taps = conv_kernel.shape[0]
    edge = -(-(taps - 1) // 16) * 16
    context = min(CTX_MAX, runs // 4)

    query_rows = rows + 2 * edge
    key_rows = query_rows + context * rows
    chunks = width // LANES
    vmem = pl.BlockSpec(memory_space=pltpu.VMEM)
    smem = pl.BlockSpec(memory_space=pltpu.SMEM)
    hbm = pl.BlockSpec(memory_space=pltpu.HBM)
    params = pltpu.CompilerParams(vmem_limit_bytes=VMEM_LIMIT)

    own, keys, values, packed_query, far, near = pl.pallas_call(
        functools.partial(pack_kernel, edge),
        out_shape=(
            jax.ShapeDtypeStruct((2 * rows, att), bf16),
            jax.ShapeDtypeStruct((rows + edge, att), bf16),
            jax.ShapeDtypeStruct((rows, att), bf16),
            jax.ShapeDtypeStruct((rows, att), bf16),
            jax.ShapeDtypeStruct((2 * edge, att), bf16),
            jax.ShapeDtypeStruct(((3 + width // att) * edge, att), bf16),
        ),
        in_specs=[hbm] * 4,
        out_specs=(vmem,) * 6,
        scratch_shapes=[pltpu.SemaphoreType.DMA((11 + width // att,))],
        compiler_params=params,
        name="pack",
    )(in_hbm(key), in_hbm(value), in_hbm(query), in_hbm(cot))
    further = [shifted(own, offset) for offset in range(2, context + 1)]
    keys = shifted(keys, 1)
    near = shifted(near, -1)
    if further:
        near, values = lax.optimization_barrier((near, values))
        values = pl.pallas_call(
            choose_kernel,
            out_shape=jax.ShapeDtypeStruct((rows, att), bf16),
            in_specs=[smem, vmem, vmem],
            out_specs=vmem,
            compiler_params=params,
            name="choose",
        )(device[None], values, further[0])
        values = lax.ppermute(values, "y", [(0, 1), (1, 0)])
    else:
        values = shifted(values, 1)
    tiles = [own, keys, values, *further]
    far = shifted(far, context + 1)

    pieces = att // 32
    layers = lax.axis_size("z")
    split = pieces == layers * lax.axis_size(PLANE_AXES) and layers & (layers - 1) == 0
    core = lax.axis_index("core").astype(jnp.int32) if split else jnp.int32(0)
    place = jnp.stack([device, core])
    blocks = query_rows // LANES
    pairs = att // LANES
    key_span = context * rows + LANES
    early, early_sums = pl.pallas_call(
        functools.partial(scores_kernel, context, rows, edge),
        out_shape=(
            jax.ShapeDtypeStruct(((blocks - 1) * pairs, 2 * LANES, key_span), bf16),
            jax.ShapeDtypeStruct((heads, (blocks - 1) * LANES), f32),
        ),
        in_specs=[smem] + [vmem] * (3 + context),
        out_specs=(vmem,) * 2,
        scratch_shapes=[
            pltpu.VMEM((query_rows, att), bf16),
            pltpu.VMEM((key_rows, att), bf16),
            pltpu.VMEM(((blocks - 1) * LANES, LANES), f32),
            pltpu.VMEM((LANES, key_span), f32),
        ],
        compiler_params=params,
        cost_estimate=cost(5 * 10**9, 10**7),
        name="scores",
    )(place, packed_query, own, keys, *further, near)
    out_frames, attended, late_sums, dhidden, keep, give, hidden, dmixed = pl.pallas_call(
        functools.partial(forward_kernel, context, rows, edge, taps),
        out_shape=(
            jax.ShapeDtypeStruct((rows, width), bf16),
            jax.ShapeDtypeStruct((rows, att), bf16),
            jax.ShapeDtypeStruct((heads, LANES), f32),
            jax.ShapeDtypeStruct((rows, width), bf16),
        )
        + (jax.ShapeDtypeStruct((pieces, chunks * 16, LANES), bf16),) * 2
        + (
            jax.ShapeDtypeStruct((chunks, query_rows, LANES), f32),
            jax.ShapeDtypeStruct((chunks, rows + edge + 8, LANES), f32),
        ),
        in_specs=[smem] + [vmem] * (6 + context) + [hbm] * 3,
        out_specs=(hbm, hbm, vmem, hbm) + (vmem,) * 4,
        scratch_shapes=[
            pltpu.VMEM((LANES, att), bf16),
            pltpu.VMEM((key_span, att), bf16),
            pltpu.VMEM((key_rows, att), bf16),
            pltpu.VMEM((query_rows, att), bf16),
            pltpu.VMEM((pairs, 2 * LANES, key_span), bf16),
            pltpu.VMEM((LANES, key_span), f32),
            pltpu.VMEM((chunks, rows + edge, LANES), f32),
            pltpu.VMEM((2, pieces, chunks * 16, LANES), bf16),
            pltpu.VMEM((att, width), bf16),
            pltpu.VMEM((taps, width), f32),
            pltpu.VMEM((rows, width), bf16),
            pltpu.VMEM((rows, width), bf16),
            pltpu.VMEM((rows, width), bf16),
            pltpu.SemaphoreType.DMA((6,)),
        ],
        compiler_params=params,
        cost_estimate=cost(8 * 10**9, 10**7),
        name="forward",
    )(
        place,
        packed_query,
        early,
        *tiles,
        far,
        near,
        in_hbm(out_weight),
        in_hbm(conv_kernel),
        in_hbm(cot),
    )
    kernel_rows = pl.pallas_call(
        functools.partial(kernel_grad_kernel, rows, edge, taps),
        out_shape=jax.ShapeDtypeStruct((pieces, 2 * chunks, LANES), bf16),
        in_specs=[vmem, vmem],
        out_specs=vmem,
        scratch_shapes=[
            pltpu.VMEM((taps * SUBLANES, LANES), f32),
            pltpu.VMEM((chunks, 2 * pieces, LANES), f32),
        ],
        compiler_params=params,
        cost_estimate=cost(2 * 10**9, 3 * 10**6),
        name="kernel_grad",
    )(hidden, dmixed)

    if split:
        mine = pl.pallas_call(
            join_kernel,
            out_shape=jax.ShapeDtypeStruct((pieces, 18 * chunks, LANES), bf16),
            in_specs=[vmem] * 3,
            out_specs=vmem,
            compiler_params=params,
            name="join",
        )(keep, other_core(give), kernel_rows)
        mine, dhidden = lax.optimization_barrier((mine, dhidden))
    query_grad, own_grads, *messages = pl.pallas_call(
        functools.partial(backward_kernel, context, rows),
        out_shape=(
            jax.ShapeDtypeStruct((rows, att), bf16),
            jax.ShapeDtypeStruct((2 * rows, att), f32),
        )
        + (jax.ShapeDtypeStruct((2 * rows, att), bf16),) * context,
        in_specs=[smem, hbm] + [vmem] * (2 + context) + [hbm, vmem, vmem, hbm, hbm],
        out_specs=(vmem,) * (2 + context),
        scratch_shapes=[
            pltpu.VMEM((rows, att), bf16),
            pltpu.VMEM((rows, width), bf16),
            pltpu.VMEM((att, width), bf16),
            pltpu.VMEM((rows, att), bf16),
            pltpu.VMEM((rows, att), bf16),
            pltpu.VMEM((context + 1, rows, rows), f32),
            pltpu.VMEM((heads, rows), f32),
            pltpu.SemaphoreType.DMA((4,)),
        ],
        compiler_params=params,
        cost_estimate=cost(6 * 10**9, 10**7),
        name="backward",
    )(place, in_hbm(query), *tiles, in_hbm(attended), late_sums, early_sums, in_hbm(dhidden), in_hbm(out_weight))
    if split:
        mine, *messages = lax.optimization_barrier((collected(mine), *messages))
    messages = dict(enumerate(messages, 1))
    if context > 1:
        swapped = lax.ppermute(messages.pop(1), "y", [(0, 1), (1, 0)])
        messages[2] = pl.pallas_call(
            relay_kernel,
            out_shape=jax.ShapeDtypeStruct((2 * rows, att), bf16),
            in_specs=[smem] + [vmem] * 2,
            out_specs=vmem,
            compiler_params=params,
            cost_estimate=cost(25 * 10**9, 10**7),
            name="relay",
        )(place, swapped, messages[2])
    else:
        swapped = jnp.zeros((2 * rows, att), bf16)
    if split:
        mine = summed_along(mine, "z")
        mine, messages = lax.optimization_barrier((mine, messages))
        mine = exchange(jnp.broadcast_to(mine, (lax.axis_size(PLANE_AXES), *mine.shape)))
        mine = mine.reshape(pieces, -1, LANES)
    messages = [shifted(message, -offset) for offset, message in messages.items()]
    key_grad, value_grad = pl.pallas_call(
        merge_kernel,
        out_shape=(jax.ShapeDtypeStruct((rows, att), bf16),) * 2,
        in_specs=[smem] + [vmem] * (2 + len(messages)),
        out_specs=(vmem,) * 2,
        compiler_params=params,
        cost_estimate=cost(8 * 10**9, 10**7),
        name="merge",
    )(place, *messages, swapped, own_grads)
    if split:
        mine, key_grad, value_grad = lax.optimization_barrier((mine, key_grad, value_grad))
        halves = (mine, other_core(mine))
    else:
        totals = lax.psum((keep, give, kernel_rows), ("x", "core", "z", "y"))
        halves = [
            jnp.concatenate([totals[0], totals[2]], axis=1),
            jnp.concatenate([totals[1], jnp.zeros_like(totals[2])], axis=1),
        ]
    scratch = [pltpu.VMEM((att // 2, width), f32), pltpu.SemaphoreType.DMA]
    weight_total = pl.pallas_call(
        unpack_near_kernel,
        out_shape=jax.ShapeDtypeStruct((att, width), f32),
        in_specs=[smem, vmem],
        out_specs=hbm,
        scratch_shapes=scratch,
        compiler_params=params,
        name="unpack_near",
    )(place, halves[0])
    weight_total, kernel_total = pl.pallas_call(
        unpack_far_kernel,
        out_shape=(
            jax.ShapeDtypeStruct((att, width), f32),
            jax.ShapeDtypeStruct((taps, width), f32),
        ),
        in_specs=[smem, vmem, vmem, hbm],
        out_specs=(hbm, hbm),
        scratch_shapes=[
            scratch[0],
            pltpu.VMEM((pieces * 2 * chunks, LANES), f32),
            pltpu.VMEM((taps, width), f32),
            scratch[1],
            scratch[1],
        ],
        input_output_aliases={3: 0},
        compiler_params=params,
        name="unpack_far",
    )(place, *halves, weight_total)
    return (
        out_frames[None],
        query_grad[None],
        key_grad[None],
        value_grad[None],
        weight_total,
        kernel_total,
    )


def solution(mesh):
    sizes = (mesh.shape["dp"] // 2, 2, mesh.shape["blk"] // 2, 2)
    fine = Mesh(mesh.devices.reshape(sizes), ("x", "core", "z", "y"))
    frames = P(("x", "core"), RUN_AXES, None)
    return jax.shard_map(
        per_device,
        mesh=fine,
        in_specs=(frames, frames, frames, P(), P(), frames),
        out_specs=(frames, frames, frames, frames, P(), P()),
        check_vma=False,
    )
```

```python
import functools
import math

import jax
import jax.numpy as jnp
from jax import lax
from jax.experimental import pallas as pl
from jax.experimental.pallas import tpu as pltpu
from jax.sharding import Mesh
from jax.sharding import PartitionSpec as P

HEAD_DIM = 64
CTX_MAX = 3
LANES = 128
SUBLANES = 8
NEGATIVE = -1e30
RUN_AXES = ("z", "y")
PLANE_AXES = ("x", "y")
VMEM_LIMIT = 28 * 1024 * 1024

NN = (((1,), (0,)), ((), ()))
NT = (((1,), (1,)), ((), ()))
TN = (((0,), (0,)), ((), ()))


def dot(a, b, dims, precision=None):
    return lax.dot_general(a, b, dims, precision=precision, preferred_element_type=jnp.float32)


def shifted(x, by):
    devices = range(lax.axis_size(RUN_AXES))
    return lax.ppermute(x, RUN_AXES, [(i, i + by) for i in devices if i + by in devices])


def in_hbm(x):
    return pltpu.with_memory_space_constraint(x, pltpu.HBM)


def cost(flops, data):
    return pl.CostEstimate(flops=flops, bytes_accessed=data, transcendentals=0)


def head_masks():
    lane = lax.broadcasted_iota(jnp.int32, (1, LANES), 1)
    first = jnp.where(lane < HEAD_DIM, 1.0, 0.0)
    return first.astype(jnp.bfloat16), (1.0 - first).astype(jnp.bfloat16)


def stack_heads(pair):
    first, second = head_masks()
    return jnp.concatenate([pair * first, pair * second], axis=0)


def merge_heads(stacked):
    rows = stacked.shape[0] // 2
    lane = lax.broadcasted_iota(jnp.int32, (rows, LANES), 1)
    return jnp.where(lane < HEAD_DIM, stacked[:rows], stacked[rows:])


def pack_kernel(
    edge,
    k_ref,
    v_ref,
    q_ref,
    cot_ref,
    own_ref,
    keys_ref,
    values_ref,
    queries_ref,
    far_ref,
    near_ref,
    sems,
):
    rows, att = k_ref.shape
    width = cot_ref.shape[1]
    head, tail = pl.ds(0, edge), pl.ds(rows - edge, edge)
    moves = [
        (k_ref, own_ref.at[pl.ds(0, rows)]),
        (v_ref, own_ref.at[pl.ds(rows, rows)]),
        (k_ref, keys_ref.at[pl.ds(0, rows)]),
        (q_ref.at[tail], keys_ref.at[pl.ds(rows, edge)]),
        (v_ref, values_ref),
        (q_ref, queries_ref),
        (k_ref.at[tail], far_ref.at[pl.ds(0, edge)]),
        (v_ref.at[tail], far_ref.at[pl.ds(edge, edge)]),
        (k_ref.at[head], near_ref.at[pl.ds(0, edge)]),
        (v_ref.at[head], near_ref.at[pl.ds(edge, edge)]),
        (q_ref.at[head], near_ref.at[pl.ds(2 * edge, edge)]),
    ]
    for part in range(width // att):
        piece = cot_ref.at[head, pl.ds(part * att, att)]
        moves.append((piece, near_ref.at[pl.ds((3 + part) * edge, edge)]))
    copies = [pltpu.make_async_copy(a, b, sems.at[i]) for i, (a, b) in enumerate(moves)]
    for copy in copies:
        copy.start()
    for copy in copies:
        copy.wait()


def choose_kernel(device_ref, even_ref, odd_ref, out_ref):
    odd = lax.rem(device_ref[0], 2)
    rows = out_ref.shape[0]

    @pl.when(odd == 0)
    def _():
        out_ref[...] = even_ref[...]

    @pl.when(odd != 0)
    def _():
        out_ref[...] = odd_ref[odd_ref.shape[0] - rows :]


def tile_places(rows, own_ref, keys_ref, values_ref, *further_refs):
    places = [(own_ref, 0, own_ref, rows), (keys_ref, 0, values_ref, 0)]
    return places + [(ref, 0, ref, rows) for ref in further_refs]


def score_block(b, place, start, span, qx, kx, bias, weights_ref):
    pairs = qx.shape[1] // LANES
    block = LANES
    keys = span + block
    row_id = lax.broadcasted_iota(jnp.int32, (block, keys), 0)
    key_id = lax.broadcasted_iota(jnp.int32, (block, keys), 1)
    distance = row_id - key_id + span
    key_time = key_id + (start - span + b * block)
    visible = (distance >= 0) & (distance < span) & (key_time >= 0)
    bias[...] = jnp.where(visible, 0.0, NEGATIVE)
    lane_id = lax.broadcasted_iota(jnp.int32, (block, LANES), 1)
    log_sums = jnp.zeros((block, LANES), jnp.float32)
    for pair in range(pairs):
        columns = slice(pair * LANES, (pair + 1) * LANES)
        qs = stack_heads(qx[b * block : (b + 1) * block, columns])
        scores = dot(qs, kx[b * block : b * block + keys, columns], NT)
        hidden_pairs = bias[...]
        scores = scores + jnp.concatenate([hidden_pairs, hidden_pairs], axis=0)
        row_max = jnp.max(scores, axis=1, keepdims=True)
        weights = jnp.exp(scores - row_max)
        row_sum = jnp.sum(weights, axis=1, keepdims=True)
        weights_ref[place * pairs + pair] = (weights * (1.0 / row_sum)).astype(jnp.bfloat16)
        log_sum = row_max + jnp.log(row_sum)
        log_sums = jnp.where(lane_id == 2 * pair, log_sum[:block], log_sums)
        log_sums = jnp.where(lane_id == 2 * pair + 1, log_sum[block:], log_sums)
    return log_sums


def scores_kernel(context, rows, edge, blocks, device_ref, q_ref, *refs):
    own_refs = refs[: 1 + context]
    keys_ref = own_refs[1]
    edge_ref, weights_ref, lse_ref, qx, kx, lx, bias = refs[1 + context :]
    span = context * rows
    scale = 1.0 / math.sqrt(HEAD_DIM)
    start = device_ref[0] * rows - edge
    for offset, ref in enumerate(own_refs):
        first = edge + (context - offset) * rows
        kx[first : first + rows] = ref[:rows]
    qx[edge : edge + rows] = q_ref[...] * scale
    if blocks[0] == 0:
        kx[:edge] = edge_ref[:edge]
        qx[:edge] = keys_ref[rows : rows + edge] * scale
    else:
        kx[edge + span + rows :] = edge_ref[:edge]
        qx[edge + rows :] = edge_ref[2 * edge : 3 * edge] * scale
    for place, b in enumerate(blocks):
        lx[place * LANES : (place + 1) * LANES] = score_block(
            b, place, start, span, qx, kx, bias, weights_ref
        )
    lse_ref[...] = jnp.transpose(lx[...])[: lse_ref.shape[0]]


def forward_kernel(context, rows, edge, taps, *refs):
    tiles = context + 2
    device_ref, late_ref, early_ref = refs[:3]
    places = tile_places(rows, *refs[3 : 3 + tiles])
    far_ref, near_ref, w_hbm, conv_hbm, cot_hbm = refs[3 + tiles : 8 + tiles]
    out_hbm, att_hbm, dhid_hbm, keep_ref, give_ref, hid, dm = refs[8 + tiles : 15 + tiles]
    vx, ax, cotx, parts, w_ref, conv_ref, cot_ref, out_ref, dhid_ref, sems = refs[15 + tiles :]

    att = ax.shape[1]
    width = w_ref.shape[1]
    span = context * rows
    query_rows = rows + 2 * edge
    block = LANES
    keys = span + block
    start = device_ref[0] * rows

    fetches = [
        pltpu.make_async_copy(source, target, sems.at[i])
        for i, (source, target) in enumerate(
            ((w_hbm, w_ref), (cot_hbm, cot_ref), (conv_hbm, conv_ref))
        )
    ]
    for fetch in fetches:
        fetch.start()

    vx[:edge] = far_ref[edge:]
    for offset, (_, _, ref, at) in enumerate(places):
        first = edge + (context - offset) * rows
        vx[first : first + rows] = ref[at : at + rows]
    vx[edge + span + rows :] = near_ref[edge : 2 * edge]

    pairs = att // LANES
    for b in range(query_rows // block):
        for pair in range(pairs):
            columns = slice(pair * LANES, (pair + 1) * LANES)
            values = vx[b * block : b * block + keys, columns]
            weights = early_ref[(b - 1) * pairs + pair] if b else late_ref[pair]
            mixed = dot(weights, values, NN)
            ax[b * block : (b + 1) * block, columns] = merge_heads(mixed).astype(jnp.bfloat16)
    stores = [pltpu.make_async_copy(ax.at[pl.ds(edge, rows)], att_hbm, sems.at[3])]
    stores[0].start()

    fetches[0].wait()
    step = 2 * LANES
    for part in range(width // step):
        product = dot(ax[...], w_ref[:, part * step : (part + 1) * step], NN)
        product = product.astype(jnp.bfloat16).astype(jnp.float32)
        time = lax.broadcasted_iota(jnp.int32, product.shape, 0) + (start - edge)
        product = jnp.where(time >= 0, product, 0.0)
        hid[2 * part] = product[:, :LANES]
        hid[2 * part + 1] = product[:, LANES:]

    fetches[1].wait()
    fetches[2].wait()
    for chunk in range(width // LANES):
        columns = slice(chunk * LANES, (chunk + 1) * LANES)
        cotx[chunk, :rows] = cot_ref[:, columns].astype(jnp.float32)
        part, lane = divmod(chunk * LANES, att)
        cotx[chunk, rows:] = near_ref[
            (3 + part) * edge : (4 + part) * edge, lane : lane + LANES
        ].astype(jnp.float32)
    dm[:, rows + edge :] = jnp.zeros_like(dm[:, rows + edge :])

    apart = -(-taps // SUBLANES)
    reach = (apart - 1) * SUBLANES
    part_rows = (rows + edge) // 2

    def convolve(chunk, carry):
        columns = pl.ds(pl.multiple_of(chunk * LANES, LANES), LANES)
        for first in range(0, rows + edge, part_rows):
            mixed = jnp.zeros((part_rows, LANES), jnp.float32)
            for shift in range(SUBLANES):
                low = edge + first - shift - reach
                window = hid[chunk, low : low + part_rows + reach]
                for tap in range(shift, taps, SUBLANES):
                    at = reach - (tap - shift)
                    mixed += conv_ref[tap : tap + 1, columns] * window[at : at + part_rows]
            sigma = jax.nn.sigmoid(mixed)
            kept = min(part_rows, rows - first)
            out_ref[first : first + kept, columns] = (mixed * sigma)[:kept].astype(jnp.bfloat16)
            dm[chunk, first : first + part_rows] = (
                cotx[chunk, first : first + part_rows] * sigma * (1.0 + mixed * (1.0 - sigma))
            )
        part = rows // 2
        for first in range(0, rows, part):
            dhidden = jnp.zeros((part, LANES), jnp.float32)
            for shift in range(SUBLANES):
                low = first + shift
                window = dm[chunk, low : low + part + reach]
                for tap in range(shift, taps, SUBLANES):
                    at = tap - shift
                    dhidden += conv_ref[tap : tap + 1, columns] * window[at : at + part]
            dhid_ref[first : first + part, columns] = dhidden.astype(jnp.bfloat16)
        return carry

    lax.fori_loop(0, width // LANES, convolve, 0)
    stores.append(pltpu.make_async_copy(out_ref, out_hbm, sems.at[4]))
    stores.append(pltpu.make_async_copy(dhid_ref, dhid_hbm, sems.at[5]))
    for store in stores[1:]:
        store.start()

    _, pieces, _, _ = parts.shape
    group = att // (2 * pieces)
    core = device_ref[1]
    own = ax[edge : edge + rows]
    for part in range(width // step):
        product = dot(own, dhid_ref[:, part * step : (part + 1) * step], TN).astype(jnp.bfloat16)
        for chunk in (2 * part, 2 * part + 1):
            tile = product[:, (chunk - 2 * part) * LANES : (chunk - 2 * part + 1) * LANES]
            for half in range(2):
                for piece in range(pieces):
                    first = (half * pieces + piece) * group
                    parts[half, piece, chunk * group : (chunk + 1) * group] = tile[
                        first : first + group
                    ]
    keep_ref[...] = parts[core]
    give_ref[...] = parts[1 - core]
    for store in stores:
        store.wait()


def kernel_grad_kernel(rows, edge, taps, hid, dm, rows_ref, ks, kp):
    chunks = hid.shape[0]
    pieces = rows_ref.shape[0]
    apart = -(-taps // SUBLANES)
    reach = (apart - 1) * SUBLANES
    part = rows // 2
    kp[...] = jnp.zeros_like(kp)

    def correlate(chunk, carry):
        for shift in range(SUBLANES):
            sums = [jnp.zeros((SUBLANES, LANES), jnp.float32)] * apart
            for first in range(0, rows, part):
                low = edge + first - shift - reach
                window = hid[chunk, low : low + part + reach]
                own = dm[chunk, first : first + part]
                for tap in range(shift, taps, SUBLANES):
                    at = reach - (tap - shift)
                    product = (own * window[at : at + part]).reshape(-1, SUBLANES, LANES)
                    sums[tap // SUBLANES] += jnp.sum(product, axis=0)
            for tap in range(shift, taps, SUBLANES):
                ks[tap * SUBLANES : (tap + 1) * SUBLANES] = sums[tap // SUBLANES]
        total = ks[pl.ds(0, taps, SUBLANES)]
        for row in range(1, SUBLANES):
            total += ks[pl.ds(row, taps, SUBLANES)]
        kp[chunk, :taps] = total
        return carry

    lax.fori_loop(0, chunks, correlate, 0)
    for piece in range(pieces):
        block = [kp[chunk, tap : tap + 1] for tap in (piece, pieces + piece) for chunk in range(chunks)]
        rows_ref[piece] = jnp.concatenate(block, axis=0).astype(jnp.bfloat16)


def join_kernel(keep_ref, given_ref, rows_ref, mine_ref):
    split = keep_ref.shape[1]
    total = keep_ref[...].astype(jnp.float32) + given_ref[...].astype(jnp.float32)
    mine_ref[:, :split] = total.astype(jnp.bfloat16)
    mine_ref[:, split:] = rows_ref[...]


def write_half(refs, half, me, scratch, weight_hbm, sems):
    slabs, slab_rows, width = scratch.shape
    pieces = refs[0].shape[0]
    group = slab_rows // pieces
    copies = []
    for slab, ref in enumerate(refs):
        for piece in range(pieces):
            for chunk in range(width // LANES):
                tile = ref[piece, chunk * group : (chunk + 1) * group].astype(jnp.float32)
                scratch[
                    slab, piece * group : (piece + 1) * group, chunk * LANES : (chunk + 1) * LANES
                ] = tile
        first = pl.multiple_of((half * slabs + (me ^ slab)) * slab_rows, slab_rows)
        target = weight_hbm.at[pl.ds(first, slab_rows)]
        copies.append(pltpu.make_async_copy(scratch.at[slab], target, sems.at[slab]))
        copies[-1].start()
    return copies


def unpack_near_kernel(device_ref, *refs):
    *near_refs, weight_hbm, scratch, sems = refs
    for copy in write_half(near_refs, device_ref[1], device_ref[2], scratch, weight_hbm, sems):
        copy.wait()


def unpack_far_kernel(device_ref, *refs):
    *refs, _, weight_hbm, kernel_hbm, scratch, blocks, kernel_ref, sems, kernel_sem = refs
    slabs = len(refs) // 2
    near_refs, far_refs = refs[:slabs], refs[slabs:]
    me = device_ref[2]
    copies = write_half(far_refs, 1 - device_ref[1], me, scratch, weight_hbm, sems)
    pieces, piece_rows, _ = near_refs[0].shape
    taps, width = kernel_ref.shape
    chunks = width // LANES
    size = 2 * chunks
    for slab in range(slabs):
        for piece in range(pieces):
            total = near_refs[slab][piece, piece_rows - size :].astype(jnp.float32)
            total += far_refs[slab][piece, piece_rows - size :].astype(jnp.float32)
            first = pl.multiple_of(((me ^ slab) * pieces + piece) * size, size)
            blocks[pl.ds(first, size)] = total
    for half in range(2):
        first = half * slabs * pieces
        count = min(slabs * pieces, taps - first)
        for chunk in range(chunks):
            columns = slice(chunk * LANES, (chunk + 1) * LANES)
            tap_rows = blocks[pl.ds(half * chunks + chunk, count, size)]
            kernel_ref[first : first + count, columns] = tap_rows
    copies.append(pltpu.make_async_copy(kernel_ref, kernel_hbm, kernel_sem))
    copies[-1].start()
    for copy in copies:
        copy.wait()


def backward_kernel(context, rows, *refs):
    tiles = context + 2
    device_ref, q_hbm = refs[:2]
    places = tile_places(rows, *refs[2 : 2 + tiles])
    att_hbm, late_ref, early_ref, dhid_hbm, w_hbm = refs[2 + tiles : 7 + tiles]
    dq_ref, own_ref = refs[7 + tiles : 9 + tiles]
    message_refs = refs[9 + tiles : 9 + tiles + context]
    q_ref, dhid_ref, w_ref, att_ref, datt, bias, lse_ref, sems = refs[9 + tiles + context :]

    att = q_ref.shape[1]
    heads = att // HEAD_DIM
    span = context * rows
    scale = 1.0 / math.sqrt(HEAD_DIM)
    start = device_ref[0] * rows

    fetches = [
        pltpu.make_async_copy(source, target, sems.at[i])
        for i, (source, target) in enumerate(
            ((w_hbm, w_ref), (dhid_hbm, dhid_ref), (q_hbm, q_ref), (att_hbm, att_ref))
        )
    ]
    for fetch in fetches:
        fetch.start()
    edge = (late_ref.shape[1] + early_ref.shape[1] - rows) // 2
    log_sums = jnp.concatenate([late_ref[...], early_ref[...]], axis=1)
    lse_ref[...] = log_sums[:, edge : edge + rows]
    for offset in range(context + 1):
        key_id = lax.broadcasted_iota(jnp.int32, (rows, rows), 0)
        row_id = lax.broadcasted_iota(jnp.int32, (rows, rows), 1)
        distance = row_id - key_id + offset * rows
        key_time = key_id + (start - offset * rows)
        visible = (distance >= 0) & (distance < span) & (key_time >= 0)
        bias[offset] = jnp.where(visible, 0.0, NEGATIVE)

    for fetch in fetches:
        fetch.wait()
    dattended = dot(dhid_ref[...], w_ref[...], NT).astype(jnp.bfloat16)
    datt[...] = dattended
    product = dattended.astype(jnp.float32) * att_ref[...].astype(jnp.float32)
    head_id = lax.broadcasted_iota(jnp.int32, (heads, att), 0)
    feature_id = lax.broadcasted_iota(jnp.int32, (heads, att), 1)
    ours = (feature_id >= head_id * HEAD_DIM) & (feature_id < (head_id + 1) * HEAD_DIM)
    deltas = dot(jnp.where(ours, 1.0, 0.0), product, NT, lax.Precision.HIGHEST)

    for pair in range(att // LANES):
        columns = slice(pair * LANES, (pair + 1) * LANES)
        qs = stack_heads(q_ref[:, columns] * scale)
        ds = stack_heads(datt[:, columns])
        log_sum = [lse_ref[2 * pair + i : 2 * pair + i + 1] for i in (0, 1)]
        delta = [deltas[2 * pair + i : 2 * pair + i + 1] for i in (0, 1)]
        log_sum = jnp.concatenate(log_sum, axis=1)
        delta = jnp.concatenate(delta, axis=1)
        dquery = jnp.zeros((2 * rows, LANES), jnp.float32)
        for offset, (k_ref, k_at, v_ref, v_at) in enumerate(places):
            kp = k_ref[k_at : k_at + rows, columns]
            vp = v_ref[v_at : v_at + rows, columns]
            hidden_pairs = jnp.concatenate([bias[offset], bias[offset]], axis=1)
            probs = jnp.exp(dot(kp, qs, NT) + hidden_pairs - log_sum)
            dprobs = dot(vp, ds, NT)
            dscores = (probs * (dprobs - delta)).astype(jnp.bfloat16)
            dvalue = dot(probs.astype(jnp.bfloat16), ds, NN)
            dkey = dot(dscores, qs, NN)
            dquery += dot(dscores, kp, TN)
            target = message_refs[offset - 1] if offset else own_ref
            target[:rows, columns] = dkey.astype(target.dtype)
            target[rows:, columns] = dvalue.astype(target.dtype)
        dq_ref[:, columns] = (merge_heads(dquery) * scale).astype(jnp.bfloat16)


def relay_kernel(device_ref, swapped_ref, message_ref, out_ref):
    odd = lax.rem(device_ref[0], 2).astype(jnp.float32)
    swapped = swapped_ref[...].astype(jnp.float32) * odd
    out_ref[...] = (message_ref[...].astype(jnp.float32) + swapped).astype(jnp.bfloat16)


def merge_kernel(device_ref, *refs):
    *message_refs, swapped_ref, own_ref, dk_ref, dv_ref = refs
    rows = dk_ref.shape[0]
    even = 1.0 - lax.rem(device_ref[0], 2).astype(jnp.float32)
    total = swapped_ref[...].astype(jnp.float32) * even
    for message_ref in message_refs:
        total += message_ref[...].astype(jnp.float32)
    total = (total + own_ref[...]).astype(jnp.bfloat16)
    dk_ref[...] = total[:rows]
    dv_ref[...] = total[rows:]


def exchange(x):
    return lax.all_to_all(x, PLANE_AXES, 0, 0, tiled=True)


def collected(x):
    x = exchange(x.reshape(lax.axis_size(PLANE_AXES), -1, LANES))
    return jnp.sum(x.astype(jnp.float32), axis=0).astype(x.dtype)


def summed_along(x, axis):
    size, step = lax.axis_size(axis), 1
    while step < size:
        other = lax.ppermute(x, axis, [(i, i ^ step) for i in range(size)])
        x = (x.astype(jnp.float32) + other.astype(jnp.float32)).astype(x.dtype)
        step *= 2
    return x


def other_core(x):
    return lax.ppermute(x, "core", [(0, 1), (1, 0)])


def per_device(queries, key_in, value_in, out_weight, conv_kernel, cotangent):
    bf16, f32 = jnp.bfloat16, jnp.float32
    query, key, value, cot = queries[0], key_in[0], value_in[0], cotangent[0]
    runs = lax.axis_size(RUN_AXES)
    device = lax.axis_index(RUN_AXES).astype(jnp.int32)
    rows, att = query.shape
    width = out_weight.shape[1]
    heads = att // HEAD_DIM
    taps = conv_kernel.shape[0]
    edge = -(-(taps - 1) // 16) * 16
    context = min(CTX_MAX, runs // 4)

    query_rows = rows + 2 * edge
    key_rows = query_rows + context * rows
    chunks = width // LANES
    vmem = pl.BlockSpec(memory_space=pltpu.VMEM)
    smem = pl.BlockSpec(memory_space=pltpu.SMEM)
    hbm = pl.BlockSpec(memory_space=pltpu.HBM)
    params = pltpu.CompilerParams(vmem_limit_bytes=VMEM_LIMIT)

    own, keys, values, packed_query, far, near = pl.pallas_call(
        functools.partial(pack_kernel, edge),
        out_shape=(
            jax.ShapeDtypeStruct((2 * rows, att), bf16),
            jax.ShapeDtypeStruct((rows + edge, att), bf16),
            jax.ShapeDtypeStruct((rows, att), bf16),
            jax.ShapeDtypeStruct((rows, att), bf16),
            jax.ShapeDtypeStruct((2 * edge, att), bf16),
            jax.ShapeDtypeStruct(((3 + width // att) * edge, att), bf16),
        ),
        in_specs=[hbm] * 4,
        out_specs=(vmem,) * 6,
        scratch_shapes=[pltpu.SemaphoreType.DMA((11 + width // att,))],
        compiler_params=params,
        name="pack",
    )(in_hbm(key), in_hbm(value), in_hbm(query), in_hbm(cot))
    further = [shifted(own, offset) for offset in range(2, context + 1)]
    keys = shifted(keys, 1)
    near = shifted(near, -1)
    if further:
        near, values = lax.optimization_barrier((near, values))
        values = pl.pallas_call(
            choose_kernel,
            out_shape=jax.ShapeDtypeStruct((rows, att), bf16),
            in_specs=[smem, vmem, vmem],
            out_specs=vmem,
            compiler_params=params,
            name="choose",
        )(device[None], values, further[0])
        values = lax.ppermute(values, "y", [(0, 1), (1, 0)])
    else:
        values = shifted(values, 1)
    tiles = [own, keys, values, *further]
    far = shifted(far, context + 1)

    pieces = att // 32
    layers = lax.axis_size("z")
    split = pieces == layers * lax.axis_size(PLANE_AXES) and layers & (layers - 1) == 0
    core = lax.axis_index("core").astype(jnp.int32) if split else jnp.int32(0)
    plane = lax.axis_size(PLANE_AXES)
    spot = lax.axis_index(PLANE_AXES).astype(jnp.int32) if split else jnp.int32(0)
    place = jnp.stack([device, core, spot])
    blocks = query_rows // LANES
    pairs = att // LANES
    key_span = context * rows + LANES

    def score(blocks, edge_rows):
        return pl.pallas_call(
            functools.partial(scores_kernel, context, rows, edge, blocks),
            out_shape=(
                jax.ShapeDtypeStruct((len(blocks) * pairs, 2 * LANES, key_span), bf16),
                jax.ShapeDtypeStruct((heads, len(blocks) * LANES), f32),
            ),
            in_specs=[smem] + [vmem] * (3 + context),
            out_specs=(vmem,) * 2,
            scratch_shapes=[
                pltpu.VMEM((query_rows, att), bf16),
                pltpu.VMEM((key_rows, att), bf16),
                pltpu.VMEM((len(blocks) * LANES, LANES), f32),
                pltpu.VMEM((LANES, key_span), f32),
            ],
            compiler_params=params,
            cost_estimate=cost(5 * 10**9, 10**7),
            name="scores",
        )(place, packed_query, own, keys, *further, edge_rows)

    early, early_sums = score(list(range(1, blocks)), near)
    late, late_sums = score([0], far)
    out_frames, attended, dhidden, keep, give, hidden, dmixed = pl.pallas_call(
        functools.partial(forward_kernel, context, rows, edge, taps),
        out_shape=(
            jax.ShapeDtypeStruct((rows, width), bf16),
            jax.ShapeDtypeStruct((rows, att), bf16),
            jax.ShapeDtypeStruct((rows, width), bf16),
        )
        + (jax.ShapeDtypeStruct((pieces, chunks * 16, LANES), bf16),) * 2
        + (
            jax.ShapeDtypeStruct((chunks, query_rows, LANES), f32),
            jax.ShapeDtypeStruct((chunks, rows + edge + 8, LANES), f32),
        ),
        in_specs=[smem] + [vmem] * (6 + context) + [hbm] * 3,
        out_specs=(hbm,) * 3 + (vmem,) * 4,
        scratch_shapes=[
            pltpu.VMEM((key_rows, att), bf16),
            pltpu.VMEM((query_rows, att), bf16),
            pltpu.VMEM((chunks, rows + edge, LANES), f32),
            pltpu.VMEM((2, pieces, chunks * 16, LANES), bf16),
            pltpu.VMEM((att, width), bf16),
            pltpu.VMEM((taps, width), f32),
            pltpu.VMEM((rows, width), bf16),
            pltpu.VMEM((rows, width), bf16),
            pltpu.VMEM((rows, width), bf16),
            pltpu.SemaphoreType.DMA((6,)),
        ],
        compiler_params=params,
        cost_estimate=cost(8 * 10**9, 10**7),
        name="forward",
    )(
        place,
        late,
        early,
        *tiles,
        far,
        near,
        in_hbm(out_weight),
        in_hbm(conv_kernel),
        in_hbm(cot),
    )
    kernel_rows = pl.pallas_call(
        functools.partial(kernel_grad_kernel, rows, edge, taps),
        out_shape=jax.ShapeDtypeStruct((pieces, 2 * chunks, LANES), bf16),
        in_specs=[vmem, vmem],
        out_specs=vmem,
        scratch_shapes=[
            pltpu.VMEM((taps * SUBLANES, LANES), f32),
            pltpu.VMEM((chunks, 2 * pieces, LANES), f32),
        ],
        compiler_params=params,
        cost_estimate=cost(2 * 10**9, 3 * 10**6),
        name="kernel_grad",
    )(hidden, dmixed)

    if split:
        mine = pl.pallas_call(
            join_kernel,
            out_shape=jax.ShapeDtypeStruct((pieces, 18 * chunks, LANES), bf16),
            in_specs=[vmem] * 3,
            out_specs=vmem,
            compiler_params=params,
            name="join",
        )(keep, other_core(give), kernel_rows)
        mine, dhidden = lax.optimization_barrier((mine, dhidden))
    query_grad, own_grads, *messages = pl.pallas_call(
        functools.partial(backward_kernel, context, rows),
        out_shape=(
            jax.ShapeDtypeStruct((rows, att), bf16),
            jax.ShapeDtypeStruct((2 * rows, att), f32),
        )
        + (jax.ShapeDtypeStruct((2 * rows, att), bf16),) * context,
        in_specs=[smem, hbm] + [vmem] * (2 + context) + [hbm, vmem, vmem, hbm, hbm],
        out_specs=(vmem,) * (2 + context),
        scratch_shapes=[
            pltpu.VMEM((rows, att), bf16),
            pltpu.VMEM((rows, width), bf16),
            pltpu.VMEM((att, width), bf16),
            pltpu.VMEM((rows, att), bf16),
            pltpu.VMEM((rows, att), bf16),
            pltpu.VMEM((context + 1, rows, rows), f32),
            pltpu.VMEM((heads, rows), f32),
            pltpu.SemaphoreType.DMA((4,)),
        ],
        compiler_params=params,
        cost_estimate=cost(6 * 10**9, 10**7),
        name="backward",
    )(place, in_hbm(query), *tiles, in_hbm(attended), late_sums, early_sums, in_hbm(dhidden), in_hbm(out_weight))
    if split:
        mine, *messages = lax.optimization_barrier((collected(mine), *messages))
    messages = dict(enumerate(messages, 1))
    if context > 1:
        swapped = lax.ppermute(messages.pop(1), "y", [(0, 1), (1, 0)])
        messages[2] = pl.pallas_call(
            relay_kernel,
            out_shape=jax.ShapeDtypeStruct((2 * rows, att), bf16),
            in_specs=[smem] + [vmem] * 2,
            out_specs=vmem,
            compiler_params=params,
            cost_estimate=cost(25 * 10**9, 10**7),
            name="relay",
        )(place, swapped, messages[2])
    else:
        swapped = jnp.zeros((2 * rows, att), bf16)
    if split:
        mine = summed_along(mine, "z")
        mine, messages = lax.optimization_barrier((mine, messages))
        mine = mine.reshape(layers, -1, LANES)
    messages = [shifted(message, -offset) for offset, message in messages.items()]
    if split:
        near_slabs = [mine] + [
            lax.ppermute(mine, PLANE_AXES, [(i, i ^ mask) for i in range(plane)])
            for mask in range(1, plane)
        ]
    key_grad, value_grad = pl.pallas_call(
        merge_kernel,
        out_shape=(jax.ShapeDtypeStruct((rows, att), bf16),) * 2,
        in_specs=[smem] + [vmem] * (2 + len(messages)),
        out_specs=(vmem,) * 2,
        compiler_params=params,
        cost_estimate=cost(8 * 10**9, 10**7),
        name="merge",
    )(place, *messages, swapped, own_grads)
    if split:
        near_slabs[-1], key_grad, value_grad = lax.optimization_barrier(
            (near_slabs[-1], key_grad, value_grad)
        )
        far_slabs = [other_core(slab) for slab in near_slabs]
    else:
        totals = lax.psum((keep, give, kernel_rows), ("x", "core", "z", "y"))
        near_slabs = jnp.concatenate([totals[0], totals[2]], axis=1)
        far_slabs = jnp.concatenate([totals[1], jnp.zeros_like(totals[2])], axis=1)
        near_slabs = jnp.split(near_slabs, plane)
        far_slabs = jnp.split(far_slabs, plane)
    slab_scratch = pltpu.VMEM((plane, att // 2 // plane, width), f32)
    slab_sems = pltpu.SemaphoreType.DMA((plane,))
    weight_total = pl.pallas_call(
        unpack_near_kernel,
        out_shape=jax.ShapeDtypeStruct((att, width), f32),
        in_specs=[smem] + [vmem] * plane,
        out_specs=hbm,
        scratch_shapes=[slab_scratch, slab_sems],
        compiler_params=params,
        cost_estimate=cost(10**9, 3 * 10**6),
        name="unpack_near",
    )(place, *near_slabs)
    weight_total, kernel_total = pl.pallas_call(
        unpack_far_kernel,
        out_shape=(
            jax.ShapeDtypeStruct((att, width), f32),
            jax.ShapeDtypeStruct((taps, width), f32),
        ),
        in_specs=[smem] + [vmem] * (2 * plane) + [hbm],
        out_specs=(hbm, hbm),
        scratch_shapes=[
            slab_scratch,
            pltpu.VMEM((pieces * 2 * chunks, LANES), f32),
            pltpu.VMEM((taps, width), f32),
            slab_sems,
            pltpu.SemaphoreType.DMA,
        ],
        input_output_aliases={1 + 2 * plane: 0},
        compiler_params=params,
        name="unpack_far",
    )(place, *near_slabs, *far_slabs, weight_total)
    return (
        out_frames[None],
        query_grad[None],
        key_grad[None],
        value_grad[None],
        weight_total,
        kernel_total,
    )


def solution(mesh):
    sizes = (mesh.shape["dp"] // 2, 2, mesh.shape["blk"] // 2, 2)
    fine = Mesh(mesh.devices.reshape(sizes), ("x", "core", "z", "y"))
    frames = P(("x", "core"), RUN_AXES, None)
    return jax.shard_map(
        per_device,
        mesh=fine,
        in_specs=(frames, frames, frames, P(), P(), frames),
        out_specs=(frames, frames, frames, frames, P(), P()),
        check_vma=False,
    )
```

```python
import functools
import math

import jax
import jax.numpy as jnp
from jax import lax
from jax.experimental import pallas as pl
from jax.experimental.pallas import tpu as pltpu
from jax.sharding import Mesh
from jax.sharding import PartitionSpec as P

HEAD_DIM = 64
CTX_MAX = 3
LANES = 128
SUBLANES = 8
NEGATIVE = -1e30
RUN_AXES = ("z", "y")
PLANE_AXES = ("x", "y")
EARLY_SLABS = (0, 2)
LATE_SLABS = (1, 3)
VMEM_LIMIT = 28 * 1024 * 1024

NN = (((1,), (0,)), ((), ()))
NT = (((1,), (1,)), ((), ()))
TN = (((0,), (0,)), ((), ()))


def dot(a, b, dims, precision=None):
    return lax.dot_general(a, b, dims, precision=precision, preferred_element_type=jnp.float32)


def shifted(x, by):
    devices = range(lax.axis_size(RUN_AXES))
    return lax.ppermute(x, RUN_AXES, [(i, i + by) for i in devices if i + by in devices])


def in_hbm(x):
    return pltpu.with_memory_space_constraint(x, pltpu.HBM)


def cost(flops, data):
    return pl.CostEstimate(flops=flops, bytes_accessed=data, transcendentals=0)


def head_masks():
    lane = lax.broadcasted_iota(jnp.int32, (1, LANES), 1)
    first = jnp.where(lane < HEAD_DIM, 1.0, 0.0)
    return first.astype(jnp.bfloat16), (1.0 - first).astype(jnp.bfloat16)


def stack_heads(pair):
    first, second = head_masks()
    return jnp.concatenate([pair * first, pair * second], axis=0)


def merge_heads(stacked):
    rows = stacked.shape[0] // 2
    lane = lax.broadcasted_iota(jnp.int32, (rows, LANES), 1)
    return jnp.where(lane < HEAD_DIM, stacked[:rows], stacked[rows:])


def pack_kernel(
    edge,
    k_ref,
    v_ref,
    q_ref,
    cot_ref,
    own_ref,
    keys_ref,
    values_ref,
    queries_ref,
    far_ref,
    near_ref,
    sems,
):
    rows, att = k_ref.shape
    width = cot_ref.shape[1]
    head, tail = pl.ds(0, edge), pl.ds(rows - edge, edge)
    moves = [
        (k_ref, own_ref.at[pl.ds(0, rows)]),
        (v_ref, own_ref.at[pl.ds(rows, rows)]),
        (k_ref, keys_ref.at[pl.ds(0, rows)]),
        (q_ref.at[tail], keys_ref.at[pl.ds(rows, edge)]),
        (v_ref, values_ref),
        (q_ref, queries_ref),
        (k_ref.at[tail], far_ref.at[pl.ds(0, edge)]),
        (v_ref.at[tail], far_ref.at[pl.ds(edge, edge)]),
        (k_ref.at[head], near_ref.at[pl.ds(0, edge)]),
        (v_ref.at[head], near_ref.at[pl.ds(edge, edge)]),
        (q_ref.at[head], near_ref.at[pl.ds(2 * edge, edge)]),
    ]
    for part in range(width // att):
        piece = cot_ref.at[head, pl.ds(part * att, att)]
        moves.append((piece, near_ref.at[pl.ds((3 + part) * edge, edge)]))
    copies = [pltpu.make_async_copy(a, b, sems.at[i]) for i, (a, b) in enumerate(moves)]
    for copy in copies:
        copy.start()
    for copy in copies:
        copy.wait()


def choose_kernel(device_ref, even_ref, odd_ref, out_ref):
    odd = lax.rem(device_ref[0], 2)
    rows = out_ref.shape[0]

    @pl.when(odd == 0)
    def _():
        out_ref[...] = even_ref[...]

    @pl.when(odd != 0)
    def _():
        out_ref[...] = odd_ref[odd_ref.shape[0] - rows :]


def tile_places(rows, own_ref, keys_ref, values_ref, *further_refs):
    places = [(own_ref, 0, own_ref, rows), (keys_ref, 0, values_ref, 0)]
    return places + [(ref, 0, ref, rows) for ref in further_refs]


def score_block(b, place, start, span, qx, kx, bias, weights_ref):
    pairs = qx.shape[1] // LANES
    block = LANES
    keys = span + block
    row_id = lax.broadcasted_iota(jnp.int32, (block, keys), 0)
    key_id = lax.broadcasted_iota(jnp.int32, (block, keys), 1)
    distance = row_id - key_id + span
    key_time = key_id + (start - span + b * block)
    visible = (distance >= 0) & (distance < span) & (key_time >= 0)
    bias[...] = jnp.where(visible, 0.0, NEGATIVE)
    lane_id = lax.broadcasted_iota(jnp.int32, (block, LANES), 1)
    log_sums = jnp.zeros((block, LANES), jnp.float32)
    for pair in range(pairs):
        columns = slice(pair * LANES, (pair + 1) * LANES)
        qs = stack_heads(qx[b * block : (b + 1) * block, columns])
        scores = dot(qs, kx[b * block : b * block + keys, columns], NT)
        hidden_pairs = bias[...]
        scores = scores + jnp.concatenate([hidden_pairs, hidden_pairs], axis=0)
        row_max = jnp.max(scores, axis=1, keepdims=True)
        weights = jnp.exp(scores - row_max)
        row_sum = jnp.sum(weights, axis=1, keepdims=True)
        weights_ref[place * pairs + pair] = (weights * (1.0 / row_sum)).astype(jnp.bfloat16)
        log_sum = row_max + jnp.log(row_sum)
        log_sums = jnp.where(lane_id == 2 * pair, log_sum[:block], log_sums)
        log_sums = jnp.where(lane_id == 2 * pair + 1, log_sum[block:], log_sums)
    return log_sums


def scores_kernel(context, rows, edge, blocks, device_ref, q_ref, *refs):
    own_refs = refs[: 1 + context]
    keys_ref = own_refs[1]
    edge_ref, weights_ref, lse_ref, qx, kx, lx, bias = refs[1 + context :]
    span = context * rows
    scale = 1.0 / math.sqrt(HEAD_DIM)
    start = device_ref[0] * rows - edge
    for offset, ref in enumerate(own_refs):
        first = edge + (context - offset) * rows
        kx[first : first + rows] = ref[:rows]
    qx[edge : edge + rows] = q_ref[...] * scale
    if blocks[0] == 0:
        kx[:edge] = edge_ref[:edge]
        qx[:edge] = keys_ref[rows : rows + edge] * scale
    else:
        kx[edge + span + rows :] = edge_ref[:edge]
        qx[edge + rows :] = edge_ref[2 * edge : 3 * edge] * scale
    for place, b in enumerate(blocks):
        lx[place * LANES : (place + 1) * LANES] = score_block(
            b, place, start, span, qx, kx, bias, weights_ref
        )
    lse_ref[...] = jnp.transpose(lx[...])[: lse_ref.shape[0]]


def forward_kernel(context, rows, edge, taps, *refs):
    tiles = context + 2
    device_ref, late_ref, early_ref = refs[:3]
    places = tile_places(rows, *refs[3 : 3 + tiles])
    far_ref, near_ref, w_hbm, conv_hbm, cot_hbm = refs[3 + tiles : 8 + tiles]
    out_hbm, att_ref, dhid_ref, keep_ref, give_ref, hid, dm, w_ref = refs[8 + tiles : 16 + tiles]
    vx, ax, cotx, parts, conv_ref, cot_ref, out_ref, sems = refs[16 + tiles :]

    att = ax.shape[1]
    width = w_ref.shape[1]
    span = context * rows
    query_rows = rows + 2 * edge
    block = LANES
    keys = span + block
    start = device_ref[0] * rows

    fetches = [
        pltpu.make_async_copy(source, target, sems.at[i])
        for i, (source, target) in enumerate(
            ((w_hbm, w_ref), (cot_hbm, cot_ref), (conv_hbm, conv_ref))
        )
    ]
    for fetch in fetches:
        fetch.start()

    vx[:edge] = far_ref[edge:]
    for offset, (_, _, ref, at) in enumerate(places):
        first = edge + (context - offset) * rows
        vx[first : first + rows] = ref[at : at + rows]
    vx[edge + span + rows :] = near_ref[edge : 2 * edge]

    pairs = att // LANES
    for b in range(query_rows // block):
        for pair in range(pairs):
            columns = slice(pair * LANES, (pair + 1) * LANES)
            values = vx[b * block : b * block + keys, columns]
            weights = early_ref[(b - 1) * pairs + pair] if b else late_ref[pair]
            mixed = dot(weights, values, NN)
            ax[b * block : (b + 1) * block, columns] = merge_heads(mixed).astype(jnp.bfloat16)
    att_ref[...] = ax[edge : edge + rows]

    fetches[0].wait()
    step = 2 * LANES
    for part in range(width // step):
        product = dot(ax[...], w_ref[:, part * step : (part + 1) * step], NN)
        product = product.astype(jnp.bfloat16).astype(jnp.float32)
        time = lax.broadcasted_iota(jnp.int32, product.shape, 0) + (start - edge)
        product = jnp.where(time >= 0, product, 0.0)
        hid[2 * part] = product[:, :LANES]
        hid[2 * part + 1] = product[:, LANES:]

    fetches[1].wait()
    fetches[2].wait()
    for chunk in range(width // LANES):
        columns = slice(chunk * LANES, (chunk + 1) * LANES)
        cotx[chunk, :rows] = cot_ref[:, columns].astype(jnp.float32)
        part, lane = divmod(chunk * LANES, att)
        cotx[chunk, rows:] = near_ref[
            (3 + part) * edge : (4 + part) * edge, lane : lane + LANES
        ].astype(jnp.float32)
    dm[:, rows + edge :] = jnp.zeros_like(dm[:, rows + edge :])

    apart = -(-taps // SUBLANES)
    reach = (apart - 1) * SUBLANES
    part_rows = (rows + edge) // 2

    def convolve(chunk, carry):
        columns = pl.ds(pl.multiple_of(chunk * LANES, LANES), LANES)
        for first in range(0, rows + edge, part_rows):
            mixed = jnp.zeros((part_rows, LANES), jnp.float32)
            for shift in range(SUBLANES):
                low = edge + first - shift - reach
                window = hid[chunk, low : low + part_rows + reach]
                for tap in range(shift, taps, SUBLANES):
                    at = reach - (tap - shift)
                    mixed += conv_ref[tap : tap + 1, columns] * window[at : at + part_rows]
            sigma = jax.nn.sigmoid(mixed)
            kept = min(part_rows, rows - first)
            out_ref[first : first + kept, columns] = (mixed * sigma)[:kept].astype(jnp.bfloat16)
            dm[chunk, first : first + part_rows] = (
                cotx[chunk, first : first + part_rows] * sigma * (1.0 + mixed * (1.0 - sigma))
            )
        part = rows // 2
        for first in range(0, rows, part):
            dhidden = jnp.zeros((part, LANES), jnp.float32)
            for shift in range(SUBLANES):
                low = first + shift
                window = dm[chunk, low : low + part + reach]
                for tap in range(shift, taps, SUBLANES):
                    at = tap - shift
                    dhidden += conv_ref[tap : tap + 1, columns] * window[at : at + part]
            dhid_ref[first : first + part, columns] = dhidden.astype(jnp.bfloat16)
        return carry

    lax.fori_loop(0, width // LANES, convolve, 0)
    store = pltpu.make_async_copy(out_ref, out_hbm, sems.at[3])
    store.start()

    _, pieces, _, _ = parts.shape
    group = att // (2 * pieces)
    core = device_ref[1]
    own = ax[edge : edge + rows]
    for part in range(width // step):
        product = dot(own, dhid_ref[:, part * step : (part + 1) * step], TN).astype(jnp.bfloat16)
        for chunk in (2 * part, 2 * part + 1):
            tile = product[:, (chunk - 2 * part) * LANES : (chunk - 2 * part + 1) * LANES]
            for half in range(2):
                for piece in range(pieces):
                    first = (half * pieces + piece) * group
                    parts[half, piece, chunk * group : (chunk + 1) * group] = tile[
                        first : first + group
                    ]
    keep_ref[...] = parts[core]
    give_ref[...] = parts[1 - core]
    store.wait()


def kernel_grad_kernel(rows, edge, taps, hid, dm, rows_ref, ks, kp):
    chunks = hid.shape[0]
    pieces = rows_ref.shape[0]
    apart = -(-taps // SUBLANES)
    reach = (apart - 1) * SUBLANES
    part = rows // 2
    kp[...] = jnp.zeros_like(kp)

    def correlate(chunk, carry):
        for shift in range(SUBLANES):
            sums = [jnp.zeros((SUBLANES, LANES), jnp.float32)] * apart
            for first in range(0, rows, part):
                low = edge + first - shift - reach
                window = hid[chunk, low : low + part + reach]
                own = dm[chunk, first : first + part]
                for tap in range(shift, taps, SUBLANES):
                    at = reach - (tap - shift)
                    product = (own * window[at : at + part]).reshape(-1, SUBLANES, LANES)
                    sums[tap // SUBLANES] += jnp.sum(product, axis=0)
            for tap in range(shift, taps, SUBLANES):
                ks[tap * SUBLANES : (tap + 1) * SUBLANES] = sums[tap // SUBLANES]
        total = ks[pl.ds(0, taps, SUBLANES)]
        for row in range(1, SUBLANES):
            total += ks[pl.ds(row, taps, SUBLANES)]
        kp[chunk, :taps] = total
        return carry

    lax.fori_loop(0, chunks, correlate, 0)
    for piece in range(pieces):
        block = [kp[chunk, tap : tap + 1] for tap in (piece, pieces + piece) for chunk in range(chunks)]
        rows_ref[piece] = jnp.concatenate(block, axis=0).astype(jnp.bfloat16)


def join_kernel(device_ref, keep_ref, given_ref, rows_ref, *slab_refs):
    split = keep_ref.shape[1]
    pieces = slab_refs[0].shape[0]
    for slab, ref in enumerate(slab_refs):
        first = (device_ref[2] ^ slab) * pieces
        for piece in range(pieces):
            total = keep_ref[first + piece].astype(jnp.float32)
            total += given_ref[first + piece].astype(jnp.float32)
            ref[piece, :split] = total.astype(jnp.bfloat16)
            ref[piece, split:] = rows_ref[first + piece]


def write_slabs(slabs, half, me, scratch, weight_hbm, sems):
    count, slab_rows, width = scratch.shape
    copies = []
    for place, (slab, ref) in enumerate(slabs):
        pieces = ref.shape[0]
        group = slab_rows // pieces
        for piece in range(pieces):
            for chunk in range(width // LANES):
                tile = ref[piece, chunk * group : (chunk + 1) * group].astype(jnp.float32)
                scratch[
                    place, piece * group : (piece + 1) * group, chunk * LANES : (chunk + 1) * LANES
                ] = tile
        plane = EARLY_SLABS + LATE_SLABS
        first = pl.multiple_of((half * len(plane) + (me ^ slab)) * slab_rows, slab_rows)
        target = weight_hbm.at[pl.ds(first, slab_rows)]
        copies.append(pltpu.make_async_copy(scratch.at[place], target, sems.at[place]))
        copies[-1].start()
    return copies


def unpack_early_kernel(device_ref, *refs):
    *near_refs, weight_hbm, scratch, sems = refs
    slabs = list(zip(EARLY_SLABS, near_refs))
    for copy in write_slabs(slabs, device_ref[1], device_ref[2], scratch, weight_hbm, sems):
        copy.wait()


def unpack_late_kernel(device_ref, *refs):
    slabs = len(EARLY_SLABS) + len(LATE_SLABS)
    near_refs, far_refs = refs[:slabs], refs[slabs : 2 * slabs]
    weight_hbm, kernel_hbm, scratch, far_scratch, blocks, kernel_ref = refs[2 * slabs + 1 : -3]
    sems, far_sems, kernel_sem = refs[-3:]
    core, me = device_ref[1], device_ref[2]
    late = [(slab, near_refs[slab]) for slab in LATE_SLABS]
    copies = write_slabs(late, core, me, scratch, weight_hbm, sems)
    far = list(enumerate(far_refs))
    copies += write_slabs(far, 1 - core, me, far_scratch, weight_hbm, far_sems)
    pieces, piece_rows, _ = near_refs[0].shape
    taps, width = kernel_ref.shape
    chunks = width // LANES
    size = 2 * chunks
    for slab in range(slabs):
        for piece in range(pieces):
            total = near_refs[slab][piece, piece_rows - size :].astype(jnp.float32)
            total += far_refs[slab][piece, piece_rows - size :].astype(jnp.float32)
            first = pl.multiple_of(((me ^ slab) * pieces + piece) * size, size)
            blocks[pl.ds(first, size)] = total
    for half in range(2):
        first = half * slabs * pieces
        count = min(slabs * pieces, taps - first)
        for chunk in range(chunks):
            columns = slice(chunk * LANES, (chunk + 1) * LANES)
            tap_rows = blocks[pl.ds(half * chunks + chunk, count, size)]
            kernel_ref[first : first + count, columns] = tap_rows
    copies.append(pltpu.make_async_copy(kernel_ref, kernel_hbm, kernel_sem))
    copies[-1].start()
    for copy in copies:
        copy.wait()


def backward_kernel(context, rows, *refs):
    tiles = context + 2
    device_ref, q_ref = refs[:2]
    places = tile_places(rows, *refs[2 : 2 + tiles])
    att_ref, late_ref, early_ref, dhid_ref, w_ref = refs[2 + tiles : 7 + tiles]
    dq_ref, own_ref = refs[7 + tiles : 9 + tiles]
    message_refs = refs[9 + tiles : 9 + tiles + context]
    datt, bias, lse_ref = refs[9 + tiles + context :]

    att = q_ref.shape[1]
    heads = att // HEAD_DIM
    span = context * rows
    scale = 1.0 / math.sqrt(HEAD_DIM)
    start = device_ref[0] * rows

    edge = (late_ref.shape[1] + early_ref.shape[1] - rows) // 2
    log_sums = jnp.concatenate([late_ref[...], early_ref[...]], axis=1)
    lse_ref[...] = log_sums[:, edge : edge + rows]
    for offset in range(context + 1):
        key_id = lax.broadcasted_iota(jnp.int32, (rows, rows), 0)
        row_id = lax.broadcasted_iota(jnp.int32, (rows, rows), 1)
        distance = row_id - key_id + offset * rows
        key_time = key_id + (start - offset * rows)
        visible = (distance >= 0) & (distance < span) & (key_time >= 0)
        bias[offset] = jnp.where(visible, 0.0, NEGATIVE)

    dattended = dot(dhid_ref[...], w_ref[...], NT).astype(jnp.bfloat16)
    datt[...] = dattended
    product = dattended.astype(jnp.float32) * att_ref[...].astype(jnp.float32)
    head_id = lax.broadcasted_iota(jnp.int32, (heads, att), 0)
    feature_id = lax.broadcasted_iota(jnp.int32, (heads, att), 1)
    ours = (feature_id >= head_id * HEAD_DIM) & (feature_id < (head_id + 1) * HEAD_DIM)
    deltas = dot(jnp.where(ours, 1.0, 0.0), product, NT, lax.Precision.HIGHEST)

    for pair in range(att // LANES):
        columns = slice(pair * LANES, (pair + 1) * LANES)
        qs = stack_heads(q_ref[:, columns] * scale)
        ds = stack_heads(datt[:, columns])
        log_sum = [lse_ref[2 * pair + i : 2 * pair + i + 1] for i in (0, 1)]
        delta = [deltas[2 * pair + i : 2 * pair + i + 1] for i in (0, 1)]
        log_sum = jnp.concatenate(log_sum, axis=1)
        delta = jnp.concatenate(delta, axis=1)
        dquery = jnp.zeros((2 * rows, LANES), jnp.float32)
        for offset, (k_ref, k_at, v_ref, v_at) in enumerate(places):
            kp = k_ref[k_at : k_at + rows, columns]
            vp = v_ref[v_at : v_at + rows, columns]
            hidden_pairs = jnp.concatenate([bias[offset], bias[offset]], axis=1)
            probs = jnp.exp(dot(kp, qs, NT) + hidden_pairs - log_sum)
            dprobs = dot(vp, ds, NT)
            dscores = (probs * (dprobs - delta)).astype(jnp.bfloat16)
            dvalue = dot(probs.astype(jnp.bfloat16), ds, NN)
            dkey = dot(dscores, qs, NN)
            dquery += dot(dscores, kp, TN)
            target = message_refs[offset - 1] if offset else own_ref
            target[:rows, columns] = dkey.astype(target.dtype)
            target[rows:, columns] = dvalue.astype(target.dtype)
        dq_ref[:, columns] = (merge_heads(dquery) * scale).astype(jnp.bfloat16)


def relay_kernel(device_ref, swapped_ref, message_ref, out_ref):
    odd = lax.rem(device_ref[0], 2).astype(jnp.float32)
    swapped = swapped_ref[...].astype(jnp.float32) * odd
    out_ref[...] = (message_ref[...].astype(jnp.float32) + swapped).astype(jnp.bfloat16)


def merge_kernel(device_ref, *refs):
    *message_refs, swapped_ref, own_ref, dk_ref, dv_ref = refs
    rows = dk_ref.shape[0]
    even = 1.0 - lax.rem(device_ref[0], 2).astype(jnp.float32)
    total = swapped_ref[...].astype(jnp.float32) * even
    for message_ref in message_refs:
        total += message_ref[...].astype(jnp.float32)
    total = (total + own_ref[...]).astype(jnp.bfloat16)
    dk_ref[...] = total[:rows]
    dv_ref[...] = total[rows:]


def from_peer(x, mask):
    devices = range(lax.axis_size(PLANE_AXES))
    return lax.ppermute(x, PLANE_AXES, [(i, i ^ mask) for i in devices])


def summed_along(x, axis):
    size, step = lax.axis_size(axis), 1
    while step < size:
        other = lax.ppermute(x, axis, [(i, i ^ step) for i in range(size)])
        x = (x.astype(jnp.float32) + other.astype(jnp.float32)).astype(x.dtype)
        step *= 2
    return x


def other_core(x):
    return lax.ppermute(x, "core", [(0, 1), (1, 0)])


def per_device(queries, key_in, value_in, out_weight, conv_kernel, cotangent):
    bf16, f32 = jnp.bfloat16, jnp.float32
    query, key, value, cot = queries[0], key_in[0], value_in[0], cotangent[0]
    runs = lax.axis_size(RUN_AXES)
    device = lax.axis_index(RUN_AXES).astype(jnp.int32)
    rows, att = query.shape
    width = out_weight.shape[1]
    heads = att // HEAD_DIM
    taps = conv_kernel.shape[0]
    edge = -(-(taps - 1) // 16) * 16
    context = min(CTX_MAX, runs // 4)

    query_rows = rows + 2 * edge
    key_rows = query_rows + context * rows
    chunks = width // LANES
    vmem = pl.BlockSpec(memory_space=pltpu.VMEM)
    smem = pl.BlockSpec(memory_space=pltpu.SMEM)
    hbm = pl.BlockSpec(memory_space=pltpu.HBM)
    params = pltpu.CompilerParams(vmem_limit_bytes=VMEM_LIMIT)

    own, keys, values, packed_query, far, near = pl.pallas_call(
        functools.partial(pack_kernel, edge),
        out_shape=(
            jax.ShapeDtypeStruct((2 * rows, att), bf16),
            jax.ShapeDtypeStruct((rows + edge, att), bf16),
            jax.ShapeDtypeStruct((rows, att), bf16),
            jax.ShapeDtypeStruct((rows, att), bf16),
            jax.ShapeDtypeStruct((2 * edge, att), bf16),
            jax.ShapeDtypeStruct(((3 + width // att) * edge, att), bf16),
        ),
        in_specs=[hbm] * 4,
        out_specs=(vmem,) * 6,
        scratch_shapes=[pltpu.SemaphoreType.DMA((11 + width // att,))],
        compiler_params=params,
        name="pack",
    )(in_hbm(key), in_hbm(value), in_hbm(query), in_hbm(cot))
    further = [shifted(own, offset) for offset in range(2, context + 1)]
    keys = shifted(keys, 1)
    near = shifted(near, -1)
    if further:
        near, values = lax.optimization_barrier((near, values))
        values = pl.pallas_call(
            choose_kernel,
            out_shape=jax.ShapeDtypeStruct((rows, att), bf16),
            in_specs=[smem, vmem, vmem],
            out_specs=vmem,
            compiler_params=params,
            name="choose",
        )(device[None], values, further[0])
        values = lax.ppermute(values, "y", [(0, 1), (1, 0)])
    else:
        values = shifted(values, 1)
    tiles = [own, keys, values, *further]
    far = shifted(far, context + 1)

    pieces = att // 32
    layers = lax.axis_size("z")
    split = pieces == layers * lax.axis_size(PLANE_AXES) and layers & (layers - 1) == 0
    core = lax.axis_index("core").astype(jnp.int32) if split else jnp.int32(0)
    plane = lax.axis_size(PLANE_AXES)
    spot = lax.axis_index(PLANE_AXES).astype(jnp.int32) if split else jnp.int32(0)
    place = jnp.stack([device, core, spot])
    blocks = query_rows // LANES
    pairs = att // LANES
    key_span = context * rows + LANES

    def score(blocks, edge_rows):
        return pl.pallas_call(
            functools.partial(scores_kernel, context, rows, edge, blocks),
            out_shape=(
                jax.ShapeDtypeStruct((len(blocks) * pairs, 2 * LANES, key_span), bf16),
                jax.ShapeDtypeStruct((heads, len(blocks) * LANES), f32),
            ),
            in_specs=[smem] + [vmem] * (3 + context),
            out_specs=(vmem,) * 2,
            scratch_shapes=[
                pltpu.VMEM((query_rows, att), bf16),
                pltpu.VMEM((key_rows, att), bf16),
                pltpu.VMEM((len(blocks) * LANES, LANES), f32),
                pltpu.VMEM((LANES, key_span), f32),
            ],
            compiler_params=params,
            cost_estimate=cost(5 * 10**9, 10**7),
            name="scores",
        )(place, packed_query, own, keys, *further, edge_rows)

    early, early_sums = score(list(range(1, blocks)), near)
    late, late_sums = score([0], far)
    out_frames, attended, dhidden, keep, give, hidden, dmixed, held_weight = pl.pallas_call(
        functools.partial(forward_kernel, context, rows, edge, taps),
        out_shape=(
            jax.ShapeDtypeStruct((rows, width), bf16),
            jax.ShapeDtypeStruct((rows, att), bf16),
            jax.ShapeDtypeStruct((rows, width), bf16),
        )
        + (jax.ShapeDtypeStruct((pieces, chunks * 16, LANES), bf16),) * 2
        + (
            jax.ShapeDtypeStruct((chunks, query_rows, LANES), f32),
            jax.ShapeDtypeStruct((chunks, rows + edge + 8, LANES), f32),
            jax.ShapeDtypeStruct((att, width), bf16),
        ),
        in_specs=[smem] + [vmem] * (6 + context) + [hbm] * 3,
        out_specs=(hbm,) + (vmem,) * 7,
        scratch_shapes=[
            pltpu.VMEM((key_rows, att), bf16),
            pltpu.VMEM((query_rows, att), bf16),
            pltpu.VMEM((chunks, rows + edge, LANES), f32),
            pltpu.VMEM((2, pieces, chunks * 16, LANES), bf16),
            pltpu.VMEM((taps, width), f32),
            pltpu.VMEM((rows, width), bf16),
            pltpu.VMEM((rows, width), bf16),
            pltpu.SemaphoreType.DMA((4,)),
        ],
        compiler_params=params,
        cost_estimate=cost(8 * 10**9, 10**7),
        name="forward",
    )(
        place,
        late,
        early,
        *tiles,
        far,
        near,
        in_hbm(out_weight),
        in_hbm(conv_kernel),
        in_hbm(cot),
    )
    kernel_rows = pl.pallas_call(
        functools.partial(kernel_grad_kernel, rows, edge, taps),
        out_shape=jax.ShapeDtypeStruct((pieces, 2 * chunks, LANES), bf16),
        in_specs=[vmem, vmem],
        out_specs=vmem,
        scratch_shapes=[
            pltpu.VMEM((taps * SUBLANES, LANES), f32),
            pltpu.VMEM((chunks, 2 * pieces, LANES), f32),
        ],
        compiler_params=params,
        cost_estimate=cost(2 * 10**9, 3 * 10**6),
        name="kernel_grad",
    )(hidden, dmixed)

    if split:
        slabs = pl.pallas_call(
            join_kernel,
            out_shape=(jax.ShapeDtypeStruct((layers, 18 * chunks, LANES), bf16),) * plane,
            in_specs=[smem] + [vmem] * 3,
            out_specs=(vmem,) * plane,
            compiler_params=params,
            name="join",
        )(place, keep, other_core(give), kernel_rows)
        *slabs, dhidden = lax.optimization_barrier((*slabs, dhidden))
        slabs = [slabs[0]] + [from_peer(slabs[mask], mask) for mask in range(1, plane)]
    query_grad, own_grads, *messages = pl.pallas_call(
        functools.partial(backward_kernel, context, rows),
        out_shape=(
            jax.ShapeDtypeStruct((rows, att), bf16),
            jax.ShapeDtypeStruct((2 * rows, att), f32),
        )
        + (jax.ShapeDtypeStruct((2 * rows, att), bf16),) * context,
        in_specs=[smem] + [vmem] * (8 + context),
        out_specs=(vmem,) * (2 + context),
        scratch_shapes=[
            pltpu.VMEM((rows, att), bf16),
            pltpu.VMEM((context + 1, rows, rows), f32),
            pltpu.VMEM((heads, rows), f32),
        ],
        compiler_params=params,
        cost_estimate=cost(6 * 10**9, 10**7),
        name="backward",
    )(place, packed_query, *tiles, attended, late_sums, early_sums, dhidden, held_weight)
    if split:
        mine = sum(slab.astype(f32) for slab in slabs).astype(bf16)
        mine, *messages = lax.optimization_barrier((mine, *messages))
    messages = dict(enumerate(messages, 1))
    if context > 1:
        swapped = lax.ppermute(messages.pop(1), "y", [(0, 1), (1, 0)])
        messages[2] = pl.pallas_call(
            relay_kernel,
            out_shape=jax.ShapeDtypeStruct((2 * rows, att), bf16),
            in_specs=[smem] + [vmem] * 2,
            out_specs=vmem,
            compiler_params=params,
            cost_estimate=cost(25 * 10**9, 10**7),
            name="relay",
        )(place, swapped, messages[2])
    else:
        swapped = jnp.zeros((2 * rows, att), bf16)
    if split:
        mine = summed_along(mine, "z")
        mine, messages = lax.optimization_barrier((mine, messages))
    messages = [shifted(message, -offset) for offset, message in messages.items()]
    if split:
        near_slabs = [mine] + [from_peer(mine, mask) for mask in range(1, plane)]
    key_grad, value_grad = pl.pallas_call(
        merge_kernel,
        out_shape=(jax.ShapeDtypeStruct((rows, att), bf16),) * 2,
        in_specs=[smem] + [vmem] * (2 + len(messages)),
        out_specs=(vmem,) * 2,
        compiler_params=params,
        cost_estimate=cost(8 * 10**9, 10**7),
        name="merge",
    )(place, *messages, swapped, own_grads)
    if split:
        far_slabs = [other_core(slab) for slab in near_slabs]
        far_slabs, key_grad, value_grad = lax.optimization_barrier(
            (far_slabs, key_grad, value_grad)
        )
    else:
        totals = lax.psum((keep, give, kernel_rows), ("x", "core", "z", "y"))
        near_slabs = jnp.concatenate([totals[0], totals[2]], axis=1)
        far_slabs = jnp.concatenate([totals[1], jnp.zeros_like(totals[2])], axis=1)
        near_slabs = jnp.split(near_slabs, plane)
        far_slabs = jnp.split(far_slabs, plane)
    def slab_scratch(count):
        return pltpu.VMEM((count, att // 2 // plane, width), f32)

    weight_total = pl.pallas_call(
        unpack_early_kernel,
        out_shape=jax.ShapeDtypeStruct((att, width), f32),
        in_specs=[smem] + [vmem] * len(EARLY_SLABS),
        out_specs=hbm,
        scratch_shapes=[
            slab_scratch(len(EARLY_SLABS)),
            pltpu.SemaphoreType.DMA((len(EARLY_SLABS),)),
        ],
        compiler_params=params,
        cost_estimate=cost(10**9, 3 * 10**6),
        name="unpack_early",
    )(place, *[near_slabs[slab] for slab in EARLY_SLABS])
    weight_total, kernel_total = pl.pallas_call(
        unpack_late_kernel,
        out_shape=(
            jax.ShapeDtypeStruct((att, width), f32),
            jax.ShapeDtypeStruct((taps, width), f32),
        ),
        in_specs=[smem] + [vmem] * (2 * plane) + [hbm],
        out_specs=(hbm, hbm),
        scratch_shapes=[
            slab_scratch(len(LATE_SLABS)),
            slab_scratch(plane),
            pltpu.VMEM((pieces * 2 * chunks, LANES), f32),
            pltpu.VMEM((taps, width), f32),
            pltpu.SemaphoreType.DMA((len(LATE_SLABS),)),
            pltpu.SemaphoreType.DMA((plane,)),
            pltpu.SemaphoreType.DMA,
        ],
        input_output_aliases={1 + 2 * plane: 0},
        compiler_params=params,
        name="unpack_late",
    )(place, *near_slabs, *far_slabs, weight_total)
    return (
        out_frames[None],
        query_grad[None],
        key_grad[None],
        value_grad[None],
        weight_total,
        kernel_total,
    )


def solution(mesh):
    sizes = (mesh.shape["dp"] // 2, 2, mesh.shape["blk"] // 2, 2)
    fine = Mesh(mesh.devices.reshape(sizes), ("x", "core", "z", "y"))
    frames = P(("x", "core"), RUN_AXES, None)
    return jax.shard_map(
        per_device,
        mesh=fine,
        in_specs=(frames, frames, frames, P(), P(), frames),
        out_specs=(frames, frames, frames, frames, P(), P()),
        check_vma=False,
    )
```

```python
import functools
import math

import jax
import jax.numpy as jnp
from jax import lax
from jax.experimental import pallas as pl
from jax.experimental.pallas import tpu as pltpu
from jax.sharding import Mesh
from jax.sharding import PartitionSpec as P

HEAD_DIM = 64
CTX_MAX = 3
LANES = 128
SUBLANES = 8
NEGATIVE = -1e30
RUN_AXES = ("z", "y")
PLANE_AXES = ("x", "y")
EARLY_SLABS = (0,)
LATE_SLABS = (1, 2, 3)
VMEM_LIMIT = 28 * 1024 * 1024

NN = (((1,), (0,)), ((), ()))
NT = (((1,), (1,)), ((), ()))
TN = (((0,), (0,)), ((), ()))


def dot(a, b, dims, precision=None):
    return lax.dot_general(a, b, dims, precision=precision, preferred_element_type=jnp.float32)


def shifted(x, by):
    devices = range(lax.axis_size(RUN_AXES))
    return lax.ppermute(x, RUN_AXES, [(i, i + by) for i in devices if i + by in devices])


def in_hbm(x):
    return pltpu.with_memory_space_constraint(x, pltpu.HBM)


def cost(flops, data):
    return pl.CostEstimate(flops=flops, bytes_accessed=data, transcendentals=0)


def head_masks():
    lane = lax.broadcasted_iota(jnp.int32, (1, LANES), 1)
    first = jnp.where(lane < HEAD_DIM, 1.0, 0.0)
    return first.astype(jnp.bfloat16), (1.0 - first).astype(jnp.bfloat16)


def stack_heads(pair):
    first, second = head_masks()
    return jnp.concatenate([pair * first, pair * second], axis=0)


def merge_heads(stacked):
    rows = stacked.shape[0] // 2
    lane = lax.broadcasted_iota(jnp.int32, (rows, LANES), 1)
    return jnp.where(lane < HEAD_DIM, stacked[:rows], stacked[rows:])


def pack_kernel(
    edge,
    k_ref,
    v_ref,
    q_ref,
    cot_ref,
    own_ref,
    keys_ref,
    values_ref,
    queries_ref,
    far_ref,
    near_ref,
    sems,
):
    rows, att = k_ref.shape
    width = cot_ref.shape[1]
    head, tail = pl.ds(0, edge), pl.ds(rows - edge, edge)
    moves = [
        (k_ref, own_ref.at[pl.ds(0, rows)]),
        (v_ref, own_ref.at[pl.ds(rows, rows)]),
        (k_ref, keys_ref.at[pl.ds(0, rows)]),
        (q_ref.at[tail], keys_ref.at[pl.ds(rows, edge)]),
        (v_ref, values_ref),
        (q_ref, queries_ref),
        (k_ref.at[tail], far_ref.at[pl.ds(0, edge)]),
        (v_ref.at[tail], far_ref.at[pl.ds(edge, edge)]),
        (k_ref.at[head], near_ref.at[pl.ds(0, edge)]),
        (v_ref.at[head], near_ref.at[pl.ds(edge, edge)]),
        (q_ref.at[head], near_ref.at[pl.ds(2 * edge, edge)]),
    ]
    for part in range(width // att):
        piece = cot_ref.at[head, pl.ds(part * att, att)]
        moves.append((piece, near_ref.at[pl.ds((3 + part) * edge, edge)]))
    copies = [pltpu.make_async_copy(a, b, sems.at[i]) for i, (a, b) in enumerate(moves)]
    for copy in copies:
        copy.start()
    for copy in copies:
        copy.wait()


def choose_kernel(device_ref, even_ref, odd_ref, out_ref):
    odd = lax.rem(device_ref[0], 2)
    rows = out_ref.shape[0]

    @pl.when(odd == 0)
    def _():
        out_ref[...] = even_ref[...]

    @pl.when(odd != 0)
    def _():
        out_ref[...] = odd_ref[odd_ref.shape[0] - rows :]


def tile_places(rows, own_ref, keys_ref, values_ref, *further_refs):
    places = [(own_ref, 0, own_ref, rows), (keys_ref, 0, values_ref, 0)]
    return places + [(ref, 0, ref, rows) for ref in further_refs]


def score_block(b, place, start, span, qx, kx, bias, weights_ref):
    pairs = qx.shape[1] // LANES
    block = LANES
    keys = span + block
    row_id = lax.broadcasted_iota(jnp.int32, (block, keys), 0)
    key_id = lax.broadcasted_iota(jnp.int32, (block, keys), 1)
    distance = row_id - key_id + span
    key_time = key_id + (start - span + b * block)
    visible = (distance >= 0) & (distance < span) & (key_time >= 0)
    bias[...] = jnp.where(visible, 0.0, NEGATIVE)
    lane_id = lax.broadcasted_iota(jnp.int32, (block, LANES), 1)
    log_sums = jnp.zeros((block, LANES), jnp.float32)
    for pair in range(pairs):
        columns = slice(pair * LANES, (pair + 1) * LANES)
        qs = stack_heads(qx[b * block : (b + 1) * block, columns])
        scores = dot(qs, kx[b * block : b * block + keys, columns], NT)
        hidden_pairs = bias[...]
        scores = scores + jnp.concatenate([hidden_pairs, hidden_pairs], axis=0)
        row_max = jnp.max(scores, axis=1, keepdims=True)
        weights = jnp.exp(scores - row_max)
        row_sum = jnp.sum(weights, axis=1, keepdims=True)
        weights_ref[place * pairs + pair] = (weights * (1.0 / row_sum)).astype(jnp.bfloat16)
        log_sum = row_max + jnp.log(row_sum)
        log_sums = jnp.where(lane_id == 2 * pair, log_sum[:block], log_sums)
        log_sums = jnp.where(lane_id == 2 * pair + 1, log_sum[block:], log_sums)
    return log_sums


def scores_kernel(context, rows, edge, blocks, device_ref, q_ref, *refs):
    own_refs = refs[: 1 + context]
    keys_ref = own_refs[1]
    edge_ref, weights_ref, lse_ref, qx, kx, lx, bias = refs[1 + context :]
    span = context * rows
    scale = 1.0 / math.sqrt(HEAD_DIM)
    start = device_ref[0] * rows - edge
    for offset, ref in enumerate(own_refs):
        first = edge + (context - offset) * rows
        kx[first : first + rows] = ref[:rows]
    qx[edge : edge + rows] = q_ref[...] * scale
    if blocks[0] == 0:
        kx[:edge] = edge_ref[:edge]
        qx[:edge] = keys_ref[rows : rows + edge] * scale
    else:
        kx[edge + span + rows :] = edge_ref[:edge]
        qx[edge + rows :] = edge_ref[2 * edge : 3 * edge] * scale
    for place, b in enumerate(blocks):
        lx[place * LANES : (place + 1) * LANES] = score_block(
            b, place, start, span, qx, kx, bias, weights_ref
        )
    lse_ref[...] = jnp.transpose(lx[...])[: lse_ref.shape[0]]


def forward_kernel(context, rows, edge, taps, *refs):
    tiles = context + 2
    device_ref, late_ref, early_ref = refs[:3]
    places = tile_places(rows, *refs[3 : 3 + tiles])
    far_ref, near_ref, w_hbm, conv_hbm, cot_hbm = refs[3 + tiles : 8 + tiles]
    out_hbm, att_ref, dhid_ref, keep_ref, give_ref, hid, dm, w_ref = refs[8 + tiles : 16 + tiles]
    vx, ax, cotx, parts, conv_ref, cot_ref, out_ref, sems = refs[16 + tiles :]

    att = ax.shape[1]
    width = w_ref.shape[1]
    span = context * rows
    query_rows = rows + 2 * edge
    block = LANES
    keys = span + block
    start = device_ref[0] * rows

    fetches = [
        pltpu.make_async_copy(source, target, sems.at[i])
        for i, (source, target) in enumerate(
            ((w_hbm, w_ref), (cot_hbm, cot_ref), (conv_hbm, conv_ref))
        )
    ]
    for fetch in fetches:
        fetch.start()

    vx[:edge] = far_ref[edge:]
    for offset, (_, _, ref, at) in enumerate(places):
        first = edge + (context - offset) * rows
        vx[first : first + rows] = ref[at : at + rows]
    vx[edge + span + rows :] = near_ref[edge : 2 * edge]

    pairs = att // LANES
    for b in range(query_rows // block):
        for pair in range(pairs):
            columns = slice(pair * LANES, (pair + 1) * LANES)
            values = vx[b * block : b * block + keys, columns]
            weights = early_ref[(b - 1) * pairs + pair] if b else late_ref[pair]
            mixed = dot(weights, values, NN)
            ax[b * block : (b + 1) * block, columns] = merge_heads(mixed).astype(jnp.bfloat16)
    att_ref[...] = ax[edge : edge + rows]

    fetches[0].wait()
    step = 2 * LANES
    for part in range(width // step):
        product = dot(ax[...], w_ref[:, part * step : (part + 1) * step], NN)
        product = product.astype(jnp.bfloat16).astype(jnp.float32)
        time = lax.broadcasted_iota(jnp.int32, product.shape, 0) + (start - edge)
        product = jnp.where(time >= 0, product, 0.0)
        hid[2 * part] = product[:, :LANES]
        hid[2 * part + 1] = product[:, LANES:]

    fetches[1].wait()
    fetches[2].wait()
    for chunk in range(width // LANES):
        columns = slice(chunk * LANES, (chunk + 1) * LANES)
        cotx[chunk, :rows] = cot_ref[:, columns].astype(jnp.float32)
        part, lane = divmod(chunk * LANES, att)
        cotx[chunk, rows:] = near_ref[
            (3 + part) * edge : (4 + part) * edge, lane : lane + LANES
        ].astype(jnp.float32)
    dm[:, rows + edge :] = jnp.zeros_like(dm[:, rows + edge :])

    apart = -(-taps // SUBLANES)
    reach = (apart - 1) * SUBLANES
    part_rows = (rows + edge) // 2

    def convolve(chunk, carry):
        columns = pl.ds(pl.multiple_of(chunk * LANES, LANES), LANES)
        for first in range(0, rows + edge, part_rows):
            mixed = jnp.zeros((part_rows, LANES), jnp.float32)
            for shift in range(SUBLANES):
                low = edge + first - shift - reach
                window = hid[chunk, low : low + part_rows + reach]
                for tap in range(shift, taps, SUBLANES):
                    at = reach - (tap - shift)
                    mixed += conv_ref[tap : tap + 1, columns] * window[at : at + part_rows]
            sigma = jax.nn.sigmoid(mixed)
            kept = min(part_rows, rows - first)
            out_ref[first : first + kept, columns] = (mixed * sigma)[:kept].astype(jnp.bfloat16)
            dm[chunk, first : first + part_rows] = (
                cotx[chunk, first : first + part_rows] * sigma * (1.0 + mixed * (1.0 - sigma))
            )
        part = rows // 2
        for first in range(0, rows, part):
            dhidden = jnp.zeros((part, LANES), jnp.float32)
            for shift in range(SUBLANES):
                low = first + shift
                window = dm[chunk, low : low + part + reach]
                for tap in range(shift, taps, SUBLANES):
                    at = tap - shift
                    dhidden += conv_ref[tap : tap + 1, columns] * window[at : at + part]
            dhid_ref[first : first + part, columns] = dhidden.astype(jnp.bfloat16)
        return carry

    lax.fori_loop(0, width // LANES, convolve, 0)
    store = pltpu.make_async_copy(out_ref, out_hbm, sems.at[3])
    store.start()

    _, pieces, _, _ = parts.shape
    group = att // (2 * pieces)
    core = device_ref[1]
    own = ax[edge : edge + rows]
    for part in range(width // step):
        product = dot(own, dhid_ref[:, part * step : (part + 1) * step], TN).astype(jnp.bfloat16)
        for chunk in (2 * part, 2 * part + 1):
            tile = product[:, (chunk - 2 * part) * LANES : (chunk - 2 * part + 1) * LANES]
            for half in range(2):
                for piece in range(pieces):
                    first = (half * pieces + piece) * group
                    parts[half, piece, chunk * group : (chunk + 1) * group] = tile[
                        first : first + group
                    ]
    keep_ref[...] = parts[core]
    give_ref[...] = parts[1 - core]
    store.wait()


def kernel_grad_kernel(rows, edge, taps, hid, dm, rows_ref, ks, kp):
    chunks = hid.shape[0]
    pieces = rows_ref.shape[0]
    apart = -(-taps // SUBLANES)
    reach = (apart - 1) * SUBLANES
    part = rows // 2
    kp[...] = jnp.zeros_like(kp)

    def correlate(chunk, carry):
        for shift in range(SUBLANES):
            sums = [jnp.zeros((SUBLANES, LANES), jnp.float32)] * apart
            for first in range(0, rows, part):
                low = edge + first - shift - reach
                window = hid[chunk, low : low + part + reach]
                own = dm[chunk, first : first + part]
                for tap in range(shift, taps, SUBLANES):
                    at = reach - (tap - shift)
                    product = (own * window[at : at + part]).reshape(-1, SUBLANES, LANES)
                    sums[tap // SUBLANES] += jnp.sum(product, axis=0)
            for tap in range(shift, taps, SUBLANES):
                ks[tap * SUBLANES : (tap + 1) * SUBLANES] = sums[tap // SUBLANES]
        total = ks[pl.ds(0, taps, SUBLANES)]
        for row in range(1, SUBLANES):
            total += ks[pl.ds(row, taps, SUBLANES)]
        kp[chunk, :taps] = total
        return carry

    lax.fori_loop(0, chunks, correlate, 0)
    for piece in range(pieces):
        block = [kp[chunk, tap : tap + 1] for tap in (piece, pieces + piece) for chunk in range(chunks)]
        rows_ref[piece] = jnp.concatenate(block, axis=0).astype(jnp.bfloat16)


def join_kernel(device_ref, keep_ref, given_ref, rows_ref, *slab_refs):
    split = keep_ref.shape[1]
    pieces = slab_refs[0].shape[0]
    for slab, ref in enumerate(slab_refs):
        first = (device_ref[2] ^ slab) * pieces
        for piece in range(pieces):
            total = keep_ref[first + piece].astype(jnp.float32)
            total += given_ref[first + piece].astype(jnp.float32)
            ref[piece, :split] = total.astype(jnp.bfloat16)
            ref[piece, split:] = rows_ref[first + piece]


def write_slabs(slabs, half, me, scratch, weight_hbm, sems):
    count, slab_rows, width = scratch.shape
    copies = []
    for place, (slab, ref) in enumerate(slabs):
        pieces = ref.shape[0]
        group = slab_rows // pieces
        for piece in range(pieces):
            for chunk in range(width // LANES):
                tile = ref[piece, chunk * group : (chunk + 1) * group].astype(jnp.float32)
                scratch[
                    place, piece * group : (piece + 1) * group, chunk * LANES : (chunk + 1) * LANES
                ] = tile
        plane = EARLY_SLABS + LATE_SLABS
        first = pl.multiple_of((half * len(plane) + (me ^ slab)) * slab_rows, slab_rows)
        target = weight_hbm.at[pl.ds(first, slab_rows)]
        copies.append(pltpu.make_async_copy(scratch.at[place], target, sems.at[place]))
        copies[-1].start()
    return copies


def unpack_early_kernel(device_ref, *refs):
    *near_refs, weight_hbm, scratch, sems = refs
    slabs = list(zip(EARLY_SLABS, near_refs))
    for copy in write_slabs(slabs, device_ref[1], device_ref[2], scratch, weight_hbm, sems):
        copy.wait()


def unpack_late_kernel(device_ref, *refs):
    slabs = len(EARLY_SLABS) + len(LATE_SLABS)
    near_refs, far_refs = refs[:slabs], refs[slabs : 2 * slabs]
    weight_hbm, kernel_hbm, scratch, far_scratch, blocks, kernel_ref = refs[2 * slabs + 1 : -3]
    sems, far_sems, kernel_sem = refs[-3:]
    core, me = device_ref[1], device_ref[2]
    late = [(slab, near_refs[slab]) for slab in LATE_SLABS]
    copies = write_slabs(late, core, me, scratch, weight_hbm, sems)
    far = list(enumerate(far_refs))
    copies += write_slabs(far, 1 - core, me, far_scratch, weight_hbm, far_sems)
    pieces, piece_rows, _ = near_refs[0].shape
    taps, width = kernel_ref.shape
    chunks = width // LANES
    size = 2 * chunks
    for slab in range(slabs):
        for piece in range(pieces):
            total = near_refs[slab][piece, piece_rows - size :].astype(jnp.float32)
            total += far_refs[slab][piece, piece_rows - size :].astype(jnp.float32)
            first = pl.multiple_of(((me ^ slab) * pieces + piece) * size, size)
            blocks[pl.ds(first, size)] = total
    for half in range(2):
        first = half * slabs * pieces
        count = min(slabs * pieces, taps - first)
        for chunk in range(chunks):
            columns = slice(chunk * LANES, (chunk + 1) * LANES)
            tap_rows = blocks[pl.ds(half * chunks + chunk, count, size)]
            kernel_ref[first : first + count, columns] = tap_rows
    copies.append(pltpu.make_async_copy(kernel_ref, kernel_hbm, kernel_sem))
    copies[-1].start()
    for copy in copies:
        copy.wait()


def backward_kernel(context, rows, *refs):
    tiles = context + 2
    device_ref, q_ref = refs[:2]
    places = tile_places(rows, *refs[2 : 2 + tiles])
    att_ref, late_ref, early_ref, dhid_ref, w_ref = refs[2 + tiles : 7 + tiles]
    dq_ref, own_ref = refs[7 + tiles : 9 + tiles]
    message_refs = refs[9 + tiles : 9 + tiles + context]
    datt, bias, lse_ref = refs[9 + tiles + context :]

    att = q_ref.shape[1]
    heads = att // HEAD_DIM
    span = context * rows
    scale = 1.0 / math.sqrt(HEAD_DIM)
    start = device_ref[0] * rows

    edge = (late_ref.shape[1] + early_ref.shape[1] - rows) // 2
    log_sums = jnp.concatenate([late_ref[...], early_ref[...]], axis=1)
    lse_ref[...] = log_sums[:, edge : edge + rows]
    for offset in range(context + 1):
        key_id = lax.broadcasted_iota(jnp.int32, (rows, rows), 0)
        row_id = lax.broadcasted_iota(jnp.int32, (rows, rows), 1)
        distance = row_id - key_id + offset * rows
        key_time = key_id + (start - offset * rows)
        visible = (distance >= 0) & (distance < span) & (key_time >= 0)
        bias[offset] = jnp.where(visible, 0.0, NEGATIVE)

    dattended = dot(dhid_ref[...], w_ref[...], NT).astype(jnp.bfloat16)
    datt[...] = dattended
    product = dattended.astype(jnp.float32) * att_ref[...].astype(jnp.float32)
    head_id = lax.broadcasted_iota(jnp.int32, (heads, att), 0)
    feature_id = lax.broadcasted_iota(jnp.int32, (heads, att), 1)
    ours = (feature_id >= head_id * HEAD_DIM) & (feature_id < (head_id + 1) * HEAD_DIM)
    deltas = dot(jnp.where(ours, 1.0, 0.0), product, NT, lax.Precision.HIGHEST)

    for pair in range(att // LANES):
        columns = slice(pair * LANES, (pair + 1) * LANES)
        qs = stack_heads(q_ref[:, columns] * scale)
        ds = stack_heads(datt[:, columns])
        log_sum = [lse_ref[2 * pair + i : 2 * pair + i + 1] for i in (0, 1)]
        delta = [deltas[2 * pair + i : 2 * pair + i + 1] for i in (0, 1)]
        log_sum = jnp.concatenate(log_sum, axis=1)
        delta = jnp.concatenate(delta, axis=1)
        dquery = jnp.zeros((2 * rows, LANES), jnp.float32)
        for offset, (k_ref, k_at, v_ref, v_at) in enumerate(places):
            kp = k_ref[k_at : k_at + rows, columns]
            vp = v_ref[v_at : v_at + rows, columns]
            hidden_pairs = jnp.concatenate([bias[offset], bias[offset]], axis=1)
            probs = jnp.exp(dot(kp, qs, NT) + hidden_pairs - log_sum)
            dprobs = dot(vp, ds, NT)
            dscores = (probs * (dprobs - delta)).astype(jnp.bfloat16)
            dvalue = dot(probs.astype(jnp.bfloat16), ds, NN)
            dkey = dot(dscores, qs, NN)
            dquery += dot(dscores, kp, TN)
            target = message_refs[offset - 1] if offset else own_ref
            target[:rows, columns] = dkey.astype(target.dtype)
            target[rows:, columns] = dvalue.astype(target.dtype)
        dq_ref[:, columns] = (merge_heads(dquery) * scale).astype(jnp.bfloat16)


def relay_kernel(device_ref, swapped_ref, message_ref, out_ref):
    odd = lax.rem(device_ref[0], 2).astype(jnp.float32)
    swapped = swapped_ref[...].astype(jnp.float32) * odd
    out_ref[...] = (message_ref[...].astype(jnp.float32) + swapped).astype(jnp.bfloat16)


def merge_kernel(device_ref, *refs):
    *message_refs, swapped_ref, own_ref, dk_ref, dv_ref = refs
    rows = dk_ref.shape[0]
    even = 1.0 - lax.rem(device_ref[0], 2).astype(jnp.float32)
    total = swapped_ref[...].astype(jnp.float32) * even
    for message_ref in message_refs:
        total += message_ref[...].astype(jnp.float32)
    total = (total + own_ref[...]).astype(jnp.bfloat16)
    dk_ref[...] = total[:rows]
    dv_ref[...] = total[rows:]


def from_peer(x, mask):
    devices = range(lax.axis_size(PLANE_AXES))
    return lax.ppermute(x, PLANE_AXES, [(i, i ^ mask) for i in devices])


def summed_along(x, axis):
    size, step = lax.axis_size(axis), 1
    while step < size:
        other = lax.ppermute(x, axis, [(i, i ^ step) for i in range(size)])
        x = (x.astype(jnp.float32) + other.astype(jnp.float32)).astype(x.dtype)
        step *= 2
    return x


def other_core(x):
    return lax.ppermute(x, "core", [(0, 1), (1, 0)])


def per_device(queries, key_in, value_in, out_weight, conv_kernel, cotangent):
    bf16, f32 = jnp.bfloat16, jnp.float32
    query, key, value, cot = queries[0], key_in[0], value_in[0], cotangent[0]
    runs = lax.axis_size(RUN_AXES)
    device = lax.axis_index(RUN_AXES).astype(jnp.int32)
    rows, att = query.shape
    width = out_weight.shape[1]
    heads = att // HEAD_DIM
    taps = conv_kernel.shape[0]
    edge = -(-(taps - 1) // 16) * 16
    context = min(CTX_MAX, runs // 4)

    query_rows = rows + 2 * edge
    key_rows = query_rows + context * rows
    chunks = width // LANES
    vmem = pl.BlockSpec(memory_space=pltpu.VMEM)
    smem = pl.BlockSpec(memory_space=pltpu.SMEM)
    hbm = pl.BlockSpec(memory_space=pltpu.HBM)
    params = pltpu.CompilerParams(vmem_limit_bytes=VMEM_LIMIT)

    own, keys, values, packed_query, far, near = pl.pallas_call(
        functools.partial(pack_kernel, edge),
        out_shape=(
            jax.ShapeDtypeStruct((2 * rows, att), bf16),
            jax.ShapeDtypeStruct((rows + edge, att), bf16),
            jax.ShapeDtypeStruct((rows, att), bf16),
            jax.ShapeDtypeStruct((rows, att), bf16),
            jax.ShapeDtypeStruct((2 * edge, att), bf16),
            jax.ShapeDtypeStruct(((3 + width // att) * edge, att), bf16),
        ),
        in_specs=[hbm] * 4,
        out_specs=(vmem,) * 6,
        scratch_shapes=[pltpu.SemaphoreType.DMA((11 + width // att,))],
        compiler_params=params,
        name="pack",
    )(in_hbm(key), in_hbm(value), in_hbm(query), in_hbm(cot))
    further = [shifted(own, offset) for offset in range(2, context + 1)]
    keys = shifted(keys, 1)
    near = shifted(near, -1)
    if further:
        values = pl.pallas_call(
            choose_kernel,
            out_shape=jax.ShapeDtypeStruct((rows, att), bf16),
            in_specs=[smem, vmem, vmem],
            out_specs=vmem,
            compiler_params=params,
            name="choose",
        )(device[None], values, further[0])
        values = lax.ppermute(values, "y", [(0, 1), (1, 0)])
    else:
        values = shifted(values, 1)
    tiles = [own, keys, values, *further]
    far = shifted(far, context + 1)

    pieces = att // 32
    layers = lax.axis_size("z")
    split = pieces == layers * lax.axis_size(PLANE_AXES) and layers & (layers - 1) == 0
    core = lax.axis_index("core").astype(jnp.int32) if split else jnp.int32(0)
    plane = lax.axis_size(PLANE_AXES)
    spot = lax.axis_index(PLANE_AXES).astype(jnp.int32) if split else jnp.int32(0)
    place = jnp.stack([device, core, spot])
    blocks = query_rows // LANES
    pairs = att // LANES
    key_span = context * rows + LANES

    def score(blocks, edge_rows):
        return pl.pallas_call(
            functools.partial(scores_kernel, context, rows, edge, blocks),
            out_shape=(
                jax.ShapeDtypeStruct((len(blocks) * pairs, 2 * LANES, key_span), bf16),
                jax.ShapeDtypeStruct((heads, len(blocks) * LANES), f32),
            ),
            in_specs=[smem] + [vmem] * (3 + context),
            out_specs=(vmem,) * 2,
            scratch_shapes=[
                pltpu.VMEM((query_rows, att), bf16),
                pltpu.VMEM((key_rows, att), bf16),
                pltpu.VMEM((len(blocks) * LANES, LANES), f32),
                pltpu.VMEM((LANES, key_span), f32),
            ],
            compiler_params=params,
            cost_estimate=cost(5 * 10**9, 10**7),
            name="scores",
        )(place, packed_query, own, keys, *further, edge_rows)

    early, early_sums = score(list(range(1, blocks)), near)
    late, late_sums = score([0], far)
    out_frames, attended, dhidden, keep, give, hidden, dmixed, held_weight = pl.pallas_call(
        functools.partial(forward_kernel, context, rows, edge, taps),
        out_shape=(
            jax.ShapeDtypeStruct((rows, width), bf16),
            jax.ShapeDtypeStruct((rows, att), bf16),
            jax.ShapeDtypeStruct((rows, width), bf16),
        )
        + (jax.ShapeDtypeStruct((pieces, chunks * 16, LANES), bf16),) * 2
        + (
            jax.ShapeDtypeStruct((chunks, query_rows, LANES), f32),
            jax.ShapeDtypeStruct((chunks, rows + edge + 8, LANES), f32),
            jax.ShapeDtypeStruct((att, width), bf16),
        ),
        in_specs=[smem] + [vmem] * (6 + context) + [hbm] * 3,
        out_specs=(hbm,) + (vmem,) * 7,
        scratch_shapes=[
            pltpu.VMEM((key_rows, att), bf16),
            pltpu.VMEM((query_rows, att), bf16),
            pltpu.VMEM((chunks, rows + edge, LANES), f32),
            pltpu.VMEM((2, pieces, chunks * 16, LANES), bf16),
            pltpu.VMEM((taps, width), f32),
            pltpu.VMEM((rows, width), bf16),
            pltpu.VMEM((rows, width), bf16),
            pltpu.SemaphoreType.DMA((4,)),
        ],
        compiler_params=params,
        cost_estimate=cost(8 * 10**9, 10**7),
        name="forward",
    )(
        place,
        late,
        early,
        *tiles,
        far,
        near,
        in_hbm(out_weight),
        in_hbm(conv_kernel),
        in_hbm(cot),
    )
    kernel_rows = pl.pallas_call(
        functools.partial(kernel_grad_kernel, rows, edge, taps),
        out_shape=jax.ShapeDtypeStruct((pieces, 2 * chunks, LANES), bf16),
        in_specs=[vmem, vmem],
        out_specs=vmem,
        scratch_shapes=[
            pltpu.VMEM((taps * SUBLANES, LANES), f32),
            pltpu.VMEM((chunks, 2 * pieces, LANES), f32),
        ],
        compiler_params=params,
        cost_estimate=cost(2 * 10**9, 3 * 10**6),
        name="kernel_grad",
    )(hidden, dmixed)

    if split:
        slabs = pl.pallas_call(
            join_kernel,
            out_shape=(jax.ShapeDtypeStruct((layers, 18 * chunks, LANES), bf16),) * plane,
            in_specs=[smem] + [vmem] * 3,
            out_specs=(vmem,) * plane,
            compiler_params=params,
            name="join",
        )(place, keep, other_core(give), kernel_rows)
        *slabs, dhidden = lax.optimization_barrier((*slabs, dhidden))
        slabs = [slabs[0]] + [from_peer(slabs[mask], mask) for mask in range(1, plane)]
    query_grad, own_grads, *messages = pl.pallas_call(
        functools.partial(backward_kernel, context, rows),
        out_shape=(
            jax.ShapeDtypeStruct((rows, att), bf16),
            jax.ShapeDtypeStruct((2 * rows, att), f32),
        )
        + (jax.ShapeDtypeStruct((2 * rows, att), bf16),) * context,
        in_specs=[smem] + [vmem] * (8 + context),
        out_specs=(vmem,) * (2 + context),
        scratch_shapes=[
            pltpu.VMEM((rows, att), bf16),
            pltpu.VMEM((context + 1, rows, rows), f32),
            pltpu.VMEM((heads, rows), f32),
        ],
        compiler_params=params,
        cost_estimate=cost(6 * 10**9, 10**7),
        name="backward",
    )(place, packed_query, *tiles, attended, late_sums, early_sums, dhidden, held_weight)
    if split:
        mine = sum(slab.astype(f32) for slab in slabs).astype(bf16)
        mine, *messages = lax.optimization_barrier((mine, *messages))
    messages = dict(enumerate(messages, 1))
    if context > 1:
        swapped = lax.ppermute(messages.pop(1), "y", [(0, 1), (1, 0)])
        messages[2] = pl.pallas_call(
            relay_kernel,
            out_shape=jax.ShapeDtypeStruct((2 * rows, att), bf16),
            in_specs=[smem] + [vmem] * 2,
            out_specs=vmem,
            compiler_params=params,
            cost_estimate=cost(25 * 10**9, 10**7),
            name="relay",
        )(place, swapped, messages[2])
    else:
        swapped = jnp.zeros((2 * rows, att), bf16)
    if split:
        mine = summed_along(mine, "z")
        mine, messages = lax.optimization_barrier((mine, messages))
    messages = [shifted(message, -offset) for offset, message in messages.items()]
    if split:
        near_slabs = [mine] + [from_peer(mine, mask) for mask in range(1, plane)]
    key_grad, value_grad = pl.pallas_call(
        merge_kernel,
        out_shape=(jax.ShapeDtypeStruct((rows, att), bf16),) * 2,
        in_specs=[smem] + [vmem] * (2 + len(messages)),
        out_specs=(vmem,) * 2,
        compiler_params=params,
        cost_estimate=cost(16 * 10**9, 10**7),
        name="merge",
    )(place, *messages, swapped, own_grads)
    if split:
        far_slabs = [other_core(slab) for slab in near_slabs]
        far_slabs, key_grad, value_grad = lax.optimization_barrier(
            (far_slabs, key_grad, value_grad)
        )
    else:
        totals = lax.psum((keep, give, kernel_rows), ("x", "core", "z", "y"))
        near_slabs = jnp.concatenate([totals[0], totals[2]], axis=1)
        far_slabs = jnp.concatenate([totals[1], jnp.zeros_like(totals[2])], axis=1)
        near_slabs = jnp.split(near_slabs, plane)
        far_slabs = jnp.split(far_slabs, plane)
    def slab_scratch(count):
        return pltpu.VMEM((count, att // 2 // plane, width), f32)

    weight_total = pl.pallas_call(
        unpack_early_kernel,
        out_shape=jax.ShapeDtypeStruct((att, width), f32),
        in_specs=[smem] + [vmem] * len(EARLY_SLABS),
        out_specs=hbm,
        scratch_shapes=[
            slab_scratch(len(EARLY_SLABS)),
            pltpu.SemaphoreType.DMA((len(EARLY_SLABS),)),
        ],
        compiler_params=params,
        cost_estimate=cost(10**9, 3 * 10**6),
        name="unpack_early",
    )(place, *[near_slabs[slab] for slab in EARLY_SLABS])
    weight_total, kernel_total = pl.pallas_call(
        unpack_late_kernel,
        out_shape=(
            jax.ShapeDtypeStruct((att, width), f32),
            jax.ShapeDtypeStruct((taps, width), f32),
        ),
        in_specs=[smem] + [vmem] * (2 * plane) + [hbm],
        out_specs=(hbm, hbm),
        scratch_shapes=[
            slab_scratch(len(LATE_SLABS)),
            slab_scratch(plane),
            pltpu.VMEM((pieces * 2 * chunks, LANES), f32),
            pltpu.VMEM((taps, width), f32),
            pltpu.SemaphoreType.DMA((len(LATE_SLABS),)),
            pltpu.SemaphoreType.DMA((plane,)),
            pltpu.SemaphoreType.DMA,
        ],
        input_output_aliases={1 + 2 * plane: 0},
        compiler_params=params,
        name="unpack_late",
    )(place, *near_slabs, *far_slabs, weight_total)
    return (
        out_frames[None],
        query_grad[None],
        key_grad[None],
        value_grad[None],
        weight_total,
        kernel_total,
    )


def solution(mesh):
    sizes = (mesh.shape["dp"] // 2, 2, mesh.shape["blk"] // 2, 2)
    fine = Mesh(mesh.devices.reshape(sizes), ("x", "core", "z", "y"))
    frames = P(("x", "core"), RUN_AXES, None)
    return jax.shard_map(
        per_device,
        mesh=fine,
        in_specs=(frames, frames, frames, P(), P(), frames),
        out_specs=(frames, frames, frames, frames, P(), P()),
        check_vma=False,
    )
```

```python
import functools
import math

import jax
import jax.numpy as jnp
from jax import lax
from jax.experimental import pallas as pl
from jax.experimental.pallas import tpu as pltpu
from jax.sharding import Mesh
from jax.sharding import PartitionSpec as P

HEAD_DIM = 64
CTX_MAX = 3
LANES = 128
SUBLANES = 8
CHUNK = 32
NEGATIVE = -1e30
RUN_AXES = ("z", "y")
PLANE_AXES = ("x", "y")
EARLY_SLABS = (0,)
LATE_SLABS = (1, 2, 3)
VMEM_LIMIT = 28 * 1024 * 1024

NN = (((1,), (0,)), ((), ()))
NT = (((1,), (1,)), ((), ()))
TN = (((0,), (0,)), ((), ()))


def dot(a, b, dims, precision=None):
    return lax.dot_general(a, b, dims, precision=precision, preferred_element_type=jnp.float32)


def shifted(x, by):
    devices = range(lax.axis_size(RUN_AXES))
    return lax.ppermute(x, RUN_AXES, [(i, i + by) for i in devices if i + by in devices])


def in_hbm(x):
    return pltpu.with_memory_space_constraint(x, pltpu.HBM)


def cost(flops, data):
    return pl.CostEstimate(flops=flops, bytes_accessed=data, transcendentals=0)


def head_masks():
    lane = lax.broadcasted_iota(jnp.int32, (1, LANES), 1)
    first = jnp.where(lane < HEAD_DIM, 1.0, 0.0)
    return first.astype(jnp.bfloat16), (1.0 - first).astype(jnp.bfloat16)


def stack_heads(pair):
    first, second = head_masks()
    return jnp.concatenate([pair * first, pair * second], axis=0)


def merge_heads(stacked):
    rows = stacked.shape[0] // 2
    lane = lax.broadcasted_iota(jnp.int32, (rows, LANES), 1)
    return jnp.where(lane < HEAD_DIM, stacked[:rows], stacked[rows:])


def pack_kernel(
    edge,
    k_ref,
    v_ref,
    q_ref,
    cot_ref,
    own_ref,
    keys_ref,
    values_ref,
    queries_ref,
    far_ref,
    near_ref,
    sems,
):
    rows, att = k_ref.shape
    width = cot_ref.shape[1]
    head, tail = pl.ds(0, edge), pl.ds(rows - edge, edge)
    moves = [
        (k_ref, own_ref.at[pl.ds(0, rows)]),
        (v_ref, own_ref.at[pl.ds(rows, rows)]),
        (k_ref, keys_ref.at[pl.ds(0, rows)]),
        (q_ref.at[tail], keys_ref.at[pl.ds(rows, edge)]),
        (v_ref, values_ref),
        (q_ref, queries_ref),
        (k_ref.at[tail], far_ref.at[pl.ds(0, edge)]),
        (v_ref.at[tail], far_ref.at[pl.ds(edge, edge)]),
        (k_ref.at[head], near_ref.at[pl.ds(0, edge)]),
        (v_ref.at[head], near_ref.at[pl.ds(edge, edge)]),
        (q_ref.at[head], near_ref.at[pl.ds(2 * edge, edge)]),
    ]
    for part in range(width // att):
        piece = cot_ref.at[head, pl.ds(part * att, att)]
        moves.append((piece, near_ref.at[pl.ds((3 + part) * edge, edge)]))
    copies = [pltpu.make_async_copy(a, b, sems.at[i]) for i, (a, b) in enumerate(moves)]
    for copy in copies:
        copy.start()
    for copy in copies:
        copy.wait()


def choose_kernel(device_ref, even_ref, odd_ref, out_ref):
    odd = lax.rem(device_ref[0], 2)
    rows = out_ref.shape[0]

    @pl.when(odd == 0)
    def _():
        out_ref[...] = even_ref[...]

    @pl.when(odd != 0)
    def _():
        out_ref[...] = odd_ref[odd_ref.shape[0] - rows :]


def tile_places(rows, own_ref, keys_ref, values_ref, *further_refs):
    places = [(own_ref, 0, own_ref, rows), (keys_ref, 0, values_ref, 0)]
    return places + [(ref, 0, ref, rows) for ref in further_refs]


def score_block(b, place, start, span, qx, kx, bias, held, weights_ref):
    pairs = qx.shape[1] // LANES
    block = LANES
    keys = span + block
    row_id = lax.broadcasted_iota(jnp.int32, (block, keys), 0)
    key_id = lax.broadcasted_iota(jnp.int32, (block, keys), 1)
    distance = row_id - key_id + span
    key_time = key_id + (start - span + b * block)
    visible = (distance >= 0) & (distance < span) & (key_time >= 0)
    bias[...] = jnp.where(visible, 0.0, NEGATIVE)
    lane_id = lax.broadcasted_iota(jnp.int32, (block, LANES), 1)
    log_sums = jnp.zeros((block, LANES), jnp.float32)
    for pair in range(pairs):
        columns = slice(pair * LANES, (pair + 1) * LANES)
        qs = stack_heads(qx[b * block : (b + 1) * block, columns])
        slot = pair % 2
        held[slot] = dot(qs, kx[b * block : b * block + keys, columns], NT)
        log_sum = []
        for first in range(0, 2 * block, CHUNK):
            at = first % block
            scores = held[slot, first : first + CHUNK] + bias[at : at + CHUNK]
            row_max = jnp.max(scores, axis=1, keepdims=True)
            weights = jnp.exp(scores - row_max)
            row_sum = jnp.sum(weights, axis=1, keepdims=True)
            weights_ref[place * pairs + pair, first : first + CHUNK] = (
                weights * (1.0 / row_sum)
            ).astype(jnp.bfloat16)
            log_sum.append(row_max + jnp.log(row_sum))
        log_sum = jnp.concatenate(log_sum, axis=0)
        log_sums = jnp.where(lane_id == 2 * pair, log_sum[:block], log_sums)
        log_sums = jnp.where(lane_id == 2 * pair + 1, log_sum[block:], log_sums)
    return log_sums


def scores_kernel(context, rows, edge, blocks, device_ref, q_ref, *refs):
    own_refs = refs[: 1 + context]
    keys_ref = own_refs[1]
    edge_ref, weights_ref, lse_ref, qx, kx, lx, bias, held = refs[1 + context :]
    span = context * rows
    scale = 1.0 / math.sqrt(HEAD_DIM)
    start = device_ref[0] * rows - edge
    for offset, ref in enumerate(own_refs):
        first = edge + (context - offset) * rows
        kx[first : first + rows] = ref[:rows]
    qx[edge : edge + rows] = q_ref[...] * scale
    if blocks[0] == 0:
        kx[:edge] = edge_ref[:edge]
        qx[:edge] = keys_ref[rows : rows + edge] * scale
    else:
        kx[edge + span + rows :] = edge_ref[:edge]
        qx[edge + rows :] = edge_ref[2 * edge : 3 * edge] * scale
    for place, b in enumerate(blocks):
        lx[place * LANES : (place + 1) * LANES] = score_block(
            b, place, start, span, qx, kx, bias, held, weights_ref
        )
    lse_ref[...] = jnp.transpose(lx[...])[: lse_ref.shape[0]]


def forward_kernel(context, rows, edge, taps, *refs):
    tiles = context + 2
    device_ref, late_ref, early_ref = refs[:3]
    places = tile_places(rows, *refs[3 : 3 + tiles])
    far_ref, near_ref, w_hbm, conv_hbm, cot_hbm = refs[3 + tiles : 8 + tiles]
    out_hbm, att_ref, dhid_ref, keep_ref, give_ref, hid, dm, w_ref = refs[8 + tiles : 16 + tiles]
    vx, ax, cotx, parts, conv_ref, cot_ref, out_ref, sems = refs[16 + tiles :]

    att = ax.shape[1]
    width = w_ref.shape[1]
    span = context * rows
    query_rows = rows + 2 * edge
    block = LANES
    keys = span + block
    start = device_ref[0] * rows

    fetches = [
        pltpu.make_async_copy(source, target, sems.at[i])
        for i, (source, target) in enumerate(
            ((w_hbm, w_ref), (cot_hbm, cot_ref), (conv_hbm, conv_ref))
        )
    ]
    for fetch in fetches:
        fetch.start()

    vx[:edge] = far_ref[edge:]
    for offset, (_, _, ref, at) in enumerate(places):
        first = edge + (context - offset) * rows
        vx[first : first + rows] = ref[at : at + rows]
    vx[edge + span + rows :] = near_ref[edge : 2 * edge]

    pairs = att // LANES
    for b in range(query_rows // block):
        for pair in range(pairs):
            columns = slice(pair * LANES, (pair + 1) * LANES)
            values = vx[b * block : b * block + keys, columns]
            weights = early_ref[(b - 1) * pairs + pair] if b else late_ref[pair]
            mixed = dot(weights, values, NN)
            ax[b * block : (b + 1) * block, columns] = merge_heads(mixed).astype(jnp.bfloat16)
    att_ref[...] = ax[edge : edge + rows]

    fetches[0].wait()
    step = 2 * LANES
    for part in range(width // step):
        product = dot(ax[...], w_ref[:, part * step : (part + 1) * step], NN)
        product = product.astype(jnp.bfloat16).astype(jnp.float32)
        time = lax.broadcasted_iota(jnp.int32, product.shape, 0) + (start - edge)
        product = jnp.where(time >= 0, product, 0.0)
        hid[2 * part] = product[:, :LANES]
        hid[2 * part + 1] = product[:, LANES:]

    fetches[1].wait()
    fetches[2].wait()
    for chunk in range(width // LANES):
        columns = slice(chunk * LANES, (chunk + 1) * LANES)
        cotx[chunk, :rows] = cot_ref[:, columns].astype(jnp.float32)
        part, lane = divmod(chunk * LANES, att)
        cotx[chunk, rows:] = near_ref[
            (3 + part) * edge : (4 + part) * edge, lane : lane + LANES
        ].astype(jnp.float32)
    dm[:, rows + edge :] = jnp.zeros_like(dm[:, rows + edge :])

    apart = -(-taps // SUBLANES)
    reach = (apart - 1) * SUBLANES
    part_rows = (rows + edge) // 2

    def convolve(chunk, carry):
        columns = pl.ds(pl.multiple_of(chunk * LANES, LANES), LANES)
        for first in range(0, rows + edge, part_rows):
            mixed = jnp.zeros((part_rows, LANES), jnp.float32)
            for shift in range(SUBLANES):
                low = edge + first - shift - reach
                window = hid[chunk, low : low + part_rows + reach]
                for tap in range(shift, taps, SUBLANES):
                    at = reach - (tap - shift)
                    mixed += conv_ref[tap : tap + 1, columns] * window[at : at + part_rows]
            sigma = jax.nn.sigmoid(mixed)
            kept = min(part_rows, rows - first)
            out_ref[first : first + kept, columns] = (mixed * sigma)[:kept].astype(jnp.bfloat16)
            dm[chunk, first : first + part_rows] = (
                cotx[chunk, first : first + part_rows] * sigma * (1.0 + mixed * (1.0 - sigma))
            )
        part = rows // 2
        for first in range(0, rows, part):
            dhidden = jnp.zeros((part, LANES), jnp.float32)
            for shift in range(SUBLANES):
                low = first + shift
                window = dm[chunk, low : low + part + reach]
                for tap in range(shift, taps, SUBLANES):
                    at = tap - shift
                    dhidden += conv_ref[tap : tap + 1, columns] * window[at : at + part]
            dhid_ref[first : first + part, columns] = dhidden.astype(jnp.bfloat16)
        return carry

    lax.fori_loop(0, width // LANES, convolve, 0)
    store = pltpu.make_async_copy(out_ref, out_hbm, sems.at[3])
    store.start()

    _, pieces, _, _ = parts.shape
    group = att // (2 * pieces)
    core = device_ref[1]
    own = ax[edge : edge + rows]
    for part in range(width // step):
        product = dot(own, dhid_ref[:, part * step : (part + 1) * step], TN).astype(jnp.bfloat16)
        for chunk in (2 * part, 2 * part + 1):
            tile = product[:, (chunk - 2 * part) * LANES : (chunk - 2 * part + 1) * LANES]
            for half in range(2):
                for piece in range(pieces):
                    first = (half * pieces + piece) * group
                    parts[half, piece, chunk * group : (chunk + 1) * group] = tile[
                        first : first + group
                    ]
    keep_ref[...] = parts[core]
    give_ref[...] = parts[1 - core]
    store.wait()


def kernel_grad_kernel(rows, edge, taps, hid, dm, rows_ref, ks, kp):
    chunks = hid.shape[0]
    pieces = rows_ref.shape[0]
    apart = -(-taps // SUBLANES)
    reach = (apart - 1) * SUBLANES
    part = rows // 2
    kp[...] = jnp.zeros_like(kp)

    def correlate(chunk, carry):
        for shift in range(SUBLANES):
            sums = [jnp.zeros((SUBLANES, LANES), jnp.float32)] * apart
            for first in range(0, rows, part):
                low = edge + first - shift - reach
                window = hid[chunk, low : low + part + reach]
                own = dm[chunk, first : first + part]
                for tap in range(shift, taps, SUBLANES):
                    at = reach - (tap - shift)
                    product = (own * window[at : at + part]).reshape(-1, SUBLANES, LANES)
                    sums[tap // SUBLANES] += jnp.sum(product, axis=0)
            for tap in range(shift, taps, SUBLANES):
                ks[tap * SUBLANES : (tap + 1) * SUBLANES] = sums[tap // SUBLANES]
        total = ks[pl.ds(0, taps, SUBLANES)]
        for row in range(1, SUBLANES):
            total += ks[pl.ds(row, taps, SUBLANES)]
        kp[chunk, :taps] = total
        return carry

    lax.fori_loop(0, chunks, correlate, 0)
    for piece in range(pieces):
        block = [kp[chunk, tap : tap + 1] for tap in (piece, pieces + piece) for chunk in range(chunks)]
        rows_ref[piece] = jnp.concatenate(block, axis=0).astype(jnp.bfloat16)


def join_kernel(device_ref, keep_ref, given_ref, rows_ref, *slab_refs):
    split = keep_ref.shape[1]
    pieces = slab_refs[0].shape[0]
    for slab, ref in enumerate(slab_refs):
        first = (device_ref[2] ^ slab) * pieces
        for piece in range(pieces):
            total = keep_ref[first + piece].astype(jnp.float32)
            total += given_ref[first + piece].astype(jnp.float32)
            ref[piece, :split] = total.astype(jnp.bfloat16)
            ref[piece, split:] = rows_ref[first + piece]


def write_slabs(slabs, half, me, scratch, weight_hbm, sems):
    count, slab_rows, width = scratch.shape
    copies = []
    for place, (slab, ref) in enumerate(slabs):
        pieces = ref.shape[0]
        group = slab_rows // pieces
        for piece in range(pieces):
            for chunk in range(width // LANES):
                tile = ref[piece, chunk * group : (chunk + 1) * group].astype(jnp.float32)
                scratch[
                    place, piece * group : (piece + 1) * group, chunk * LANES : (chunk + 1) * LANES
                ] = tile
        plane = EARLY_SLABS + LATE_SLABS
        first = pl.multiple_of((half * len(plane) + (me ^ slab)) * slab_rows, slab_rows)
        target = weight_hbm.at[pl.ds(first, slab_rows)]
        copies.append(pltpu.make_async_copy(scratch.at[place], target, sems.at[place]))
        copies[-1].start()
    return copies


def unpack_early_kernel(device_ref, *refs):
    *near_refs, weight_hbm, scratch, sems = refs
    slabs = list(zip(EARLY_SLABS, near_refs))
    for copy in write_slabs(slabs, device_ref[1], device_ref[2], scratch, weight_hbm, sems):
        copy.wait()


def unpack_late_kernel(device_ref, *refs):
    slabs = len(EARLY_SLABS) + len(LATE_SLABS)
    near_refs, far_refs = refs[:slabs], refs[slabs : 2 * slabs]
    weight_hbm, kernel_hbm, scratch, far_scratch, blocks, kernel_ref = refs[2 * slabs + 1 : -3]
    sems, far_sems, kernel_sem = refs[-3:]
    core, me = device_ref[1], device_ref[2]
    late = [(slab, near_refs[slab]) for slab in LATE_SLABS]
    copies = write_slabs(late, core, me, scratch, weight_hbm, sems)
    far = list(enumerate(far_refs))
    copies += write_slabs(far, 1 - core, me, far_scratch, weight_hbm, far_sems)
    pieces, piece_rows, _ = near_refs[0].shape
    taps, width = kernel_ref.shape
    chunks = width // LANES
    size = 2 * chunks
    for slab in range(slabs):
        for piece in range(pieces):
            total = near_refs[slab][piece, piece_rows - size :].astype(jnp.float32)
            total += far_refs[slab][piece, piece_rows - size :].astype(jnp.float32)
            first = pl.multiple_of(((me ^ slab) * pieces + piece) * size, size)
            blocks[pl.ds(first, size)] = total
    for half in range(2):
        first = half * slabs * pieces
        count = min(slabs * pieces, taps - first)
        for chunk in range(chunks):
            columns = slice(chunk * LANES, (chunk + 1) * LANES)
            tap_rows = blocks[pl.ds(half * chunks + chunk, count, size)]
            kernel_ref[first : first + count, columns] = tap_rows
    copies.append(pltpu.make_async_copy(kernel_ref, kernel_hbm, kernel_sem))
    copies[-1].start()
    for copy in copies:
        copy.wait()


def backward_kernel(context, rows, *refs):
    tiles = context + 2
    device_ref, q_ref = refs[:2]
    places = tile_places(rows, *refs[2 : 2 + tiles])
    att_ref, late_ref, early_ref, dhid_ref, w_ref = refs[2 + tiles : 7 + tiles]
    dq_ref, own_ref = refs[7 + tiles : 9 + tiles]
    message_refs = refs[9 + tiles : 9 + tiles + context]
    datt, bias, lse_ref, scores, dprobs, probs, dscores = refs[9 + tiles + context :]

    att = q_ref.shape[1]
    heads = att // HEAD_DIM
    span = context * rows
    scale = 1.0 / math.sqrt(HEAD_DIM)
    start = device_ref[0] * rows

    edge = (late_ref.shape[1] + early_ref.shape[1] - rows) // 2
    log_sums = jnp.concatenate([late_ref[...], early_ref[...]], axis=1)
    lse_ref[...] = log_sums[:, edge : edge + rows]
    for offset in range(context + 1):
        key_id = lax.broadcasted_iota(jnp.int32, (rows, rows), 0)
        row_id = lax.broadcasted_iota(jnp.int32, (rows, rows), 1)
        distance = row_id - key_id + offset * rows
        key_time = key_id + (start - offset * rows)
        visible = (distance >= 0) & (distance < span) & (key_time >= 0)
        bias[offset] = jnp.where(visible, 0.0, NEGATIVE)

    dattended = dot(dhid_ref[...], w_ref[...], NT).astype(jnp.bfloat16)
    datt[...] = dattended
    product = dattended.astype(jnp.float32) * att_ref[...].astype(jnp.float32)
    head_id = lax.broadcasted_iota(jnp.int32, (heads, att), 0)
    feature_id = lax.broadcasted_iota(jnp.int32, (heads, att), 1)
    ours = (feature_id >= head_id * HEAD_DIM) & (feature_id < (head_id + 1) * HEAD_DIM)
    deltas = dot(jnp.where(ours, 1.0, 0.0), product, NT, lax.Precision.HIGHEST)

    for pair in range(att // LANES):
        columns = slice(pair * LANES, (pair + 1) * LANES)
        qs = stack_heads(q_ref[:, columns] * scale)
        ds = stack_heads(datt[:, columns])
        log_sum = [lse_ref[2 * pair + i : 2 * pair + i + 1] for i in (0, 1)]
        delta = [deltas[2 * pair + i : 2 * pair + i + 1] for i in (0, 1)]
        log_sum = jnp.concatenate(log_sum, axis=1)
        delta = jnp.concatenate(delta, axis=1)
        dquery = jnp.zeros((2 * rows, LANES), jnp.float32)
        for offset, (k_ref, k_at, v_ref, v_at) in enumerate(places):
            kp = k_ref[k_at : k_at + rows, columns]
            vp = v_ref[v_at : v_at + rows, columns]
            slot = offset % 2
            scores[slot] = dot(kp, qs, NT)
            dprobs[slot] = dot(vp, ds, NT)
            for first in range(0, rows, CHUNK):
                part = slice(first, first + CHUNK)
                hidden_pairs = jnp.concatenate([bias[offset, part], bias[offset, part]], axis=1)
                chance = jnp.exp(scores[slot, part] + hidden_pairs - log_sum)
                dscore = chance * (dprobs[slot, part] - delta)
                probs[slot, part] = chance.astype(jnp.bfloat16)
                dscores[slot, part] = dscore.astype(jnp.bfloat16)
            dvalue = dot(probs[slot], ds, NN)
            dkey = dot(dscores[slot], qs, NN)
            dquery += dot(dscores[slot], kp, TN)
            target = message_refs[offset - 1] if offset else own_ref
            target[:rows, columns] = dkey.astype(target.dtype)
            target[rows:, columns] = dvalue.astype(target.dtype)
        dq_ref[:, columns] = (merge_heads(dquery) * scale).astype(jnp.bfloat16)


def relay_kernel(device_ref, swapped_ref, message_ref, out_ref):
    odd = lax.rem(device_ref[0], 2).astype(jnp.float32)
    for first in range(0, out_ref.shape[0], CHUNK):
        part = slice(first, first + CHUNK)
        total = message_ref[part].astype(jnp.float32) + swapped_ref[part].astype(jnp.float32) * odd
        out_ref[part] = total.astype(jnp.bfloat16)


def merge_kernel(device_ref, *refs):
    *message_refs, swapped_ref, own_ref, dk_ref, dv_ref = refs
    rows = dk_ref.shape[0]
    even = 1.0 - lax.rem(device_ref[0], 2).astype(jnp.float32)
    for first in range(0, 2 * rows, CHUNK):
        part = slice(first, first + CHUNK)
        total = own_ref[part] + swapped_ref[part].astype(jnp.float32) * even
        for message_ref in message_refs:
            total += message_ref[part].astype(jnp.float32)
        target = dk_ref if first < rows else dv_ref
        at = first % rows
        target[at : at + CHUNK] = total.astype(jnp.bfloat16)


def from_peer(x, mask):
    devices = range(lax.axis_size(PLANE_AXES))
    return lax.ppermute(x, PLANE_AXES, [(i, i ^ mask) for i in devices])


def summed_along(x, axis):
    size, step = lax.axis_size(axis), 1
    while step < size:
        other = lax.ppermute(x, axis, [(i, i ^ step) for i in range(size)])
        x = (x.astype(jnp.float32) + other.astype(jnp.float32)).astype(x.dtype)
        step *= 2
    return x


def other_core(x):
    return lax.ppermute(x, "core", [(0, 1), (1, 0)])


def per_device(queries, key_in, value_in, out_weight, conv_kernel, cotangent):
    bf16, f32 = jnp.bfloat16, jnp.float32
    query, key, value, cot = queries[0], key_in[0], value_in[0], cotangent[0]
    runs = lax.axis_size(RUN_AXES)
    device = lax.axis_index(RUN_AXES).astype(jnp.int32)
    rows, att = query.shape
    width = out_weight.shape[1]
    heads = att // HEAD_DIM
    taps = conv_kernel.shape[0]
    edge = -(-(taps - 1) // 16) * 16
    context = min(CTX_MAX, runs // 4)

    query_rows = rows + 2 * edge
    key_rows = query_rows + context * rows
    chunks = width // LANES
    vmem = pl.BlockSpec(memory_space=pltpu.VMEM)
    smem = pl.BlockSpec(memory_space=pltpu.SMEM)
    hbm = pl.BlockSpec(memory_space=pltpu.HBM)
    params = pltpu.CompilerParams(vmem_limit_bytes=VMEM_LIMIT)

    own, keys, values, packed_query, far, near = pl.pallas_call(
        functools.partial(pack_kernel, edge),
        out_shape=(
            jax.ShapeDtypeStruct((2 * rows, att), bf16),
            jax.ShapeDtypeStruct((rows + edge, att), bf16),
            jax.ShapeDtypeStruct((rows, att), bf16),
            jax.ShapeDtypeStruct((rows, att), bf16),
            jax.ShapeDtypeStruct((2 * edge, att), bf16),
            jax.ShapeDtypeStruct(((3 + width // att) * edge, att), bf16),
        ),
        in_specs=[hbm] * 4,
        out_specs=(vmem,) * 6,
        scratch_shapes=[pltpu.SemaphoreType.DMA((11 + width // att,))],
        compiler_params=params,
        name="pack",
    )(in_hbm(key), in_hbm(value), in_hbm(query), in_hbm(cot))
    further = [shifted(own, offset) for offset in range(2, context + 1)]
    keys = shifted(keys, 1)
    near = shifted(near, -1)
    if further:
        values = pl.pallas_call(
            choose_kernel,
            out_shape=jax.ShapeDtypeStruct((rows, att), bf16),
            in_specs=[smem, vmem, vmem],
            out_specs=vmem,
            compiler_params=params,
            name="choose",
        )(device[None], values, further[0])
        values = lax.ppermute(values, "y", [(0, 1), (1, 0)])
    else:
        values = shifted(values, 1)
    tiles = [own, keys, values, *further]
    far = shifted(far, context + 1)

    pieces = att // 32
    layers = lax.axis_size("z")
    split = pieces == layers * lax.axis_size(PLANE_AXES) and layers & (layers - 1) == 0
    core = lax.axis_index("core").astype(jnp.int32) if split else jnp.int32(0)
    plane = lax.axis_size(PLANE_AXES)
    spot = lax.axis_index(PLANE_AXES).astype(jnp.int32) if split else jnp.int32(0)
    place = jnp.stack([device, core, spot])
    blocks = query_rows // LANES
    pairs = att // LANES
    key_span = context * rows + LANES

    def score(blocks, edge_rows):
        return pl.pallas_call(
            functools.partial(scores_kernel, context, rows, edge, blocks),
            out_shape=(
                jax.ShapeDtypeStruct((len(blocks) * pairs, 2 * LANES, key_span), bf16),
                jax.ShapeDtypeStruct((heads, len(blocks) * LANES), f32),
            ),
            in_specs=[smem] + [vmem] * (3 + context),
            out_specs=(vmem,) * 2,
            scratch_shapes=[
                pltpu.VMEM((query_rows, att), bf16),
                pltpu.VMEM((key_rows, att), bf16),
                pltpu.VMEM((len(blocks) * LANES, LANES), f32),
                pltpu.VMEM((LANES, key_span), f32),
                pltpu.VMEM((2, 2 * LANES, key_span), f32),
            ],
            compiler_params=params,
            cost_estimate=cost(5 * 10**9, 10**7),
            name="scores",
        )(place, packed_query, own, keys, *further, edge_rows)

    early, early_sums = score(list(range(1, blocks)), near)
    late, late_sums = score([0], far)
    out_frames, attended, dhidden, keep, give, hidden, dmixed, held_weight = pl.pallas_call(
        functools.partial(forward_kernel, context, rows, edge, taps),
        out_shape=(
            jax.ShapeDtypeStruct((rows, width), bf16),
            jax.ShapeDtypeStruct((rows, att), bf16),
            jax.ShapeDtypeStruct((rows, width), bf16),
        )
        + (jax.ShapeDtypeStruct((pieces, chunks * 16, LANES), bf16),) * 2
        + (
            jax.ShapeDtypeStruct((chunks, query_rows, LANES), f32),
            jax.ShapeDtypeStruct((chunks, rows + edge + 8, LANES), f32),
            jax.ShapeDtypeStruct((att, width), bf16),
        ),
        in_specs=[smem] + [vmem] * (6 + context) + [hbm] * 3,
        out_specs=(hbm,) + (vmem,) * 7,
        scratch_shapes=[
            pltpu.VMEM((key_rows, att), bf16),
            pltpu.VMEM((query_rows, att), bf16),
            pltpu.VMEM((chunks, rows + edge, LANES), f32),
            pltpu.VMEM((2, pieces, chunks * 16, LANES), bf16),
            pltpu.VMEM((taps, width), f32),
            pltpu.VMEM((rows, width), bf16),
            pltpu.VMEM((rows, width), bf16),
            pltpu.SemaphoreType.DMA((4,)),
        ],
        compiler_params=params,
        cost_estimate=cost(8 * 10**9, 10**7),
        name="forward",
    )(
        place,
        late,
        early,
        *tiles,
        far,
        near,
        in_hbm(out_weight),
        in_hbm(conv_kernel),
        in_hbm(cot),
    )
    kernel_rows = pl.pallas_call(
        functools.partial(kernel_grad_kernel, rows, edge, taps),
        out_shape=jax.ShapeDtypeStruct((pieces, 2 * chunks, LANES), bf16),
        in_specs=[vmem, vmem],
        out_specs=vmem,
        scratch_shapes=[
            pltpu.VMEM((taps * SUBLANES, LANES), f32),
            pltpu.VMEM((chunks, 2 * pieces, LANES), f32),
        ],
        compiler_params=params,
        cost_estimate=cost(2 * 10**9, 3 * 10**6),
        name="kernel_grad",
    )(hidden, dmixed)

    if split:
        slabs = pl.pallas_call(
            join_kernel,
            out_shape=(jax.ShapeDtypeStruct((layers, 18 * chunks, LANES), bf16),) * plane,
            in_specs=[smem] + [vmem] * 3,
            out_specs=(vmem,) * plane,
            compiler_params=params,
            name="join",
        )(place, keep, other_core(give), kernel_rows)
        *slabs, dhidden = lax.optimization_barrier((*slabs, dhidden))
        slabs = [slabs[0]] + [from_peer(slabs[mask], mask) for mask in range(1, plane)]
    query_grad, own_grads, *messages = pl.pallas_call(
        functools.partial(backward_kernel, context, rows),
        out_shape=(
            jax.ShapeDtypeStruct((rows, att), bf16),
            jax.ShapeDtypeStruct((2 * rows, att), f32),
        )
        + (jax.ShapeDtypeStruct((2 * rows, att), bf16),) * context,
        in_specs=[smem] + [vmem] * (8 + context),
        out_specs=(vmem,) * (2 + context),
        scratch_shapes=[
            pltpu.VMEM((rows, att), bf16),
            pltpu.VMEM((context + 1, rows, rows), f32),
            pltpu.VMEM((heads, rows), f32),
            pltpu.VMEM((2, rows, 2 * rows), f32),
            pltpu.VMEM((2, rows, 2 * rows), f32),
            pltpu.VMEM((2, rows, 2 * rows), bf16),
            pltpu.VMEM((2, rows, 2 * rows), bf16),
        ],
        compiler_params=params,
        cost_estimate=cost(6 * 10**9, 10**7),
        name="backward",
    )(place, packed_query, *tiles, attended, late_sums, early_sums, dhidden, held_weight)
    if split:
        mine = sum(slab.astype(f32) for slab in slabs).astype(bf16)
        mine, *messages = lax.optimization_barrier((mine, *messages))
    messages = dict(enumerate(messages, 1))
    if context > 1:
        swapped = lax.ppermute(messages.pop(1), "y", [(0, 1), (1, 0)])
        messages[2] = pl.pallas_call(
            relay_kernel,
            out_shape=jax.ShapeDtypeStruct((2 * rows, att), bf16),
            in_specs=[smem] + [vmem] * 2,
            out_specs=vmem,
            compiler_params=params,
            cost_estimate=cost(25 * 10**9, 10**7),
            name="relay",
        )(place, swapped, messages[2])
    else:
        swapped = jnp.zeros((2 * rows, att), bf16)
    if split:
        mine = summed_along(mine, "z")
        mine, messages = lax.optimization_barrier((mine, messages))
    messages = [shifted(message, -offset) for offset, message in messages.items()]
    if split:
        near_slabs = [mine] + [from_peer(mine, mask) for mask in range(1, plane)]
    key_grad, value_grad = pl.pallas_call(
        merge_kernel,
        out_shape=(jax.ShapeDtypeStruct((rows, att), bf16),) * 2,
        in_specs=[smem] + [vmem] * (2 + len(messages)),
        out_specs=(vmem,) * 2,
        compiler_params=params,
        cost_estimate=cost(16 * 10**9, 10**7),
        name="merge",
    )(place, *messages, swapped, own_grads)
    if split:
        far_slabs = [other_core(slab) for slab in near_slabs]
        far_slabs, key_grad, value_grad = lax.optimization_barrier(
            (far_slabs, key_grad, value_grad)
        )
    else:
        totals = lax.psum((keep, give, kernel_rows), ("x", "core", "z", "y"))
        near_slabs = jnp.concatenate([totals[0], totals[2]], axis=1)
        far_slabs = jnp.concatenate([totals[1], jnp.zeros_like(totals[2])], axis=1)
        near_slabs = jnp.split(near_slabs, plane)
        far_slabs = jnp.split(far_slabs, plane)
    def slab_scratch(count):
        return pltpu.VMEM((count, att // 2 // plane, width), f32)

    weight_total = pl.pallas_call(
        unpack_early_kernel,
        out_shape=jax.ShapeDtypeStruct((att, width), f32),
        in_specs=[smem] + [vmem] * len(EARLY_SLABS),
        out_specs=hbm,
        scratch_shapes=[
            slab_scratch(len(EARLY_SLABS)),
            pltpu.SemaphoreType.DMA((len(EARLY_SLABS),)),
        ],
        compiler_params=params,
        cost_estimate=cost(10**9, 3 * 10**6),
        name="unpack_early",
    )(place, *[near_slabs[slab] for slab in EARLY_SLABS])
    weight_total, kernel_total = pl.pallas_call(
        unpack_late_kernel,
        out_shape=(
            jax.ShapeDtypeStruct((att, width), f32),
            jax.ShapeDtypeStruct((taps, width), f32),
        ),
        in_specs=[smem] + [vmem] * (2 * plane) + [hbm],
        out_specs=(hbm, hbm),
        scratch_shapes=[
            slab_scratch(len(LATE_SLABS)),
            slab_scratch(plane),
            pltpu.VMEM((pieces * 2 * chunks, LANES), f32),
            pltpu.VMEM((taps, width), f32),
            pltpu.SemaphoreType.DMA((len(LATE_SLABS),)),
            pltpu.SemaphoreType.DMA((plane,)),
            pltpu.SemaphoreType.DMA,
        ],
        input_output_aliases={1 + 2 * plane: 0},
        compiler_params=params,
        name="unpack_late",
    )(place, *near_slabs, *far_slabs, weight_total)
    return (
        out_frames[None],
        query_grad[None],
        key_grad[None],
        value_grad[None],
        weight_total,
        kernel_total,
    )


def solution(mesh):
    sizes = (mesh.shape["dp"] // 2, 2, mesh.shape["blk"] // 2, 2)
    fine = Mesh(mesh.devices.reshape(sizes), ("x", "core", "z", "y"))
    frames = P(("x", "core"), RUN_AXES, None)
    return jax.shard_map(
        per_device,
        mesh=fine,
        in_specs=(frames, frames, frames, P(), P(), frames),
        out_specs=(frames, frames, frames, frames, P(), P()),
        check_vma=False,
    )
```

```python
import functools
import math

import jax
import jax.numpy as jnp
from jax import lax
from jax.experimental import pallas as pl
from jax.experimental.pallas import tpu as pltpu
from jax.sharding import Mesh
from jax.sharding import PartitionSpec as P

HEAD_DIM = 64
CTX_MAX = 3
LANES = 128
SUBLANES = 8
NEGATIVE = -1e30
RUN_AXES = ("z", "y")
PLANE_AXES = ("x", "y")
EARLY_SLABS = (0,)
LATE_SLABS = (1, 2, 3)
VMEM_LIMIT = 28 * 1024 * 1024

NN = (((1,), (0,)), ((), ()))
NT = (((1,), (1,)), ((), ()))
TN = (((0,), (0,)), ((), ()))


def dot(a, b, dims, precision=None):
    return lax.dot_general(a, b, dims, precision=precision, preferred_element_type=jnp.float32)


def shifted(x, by):
    devices = range(lax.axis_size(RUN_AXES))
    return lax.ppermute(x, RUN_AXES, [(i, i + by) for i in devices if i + by in devices])


def in_hbm(x):
    return pltpu.with_memory_space_constraint(x, pltpu.HBM)


def cost(flops, data):
    return pl.CostEstimate(flops=flops, bytes_accessed=data, transcendentals=0)


def located(kernel, split):
    def run(*refs):
        device = lax.axis_index("z") * 2 + lax.axis_index("y")
        core = lax.axis_index("core") if split else 0
        spot = lax.axis_index("x") * 2 + lax.axis_index("y") if split else 0
        return kernel((device, core, spot), *refs)

    return run


def head_masks():
    lane = lax.broadcasted_iota(jnp.int32, (1, LANES), 1)
    first = jnp.where(lane < HEAD_DIM, 1.0, 0.0)
    return first.astype(jnp.bfloat16), (1.0 - first).astype(jnp.bfloat16)


def stack_heads(pair):
    first, second = head_masks()
    return jnp.concatenate([pair * first, pair * second], axis=0)


def merge_heads(stacked):
    rows = stacked.shape[0] // 2
    lane = lax.broadcasted_iota(jnp.int32, (rows, LANES), 1)
    return jnp.where(lane < HEAD_DIM, stacked[:rows], stacked[rows:])


def pack_kernel(
    edge,
    k_ref,
    v_ref,
    q_ref,
    cot_ref,
    own_ref,
    keys_ref,
    values_ref,
    queries_ref,
    far_ref,
    near_ref,
    sems,
):
    rows, att = k_ref.shape
    width = cot_ref.shape[1]
    head, tail = pl.ds(0, edge), pl.ds(rows - edge, edge)
    moves = [
        (k_ref, own_ref.at[pl.ds(0, rows)]),
        (v_ref, own_ref.at[pl.ds(rows, rows)]),
        (k_ref, keys_ref.at[pl.ds(0, rows)]),
        (q_ref.at[tail], keys_ref.at[pl.ds(rows, edge)]),
        (v_ref, values_ref),
        (q_ref, queries_ref),
        (k_ref.at[tail], far_ref.at[pl.ds(0, edge)]),
        (v_ref.at[tail], far_ref.at[pl.ds(edge, edge)]),
        (k_ref.at[head], near_ref.at[pl.ds(0, edge)]),
        (v_ref.at[head], near_ref.at[pl.ds(edge, edge)]),
        (q_ref.at[head], near_ref.at[pl.ds(2 * edge, edge)]),
    ]
    for part in range(width // att):
        piece = cot_ref.at[head, pl.ds(part * att, att)]
        moves.append((piece, near_ref.at[pl.ds((3 + part) * edge, edge)]))
    copies = [pltpu.make_async_copy(a, b, sems.at[i]) for i, (a, b) in enumerate(moves)]
    for copy in copies:
        copy.start()
    for copy in copies:
        copy.wait()


def choose_kernel(device_ref, even_ref, odd_ref, out_ref):
    odd = lax.rem(device_ref[0], 2)
    rows = out_ref.shape[0]

    @pl.when(odd == 0)
    def _():
        out_ref[...] = even_ref[...]

    @pl.when(odd != 0)
    def _():
        out_ref[...] = odd_ref[odd_ref.shape[0] - rows :]


def tile_places(rows, own_ref, keys_ref, values_ref, *further_refs):
    places = [(own_ref, 0, own_ref, rows), (keys_ref, 0, values_ref, 0)]
    return places + [(ref, 0, ref, rows) for ref in further_refs]


def score_block(b, place, start, span, qx, kx, bias, weights_ref):
    pairs = qx.shape[1] // LANES
    block = LANES
    keys = span + block
    row_id = lax.broadcasted_iota(jnp.int32, (block, keys), 0)
    key_id = lax.broadcasted_iota(jnp.int32, (block, keys), 1)
    distance = row_id - key_id + span
    key_time = key_id + (start - span + b * block)
    visible = (distance >= 0) & (distance < span) & (key_time >= 0)
    bias[...] = jnp.where(visible, 0.0, NEGATIVE)
    lane_id = lax.broadcasted_iota(jnp.int32, (block, LANES), 1)
    log_sums = jnp.zeros((block, LANES), jnp.float32)
    for pair in range(pairs):
        columns = slice(pair * LANES, (pair + 1) * LANES)
        qs = stack_heads(qx[b * block : (b + 1) * block, columns])
        scores = dot(qs, kx[b * block : b * block + keys, columns], NT)
        hidden_pairs = bias[...]
        scores = scores + jnp.concatenate([hidden_pairs, hidden_pairs], axis=0)
        row_max = jnp.max(scores, axis=1, keepdims=True)
        weights = jnp.exp(scores - row_max)
        row_sum = jnp.sum(weights, axis=1, keepdims=True)
        weights_ref[place * pairs + pair] = (weights * (1.0 / row_sum)).astype(jnp.bfloat16)
        log_sum = row_max + jnp.log(row_sum)
        log_sums = jnp.where(lane_id == 2 * pair, log_sum[:block], log_sums)
        log_sums = jnp.where(lane_id == 2 * pair + 1, log_sum[block:], log_sums)
    return log_sums


def scores_kernel(context, rows, edge, blocks, device_ref, q_ref, *refs):
    own_refs = refs[: 1 + context]
    keys_ref = own_refs[1]
    edge_ref, weights_ref, lse_ref, qx, kx, lx, bias = refs[1 + context :]
    span = context * rows
    scale = 1.0 / math.sqrt(HEAD_DIM)
    start = device_ref[0] * rows - edge
    for offset, ref in enumerate(own_refs):
        first = edge + (context - offset) * rows
        kx[first : first + rows] = ref[:rows]
    qx[edge : edge + rows] = q_ref[...] * scale
    if blocks[0] == 0:
        kx[:edge] = edge_ref[:edge]
        qx[:edge] = keys_ref[rows : rows + edge] * scale
    else:
        kx[edge + span + rows :] = edge_ref[:edge]
        qx[edge + rows :] = edge_ref[2 * edge : 3 * edge] * scale
    for place, b in enumerate(blocks):
        lx[place * LANES : (place + 1) * LANES] = score_block(
            b, place, start, span, qx, kx, bias, weights_ref
        )
    lse_ref[...] = jnp.transpose(lx[...])[: lse_ref.shape[0]]


def forward_kernel(context, rows, edge, taps, *refs):
    tiles = context + 2
    device_ref, late_ref, early_ref = refs[:3]
    places = tile_places(rows, *refs[3 : 3 + tiles])
    far_ref, near_ref, w_hbm, conv_hbm, cot_hbm = refs[3 + tiles : 8 + tiles]
    out_hbm, att_ref, dhid_ref, keep_ref, give_ref, hid, dm, w_ref = refs[8 + tiles : 16 + tiles]
    vx, ax, cotx, parts, conv_ref, cot_ref, out_ref, sems = refs[16 + tiles :]

    att = ax.shape[1]
    width = w_ref.shape[1]
    span = context * rows
    query_rows = rows + 2 * edge
    block = LANES
    keys = span + block
    start = device_ref[0] * rows

    fetches = [
        pltpu.make_async_copy(source, target, sems.at[i])
        for i, (source, target) in enumerate(
            ((w_hbm, w_ref), (cot_hbm, cot_ref), (conv_hbm, conv_ref))
        )
    ]
    for fetch in fetches:
        fetch.start()

    vx[:edge] = far_ref[edge:]
    for offset, (_, _, ref, at) in enumerate(places):
        first = edge + (context - offset) * rows
        vx[first : first + rows] = ref[at : at + rows]
    vx[edge + span + rows :] = near_ref[edge : 2 * edge]

    pairs = att // LANES
    for b in range(query_rows // block):
        for pair in range(pairs):
            columns = slice(pair * LANES, (pair + 1) * LANES)
            values = vx[b * block : b * block + keys, columns]
            weights = early_ref[(b - 1) * pairs + pair] if b else late_ref[pair]
            mixed = dot(weights, values, NN)
            ax[b * block : (b + 1) * block, columns] = merge_heads(mixed).astype(jnp.bfloat16)
    att_ref[...] = ax[edge : edge + rows]

    fetches[0].wait()
    step = 2 * LANES
    for part in range(width // step):
        product = dot(ax[...], w_ref[:, part * step : (part + 1) * step], NN)
        product = product.astype(jnp.bfloat16).astype(jnp.float32)
        time = lax.broadcasted_iota(jnp.int32, product.shape, 0) + (start - edge)
        product = jnp.where(time >= 0, product, 0.0)
        hid[2 * part] = product[:, :LANES]
        hid[2 * part + 1] = product[:, LANES:]

    fetches[1].wait()
    fetches[2].wait()
    for chunk in range(width // LANES):
        columns = slice(chunk * LANES, (chunk + 1) * LANES)
        cotx[chunk, :rows] = cot_ref[:, columns].astype(jnp.float32)
        part, lane = divmod(chunk * LANES, att)
        cotx[chunk, rows:] = near_ref[
            (3 + part) * edge : (4 + part) * edge, lane : lane + LANES
        ].astype(jnp.float32)
    dm[:, rows + edge :] = jnp.zeros_like(dm[:, rows + edge :])

    apart = -(-taps // SUBLANES)
    reach = (apart - 1) * SUBLANES
    part_rows = (rows + edge) // 2

    def convolve(chunk, carry):
        columns = pl.ds(pl.multiple_of(chunk * LANES, LANES), LANES)
        for first in range(0, rows + edge, part_rows):
            mixed = jnp.zeros((part_rows, LANES), jnp.float32)
            for shift in range(SUBLANES):
                low = edge + first - shift - reach
                window = hid[chunk, low : low + part_rows + reach]
                for tap in range(shift, taps, SUBLANES):
                    at = reach - (tap - shift)
                    mixed += conv_ref[tap : tap + 1, columns] * window[at : at + part_rows]
            sigma = jax.nn.sigmoid(mixed)
            kept = min(part_rows, rows - first)
            out_ref[first : first + kept, columns] = (mixed * sigma)[:kept].astype(jnp.bfloat16)
            dm[chunk, first : first + part_rows] = (
                cotx[chunk, first : first + part_rows] * sigma * (1.0 + mixed * (1.0 - sigma))
            )
        part = rows // 2
        for first in range(0, rows, part):
            dhidden = jnp.zeros((part, LANES), jnp.float32)
            for shift in range(SUBLANES):
                low = first + shift
                window = dm[chunk, low : low + part + reach]
                for tap in range(shift, taps, SUBLANES):
                    at = tap - shift
                    dhidden += conv_ref[tap : tap + 1, columns] * window[at : at + part]
            dhid_ref[first : first + part, columns] = dhidden.astype(jnp.bfloat16)
        return carry

    lax.fori_loop(0, width // LANES, convolve, 0)
    store = pltpu.make_async_copy(out_ref, out_hbm, sems.at[3])
    store.start()

    _, pieces, _, _ = parts.shape
    group = att // (2 * pieces)
    core = device_ref[1]
    own = ax[edge : edge + rows]
    for part in range(width // step):
        product = dot(own, dhid_ref[:, part * step : (part + 1) * step], TN).astype(jnp.bfloat16)
        for chunk in (2 * part, 2 * part + 1):
            tile = product[:, (chunk - 2 * part) * LANES : (chunk - 2 * part + 1) * LANES]
            for half in range(2):
                for piece in range(pieces):
                    first = (half * pieces + piece) * group
                    parts[half, piece, chunk * group : (chunk + 1) * group] = tile[
                        first : first + group
                    ]
    keep_ref[...] = parts[core]
    give_ref[...] = parts[1 - core]
    store.wait()


def kernel_grad_kernel(rows, edge, taps, hid, dm, rows_ref, ks, kp):
    chunks = hid.shape[0]
    pieces = rows_ref.shape[0]
    apart = -(-taps // SUBLANES)
    reach = (apart - 1) * SUBLANES
    part = rows // 2
    kp[...] = jnp.zeros_like(kp)

    def correlate(chunk, carry):
        for shift in range(SUBLANES):
            sums = [jnp.zeros((SUBLANES, LANES), jnp.float32)] * apart
            for first in range(0, rows, part):
                low = edge + first - shift - reach
                window = hid[chunk, low : low + part + reach]
                own = dm[chunk, first : first + part]
                for tap in range(shift, taps, SUBLANES):
                    at = reach - (tap - shift)
                    product = (own * window[at : at + part]).reshape(-1, SUBLANES, LANES)
                    sums[tap // SUBLANES] += jnp.sum(product, axis=0)
            for tap in range(shift, taps, SUBLANES):
                ks[tap * SUBLANES : (tap + 1) * SUBLANES] = sums[tap // SUBLANES]
        total = ks[pl.ds(0, taps, SUBLANES)]
        for row in range(1, SUBLANES):
            total += ks[pl.ds(row, taps, SUBLANES)]
        kp[chunk, :taps] = total
        return carry

    lax.fori_loop(0, chunks, correlate, 0)
    for piece in range(pieces):
        block = [kp[chunk, tap : tap + 1] for tap in (piece, pieces + piece) for chunk in range(chunks)]
        rows_ref[piece] = jnp.concatenate(block, axis=0).astype(jnp.bfloat16)


def join_kernel(device_ref, keep_ref, given_ref, rows_ref, *slab_refs):
    split = keep_ref.shape[1]
    pieces = slab_refs[0].shape[0]
    for slab, ref in enumerate(slab_refs):
        first = (device_ref[2] ^ slab) * pieces
        for piece in range(pieces):
            total = keep_ref[first + piece].astype(jnp.float32)
            total += given_ref[first + piece].astype(jnp.float32)
            ref[piece, :split] = total.astype(jnp.bfloat16)
            ref[piece, split:] = rows_ref[first + piece]


def write_slabs(slabs, half, me, scratch, weight_hbm, sems):
    count, slab_rows, width = scratch.shape
    copies = []
    for place, (slab, ref) in enumerate(slabs):
        pieces = ref.shape[0]
        group = slab_rows // pieces
        for piece in range(pieces):
            for chunk in range(width // LANES):
                tile = ref[piece, chunk * group : (chunk + 1) * group].astype(jnp.float32)
                scratch[
                    place, piece * group : (piece + 1) * group, chunk * LANES : (chunk + 1) * LANES
                ] = tile
        plane = EARLY_SLABS + LATE_SLABS
        first = pl.multiple_of((half * len(plane) + (me ^ slab)) * slab_rows, slab_rows)
        target = weight_hbm.at[pl.ds(first, slab_rows)]
        copies.append(pltpu.make_async_copy(scratch.at[place], target, sems.at[place]))
        copies[-1].start()
    return copies


def unpack_early_kernel(device_ref, *refs):
    *near_refs, weight_hbm, scratch, sems = refs
    slabs = list(zip(EARLY_SLABS, near_refs))
    for copy in write_slabs(slabs, device_ref[1], device_ref[2], scratch, weight_hbm, sems):
        copy.wait()


def unpack_late_kernel(device_ref, *refs):
    slabs = len(EARLY_SLABS) + len(LATE_SLABS)
    near_refs, far_refs = refs[:slabs], refs[slabs : 2 * slabs]
    weight_hbm, kernel_hbm, scratch, far_scratch, blocks, kernel_ref = refs[2 * slabs + 1 : -3]
    sems, far_sems, kernel_sem = refs[-3:]
    core, me = device_ref[1], device_ref[2]
    late = [(slab, near_refs[slab]) for slab in LATE_SLABS]
    copies = write_slabs(late, core, me, scratch, weight_hbm, sems)
    far = list(enumerate(far_refs))
    copies += write_slabs(far, 1 - core, me, far_scratch, weight_hbm, far_sems)
    pieces, piece_rows, _ = near_refs[0].shape
    taps, width = kernel_ref.shape
    chunks = width // LANES
    size = 2 * chunks
    for slab in range(slabs):
        for piece in range(pieces):
            total = near_refs[slab][piece, piece_rows - size :].astype(jnp.float32)
            total += far_refs[slab][piece, piece_rows - size :].astype(jnp.float32)
            first = pl.multiple_of(((me ^ slab) * pieces + piece) * size, size)
            blocks[pl.ds(first, size)] = total
    for half in range(2):
        first = half * slabs * pieces
        count = min(slabs * pieces, taps - first)
        for chunk in range(chunks):
            columns = slice(chunk * LANES, (chunk + 1) * LANES)
            tap_rows = blocks[pl.ds(half * chunks + chunk, count, size)]
            kernel_ref[first : first + count, columns] = tap_rows
    copies.append(pltpu.make_async_copy(kernel_ref, kernel_hbm, kernel_sem))
    copies[-1].start()
    for copy in copies:
        copy.wait()


def backward_kernel(context, rows, *refs):
    tiles = context + 2
    device_ref, q_ref = refs[:2]
    places = tile_places(rows, *refs[2 : 2 + tiles])
    att_ref, late_ref, early_ref, dhid_ref, w_ref = refs[2 + tiles : 7 + tiles]
    dq_ref, own_ref = refs[7 + tiles : 9 + tiles]
    message_refs = refs[9 + tiles : 9 + tiles + context]
    datt, bias, lse_ref = refs[9 + tiles + context :]

    att = q_ref.shape[1]
    heads = att // HEAD_DIM
    span = context * rows
    scale = 1.0 / math.sqrt(HEAD_DIM)
    start = device_ref[0] * rows

    edge = (late_ref.shape[1] + early_ref.shape[1] - rows) // 2
    log_sums = jnp.concatenate([late_ref[...], early_ref[...]], axis=1)
    lse_ref[...] = log_sums[:, edge : edge + rows]
    for offset in range(context + 1):
        key_id = lax.broadcasted_iota(jnp.int32, (rows, rows), 0)
        row_id = lax.broadcasted_iota(jnp.int32, (rows, rows), 1)
        distance = row_id - key_id + offset * rows
        key_time = key_id + (start - offset * rows)
        visible = (distance >= 0) & (distance < span) & (key_time >= 0)
        bias[offset] = jnp.where(visible, 0.0, NEGATIVE)

    dattended = dot(dhid_ref[...], w_ref[...], NT).astype(jnp.bfloat16)
    datt[...] = dattended
    product = dattended.astype(jnp.float32) * att_ref[...].astype(jnp.float32)
    head_id = lax.broadcasted_iota(jnp.int32, (heads, att), 0)
    feature_id = lax.broadcasted_iota(jnp.int32, (heads, att), 1)
    ours = (feature_id >= head_id * HEAD_DIM) & (feature_id < (head_id + 1) * HEAD_DIM)
    deltas = dot(jnp.where(ours, 1.0, 0.0), product, NT, lax.Precision.HIGHEST)

    for pair in range(att // LANES):
        columns = slice(pair * LANES, (pair + 1) * LANES)
        qs = stack_heads(q_ref[:, columns] * scale)
        ds = stack_heads(datt[:, columns])
        log_sum = [lse_ref[2 * pair + i : 2 * pair + i + 1] for i in (0, 1)]
        delta = [deltas[2 * pair + i : 2 * pair + i + 1] for i in (0, 1)]
        log_sum = jnp.concatenate(log_sum, axis=1)
        delta = jnp.concatenate(delta, axis=1)
        dquery = jnp.zeros((2 * rows, LANES), jnp.float32)
        for offset, (k_ref, k_at, v_ref, v_at) in enumerate(places):
            kp = k_ref[k_at : k_at + rows, columns]
            vp = v_ref[v_at : v_at + rows, columns]
            hidden_pairs = jnp.concatenate([bias[offset], bias[offset]], axis=1)
            probs = jnp.exp(dot(kp, qs, NT) + hidden_pairs - log_sum)
            dprobs = dot(vp, ds, NT)
            dscores = (probs * (dprobs - delta)).astype(jnp.bfloat16)
            dvalue = dot(probs.astype(jnp.bfloat16), ds, NN)
            dkey = dot(dscores, qs, NN)
            dquery += dot(dscores, kp, TN)
            target = message_refs[offset - 1] if offset else own_ref
            target[:rows, columns] = dkey.astype(target.dtype)
            target[rows:, columns] = dvalue.astype(target.dtype)
        dq_ref[:, columns] = (merge_heads(dquery) * scale).astype(jnp.bfloat16)


def relay_kernel(device_ref, swapped_ref, message_ref, out_ref):
    odd = lax.rem(device_ref[0], 2).astype(jnp.float32)
    swapped = swapped_ref[...].astype(jnp.float32) * odd
    out_ref[...] = (message_ref[...].astype(jnp.float32) + swapped).astype(jnp.bfloat16)


def merge_kernel(device_ref, *refs):
    *message_refs, swapped_ref, own_ref, dk_ref, dv_ref = refs
    rows = dk_ref.shape[0]
    even = 1.0 - lax.rem(device_ref[0], 2).astype(jnp.float32)
    total = swapped_ref[...].astype(jnp.float32) * even
    for message_ref in message_refs:
        total += message_ref[...].astype(jnp.float32)
    total = (total + own_ref[...]).astype(jnp.bfloat16)
    dk_ref[...] = total[:rows]
    dv_ref[...] = total[rows:]


def from_peer(x, mask):
    devices = range(lax.axis_size(PLANE_AXES))
    return lax.ppermute(x, PLANE_AXES, [(i, i ^ mask) for i in devices])


def summed_along(x, axis):
    size, step = lax.axis_size(axis), 1
    while step < size:
        other = lax.ppermute(x, axis, [(i, i ^ step) for i in range(size)])
        x = (x.astype(jnp.float32) + other.astype(jnp.float32)).astype(x.dtype)
        step *= 2
    return x


def other_core(x):
    return lax.ppermute(x, "core", [(0, 1), (1, 0)])


def per_device(queries, key_in, value_in, out_weight, conv_kernel, cotangent):
    bf16, f32 = jnp.bfloat16, jnp.float32
    query, key, value, cot = queries[0], key_in[0], value_in[0], cotangent[0]
    runs = lax.axis_size(RUN_AXES)
    rows, att = query.shape
    width = out_weight.shape[1]
    heads = att // HEAD_DIM
    taps = conv_kernel.shape[0]
    edge = -(-(taps - 1) // 16) * 16
    context = min(CTX_MAX, runs // 4)

    query_rows = rows + 2 * edge
    key_rows = query_rows + context * rows
    chunks = width // LANES
    vmem = pl.BlockSpec(memory_space=pltpu.VMEM)
    hbm = pl.BlockSpec(memory_space=pltpu.HBM)
    params = pltpu.CompilerParams(vmem_limit_bytes=VMEM_LIMIT)

    pieces = att // 32
    layers = lax.axis_size("z")
    split = pieces == layers * lax.axis_size(PLANE_AXES) and layers & (layers - 1) == 0
    plane = lax.axis_size(PLANE_AXES)

    own, keys, values, packed_query, far, near = pl.pallas_call(
        functools.partial(pack_kernel, edge),
        out_shape=(
            jax.ShapeDtypeStruct((2 * rows, att), bf16),
            jax.ShapeDtypeStruct((rows + edge, att), bf16),
            jax.ShapeDtypeStruct((rows, att), bf16),
            jax.ShapeDtypeStruct((rows, att), bf16),
            jax.ShapeDtypeStruct((2 * edge, att), bf16),
            jax.ShapeDtypeStruct(((3 + width // att) * edge, att), bf16),
        ),
        in_specs=[hbm] * 4,
        out_specs=(vmem,) * 6,
        scratch_shapes=[pltpu.SemaphoreType.DMA((11 + width // att,))],
        compiler_params=params,
        name="pack",
    )(in_hbm(key), in_hbm(value), in_hbm(query), in_hbm(cot))
    further = [shifted(own, offset) for offset in range(2, context + 1)]
    keys = shifted(keys, 1)
    near = shifted(near, -1)
    if further:
        values = pl.pallas_call(
            located(choose_kernel, split),
            out_shape=jax.ShapeDtypeStruct((rows, att), bf16),
            in_specs=[vmem, vmem],
            out_specs=vmem,
            compiler_params=params,
            name="choose",
        )(values, further[0])
        values = lax.ppermute(values, "y", [(0, 1), (1, 0)])
    else:
        values = shifted(values, 1)
    tiles = [own, keys, values, *further]
    far = shifted(far, context + 1)

    blocks = query_rows // LANES
    pairs = att // LANES
    key_span = context * rows + LANES

    def score(blocks, edge_rows):
        return pl.pallas_call(
            located(functools.partial(scores_kernel, context, rows, edge, blocks), split),
            out_shape=(
                jax.ShapeDtypeStruct((len(blocks) * pairs, 2 * LANES, key_span), bf16),
                jax.ShapeDtypeStruct((heads, len(blocks) * LANES), f32),
            ),
            in_specs=[vmem] * (3 + context),
            out_specs=(vmem,) * 2,
            scratch_shapes=[
                pltpu.VMEM((query_rows, att), bf16),
                pltpu.VMEM((key_rows, att), bf16),
                pltpu.VMEM((len(blocks) * LANES, LANES), f32),
                pltpu.VMEM((LANES, key_span), f32),
            ],
            compiler_params=params,
            cost_estimate=cost(5 * 10**9, 10**7),
            name="scores",
        )(packed_query, own, keys, *further, edge_rows)

    early, early_sums = score(list(range(1, blocks)), near)
    late, late_sums = score([0], far)
    out_frames, attended, dhidden, keep, give, hidden, dmixed, held_weight = pl.pallas_call(
        located(functools.partial(forward_kernel, context, rows, edge, taps), split),
        out_shape=(
            jax.ShapeDtypeStruct((rows, width), bf16),
            jax.ShapeDtypeStruct((rows, att), bf16),
            jax.ShapeDtypeStruct((rows, width), bf16),
        )
        + (jax.ShapeDtypeStruct((pieces, chunks * 16, LANES), bf16),) * 2
        + (
            jax.ShapeDtypeStruct((chunks, query_rows, LANES), f32),
            jax.ShapeDtypeStruct((chunks, rows + edge + 8, LANES), f32),
            jax.ShapeDtypeStruct((att, width), bf16),
        ),
        in_specs=[vmem] * (6 + context) + [hbm] * 3,
        out_specs=(hbm,) + (vmem,) * 7,
        scratch_shapes=[
            pltpu.VMEM((key_rows, att), bf16),
            pltpu.VMEM((query_rows, att), bf16),
            pltpu.VMEM((chunks, rows + edge, LANES), f32),
            pltpu.VMEM((2, pieces, chunks * 16, LANES), bf16),
            pltpu.VMEM((taps, width), f32),
            pltpu.VMEM((rows, width), bf16),
            pltpu.VMEM((rows, width), bf16),
            pltpu.SemaphoreType.DMA((4,)),
        ],
        compiler_params=params,
        cost_estimate=cost(8 * 10**9, 10**7),
        name="forward",
    )(
        late,
        early,
        *tiles,
        far,
        near,
        in_hbm(out_weight),
        in_hbm(conv_kernel),
        in_hbm(cot),
    )
    kernel_rows = pl.pallas_call(
        functools.partial(kernel_grad_kernel, rows, edge, taps),
        out_shape=jax.ShapeDtypeStruct((pieces, 2 * chunks, LANES), bf16),
        in_specs=[vmem, vmem],
        out_specs=vmem,
        scratch_shapes=[
            pltpu.VMEM((taps * SUBLANES, LANES), f32),
            pltpu.VMEM((chunks, 2 * pieces, LANES), f32),
        ],
        compiler_params=params,
        cost_estimate=cost(2 * 10**9, 3 * 10**6),
        name="kernel_grad",
    )(hidden, dmixed)

    if split:
        slabs = pl.pallas_call(
            located(join_kernel, split),
            out_shape=(jax.ShapeDtypeStruct((layers, 18 * chunks, LANES), bf16),) * plane,
            in_specs=[vmem] * 3,
            out_specs=(vmem,) * plane,
            compiler_params=params,
            name="join",
        )(keep, other_core(give), kernel_rows)
        *slabs, dhidden = lax.optimization_barrier((*slabs, dhidden))
        slabs = [slabs[0]] + [from_peer(slabs[mask], mask) for mask in range(1, plane)]
    query_grad, own_grads, *messages = pl.pallas_call(
        located(functools.partial(backward_kernel, context, rows), split),
        out_shape=(
            jax.ShapeDtypeStruct((rows, att), bf16),
            jax.ShapeDtypeStruct((2 * rows, att), f32),
        )
        + (jax.ShapeDtypeStruct((2 * rows, att), bf16),) * context,
        in_specs=[vmem] * (8 + context),
        out_specs=(vmem,) * (2 + context),
        scratch_shapes=[
            pltpu.VMEM((rows, att), bf16),
            pltpu.VMEM((context + 1, rows, rows), f32),
            pltpu.VMEM((heads, rows), f32),
        ],
        compiler_params=params,
        cost_estimate=cost(6 * 10**9, 10**7),
        name="backward",
    )(packed_query, *tiles, attended, late_sums, early_sums, dhidden, held_weight)
    if split:
        mine = sum(slab.astype(f32) for slab in slabs).astype(bf16)
        mine, *messages = lax.optimization_barrier((mine, *messages))
    messages = dict(enumerate(messages, 1))
    if context > 1:
        swapped = lax.ppermute(messages.pop(1), "y", [(0, 1), (1, 0)])
        messages[2] = pl.pallas_call(
            located(relay_kernel, split),
            out_shape=jax.ShapeDtypeStruct((2 * rows, att), bf16),
            in_specs=[vmem] * 2,
            out_specs=vmem,
            compiler_params=params,
            cost_estimate=cost(25 * 10**9, 10**7),
            name="relay",
        )(swapped, messages[2])
    else:
        swapped = jnp.zeros((2 * rows, att), bf16)
    if split:
        mine = summed_along(mine, "z")
        mine, messages = lax.optimization_barrier((mine, messages))
    messages = [shifted(message, -offset) for offset, message in messages.items()]
    if split:
        near_slabs = [mine] + [from_peer(mine, mask) for mask in range(1, plane)]
    key_grad, value_grad = pl.pallas_call(
        located(merge_kernel, split),
        out_shape=(jax.ShapeDtypeStruct((rows, att), bf16),) * 2,
        in_specs=[vmem] * (2 + len(messages)),
        out_specs=(vmem,) * 2,
        compiler_params=params,
        cost_estimate=cost(16 * 10**9, 10**7),
        name="merge",
    )(*messages, swapped, own_grads)
    if split:
        far_slabs = [other_core(slab) for slab in near_slabs]
        far_slabs, key_grad, value_grad = lax.optimization_barrier(
            (far_slabs, key_grad, value_grad)
        )
    else:
        totals = lax.psum((keep, give, kernel_rows), ("x", "core", "z", "y"))
        near_slabs = jnp.concatenate([totals[0], totals[2]], axis=1)
        far_slabs = jnp.concatenate([totals[1], jnp.zeros_like(totals[2])], axis=1)
        near_slabs = jnp.split(near_slabs, plane)
        far_slabs = jnp.split(far_slabs, plane)
    def slab_scratch(count):
        return pltpu.VMEM((count, att // 2 // plane, width), f32)

    weight_total = pl.pallas_call(
        located(unpack_early_kernel, split),
        out_shape=jax.ShapeDtypeStruct((att, width), f32),
        in_specs=[vmem] * len(EARLY_SLABS),
        out_specs=hbm,
        scratch_shapes=[
            slab_scratch(len(EARLY_SLABS)),
            pltpu.SemaphoreType.DMA((len(EARLY_SLABS),)),
        ],
        compiler_params=params,
        cost_estimate=cost(10**9, 3 * 10**6),
        name="unpack_early",
    )(*[near_slabs[slab] for slab in EARLY_SLABS])
    weight_total, kernel_total = pl.pallas_call(
        located(unpack_late_kernel, split),
        out_shape=(
            jax.ShapeDtypeStruct((att, width), f32),
            jax.ShapeDtypeStruct((taps, width), f32),
        ),
        in_specs=[vmem] * (2 * plane) + [hbm],
        out_specs=(hbm, hbm),
        scratch_shapes=[
            slab_scratch(len(LATE_SLABS)),
            slab_scratch(plane),
            pltpu.VMEM((pieces * 2 * chunks, LANES), f32),
            pltpu.VMEM((taps, width), f32),
            pltpu.SemaphoreType.DMA((len(LATE_SLABS),)),
            pltpu.SemaphoreType.DMA((plane,)),
            pltpu.SemaphoreType.DMA,
        ],
        input_output_aliases={2 * plane: 0},
        compiler_params=params,
        name="unpack_late",
    )(*near_slabs, *far_slabs, weight_total)
    return (
        out_frames[None],
        query_grad[None],
        key_grad[None],
        value_grad[None],
        weight_total,
        kernel_total,
    )


def solution(mesh):
    sizes = (mesh.shape["dp"] // 2, 2, mesh.shape["blk"] // 2, 2)
    fine = Mesh(mesh.devices.reshape(sizes), ("x", "core", "z", "y"))
    frames = P(("x", "core"), RUN_AXES, None)
    return jax.shard_map(
        per_device,
        mesh=fine,
        in_specs=(frames, frames, frames, P(), P(), frames),
        out_specs=(frames, frames, frames, frames, P(), P()),
        check_vma=False,
    )
```

```python
import functools
import math

import jax
import jax.numpy as jnp
from jax import lax
from jax.experimental import pallas as pl
from jax.experimental.pallas import tpu as pltpu
from jax.sharding import Mesh
from jax.sharding import PartitionSpec as P

HEAD_DIM = 64
CTX_MAX = 3
LANES = 128
SUBLANES = 8
NEGATIVE = -1e30
RUN_AXES = ("z", "y")
PLANE_AXES = ("x", "y")
EARLY_SLABS = (0,)
LATE_SLABS = (1, 2, 3)
VMEM_LIMIT = 28 * 1024 * 1024

NN = (((1,), (0,)), ((), ()))
NT = (((1,), (1,)), ((), ()))
TN = (((0,), (0,)), ((), ()))


def dot(a, b, dims, precision=None):
    return lax.dot_general(a, b, dims, precision=precision, preferred_element_type=jnp.float32)


def shifted(x, by):
    devices = range(lax.axis_size(RUN_AXES))
    return lax.ppermute(x, RUN_AXES, [(i, i + by) for i in devices if i + by in devices])


def in_hbm(x):
    return pltpu.with_memory_space_constraint(x, pltpu.HBM)


def cost(flops, data):
    return pl.CostEstimate(flops=flops, bytes_accessed=data, transcendentals=0)


def located(kernel, split):
    def run(*refs):
        device = lax.axis_index("z") * 2 + lax.axis_index("y")
        core = lax.axis_index("core") if split else 0
        spot = lax.axis_index("x") * 2 + lax.axis_index("y") if split else 0
        return kernel((device, core, spot), *refs)

    return run


def head_masks():
    lane = lax.broadcasted_iota(jnp.int32, (1, LANES), 1)
    first = jnp.where(lane < HEAD_DIM, 1.0, 0.0)
    return first.astype(jnp.bfloat16), (1.0 - first).astype(jnp.bfloat16)


def stack_heads(pair):
    first, second = head_masks()
    return jnp.concatenate([pair * first, pair * second], axis=0)


def merge_heads(stacked):
    rows = stacked.shape[0] // 2
    lane = lax.broadcasted_iota(jnp.int32, (rows, LANES), 1)
    return jnp.where(lane < HEAD_DIM, stacked[:rows], stacked[rows:])


def pack_kernel(
    edge,
    k_ref,
    v_ref,
    q_ref,
    cot_ref,
    own_ref,
    keys_ref,
    values_ref,
    queries_ref,
    far_ref,
    near_ref,
    sems,
):
    rows, att = k_ref.shape
    width = cot_ref.shape[1]
    head, tail = pl.ds(0, edge), pl.ds(rows - edge, edge)
    moves = [
        (k_ref, own_ref.at[pl.ds(0, rows)]),
        (v_ref, own_ref.at[pl.ds(rows, rows)]),
        (k_ref, keys_ref.at[pl.ds(0, rows)]),
        (q_ref.at[tail], keys_ref.at[pl.ds(rows, edge)]),
        (v_ref, values_ref),
        (q_ref, queries_ref),
        (k_ref.at[tail], far_ref.at[pl.ds(0, edge)]),
        (v_ref.at[tail], far_ref.at[pl.ds(edge, edge)]),
        (k_ref.at[head], near_ref.at[pl.ds(0, edge)]),
        (v_ref.at[head], near_ref.at[pl.ds(edge, edge)]),
        (q_ref.at[head], near_ref.at[pl.ds(2 * edge, edge)]),
    ]
    for part in range(width // att):
        piece = cot_ref.at[head, pl.ds(part * att, att)]
        moves.append((piece, near_ref.at[pl.ds((3 + part) * edge, edge)]))
    copies = [pltpu.make_async_copy(a, b, sems.at[i]) for i, (a, b) in enumerate(moves)]
    for copy in copies:
        copy.start()
    for copy in copies:
        copy.wait()


def choose_kernel(device_ref, even_ref, odd_ref, out_ref):
    odd = lax.rem(device_ref[0], 2)
    rows = out_ref.shape[0]

    @pl.when(odd == 0)
    def _():
        out_ref[...] = even_ref[...]

    @pl.when(odd != 0)
    def _():
        out_ref[...] = odd_ref[odd_ref.shape[0] - rows :]


def tile_places(rows, own_ref, keys_ref, values_ref, *further_refs):
    places = [(own_ref, 0, own_ref, rows), (keys_ref, 0, values_ref, 0)]
    return places + [(ref, 0, ref, rows) for ref in further_refs]


def score_block(b, place, start, span, qx, kx, bias, weights_ref):
    pairs = qx.shape[1] // LANES
    block = LANES
    keys = span + block
    row_id = lax.broadcasted_iota(jnp.int32, (block, keys), 0)
    key_id = lax.broadcasted_iota(jnp.int32, (block, keys), 1)
    distance = row_id - key_id + span
    key_time = key_id + (start - span + b * block)
    visible = (distance >= 0) & (distance < span) & (key_time >= 0)
    bias[...] = jnp.where(visible, 0.0, NEGATIVE)
    lane_id = lax.broadcasted_iota(jnp.int32, (block, LANES), 1)
    log_sums = jnp.zeros((block, LANES), jnp.float32)
    for pair in range(pairs):
        columns = slice(pair * LANES, (pair + 1) * LANES)
        qs = stack_heads(qx[b * block : (b + 1) * block, columns])
        scores = dot(qs, kx[b * block : b * block + keys, columns], NT)
        hidden_pairs = bias[...]
        scores = scores + jnp.concatenate([hidden_pairs, hidden_pairs], axis=0)
        row_max = jnp.max(scores, axis=1, keepdims=True)
        weights = jnp.exp(scores - row_max)
        row_sum = jnp.sum(weights, axis=1, keepdims=True)
        weights_ref[place * pairs + pair] = (weights * (1.0 / row_sum)).astype(jnp.bfloat16)
        log_sum = row_max + jnp.log(row_sum)
        log_sums = jnp.where(lane_id == 2 * pair, log_sum[:block], log_sums)
        log_sums = jnp.where(lane_id == 2 * pair + 1, log_sum[block:], log_sums)
    return log_sums


def scores_kernel(context, rows, edge, blocks, device_ref, q_ref, *refs):
    own_refs = refs[: 1 + context]
    keys_ref = own_refs[1]
    edge_ref, weights_ref, lse_ref, qx, kx, lx, bias = refs[1 + context :]
    span = context * rows
    scale = 1.0 / math.sqrt(HEAD_DIM)
    start = device_ref[0] * rows - edge
    for offset, ref in enumerate(own_refs):
        first = edge + (context - offset) * rows
        kx[first : first + rows] = ref[:rows]
    qx[edge : edge + rows] = q_ref[...] * scale
    if blocks[0] == 0:
        kx[:edge] = edge_ref[:edge]
        qx[:edge] = keys_ref[rows : rows + edge] * scale
    else:
        kx[edge + span + rows :] = edge_ref[:edge]
        qx[edge + rows :] = edge_ref[2 * edge : 3 * edge] * scale
    for place, b in enumerate(blocks):
        lx[place * LANES : (place + 1) * LANES] = score_block(
            b, place, start, span, qx, kx, bias, weights_ref
        )
    lse_ref[...] = jnp.transpose(lx[...])[: lse_ref.shape[0]]


def forward_kernel(context, rows, edge, taps, *refs):
    tiles = context + 2
    device_ref, late_ref, early_ref = refs[:3]
    places = tile_places(rows, *refs[3 : 3 + tiles])
    far_ref, near_ref, w_hbm, conv_hbm, cot_hbm = refs[3 + tiles : 8 + tiles]
    out_hbm, att_ref, dhid_ref, keep_ref, give_ref, hid, dm, w_ref = refs[8 + tiles : 16 + tiles]
    vx, ax, cotx, parts, conv_ref, cot_ref, out_ref, sems = refs[16 + tiles :]

    att = ax.shape[1]
    width = w_ref.shape[1]
    span = context * rows
    query_rows = rows + 2 * edge
    block = LANES
    keys = span + block
    start = device_ref[0] * rows

    fetches = [
        pltpu.make_async_copy(source, target, sems.at[i])
        for i, (source, target) in enumerate(
            ((w_hbm, w_ref), (cot_hbm, cot_ref), (conv_hbm, conv_ref))
        )
    ]
    for fetch in fetches:
        fetch.start()

    vx[:edge] = far_ref[edge:]
    for offset, (_, _, ref, at) in enumerate(places):
        first = edge + (context - offset) * rows
        vx[first : first + rows] = ref[at : at + rows]
    vx[edge + span + rows :] = near_ref[edge : 2 * edge]

    pairs = att // LANES
    for b in range(query_rows // block):
        for pair in range(pairs):
            columns = slice(pair * LANES, (pair + 1) * LANES)
            values = vx[b * block : b * block + keys, columns]
            weights = early_ref[(b - 1) * pairs + pair] if b else late_ref[pair]
            mixed = dot(weights, values, NN)
            ax[b * block : (b + 1) * block, columns] = merge_heads(mixed).astype(jnp.bfloat16)
    att_ref[...] = ax[edge : edge + rows]

    fetches[0].wait()
    step = 2 * LANES
    for part in range(width // step):
        product = dot(ax[...], w_ref[:, part * step : (part + 1) * step], NN)
        product = product.astype(jnp.bfloat16).astype(jnp.float32)
        time = lax.broadcasted_iota(jnp.int32, product.shape, 0) + (start - edge)
        product = jnp.where(time >= 0, product, 0.0)
        hid[2 * part] = product[:, :LANES]
        hid[2 * part + 1] = product[:, LANES:]

    fetches[1].wait()
    fetches[2].wait()
    for chunk in range(width // LANES):
        columns = slice(chunk * LANES, (chunk + 1) * LANES)
        cotx[chunk, :rows] = cot_ref[:, columns].astype(jnp.float32)
        part, lane = divmod(chunk * LANES, att)
        cotx[chunk, rows:] = near_ref[
            (3 + part) * edge : (4 + part) * edge, lane : lane + LANES
        ].astype(jnp.float32)
    dm[:, rows + edge :] = jnp.zeros_like(dm[:, rows + edge :])

    apart = -(-taps // SUBLANES)
    reach = (apart - 1) * SUBLANES
    part_rows = (rows + edge) // 2

    def convolve(chunk, carry):
        columns = pl.ds(pl.multiple_of(chunk * LANES, LANES), LANES)
        for first in range(0, rows + edge, part_rows):
            mixed = jnp.zeros((part_rows, LANES), jnp.float32)
            for shift in range(SUBLANES):
                low = edge + first - shift - reach
                window = hid[chunk, low : low + part_rows + reach]
                for tap in range(shift, taps, SUBLANES):
                    at = reach - (tap - shift)
                    mixed += conv_ref[tap : tap + 1, columns] * window[at : at + part_rows]
            sigma = jax.nn.sigmoid(mixed)
            kept = min(part_rows, rows - first)
            out_ref[first : first + kept, columns] = (mixed * sigma)[:kept].astype(jnp.bfloat16)
            dm[chunk, first : first + part_rows] = (
                cotx[chunk, first : first + part_rows] * sigma * (1.0 + mixed * (1.0 - sigma))
            )
        part = rows // 2
        for first in range(0, rows, part):
            dhidden = jnp.zeros((part, LANES), jnp.float32)
            for shift in range(SUBLANES):
                low = first + shift
                window = dm[chunk, low : low + part + reach]
                for tap in range(shift, taps, SUBLANES):
                    at = tap - shift
                    dhidden += conv_ref[tap : tap + 1, columns] * window[at : at + part]
            dhid_ref[first : first + part, columns] = dhidden.astype(jnp.bfloat16)
        return carry

    lax.fori_loop(0, width // LANES, convolve, 0, unroll=2)
    store = pltpu.make_async_copy(out_ref, out_hbm, sems.at[3])
    store.start()

    _, pieces, _, _ = parts.shape
    group = att // (2 * pieces)
    core = device_ref[1]
    own = ax[edge : edge + rows]
    for part in range(width // step):
        product = dot(own, dhid_ref[:, part * step : (part + 1) * step], TN).astype(jnp.bfloat16)
        for chunk in (2 * part, 2 * part + 1):
            tile = product[:, (chunk - 2 * part) * LANES : (chunk - 2 * part + 1) * LANES]
            for half in range(2):
                for piece in range(pieces):
                    first = (half * pieces + piece) * group
                    parts[half, piece, chunk * group : (chunk + 1) * group] = tile[
                        first : first + group
                    ]
    keep_ref[...] = parts[core]
    give_ref[...] = parts[1 - core]
    store.wait()


def kernel_grad_kernel(rows, edge, taps, hid, dm, rows_ref, ks, kp):
    chunks = hid.shape[0]
    pieces = rows_ref.shape[0]
    apart = -(-taps // SUBLANES)
    reach = (apart - 1) * SUBLANES
    part = rows // 2
    kp[...] = jnp.zeros_like(kp)

    def correlate(chunk, carry):
        for shift in range(SUBLANES):
            sums = [jnp.zeros((SUBLANES, LANES), jnp.float32)] * apart
            for first in range(0, rows, part):
                low = edge + first - shift - reach
                window = hid[chunk, low : low + part + reach]
                own = dm[chunk, first : first + part]
                for tap in range(shift, taps, SUBLANES):
                    at = reach - (tap - shift)
                    product = (own * window[at : at + part]).reshape(-1, SUBLANES, LANES)
                    sums[tap // SUBLANES] += jnp.sum(product, axis=0)
            for tap in range(shift, taps, SUBLANES):
                ks[tap * SUBLANES : (tap + 1) * SUBLANES] = sums[tap // SUBLANES]
        total = ks[pl.ds(0, taps, SUBLANES)]
        for row in range(1, SUBLANES):
            total += ks[pl.ds(row, taps, SUBLANES)]
        kp[chunk, :taps] = total
        return carry

    lax.fori_loop(0, chunks, correlate, 0, unroll=2)
    for piece in range(pieces):
        block = [kp[chunk, tap : tap + 1] for tap in (piece, pieces + piece) for chunk in range(chunks)]
        rows_ref[piece] = jnp.concatenate(block, axis=0).astype(jnp.bfloat16)


def join_kernel(device_ref, keep_ref, given_ref, rows_ref, *slab_refs):
    split = keep_ref.shape[1]
    pieces = slab_refs[0].shape[0]
    for slab, ref in enumerate(slab_refs):
        first = (device_ref[2] ^ slab) * pieces
        for piece in range(pieces):
            total = keep_ref[first + piece].astype(jnp.float32)
            total += given_ref[first + piece].astype(jnp.float32)
            ref[piece, :split] = total.astype(jnp.bfloat16)
            ref[piece, split:] = rows_ref[first + piece]


def write_slabs(slabs, half, me, scratch, weight_hbm, sems):
    count, slab_rows, width = scratch.shape
    copies = []
    for place, (slab, ref) in enumerate(slabs):
        pieces = ref.shape[0]
        group = slab_rows // pieces
        for piece in range(pieces):
            for chunk in range(width // LANES):
                tile = ref[piece, chunk * group : (chunk + 1) * group].astype(jnp.float32)
                scratch[
                    place, piece * group : (piece + 1) * group, chunk * LANES : (chunk + 1) * LANES
                ] = tile
        plane = EARLY_SLABS + LATE_SLABS
        first = pl.multiple_of((half * len(plane) + (me ^ slab)) * slab_rows, slab_rows)
        target = weight_hbm.at[pl.ds(first, slab_rows)]
        copies.append(pltpu.make_async_copy(scratch.at[place], target, sems.at[place]))
        copies[-1].start()
    return copies


def unpack_early_kernel(device_ref, *refs):
    *near_refs, weight_hbm, scratch, sems = refs
    slabs = list(zip(EARLY_SLABS, near_refs))
    for copy in write_slabs(slabs, device_ref[1], device_ref[2], scratch, weight_hbm, sems):
        copy.wait()


def unpack_late_kernel(device_ref, *refs):
    slabs = len(EARLY_SLABS) + len(LATE_SLABS)
    near_refs, far_refs = refs[:slabs], refs[slabs : 2 * slabs]
    weight_hbm, kernel_hbm, scratch, far_scratch, blocks, kernel_ref = refs[2 * slabs + 1 : -3]
    sems, far_sems, kernel_sem = refs[-3:]
    core, me = device_ref[1], device_ref[2]
    late = [(slab, near_refs[slab]) for slab in LATE_SLABS]
    copies = write_slabs(late, core, me, scratch, weight_hbm, sems)
    far = list(enumerate(far_refs))
    copies += write_slabs(far, 1 - core, me, far_scratch, weight_hbm, far_sems)
    pieces, piece_rows, _ = near_refs[0].shape
    taps, width = kernel_ref.shape
    chunks = width // LANES
    size = 2 * chunks
    for slab in range(slabs):
        for piece in range(pieces):
            total = near_refs[slab][piece, piece_rows - size :].astype(jnp.float32)
            total += far_refs[slab][piece, piece_rows - size :].astype(jnp.float32)
            first = pl.multiple_of(((me ^ slab) * pieces + piece) * size, size)
            blocks[pl.ds(first, size)] = total
    for half in range(2):
        first = half * slabs * pieces
        count = min(slabs * pieces, taps - first)
        for chunk in range(chunks):
            columns = slice(chunk * LANES, (chunk + 1) * LANES)
            tap_rows = blocks[pl.ds(half * chunks + chunk, count, size)]
            kernel_ref[first : first + count, columns] = tap_rows
    copies.append(pltpu.make_async_copy(kernel_ref, kernel_hbm, kernel_sem))
    copies[-1].start()
    for copy in copies:
        copy.wait()


def backward_kernel(context, rows, *refs):
    tiles = context + 2
    device_ref, q_ref = refs[:2]
    places = tile_places(rows, *refs[2 : 2 + tiles])
    att_ref, late_ref, early_ref, dhid_ref, w_ref = refs[2 + tiles : 7 + tiles]
    dq_ref, own_ref = refs[7 + tiles : 9 + tiles]
    message_refs = refs[9 + tiles : 9 + tiles + context]
    datt, bias, lse_ref = refs[9 + tiles + context :]

    att = q_ref.shape[1]
    heads = att // HEAD_DIM
    span = context * rows
    scale = 1.0 / math.sqrt(HEAD_DIM)
    start = device_ref[0] * rows

    edge = (late_ref.shape[1] + early_ref.shape[1] - rows) // 2
    log_sums = jnp.concatenate([late_ref[...], early_ref[...]], axis=1)
    lse_ref[...] = log_sums[:, edge : edge + rows]
    for offset in range(context + 1):
        key_id = lax.broadcasted_iota(jnp.int32, (rows, rows), 0)
        row_id = lax.broadcasted_iota(jnp.int32, (rows, rows), 1)
        distance = row_id - key_id + offset * rows
        key_time = key_id + (start - offset * rows)
        visible = (distance >= 0) & (distance < span) & (key_time >= 0)
        bias[offset] = jnp.where(visible, 0.0, NEGATIVE)

    dattended = dot(dhid_ref[...], w_ref[...], NT).astype(jnp.bfloat16)
    datt[...] = dattended
    product = dattended.astype(jnp.float32) * att_ref[...].astype(jnp.float32)
    head_id = lax.broadcasted_iota(jnp.int32, (heads, att), 0)
    feature_id = lax.broadcasted_iota(jnp.int32, (heads, att), 1)
    ours = (feature_id >= head_id * HEAD_DIM) & (feature_id < (head_id + 1) * HEAD_DIM)
    deltas = dot(jnp.where(ours, 1.0, 0.0), product, NT, lax.Precision.HIGHEST)

    for pair in range(att // LANES):
        columns = slice(pair * LANES, (pair + 1) * LANES)
        qs = stack_heads(q_ref[:, columns] * scale)
        ds = stack_heads(datt[:, columns])
        log_sum = [lse_ref[2 * pair + i : 2 * pair + i + 1] for i in (0, 1)]
        delta = [deltas[2 * pair + i : 2 * pair + i + 1] for i in (0, 1)]
        log_sum = jnp.concatenate(log_sum, axis=1)
        delta = jnp.concatenate(delta, axis=1)
        dquery = jnp.zeros((2 * rows, LANES), jnp.float32)
        for offset, (k_ref, k_at, v_ref, v_at) in enumerate(places):
            kp = k_ref[k_at : k_at + rows, columns]
            vp = v_ref[v_at : v_at + rows, columns]
            hidden_pairs = jnp.concatenate([bias[offset], bias[offset]], axis=1)
            probs = jnp.exp(dot(kp, qs, NT) + hidden_pairs - log_sum)
            dprobs = dot(vp, ds, NT)
            dscores = (probs * (dprobs - delta)).astype(jnp.bfloat16)
            dvalue = dot(probs.astype(jnp.bfloat16), ds, NN)
            dkey = dot(dscores, qs, NN)
            dquery += dot(dscores, kp, TN)
            target = message_refs[offset - 1] if offset else own_ref
            target[:rows, columns] = dkey.astype(target.dtype)
            target[rows:, columns] = dvalue.astype(target.dtype)
        dq_ref[:, columns] = (merge_heads(dquery) * scale).astype(jnp.bfloat16)


def relay_kernel(device_ref, swapped_ref, message_ref, out_ref):
    odd = lax.rem(device_ref[0], 2).astype(jnp.float32)
    swapped = swapped_ref[...].astype(jnp.float32) * odd
    out_ref[...] = (message_ref[...].astype(jnp.float32) + swapped).astype(jnp.bfloat16)


def merge_kernel(device_ref, *refs):
    *message_refs, swapped_ref, own_ref, dk_ref, dv_ref = refs
    rows = dk_ref.shape[0]
    even = 1.0 - lax.rem(device_ref[0], 2).astype(jnp.float32)
    total = swapped_ref[...].astype(jnp.float32) * even
    for message_ref in message_refs:
        total += message_ref[...].astype(jnp.float32)
    total = (total + own_ref[...]).astype(jnp.bfloat16)
    dk_ref[...] = total[:rows]
    dv_ref[...] = total[rows:]


def from_peer(x, mask):
    devices = range(lax.axis_size(PLANE_AXES))
    return lax.ppermute(x, PLANE_AXES, [(i, i ^ mask) for i in devices])


def summed_along(x, axis):
    size, step = lax.axis_size(axis), 1
    while step < size:
        other = lax.ppermute(x, axis, [(i, i ^ step) for i in range(size)])
        x = (x.astype(jnp.float32) + other.astype(jnp.float32)).astype(x.dtype)
        step *= 2
    return x


def other_core(x):
    return lax.ppermute(x, "core", [(0, 1), (1, 0)])


def per_device(queries, key_in, value_in, out_weight, conv_kernel, cotangent):
    bf16, f32 = jnp.bfloat16, jnp.float32
    query, key, value, cot = queries[0], key_in[0], value_in[0], cotangent[0]
    runs = lax.axis_size(RUN_AXES)
    rows, att = query.shape
    width = out_weight.shape[1]
    heads = att // HEAD_DIM
    taps = conv_kernel.shape[0]
    edge = -(-(taps - 1) // 16) * 16
    context = min(CTX_MAX, runs // 4)

    query_rows = rows + 2 * edge
    key_rows = query_rows + context * rows
    chunks = width // LANES
    vmem = pl.BlockSpec(memory_space=pltpu.VMEM)
    hbm = pl.BlockSpec(memory_space=pltpu.HBM)
    params = pltpu.CompilerParams(vmem_limit_bytes=VMEM_LIMIT)

    pieces = att // 32
    layers = lax.axis_size("z")
    split = pieces == layers * lax.axis_size(PLANE_AXES) and layers & (layers - 1) == 0
    plane = lax.axis_size(PLANE_AXES)

    own, keys, values, packed_query, far, near = pl.pallas_call(
        functools.partial(pack_kernel, edge),
        out_shape=(
            jax.ShapeDtypeStruct((2 * rows, att), bf16),
            jax.ShapeDtypeStruct((rows + edge, att), bf16),
            jax.ShapeDtypeStruct((rows, att), bf16),
            jax.ShapeDtypeStruct((rows, att), bf16),
            jax.ShapeDtypeStruct((2 * edge, att), bf16),
            jax.ShapeDtypeStruct(((3 + width // att) * edge, att), bf16),
        ),
        in_specs=[hbm] * 4,
        out_specs=(vmem,) * 6,
        scratch_shapes=[pltpu.SemaphoreType.DMA((11 + width // att,))],
        compiler_params=params,
        name="pack",
    )(in_hbm(key), in_hbm(value), in_hbm(query), in_hbm(cot))
    further = [shifted(own, offset) for offset in range(2, context + 1)]
    keys = shifted(keys, 1)
    near = shifted(near, -1)
    if further:
        values = pl.pallas_call(
            located(choose_kernel, split),
            out_shape=jax.ShapeDtypeStruct((rows, att), bf16),
            in_specs=[vmem, vmem],
            out_specs=vmem,
            compiler_params=params,
            name="choose",
        )(values, further[0])
        values = lax.ppermute(values, "y", [(0, 1), (1, 0)])
    else:
        values = shifted(values, 1)
    tiles = [own, keys, values, *further]
    far = shifted(far, context + 1)

    blocks = query_rows // LANES
    pairs = att // LANES
    key_span = context * rows + LANES

    def score(blocks, edge_rows):
        return pl.pallas_call(
            located(functools.partial(scores_kernel, context, rows, edge, blocks), split),
            out_shape=(
                jax.ShapeDtypeStruct((len(blocks) * pairs, 2 * LANES, key_span), bf16),
                jax.ShapeDtypeStruct((heads, len(blocks) * LANES), f32),
            ),
            in_specs=[vmem] * (3 + context),
            out_specs=(vmem,) * 2,
            scratch_shapes=[
                pltpu.VMEM((query_rows, att), bf16),
                pltpu.VMEM((key_rows, att), bf16),
                pltpu.VMEM((len(blocks) * LANES, LANES), f32),
                pltpu.VMEM((LANES, key_span), f32),
            ],
            compiler_params=params,
            cost_estimate=cost(5 * 10**9, 10**7),
            name="scores",
        )(packed_query, own, keys, *further, edge_rows)

    early, early_sums = score(list(range(1, blocks)), near)
    late, late_sums = score([0], far)
    out_frames, attended, dhidden, keep, give, hidden, dmixed, held_weight = pl.pallas_call(
        located(functools.partial(forward_kernel, context, rows, edge, taps), split),
        out_shape=(
            jax.ShapeDtypeStruct((rows, width), bf16),
            jax.ShapeDtypeStruct((rows, att), bf16),
            jax.ShapeDtypeStruct((rows, width), bf16),
        )
        + (jax.ShapeDtypeStruct((pieces, chunks * 16, LANES), bf16),) * 2
        + (
            jax.ShapeDtypeStruct((chunks, query_rows, LANES), f32),
            jax.ShapeDtypeStruct((chunks, rows + edge + 8, LANES), f32),
            jax.ShapeDtypeStruct((att, width), bf16),
        ),
        in_specs=[vmem] * (6 + context) + [hbm] * 3,
        out_specs=(hbm,) + (vmem,) * 7,
        scratch_shapes=[
            pltpu.VMEM((key_rows, att), bf16),
            pltpu.VMEM((query_rows, att), bf16),
            pltpu.VMEM((chunks, rows + edge, LANES), f32),
            pltpu.VMEM((2, pieces, chunks * 16, LANES), bf16),
            pltpu.VMEM((taps, width), f32),
            pltpu.VMEM((rows, width), bf16),
            pltpu.VMEM((rows, width), bf16),
            pltpu.SemaphoreType.DMA((4,)),
        ],
        compiler_params=params,
        cost_estimate=cost(8 * 10**9, 10**7),
        name="forward",
    )(
        late,
        early,
        *tiles,
        far,
        near,
        in_hbm(out_weight),
        in_hbm(conv_kernel),
        in_hbm(cot),
    )
    kernel_rows = pl.pallas_call(
        functools.partial(kernel_grad_kernel, rows, edge, taps),
        out_shape=jax.ShapeDtypeStruct((pieces, 2 * chunks, LANES), bf16),
        in_specs=[vmem, vmem],
        out_specs=vmem,
        scratch_shapes=[
            pltpu.VMEM((taps * SUBLANES, LANES), f32),
            pltpu.VMEM((chunks, 2 * pieces, LANES), f32),
        ],
        compiler_params=params,
        cost_estimate=cost(2 * 10**9, 3 * 10**6),
        name="kernel_grad",
    )(hidden, dmixed)

    if split:
        slabs = pl.pallas_call(
            located(join_kernel, split),
            out_shape=(jax.ShapeDtypeStruct((layers, 18 * chunks, LANES), bf16),) * plane,
            in_specs=[vmem] * 3,
            out_specs=(vmem,) * plane,
            compiler_params=params,
            name="join",
        )(keep, other_core(give), kernel_rows)
        *slabs, dhidden = lax.optimization_barrier((*slabs, dhidden))
        slabs = [slabs[0]] + [from_peer(slabs[mask], mask) for mask in range(1, plane)]
    query_grad, own_grads, *messages = pl.pallas_call(
        located(functools.partial(backward_kernel, context, rows), split),
        out_shape=(
            jax.ShapeDtypeStruct((rows, att), bf16),
            jax.ShapeDtypeStruct((2 * rows, att), f32),
        )
        + (jax.ShapeDtypeStruct((2 * rows, att), bf16),) * context,
        in_specs=[vmem] * (8 + context),
        out_specs=(vmem,) * (2 + context),
        scratch_shapes=[
            pltpu.VMEM((rows, att), bf16),
            pltpu.VMEM((context + 1, rows, rows), f32),
            pltpu.VMEM((heads, rows), f32),
        ],
        compiler_params=params,
        cost_estimate=cost(6 * 10**9, 10**7),
        name="backward",
    )(packed_query, *tiles, attended, late_sums, early_sums, dhidden, held_weight)
    if split:
        mine = sum(slab.astype(f32) for slab in slabs).astype(bf16)
        mine, *messages = lax.optimization_barrier((mine, *messages))
    messages = dict(enumerate(messages, 1))
    if context > 1:
        swapped = lax.ppermute(messages.pop(1), "y", [(0, 1), (1, 0)])
        messages[2] = pl.pallas_call(
            located(relay_kernel, split),
            out_shape=jax.ShapeDtypeStruct((2 * rows, att), bf16),
            in_specs=[vmem] * 2,
            out_specs=vmem,
            compiler_params=params,
            cost_estimate=cost(25 * 10**9, 10**7),
            name="relay",
        )(swapped, messages[2])
    else:
        swapped = jnp.zeros((2 * rows, att), bf16)
    if split:
        mine = summed_along(mine, "z")
        mine, messages = lax.optimization_barrier((mine, messages))
    messages = [shifted(message, -offset) for offset, message in messages.items()]
    if split:
        near_slabs = [mine] + [from_peer(mine, mask) for mask in range(1, plane)]
    key_grad, value_grad = pl.pallas_call(
        located(merge_kernel, split),
        out_shape=(jax.ShapeDtypeStruct((rows, att), bf16),) * 2,
        in_specs=[vmem] * (2 + len(messages)),
        out_specs=(vmem,) * 2,
        compiler_params=params,
        cost_estimate=cost(16 * 10**9, 10**7),
        name="merge",
    )(*messages, swapped, own_grads)
    if split:
        far_slabs = [other_core(slab) for slab in near_slabs]
        far_slabs, key_grad, value_grad = lax.optimization_barrier(
            (far_slabs, key_grad, value_grad)
        )
    else:
        totals = lax.psum((keep, give, kernel_rows), ("x", "core", "z", "y"))
        near_slabs = jnp.concatenate([totals[0], totals[2]], axis=1)
        far_slabs = jnp.concatenate([totals[1], jnp.zeros_like(totals[2])], axis=1)
        near_slabs = jnp.split(near_slabs, plane)
        far_slabs = jnp.split(far_slabs, plane)
    def slab_scratch(count):
        return pltpu.VMEM((count, att // 2 // plane, width), f32)

    weight_total = pl.pallas_call(
        located(unpack_early_kernel, split),
        out_shape=jax.ShapeDtypeStruct((att, width), f32),
        in_specs=[vmem] * len(EARLY_SLABS),
        out_specs=hbm,
        scratch_shapes=[
            slab_scratch(len(EARLY_SLABS)),
            pltpu.SemaphoreType.DMA((len(EARLY_SLABS),)),
        ],
        compiler_params=params,
        cost_estimate=cost(10**9, 3 * 10**6),
        name="unpack_early",
    )(*[near_slabs[slab] for slab in EARLY_SLABS])
    weight_total, kernel_total = pl.pallas_call(
        located(unpack_late_kernel, split),
        out_shape=(
            jax.ShapeDtypeStruct((att, width), f32),
            jax.ShapeDtypeStruct((taps, width), f32),
        ),
        in_specs=[vmem] * (2 * plane) + [hbm],
        out_specs=(hbm, hbm),
        scratch_shapes=[
            slab_scratch(len(LATE_SLABS)),
            slab_scratch(plane),
            pltpu.VMEM((pieces * 2 * chunks, LANES), f32),
            pltpu.VMEM((taps, width), f32),
            pltpu.SemaphoreType.DMA((len(LATE_SLABS),)),
            pltpu.SemaphoreType.DMA((plane,)),
            pltpu.SemaphoreType.DMA,
        ],
        input_output_aliases={2 * plane: 0},
        compiler_params=params,
        name="unpack_late",
    )(*near_slabs, *far_slabs, weight_total)
    return (
        out_frames[None],
        query_grad[None],
        key_grad[None],
        value_grad[None],
        weight_total,
        kernel_total,
    )


def solution(mesh):
    sizes = (mesh.shape["dp"] // 2, 2, mesh.shape["blk"] // 2, 2)
    fine = Mesh(mesh.devices.reshape(sizes), ("x", "core", "z", "y"))
    frames = P(("x", "core"), RUN_AXES, None)
    return jax.shard_map(
        per_device,
        mesh=fine,
        in_specs=(frames, frames, frames, P(), P(), frames),
        out_specs=(frames, frames, frames, frames, P(), P()),
        check_vma=False,
    )
```
